32 devices in a mesh: dp: 8 (over y, x, core), tp: 4 (over z).
Axes of the slice: x: 2, y: 2, z: 4, core: 2. Of those that a mesh axis runs over, the one named last changes fastest.
Arguments:
- tokens: bfloat16 [16384, 768], P('dp'), may hold values from -6 to 6
- segment_ids: int32 [32, 512], P('dp'), may hold values from 0 to 7, never falling along the last dimension, each value on 1 to 256 neighbouring positions
- pair_order: int32 [256], replicated, may hold values from 0 to 255, each once
- w_query: bfloat16 [768, 768], P(None, 'tp'), may hold values from -0.0546875 to 0.0546875
- w_key: bfloat16 [768, 768], P(None, 'tp'), may hold values from -0.21875 to 0.21875
- w_value: bfloat16 [768, 768], P(None, 'tp'), may hold values from -0.21875 to 0.21875
- w_out: bfloat16 [768, 768], P('tp'), may hold values from -0.625 to 0.625
- rel_bias: float32 [32, 12], P(None, 'tp'), may hold values from -4 to 4
- gain_attn: float32 [768], replicated, may hold values from 0.5 to 1.5
- w_hidden: bfloat16 [768, 3072], P(None, 'tp'), may hold values from -0.21875 to 0.21875
- w_down: bfloat16 [3072, 768], P('tp'), may hold values from -0.109375 to 0.109375
- gain_ffn: float32 [768], replicated, may hold values from 0.5 to 1.5
- gain_final: float32 [768], replicated, may hold values from 0.5 to 1.5
- w_project: bfloat16 [768, 768], replicated, may hold values from -0.21875 to 0.21875
Outputs:
- layer_out: bfloat16 [16384, 768], P('dp')
- d_tokens: float32 [16384, 768], P('dp')
- grad_query: float32 [768, 768], P('dp', 'tp')
- grad_key: float32 [768, 768], P('dp', 'tp')
- grad_value: float32 [768, 768], P('dp', 'tp')
- grad_out: float32 [768, 768], P('tp', 'dp')
- grad_rel_bias: float32 [32, 12], P(None, 'tp')
- grad_gain_attn: float32 [768], P('dp')
- grad_hidden: float32 [768, 3072], P('dp', 'tp')
- grad_down: float32 [3072, 768], P('tp', 'dp')
- grad_gain_ffn: float32 [768], P('dp')
- grad_gain_final: float32 [768], P('dp')
- grad_project: float32 [768, 768], P('dp')
The draws below stay inside these ranges and needn't reach their ends.
Inputs may be any that keep to these rules, and one draw needn't show every extreme that they name: `segment_ids`: within each row the segment numbers never fall, and every number from 0 to 7 appears. `pair_order`: every number appears once.
All inputs are finite; a program needn't handle non-finite values.
Results may differ from the reference program's by a relative error of at most 0.034.
Values may be sent and summed in bfloat16 or wider, within the bound.
No kernel may reach another device: no remote copies, remote signals or barrier semaphores. Data moves between devices by JAX's collectives and lax.ppermute only.
A program may use at most 192 MiB of HBM per device.

```python
import math
import jax
import jax.numpy as jnp
import numpy as np
from jax import lax

D = 768
HEADS = 12
HEAD_DIM = 64
FF = 3072
BUCKETS = 32
MAX_DIST = 128
OUT_DIM = 768
LEN = 512
SEG_ROW = 8
ROWS_DEV = 4
ROWS = 32
TOKENS = 16384
SLOTS = 256
N_TP = 4


def levels(stream_key, extent, pieces, low, largest):
    loudness, own = 1.0, jax.random.fold_in(stream_key, 6)
    for axis_at, shards_of in pieces:
        steps = jnp.exp(jax.random.uniform(jax.random.fold_in(own, axis_at), (shards_of,), jnp.float32, low / len(pieces), largest / len(pieces)))
        loudness = loudness * jnp.repeat(steps, extent[axis_at] // shards_of).reshape([-1 if axis == axis_at else 1 for axis in range(len(extent))])
    return loudness


def length_profile(number_of, total, most, slope):
    portions = [(1 << 20) // math.isqrt(rank ** slope) + 1 for rank in range(2, number_of + 1)]
    spare, counts = total - most - (number_of - 1), [1] * (number_of - 1)
    while spare > 0:
        free = [i for i in range(number_of - 1) if counts[i] < most]
        mass, remaining = sum([portions[i] for i in free]), spare
        for i in free:
            more = min(most - counts[i], max(1, remaining * portions[i] // mass), spare)
            counts[i] = counts[i] + more
            spare = spare - more
    return np.array([most] + counts)


def ragged(rng, amount, total, bound, lean):
    if amount == 2:
        one = jax.random.randint(rng, (), max(1, total - bound), min(bound, total - 1) + 1)
        return jnp.stack([one, total - one])
    tallies = jnp.asarray(length_profile(amount, total, bound, lean), jnp.int32)
    pairs = (amount - 1) // 2
    donor, sink = tallies[1:1 + 2 * pairs:2], tallies[2:2 + 2 * pairs:2]
    slack = jnp.minimum(donor - 1, bound - sink)
    shifted = jax.random.randint(jax.random.fold_in(rng, 1), (pairs,), 0, 1 << 20) % (slack + 1)
    tallies = tallies.at[1:1 + 2 * pairs:2].set(donor - shifted).at[2:2 + 2 * pairs:2].set(sink + shifted)
    return tallies[jax.random.permutation(jax.random.fold_in(rng, 2), amount)]


def centred(own_key, shape, scale, reach, pieces=(), kind=jnp.bfloat16):
    loudness = levels(own_key, shape, pieces, -0.22, 0.18) if pieces else 1.0
    values = jax.random.normal(own_key, shape, jnp.float32) * scale * loudness
    return jnp.minimum(jnp.maximum(values, -reach), reach).astype(kind)


def setup_inputs(seed: int = 0) -> dict:
    keys = jax.random.split(jax.random.key(seed), 15)
    tokens = centred(keys[0], (TOKENS, D), 1.0, 6.0, ((0, 8),))
    segment_ids = jax.vmap(lambda own: jnp.searchsorted(jnp.cumsum(ragged(own, SEG_ROW, LEN, LEN // 2, 1)), jnp.arange(LEN), side="right"))(jax.random.split(keys[1], ROWS)).reshape((ROWS, LEN)).astype(jnp.int32)
    pair_order = jax.random.permutation(keys[2], SLOTS).astype(jnp.int32)
    w_query = centred(keys[3], (D, HEADS * HEAD_DIM), (16 * D) ** -0.5, 0.0546875, ((1, 4),))
    w_key = centred(keys[4], (D, HEADS * HEAD_DIM), D ** -0.5, 0.21875, ((1, 4),))
    w_value = centred(keys[5], (D, HEADS * HEAD_DIM), D ** -0.5, 0.21875, ((1, 4),))
    w_out = centred(keys[6], (HEADS * HEAD_DIM, D), (D // 8) ** -0.5, 0.625, ((0, 4),))
    rel_bias = centred(keys[7], (BUCKETS, HEADS), 1.0, 4.0, ((1, 4),), jnp.float32)
    gain_attn = jnp.clip(1.0 + 0.1 * jax.random.normal(keys[8], (D,), jnp.float32), 0.5, 1.5)
    w_hidden = centred(keys[9], (D, FF), D ** -0.5, 0.21875, ((1, 4),))
    w_down = centred(keys[10], (FF, D), FF ** -0.5, 0.109375, ((0, 4),))
    gain_ffn = jnp.clip(1.0 + 0.1 * jax.random.normal(keys[11], (D,), jnp.float32), 0.5, 1.5)
    gain_final = jnp.clip(1.0 + 0.1 * jax.random.normal(keys[12], (D,), jnp.float32), 0.5, 1.5)
    w_project = centred(keys[13], (D, OUT_DIM), D ** -0.5, 0.21875)
    return dict(tokens=tokens, segment_ids=segment_ids, pair_order=pair_order, w_query=w_query, w_key=w_key, w_value=w_value, w_out=w_out, rel_bias=rel_bias, gain_attn=gain_attn, w_hidden=w_hidden, w_down=w_down, gain_ffn=gain_ffn, gain_final=gain_final, w_project=w_project)


epsilon = 1e-06
logit_scale = 50.0
loss_scale = 128.0
masked_value = -1e+30

@jax.custom_vjp
def low(v):
    return lax.optimization_barrier(v.astype(jnp.bfloat16)).astype(jnp.float32)

@jax.custom_vjp
def low_back(v):
    return v

def low_keep(v):
    return (low(v), None)

def low_pass(kept, grad):
    return (grad,)

def back_keep(v):
    return (v, None)

def back_low(kept, grad):
    return (low(grad),)
low.defvjp(low_keep, low_pass)
low_back.defvjp(back_keep, back_low)

def bucket_table(length, bucket_count, distance):
    half_count = bucket_count // 2
    exact_count = half_count // 2
    offsets = np.arange(length)[None, :] - np.arange(length)[:, None]
    far_side = np.where(offsets > 0, half_count, 0)
    magnitude = np.abs(offsets)
    logged = np.log(np.maximum(magnitude, exact_count) / exact_count) / math.log(distance / exact_count) * (half_count - exact_count)
    far_bucket = np.minimum(exact_count + logged.astype(np.int64), half_count - 1)
    return (far_side + np.where(magnitude < exact_count, magnitude, far_bucket)).astype(np.int32)

def twice(values):
    return low_back(low(values))

def rms(values, gain_vec):
    return values * lax.rsqrt(lax.optimization_barrier(jnp.mean(values * values, -1, keepdims=True)) + epsilon) * gain_vec

def reference(tokens, segment_ids, pair_order, w_query, w_key, w_value, w_out, rel_bias, gain_attn, w_hidden, w_down, gain_ffn, gain_final, w_project):
    highest = lax.Precision.HIGHEST
    bucket_ids = jnp.asarray(bucket_table(LEN, BUCKETS, MAX_DIST))
    group_count = ROWS // ROWS_DEV
    seg_blocks = segment_ids.reshape(group_count, ROWS_DEV, LEN)
    slot_index = jnp.arange(SEG_ROW, dtype=jnp.int32)
    head_cols = HEADS * HEAD_DIM // N_TP

    def forward(x_all, query_w, key_w, value_w, out_w, table, gain_one, hidden_w, down_w, gain_two, gain_end, project_w):
        rel_field = jnp.transpose(jnp.take(table, bucket_ids, axis=0), (2, 0, 1))

        def block(x_block, seg_block):
            groups_here = x_block.shape[0]
            normed_one = low(rms(x_block, gain_one))
            queries = twice(jnp.einsum('gtd,de->gte', normed_one, query_w, precision=highest)).reshape(groups_here, LEN, HEADS, HEAD_DIM)
            key_vecs = twice(jnp.einsum('gtd,de->gte', normed_one, key_w, precision=highest)).reshape(groups_here, LEN, HEADS, HEAD_DIM)
            val_vecs = twice(jnp.einsum('gtd,de->gte', normed_one, value_w, precision=highest)).reshape(groups_here, LEN, HEADS, HEAD_DIM)
            scores = jnp.einsum('gihc,gjhc->ghij', queries, key_vecs, precision=highest) + rel_field[None]
            same_seg = seg_block[:, :, None] == seg_block[:, None, :]
            scores = low_back(jnp.where(same_seg[:, None], scores, masked_value))
            probs = low(jax.nn.softmax(scores, axis=-1))
            context = twice(jnp.einsum('ghij,gjhc->gihc', probs, val_vecs, precision=highest))
            context = context.reshape(groups_here, LEN, N_TP, head_cols)
            partial_out = low(jnp.einsum('gtpk,pkd->gtpd', context, out_w.reshape(N_TP, head_cols, D), precision=highest))
            middle = x_block + low_back(lax.optimization_barrier(jnp.sum(partial_out, axis=2)))
            normed_two = low(rms(middle, gain_two))
            pre_act = low_back(jnp.einsum('gtd,df->gtf', normed_two, hidden_w, precision=highest))
            hidden = low(jax.nn.gelu(pre_act, approximate=True)).reshape(groups_here, LEN, N_TP, FF // N_TP)
            partial_ffn = low(jnp.einsum('gtpf,pfd->gtpd', hidden, down_w.reshape(N_TP, FF // N_TP, D), precision=highest))
            result = middle + low_back(lax.optimization_barrier(jnp.sum(partial_ffn, axis=2)))
            final = rms(result, gain_end)
            member = (seg_block[:, :, None] == slot_index[None, None, :]).astype(jnp.float32)
            pooled = jnp.einsum('gts,gtd->gsd', member, final, precision=highest) / lax.optimization_barrier(jnp.sum(member, axis=1))[:, :, None]
            return (final, pooled)
        step_fn = jax.checkpoint(block)

        def scan_step(carry, inputs):
            return (carry, step_fn(inputs[0], inputs[1]))
        unused, (final_all, pooled_all) = lax.scan(scan_step, None, (x_all, seg_blocks))
        pooled_flat = pooled_all.reshape(SLOTS, D)
        projected = low_back(jnp.dot(low(pooled_flat), project_w, precision=highest))
        unit_vec = projected * lax.rsqrt(lax.optimization_barrier(jnp.sum(projected * projected, -1, keepdims=True)) + epsilon)
        embedded = low(unit_vec)
        self_mask = jnp.eye(SLOTS, dtype=bool)
        similar = jnp.where(self_mask, masked_value, logit_scale * jnp.dot(embedded, embedded.T, precision=highest))
        pair_ids = pair_order // 2
        partner = (pair_ids[:, None] == pair_ids[None, :]) & jnp.logical_not(self_mask)
        slot_terms = jax.nn.logsumexp(similar, axis=-1) - lax.optimization_barrier(jnp.sum(jnp.where(partner, similar, 0.0), axis=-1))
        return (loss_scale * jnp.sum(slot_terms), final_all)
    floats = (tokens.astype(jnp.float32).reshape(group_count, ROWS_DEV, LEN, D), w_query.astype(jnp.float32), w_key.astype(jnp.float32), w_value.astype(jnp.float32), w_out.astype(jnp.float32), rel_bias, gain_attn, w_hidden.astype(jnp.float32), w_down.astype(jnp.float32), gain_ffn, gain_final, w_project.astype(jnp.float32))
    objective, pullback, final_all = jax.vjp(forward, *floats, has_aux=True)
    grads = pullback(jnp.ones_like(objective))
    return (final_all.reshape(TOKENS, D).astype(jnp.bfloat16), grads[0].reshape(TOKENS, D), grads[1], grads[2], grads[3], grads[4], grads[5], grads[6], grads[7], grads[8], grads[9], grads[10], grads[11])
```

```python
import functools
import math

import jax
import jax.numpy as jnp
import numpy as np
from jax import lax
from jax.experimental import pallas as pl
from jax.experimental.pallas import tpu as pltpu
from jax.sharding import PartitionSpec as P

MAX_DIST = 128
SEG_ROW = 8
TILE = 128
VMEM = 52 * 2**20

epsilon = 1e-06
logit_scale = 50.0
loss_scale = 128.0
masked_value = -1e30
highest = lax.Precision.HIGHEST
f32 = jnp.float32
bf16 = jnp.bfloat16

NN = (((1,), (0,)), ((), ()))
NT = (((1,), (1,)), ((), ()))
TN = (((0,), (0,)), ((), ()))


def dg(a, b, dims):
    return lax.dot_general(a, b, dims, preferred_element_type=f32)


def bucket_of(offsets, bucket_count, distance):
    half_count = bucket_count // 2
    exact_count = half_count // 2
    far_side = np.where(offsets > 0, half_count, 0)
    magnitude = np.abs(offsets)
    logged = (
        np.log(np.maximum(magnitude, exact_count) / exact_count)
        / math.log(distance / exact_count)
        * (half_count - exact_count)
    )
    far_bucket = np.minimum(exact_count + logged.astype(np.int64), half_count - 1)
    return (far_side + np.where(magnitude < exact_count, magnitude, far_bucket)).astype(np.int32)


def bias_lanes(bucket_count):
    lanes = np.arange(4 * TILE)
    lanes = np.where(lanes >= 2 * TILE, lanes - 4 * TILE, lanes)
    return np.eye(bucket_count, dtype=np.float32)[bucket_of(-lanes, bucket_count, MAX_DIST)].T


def grad_lanes(bucket_count):
    sub = np.arange(8)[:, None]
    lane = np.arange(4 * TILE)[None, :]
    y = (lane - sub) % (4 * TILE)
    y = np.where(y >= 2 * TILE, y - 4 * TILE, y)
    near = bucket_of(-y, bucket_count, MAX_DIST)
    up = np.full((8, TILE), bucket_of(np.array(MAX_DIST), bucket_count, MAX_DIST))
    down = np.full((8, TILE), bucket_of(np.array(-MAX_DIST), bucket_count, MAX_DIST))
    ids = np.concatenate([near, up, down], 1).reshape(-1)
    return np.eye(bucket_count, dtype=np.float32)[ids]


def spread_bias(vec_ref, bias_s, heads):
    for h in range(heads):
        wide = jnp.broadcast_to(vec_ref[0, h : h + 1, :], (TILE, 4 * TILE))
        bias_s[h] = pltpu.roll(wide, 0, 1, stride=1, stride_axis=0)


def with_bias(tile, offset, h, bias_s, vec_ref):
    if offset == 0:
        return tile + bias_s[h, :, 0:TILE]
    if offset == 1:
        return tile + bias_s[h, :, 3 * TILE : 4 * TILE]
    if offset == -1:
        return tile + bias_s[h, :, TILE : 2 * TILE]
    lane = 2 * TILE + 1 if offset > 1 else 2 * TILE - 1
    return tile + vec_ref[0, h : h + 1, lane : lane + 1]


def masks(seg):
    hot = lax.broadcasted_iota(jnp.int32, (16, seg.shape[-1]), 0) == seg
    return (
        jnp.where(hot, 0.0, masked_value).astype(bf16),
        jnp.where(hot, 1.0, 0.0).astype(bf16),
    )


def attn_kernel(heads, hd, a1_ref, w_ref, vec_ref, seg_ref, *rest):
    qkv_ref, lse_ref, ctx_ref, bias_s = rest[-4:]
    length = a1_ref.shape[0]
    blocks = length // TILE

    @pl.when(pl.program_id(1) == 0)
    def _():
        spread_bias(vec_ref, bias_s, heads)

    qkv_ref[0, 0] = dg(w_ref[0], a1_ref[...], NT).astype(bf16)
    q_mask, k_mask = masks(seg_ref[0])
    ones = jnp.ones((16, length), bf16)
    for h in range(heads):
        q_t = jnp.concatenate([qkv_ref[0, 0, h * hd : (h + 1) * hd], q_mask], 0)
        k_t = jnp.concatenate([qkv_ref[0, 0, (heads + h) * hd : (heads + h + 1) * hd], k_mask], 0)
        v_t = jnp.concatenate(
            [qkv_ref[0, 0, (2 * heads + h) * hd : (2 * heads + h + 1) * hd], ones], 0
        )
        scores = dg(k_t.T, q_t, NN)
        columns = []
        tops = []
        for i in range(blocks):
            tiles = [
                with_bias(
                    scores[j * TILE : (j + 1) * TILE, i * TILE : (i + 1) * TILE],
                    j - i,
                    h,
                    bias_s,
                    vec_ref,
                )
                for j in range(blocks)
            ]
            top = jnp.max(functools.reduce(jnp.maximum, tiles), 0, keepdims=True)
            tops.append(top)
            columns.append(jnp.concatenate([jnp.exp(t - top).astype(bf16) for t in tiles], 0))
        mixed = dg(v_t, jnp.concatenate(columns, 1), NN)
        total = mixed[hd : hd + 1]
        lse_ref[0, 0, h : h + 1, :] = jnp.concatenate(tops, 1) + jnp.log(total)
        ctx_ref[0, 0, h * hd : (h + 1) * hd, :] = (mixed[:hd] / total).astype(bf16)


def attention(a1, weights, vecs, segs, first, slots, earlier=None):
    rows, _, length = segs.shape
    width = a1.shape[1]
    heads = vecs.shape[1]
    hd = width // (4 * heads)
    cols = heads * hd
    count = weights.shape[0]
    grid_spec = dict(
        grid=(count, rows),
        in_specs=[
            pl.BlockSpec((length, width), lambda s, r: (r, 0)),
            pl.BlockSpec((1, 3 * cols, width), lambda s, r: (s, 0, 0)),
            pl.BlockSpec((1, heads, 4 * TILE), lambda s, r: (s, 0, 0)),
            pl.BlockSpec((1, 1, length), lambda s, r: (r, 0, 0)),
        ]
        + ([] if earlier is None else [pl.BlockSpec(memory_space=pl.ANY)] * 3),
        out_specs=[
            pl.BlockSpec((1, 1, 3 * cols, length), lambda s, r: (s + first, r, 0, 0)),
            pl.BlockSpec((1, 1, heads, length), lambda s, r: (s + first, r, 0, 0)),
            pl.BlockSpec((1, 1, cols, length), lambda s, r: (s + first, r, 0, 0)),
        ],
    )
    steps = count * rows
    return pl.pallas_call(
        functools.partial(attn_kernel, heads, hd),
        out_shape=[
            jax.ShapeDtypeStruct((slots, rows, 3 * cols, length), bf16),
            jax.ShapeDtypeStruct((slots, rows, heads, length), f32),
            jax.ShapeDtypeStruct((slots, rows, cols, length), bf16),
        ],
        scratch_shapes=[pltpu.VMEM((heads, TILE, 4 * TILE), f32)],
        input_output_aliases={} if earlier is None else {4: 0, 5: 1, 6: 2},
        compiler_params=pltpu.CompilerParams(vmem_limit_bytes=VMEM),
        cost_estimate=pl.CostEstimate(
            flops=steps * 9 * 10**8, bytes_accessed=steps * 2**21, transcendentals=steps * 10**6
        ),
        name="attention",
        **grid_spec,
    )(a1, weights, vecs, segs, *([] if earlier is None else earlier))


def inv_rms(values):
    return lax.rsqrt(jnp.mean(values * values, -1, keepdims=True) + epsilon)


def mid_kernel(x_ref, ctx_ref, w0_ref, w1_ref, gain_ref, mid_ref, a2_ref):
    parts = [
        dg(ctx_ref[k, 0], w0_ref[...] if k == 0 else w1_ref[k - 1], TN).astype(bf16).astype(f32)
        for k in range(ctx_ref.shape[0])
    ]
    mid = x_ref[...].astype(f32) + tree(parts)
    mid_ref[...] = mid
    a2_ref[...] = (mid * inv_rms(mid) * gain_ref[...]).astype(bf16)


def tree(parts):
    while len(parts) > 1:
        parts = [parts[i] + parts[i + 1] for i in range(0, len(parts), 2)]
    return parts[0]


def middle(x, ctx, own_a, far_a, gain):
    slots, rows, cols, length = ctx.shape
    width = x.shape[1]
    return pl.pallas_call(
        mid_kernel,
        grid=(rows,),
        in_specs=[
            pl.BlockSpec((length, width), lambda r: (r, 0)),
            pl.BlockSpec((slots, 1, cols, length), lambda r: (0, r, 0, 0)),
            pl.BlockSpec((cols, width), lambda r: (3, 0)),
            pl.BlockSpec((slots - 1, cols, width), lambda r: (0, 3, 0)),
            pl.BlockSpec((1, width), lambda r: (0, 0)),
        ],
        out_specs=[pl.BlockSpec((length, width), lambda r: (r, 0))] * 2,
        out_shape=[
            jax.ShapeDtypeStruct(x.shape, f32),
            jax.ShapeDtypeStruct(x.shape, bf16),
        ],
        compiler_params=pltpu.CompilerParams(vmem_limit_bytes=VMEM),
        name="middle",
    )(x, ctx, own_a, far_a, gain)


GELU_A = math.sqrt(2.0 / math.pi)
GELU_B = 0.044715


def gelu_pair(v):
    square = v * v
    t = jnp.tanh(GELU_A * v * (1.0 + GELU_B * square))
    half = 0.5 * (1.0 + t)
    slope = half + 0.5 * v * (1.0 - t * t) * (GELU_A * (1.0 + 3.0 * GELU_B * square))
    return v * half, slope


def ffn_own_kernel(a2_ref, b_ref, c_ref, part_ref, hid_ref, slope_ref):
    hidden, slope = gelu_pair(dg(a2_ref[...], b_ref[...], NN))
    hidden = hidden.astype(bf16)
    hid_ref[...] = hidden
    slope_ref[...] = slope.astype(bf16)
    part_ref[...] = dg(hidden, c_ref[...], NN).astype(bf16)


def ffn_own(a2, own_b, own_c, rows):
    tokens, width = a2.shape
    length = tokens // rows
    units = own_b.shape[1]
    return pl.pallas_call(
        ffn_own_kernel,
        grid=(rows,),
        in_specs=[
            pl.BlockSpec((length, width), lambda r: (r, 0)),
            pl.BlockSpec((width, units), lambda r: (0, 0)),
            pl.BlockSpec((units, width), lambda r: (0, 0)),
        ],
        out_specs=[
            pl.BlockSpec((length, width), lambda r: (r, 0)),
            pl.BlockSpec((length, units), lambda r: (r, 0)),
            pl.BlockSpec((length, units), lambda r: (r, 0)),
        ],
        out_shape=[
            jax.ShapeDtypeStruct((tokens, width), bf16),
            jax.ShapeDtypeStruct((tokens, units), bf16),
            jax.ShapeDtypeStruct((tokens, units), bf16),
        ],
        compiler_params=pltpu.CompilerParams(vmem_limit_bytes=VMEM),
        name="ffn_own",
    )(a2, own_b, own_c)


def ffn_far_kernel(
    row_ref,
    a2_ref,
    mid_ref,
    part_ref,
    own_slope_ref,
    b_ref,
    c_ref,
    gain_ref,
    seg_ref,
    out_ref,
    res_ref,
    pool_ref,
    slope_ref,
):
    mine = pl.program_id(0) == row_ref[0]
    parts = [part_ref[...].astype(f32)]
    for k in range(b_ref.shape[0]):
        hidden, slope = gelu_pair(dg(a2_ref[...], b_ref[k], NN))

        @pl.when(mine)
        def _():
            slope_ref[k + 1] = slope.astype(bf16)

        parts.append(dg(hidden.astype(bf16), c_ref[k], NN).astype(bf16).astype(f32))

    @pl.when(mine)
    def _():
        slope_ref[0] = own_slope_ref[...]

    res = mid_ref[...] + tree(parts)
    res_ref[...] = res
    final = (res * inv_rms(res) * gain_ref[...]).astype(bf16)
    out_ref[...] = final
    seg = seg_ref[0]
    hot = lax.broadcasted_iota(jnp.int32, (SEG_ROW, seg.shape[-1]), 0) == seg
    member = jnp.where(hot, 1.0, 0.0)
    pool_ref[...] = dg(member.astype(bf16), final, NN) / jnp.sum(member, 1, keepdims=True)


def ffn_far(row, a2, mid, part, own_slope, far_b, far_c, gain, segs):
    rows, _, length = segs.shape
    tokens, width = a2.shape
    others, _, units = far_b.shape
    by_row = lambda r, row: (r, 0)
    whole3 = lambda r, row: (0, 0, 0)
    return pl.pallas_call(
        ffn_far_kernel,
        grid_spec=pltpu.PrefetchScalarGridSpec(
            num_scalar_prefetch=1,
            grid=(rows,),
            in_specs=[
                pl.BlockSpec((length, width), by_row),
                pl.BlockSpec((length, width), by_row),
                pl.BlockSpec((length, width), by_row),
                pl.BlockSpec((length, units), by_row),
                pl.BlockSpec((others, width, units), whole3),
                pl.BlockSpec((others, units, width), whole3),
                pl.BlockSpec((1, width), lambda r, row: (0, 0)),
                pl.BlockSpec((1, 1, length), lambda r, row: (r, 0, 0)),
            ],
            out_specs=[
                pl.BlockSpec((length, width), by_row),
                pl.BlockSpec((length, width), by_row),
                pl.BlockSpec((SEG_ROW, width), by_row),
                pl.BlockSpec((others + 1, length, units), whole3),
            ],
        ),
        out_shape=[
            jax.ShapeDtypeStruct((tokens, width), bf16),
            jax.ShapeDtypeStruct((tokens, width), f32),
            jax.ShapeDtypeStruct((rows * SEG_ROW, width), f32),
            jax.ShapeDtypeStruct((others + 1, length, units), bf16),
        ],
        compiler_params=pltpu.CompilerParams(vmem_limit_bytes=VMEM),
        name="ffn_far",
    )(row, a2, mid, part, own_slope, far_b, far_c, gain, segs)


def loss_math(pooled, project, pair_col, pair_row, gain):
    slots = pooled.shape[0]
    projected = dg(pooled, project, NN)
    inv_norm = lax.rsqrt(jnp.sum(projected * projected, -1, keepdims=True) + epsilon)
    unit = projected * inv_norm
    embedded = unit.astype(bf16)
    similar = logit_scale * dg(embedded, embedded, NT)
    rows = lax.broadcasted_iota(jnp.int32, (slots, slots), 0)
    columns = lax.broadcasted_iota(jnp.int32, (slots, slots), 1)
    same = rows == columns
    similar = jnp.where(same, masked_value, similar)
    partner = jnp.where((pair_col == pair_row) & jnp.logical_not(same), 2.0, 0.0)

    def total(axis):
        top = jnp.max(similar, axis, keepdims=True)
        return top + jnp.log(jnp.sum(jnp.exp(similar - top), axis, keepdims=True))

    both = jnp.exp(similar - total(1)) + jnp.exp(similar - total(0)) - partner
    high = both.astype(bf16)
    low = (both - high.astype(f32)).astype(bf16)
    d_unit = (loss_scale * logit_scale) * (dg(high, embedded, NN) + dg(low, embedded, NN))
    d_proj = inv_norm * (d_unit - unit * jnp.sum(d_unit * unit, -1, keepdims=True))
    d_proj = d_proj.astype(bf16)
    d_pooled = dg(d_proj, project, NT)
    d_gain = jnp.sum(d_pooled * pooled.astype(f32), 0, keepdims=True) / gain
    return d_proj, d_pooled, d_gain


def loss_kernel(
    pooled_ref, cols_ref, project_ref, pc_ref, pr_ref, gain_ref, dpool_ref, dproj_ref, dgain_ref
):
    d_proj, d_pooled, d_gain = loss_math(
        pooled_ref[...], project_ref[...], pc_ref[...], pr_ref[...], gain_ref[...]
    )
    dpool_ref[...] = d_pooled
    dproj_ref[...] = dg(cols_ref[...], d_proj, TN)
    dgain_ref[...] = d_gain


def loss_head(pooled, own_cols, project, pairs, gain):
    slots, width = pooled.shape
    pair_col = pairs[:, None]
    pair_row = pairs[None, :]
    if slots > 512:
        d_proj, d_pooled, d_gain = loss_math(pooled, project, pair_col, pair_row, gain)
        return d_pooled, dg(own_cols, d_proj, TN), d_gain
    return pl.pallas_call(
        loss_kernel,
        out_shape=[
            jax.ShapeDtypeStruct((slots, width), f32),
            jax.ShapeDtypeStruct((own_cols.shape[1], project.shape[1]), f32),
            jax.ShapeDtypeStruct((1, width), f32),
        ],
        compiler_params=pltpu.CompilerParams(vmem_limit_bytes=VMEM),
        name="loss_head",
    )(pooled, own_cols, project, pair_col, pair_row, gain)


def d_result_of(res, seg, d_pool, gain):
    hot = lax.broadcasted_iota(jnp.int32, (SEG_ROW, seg.shape[-1]), 0) == seg
    member = jnp.where(hot, 1.0, 0.0)
    per_token = d_pool / jnp.sum(member, 1, keepdims=True)
    high = per_token.astype(bf16)
    low = (per_token - high.astype(f32)).astype(bf16)
    twice = jnp.concatenate([member, member], 0).astype(bf16)
    d_final = dg(twice, jnp.concatenate([high, low], 0), TN)
    scale = inv_rms(res)
    unit = res * scale
    weighted = d_final * gain
    return scale * (weighted - unit * jnp.mean(weighted * unit, -1, keepdims=True))


def ffn_back_kernel(
    row_ref,
    res_ref,
    mid_ref,
    seg_ref,
    dpool_ref,
    gain_end_ref,
    gain_ref,
    slope_ref,
    b_ref,
    c_ref,
    wo_ref,
    dmid_ref,
    dattn_ref,
    dctx_ref,
    dgain_ref,
    dres_s,
    low_s,
    sum_s,
):
    k = pl.program_id(0)

    @pl.when(k == 0)
    def _():
        d_res = d_result_of(res_ref[...], seg_ref[0], dpool_ref[...], gain_end_ref[...])
        dres_s[...] = d_res
        low_s[...] = d_res.astype(bf16)

    d_pre = (dg(low_s[...], c_ref[0], NT) * slope_ref[0].astype(f32)).astype(bf16)
    part = dg(d_pre, b_ref[0], NT)

    @pl.when(k == 0)
    def _():
        sum_s[...] = part

    @pl.when(k > 0)
    def _():
        sum_s[...] += part

    @pl.when(k == pl.num_programs(0) - 1)
    def _():
        mid = mid_ref[...]
        scale = inv_rms(mid)
        unit = mid * scale
        grad = sum_s[...]
        weighted = grad * gain_ref[...]
        d_mid = dres_s[...] + scale * (weighted - unit * jnp.mean(weighted * unit, -1, keepdims=True))
        dgain_ref[...] = jnp.sum(grad * unit, 0, keepdims=True)
        dmid_ref[...] = d_mid
        low = d_mid.astype(bf16)
        dattn_ref[...] = low
        for s in range(wo_ref.shape[0]):
            dctx_ref[s] = dg(wo_ref[s], low, NT).astype(bf16)


def ffn_back(row, res, mid, segs, d_pool, gain_end, gain, slope, all_a, all_b, all_c):
    rows, _, length = segs.shape
    tokens, width = res.shape
    slots, _, units = all_b.shape
    cols = width // 4
    own = lambda k, row: (row[0], 0)
    slot = lambda k, row: (k, 0, 0)
    fixed = lambda k, row: (0, 0)
    return pl.pallas_call(
        ffn_back_kernel,
        grid_spec=pltpu.PrefetchScalarGridSpec(
            num_scalar_prefetch=1,
            grid=(slots,),
            in_specs=[
                pl.BlockSpec((length, width), own),
                pl.BlockSpec((length, width), own),
                pl.BlockSpec((1, 1, length), lambda k, row: (row[0], 0, 0)),
                pl.BlockSpec((SEG_ROW, width), own),
                pl.BlockSpec((1, width), fixed),
                pl.BlockSpec((1, width), fixed),
                pl.BlockSpec((1, length, units), slot),
                pl.BlockSpec((1, width, units), slot),
                pl.BlockSpec((1, units, width), slot),
                pl.BlockSpec((slots, cols, width), lambda k, row: (0, 3, 0)),
            ],
            out_specs=[
                pl.BlockSpec((length, width), fixed),
                pl.BlockSpec((length, width), fixed),
                pl.BlockSpec((slots, cols, length), lambda k, row: (0, 0, 0)),
                pl.BlockSpec((1, width), fixed),
            ],
            scratch_shapes=[
                pltpu.VMEM((length, width), f32),
                pltpu.VMEM((length, width), bf16),
                pltpu.VMEM((length, width), f32),
            ],
        ),
        out_shape=[
            jax.ShapeDtypeStruct((length, width), f32),
            jax.ShapeDtypeStruct((length, width), bf16),
            jax.ShapeDtypeStruct((slots, cols, length), bf16),
            jax.ShapeDtypeStruct((1, width), f32),
        ],
        compiler_params=pltpu.CompilerParams(vmem_limit_bytes=VMEM),
        name="ffn_back",
    )(row, res, mid, segs, d_pool, gain_end, gain, slope, all_b, all_c, all_a)


def fold(tile):
    lanes = tile.shape[1]
    total = tile[0:8]
    for b in range(1, TILE // 8):
        total = total + pltpu.roll(tile[8 * b : 8 * b + 8], lanes - 8 * b, 1)
    return total


def attn_back_kernel(
    heads,
    hd,
    row_ref,
    qkv_ref,
    lse_ref,
    ctx_ref,
    dctx_ref,
    vec_ref,
    seg_ref,
    w_ref,
    x_ref,
    dmid_ref,
    gain_ref,
    dqkv_ref,
    fold_ref,
    dtok_ref,
    dgain_ref,
    bias_s,
    sum_s,
):
    slot = pl.program_id(0)
    length = qkv_ref.shape[-1]
    blocks = length // TILE
    spread_bias(vec_ref, bias_s, heads)
    q_mask, k_mask = masks(seg_ref[0])
    for h in range(heads):
        q_low = qkv_ref[0, 0, h * hd : (h + 1) * hd]
        k_low = qkv_ref[0, 0, (heads + h) * hd : (heads + h + 1) * hd]
        v_low = qkv_ref[0, 0, (2 * heads + h) * hd : (2 * heads + h + 1) * hd]
        dc = dctx_ref[0, h * hd : (h + 1) * hd]
        c = ctx_ref[0, 0, h * hd : (h + 1) * hd]
        delta = jnp.sum(dc.astype(f32) * c.astype(f32), 0, keepdims=True)
        lse = lse_ref[0, 0, h : h + 1]
        scores = dg(
            jnp.concatenate([k_low, k_mask], 0).T, jnp.concatenate([q_low, q_mask], 0), NN
        )
        d_probs = dg(v_low.T, dc, NN)
        probs_cols = []
        score_cols = []
        near = [None, None, None]
        far = [None, None]
        for i in range(blocks):
            at = slice(i * TILE, (i + 1) * TILE)
            probs = []
            grads = []
            for j in range(blocks):
                to = slice(j * TILE, (j + 1) * TILE)
                tile = with_bias(scores[to, at], j - i, h, bias_s, vec_ref)
                prob = jnp.exp(tile - lse[:, at])
                grad = prob * (d_probs[to, at] - delta[:, at])
                probs.append(prob.astype(bf16))
                grads.append(grad.astype(bf16))
                if abs(j - i) <= 1:
                    old = near[j - i + 1]
                    near[j - i + 1] = grad if old is None else old + grad
                else:
                    old = far[int(j < i)]
                    far[int(j < i)] = grad if old is None else old + grad
            probs_cols.append(jnp.concatenate(probs, 0))
            score_cols.append(jnp.concatenate(grads, 0))
        probs = jnp.concatenate(probs_cols, 1)
        grads = jnp.concatenate(score_cols, 1)
        dqkv_ref[0, h * hd : (h + 1) * hd] = dg(k_low, grads, NN).astype(bf16)
        dqkv_ref[0, (heads + h) * hd : (heads + h + 1) * hd] = dg(q_low, grads, NT).astype(bf16)
        dqkv_ref[0, (2 * heads + h) * hd : (2 * heads + h + 1) * hd] = dg(dc, probs, NT).astype(
            bf16
        )
        band = jnp.concatenate([near[1], near[0], jnp.zeros_like(near[0]), near[2]], 1)
        fold_ref[0, h, :, : 4 * TILE] = fold(band)
        for side in range(2):
            total = far[side][0:8]
            for b in range(1, TILE // 8):
                total = total + far[side][8 * b : 8 * b + 8]
            fold_ref[0, h, :, (4 + side) * TILE : (5 + side) * TILE] = total
    part = dg(dqkv_ref[0], w_ref[0], TN)

    @pl.when(slot == 0)
    def _():
        sum_s[...] = part

    @pl.when(slot > 0)
    def _():
        sum_s[...] += part

    @pl.when(slot == pl.num_programs(0) - 1)
    def _():
        x = x_ref[...].astype(f32)
        scale = inv_rms(x)
        unit = x * scale
        grad = sum_s[...]
        weighted = grad * gain_ref[...]
        d_tok = dmid_ref[...] + scale * (weighted - unit * jnp.mean(weighted * unit, -1, keepdims=True))
        dtok_ref[...] = d_tok.astype(bf16)
        dgain_ref[...] = jnp.sum(grad * unit, 0, keepdims=True)


def attn_back(row, qkv, lse, ctx, d_ctx, vecs, segs, all_a, x, d_mid, gain):
    slots, rows, cols3, length = qkv.shape
    heads = lse.shape[2]
    cols = cols3 // 3
    width = x.shape[1]
    own4 = lambda k, row: (k, row[0], 0, 0)
    slot = lambda k, row: (k, 0, 0)
    fixed = lambda k, row: (0, 0)
    return pl.pallas_call(
        functools.partial(attn_back_kernel, heads, cols // heads),
        grid_spec=pltpu.PrefetchScalarGridSpec(
            num_scalar_prefetch=1,
            grid=(slots,),
            in_specs=[
                pl.BlockSpec((1, 1, cols3, length), own4),
                pl.BlockSpec((1, 1, heads, length), own4),
                pl.BlockSpec((1, 1, cols, length), own4),
                pl.BlockSpec((1, cols, length), slot),
                pl.BlockSpec((1, heads, 4 * TILE), slot),
                pl.BlockSpec((1, 1, length), lambda k, row: (row[0], 0, 0)),
                pl.BlockSpec((1, cols3, width), slot),
                pl.BlockSpec((length, width), lambda k, row: (row[0], 0)),
                pl.BlockSpec((length, width), fixed),
                pl.BlockSpec((1, width), fixed),
            ],
            out_specs=[
                pl.BlockSpec((1, cols3, length), slot),
                pl.BlockSpec((1, heads, 8, 6 * TILE), lambda k, row: (k, 0, 0, 0)),
                pl.BlockSpec((length, width), fixed),
                pl.BlockSpec((1, width), fixed),
            ],
            scratch_shapes=[
                pltpu.VMEM((heads, TILE, 4 * TILE), f32),
                pltpu.VMEM((length, width), f32),
            ],
        ),
        out_shape=[
            jax.ShapeDtypeStruct((slots, cols3, length), bf16),
            jax.ShapeDtypeStruct((slots, heads, 8, 6 * TILE), f32),
            jax.ShapeDtypeStruct((length, width), bf16),
            jax.ShapeDtypeStruct((1, width), f32),
        ],
        compiler_params=pltpu.CompilerParams(vmem_limit_bytes=VMEM),
        name="attn_back",
    )(row, qkv, lse, ctx, d_ctx, vecs, segs, all_a, x, d_mid, gain)


def attn_weights_kernel(row_ref, a1_ref, dattn_ref, dqkv_ref, ctx_ref, out_ref, a1_s, dattn_s):
    @pl.when(pl.program_id(0) == 0)
    def _():
        a1_s[...] = a1_ref[...].T
        dattn_s[...] = dattn_ref[...].T

    cols3 = dqkv_ref.shape[1]
    out_ref[0, :, :cols3] = dg(a1_s[...], dqkv_ref[0], NT).astype(bf16)
    out_ref[0, :, cols3:] = dg(dattn_s[...], ctx_ref[0, 0], NT).astype(bf16)


def attn_weights(row, a1, d_attn, d_qkv, ctx):
    slots, cols3, length = d_qkv.shape
    cols = ctx.shape[2]
    width = a1.shape[1]
    return pl.pallas_call(
        attn_weights_kernel,
        grid_spec=pltpu.PrefetchScalarGridSpec(
            num_scalar_prefetch=1,
            grid=(slots,),
            in_specs=[
                pl.BlockSpec((length, width), lambda k, row: (row[0], 0)),
                pl.BlockSpec((length, width), lambda k, row: (0, 0)),
                pl.BlockSpec((1, cols3, length), lambda k, row: (k, 0, 0)),
                pl.BlockSpec((1, 1, cols, length), lambda k, row: (k, row[0], 0, 0)),
            ],
            out_specs=pl.BlockSpec((1, width, cols3 + cols), lambda k, row: (k, 0, 0)),
            scratch_shapes=[pltpu.VMEM((width, length), bf16)] * 2,
        ),
        out_shape=jax.ShapeDtypeStruct((slots, width, cols3 + cols), bf16),
        compiler_params=pltpu.CompilerParams(vmem_limit_bytes=VMEM),
        name="attn_weights",
    )(row, a1, d_attn, d_qkv, ctx)


def ffn_weights_kernel(
    res_ref, seg_ref, dpool_ref, gain_ref, a2_ref, hid_ref, slope_ref, c_ref, out_ref, up_s, down_s
):
    r = pl.program_id(0)
    low = d_result_of(res_ref[...], seg_ref[0], dpool_ref[...], gain_ref[...]).astype(bf16)
    d_pre = (dg(low, c_ref[...], NT) * slope_ref[...].astype(f32)).astype(bf16)
    up = dg(a2_ref[...], d_pre, TN)
    down = dg(low, hid_ref[...], TN)

    @pl.when(r == 0)
    def _():
        up_s[...] = up
        down_s[...] = down

    @pl.when(r > 0)
    def _():
        up_s[...] += up
        down_s[...] += down

    @pl.when(r == pl.num_programs(0) - 1)
    def _():
        out_ref[0] = up_s[...].astype(bf16)
        out_ref[1] = down_s[...].astype(bf16)


def ffn_weights(res, segs, d_pool, gain, a2, hidden, slope, own_c):
    rows, _, length = segs.shape
    width = res.shape[1]
    units = hidden.shape[1]
    by_row = lambda r: (r, 0)
    return pl.pallas_call(
        ffn_weights_kernel,
        grid=(rows,),
        in_specs=[
            pl.BlockSpec((length, width), by_row),
            pl.BlockSpec((1, 1, length), lambda r: (r, 0, 0)),
            pl.BlockSpec((SEG_ROW, width), by_row),
            pl.BlockSpec((1, width), lambda r: (0, 0)),
            pl.BlockSpec((length, width), by_row),
            pl.BlockSpec((length, units), by_row),
            pl.BlockSpec((length, units), by_row),
            pl.BlockSpec((units, width), lambda r: (0, 0)),
        ],
        out_specs=pl.BlockSpec((2, width, units), lambda r: (0, 0, 0)),
        scratch_shapes=[pltpu.VMEM((width, units), f32)] * 2,
        out_shape=jax.ShapeDtypeStruct((2, width, units), bf16),
        compiler_params=pltpu.CompilerParams(vmem_limit_bytes=VMEM),
        name="ffn_weights",
    )(res, segs, d_pool, gain, a2, hidden, slope, own_c)


def shards(
    n_dp,
    n_tp,
    tokens,
    segment_ids,
    pair_order,
    w_query,
    w_key,
    w_value,
    w_out,
    rel_bias,
    gain_attn,
    w_hidden,
    w_down,
    gain_ffn,
    gain_final,
    w_project,
):
    rows, length = segment_ids.shape
    bucket_count, heads = rel_bias.shape
    width = tokens.shape[1]
    dp = lax.axis_index("dp")
    tp = lax.axis_index("tp")
    share = math.gcd(n_dp, 8)
    mates = [[(i, i ^ m) for i in range(n_dp)] for m in range(share)]
    levels = [[(i, i ^ k) for i in range(n_tp)] for k in range(n_tp)]

    def over_dp(value, m):
        return lax.ppermute(value, "dp", mates[m])

    def over_tp(value, k):
        return lax.ppermute(value, "tp", levels[k])

    pack_a = jnp.concatenate([w_query.T, w_key.T, w_value.T, w_out], 0)
    slices = width // share
    low_bits = dp % share

    def fetch(pack):
        mine = lax.dynamic_slice_in_dim(pack, low_bits * slices, slices, 0)
        far = jnp.stack([over_tp(mine, k) for k in range(1, n_tp)])
        if share == 8:
            pieces = {0: far}
            for m in (2, 4, 6):
                pieces[m] = over_dp(far, m)
            for m in (0, 2, 4, 6):
                pieces[m + 1] = over_dp(pieces[m], 1)
        else:
            pieces = {m: over_dp(far, m) if m else far for m in range(share)}
        order = low_bits ^ jnp.arange(share, dtype=jnp.int32)
        stacked = jnp.stack([pieces[m] for m in range(share)])
        sorted_pieces = jnp.take(stacked, order, axis=0)
        return jnp.swapaxes(sorted_pieces, 0, 1).reshape(n_tp - 1, width, pack.shape[1])

    def levels_of(value):
        return jnp.stack([value] + [over_tp(value, k) for k in range(1, n_tp)])

    far_a = fetch(pack_a)
    far_b = fetch(w_hidden)
    far_c = fetch(w_down)
    tables = levels_of(rel_bias)
    vecs = jnp.einsum("kbh,bn->khn", tables, bias_lanes(bucket_count), precision=highest)
    segs = segment_ids[:, None, :]
    row = tp[None].astype(jnp.int32)
    one = gain_attn[None]
    two = gain_ffn[None]
    end = gain_final[None]

    x = tokens.astype(f32)
    a1 = (x * inv_rms(x) * one).astype(bf16)
    state = attention(a1, pack_a[None], vecs[:1], segs, 0, n_tp)
    qkv, lse, ctx = attention(a1, far_a, vecs[1:], segs, 1, n_tp, state)
    mid, a2 = middle(tokens, ctx, pack_a, far_a, two)
    part, hidden, slope = ffn_own(a2, w_hidden, w_down, rows)
    layer_out, res, pooled, slopes = ffn_far(
        row, a2, mid, part, slope, far_b, far_c, end, segs
    )
    pooled_all = lax.all_gather(pooled.astype(bf16), "dp", axis=0, tiled=True)
    block = width // n_dp
    own_cols = lax.dynamic_slice_in_dim(pooled_all, dp * block, block, 1)
    d_pool_all, grad_project, d_gain_end = loss_head(
        pooled_all, own_cols, w_project, pair_order // 2, end
    )
    slots_here = rows * SEG_ROW
    d_pool = lax.dynamic_slice_in_dim(d_pool_all, dp * slots_here, slots_here, 0)
    grad_gain_final = lax.dynamic_slice_in_dim(d_gain_end[0], dp * block, block, 0)

    all_a = jnp.concatenate([pack_a[None], far_a])
    all_b = jnp.concatenate([w_hidden[None], far_b])
    all_c = jnp.concatenate([w_down[None], far_c])
    d_mid, d_attn, d_ctx, d_gain_two = ffn_back(
        row, res, mid, segs, d_pool, end, two, slopes, all_a, all_b, all_c
    )
    d_qkv, folded, d_tok, d_gain_one = attn_back(
        row, qkv, lse, ctx, d_ctx, vecs, segs, all_a, tokens, d_mid, one
    )
    grads_a = attn_weights(row, a1, d_attn, d_qkv, ctx)
    grads_f = ffn_weights(res, segs, d_pool, end, a2, hidden, slope, w_down)

    below, above = [d_tok], [d_tok]
    up = [(i, i + 1) for i in range(n_tp - 1)]
    down = [(i + 1, i) for i in range(n_tp - 1)]
    for _ in range(n_tp - 1):
        below.append(lax.ppermute(below[-1], "tp", up))
        above.append(lax.ppermute(above[-1], "tp", down))
    line = jnp.concatenate(below[::-1] + above[1:])
    d_tokens = lax.dynamic_slice_in_dim(line, (n_tp - 1 - tp) * length, rows * length, 0)
    d_tokens = d_tokens.astype(f32)

    def reduce_dp(value):
        lead = value.shape[:-2]
        parts = value.reshape(lead + (n_dp, block, value.shape[-1]))
        at = len(lead)
        if n_dp != 8:
            summed = lax.psum_scatter(value.astype(f32), "dp", scatter_dimension=at, tiled=True)
            return summed
        parts = parts.reshape(lead + (4, 2, block, value.shape[-1]))
        core = dp % 2
        chip = dp // 2
        keep = lax.dynamic_index_in_dim(parts, core, at + 1, keepdims=False)
        give = lax.dynamic_index_in_dim(parts, 1 - core, at + 1, keepdims=False)
        pair = (keep.astype(f32) + over_dp(give, 1).astype(f32)).astype(bf16)
        took = [lax.dynamic_index_in_dim(pair, chip, at, keepdims=False)]
        for m in (1, 2, 3):
            send = lax.dynamic_index_in_dim(pair, chip ^ m, at, keepdims=False)
            took.append(over_dp(send, 2 * m))
        return tree([t.astype(f32) for t in took])

    own_a = reduce_dp(grads_a).astype(bf16)
    own_f = reduce_dp(grads_f)
    grad_a = tree([own_a[0].astype(f32)] + [over_tp(own_a[k], k).astype(f32) for k in range(1, n_tp)])
    cols = width // 4
    d_rel = jnp.einsum(
        "khn,nb->kbh",
        folded.reshape(n_tp, heads, -1),
        grad_lanes(bucket_count),
        precision=highest,
    )
    d_rel_here = tree([d_rel[0]] + [over_tp(d_rel[k], k) for k in range(1, n_tp)])
    gains = jnp.stack([d_gain_one[0], d_gain_two[0]])
    gains = tree([gains] + [over_tp(gains, k) for k in range(1, n_tp)])
    d_rel_here, gains = lax.psum((d_rel_here, gains), "dp")
    gains = lax.dynamic_slice_in_dim(gains, dp * block, block, 1)
    return (
        layer_out,
        d_tokens,
        grad_a[:, :cols],
        grad_a[:, cols : 2 * cols],
        grad_a[:, 2 * cols : 3 * cols],
        grad_a[:, 3 * cols :].T,
        d_rel_here,
        gains[0],
        own_f[0],
        own_f[1].T,
        gains[1],
        grad_gain_final,
        grad_project,
    )


def solution(mesh):
    placed = (
        P("dp", None),
        P("dp", None),
        P(),
        P(None, "tp"),
        P(None, "tp"),
        P(None, "tp"),
        P("tp", None),
        P(None, "tp"),
        P(),
        P(None, "tp"),
        P("tp", None),
        P(),
        P(),
        P(),
    )
    return jax.shard_map(
        functools.partial(shards, mesh.shape["dp"], mesh.shape["tp"]),
        mesh=mesh,
        in_specs=placed,
        out_specs=(
            P("dp", None),
            P("dp", None),
            P("dp", "tp"),
            P("dp", "tp"),
            P("dp", "tp"),
            P("tp", "dp"),
            P(None, "tp"),
            P("dp"),
            P("dp", "tp"),
            P("tp", "dp"),
            P("dp"),
            P("dp"),
            P("dp", None),
        ),
        check_vma=False,
    )
```

```python
import functools
import math

import jax
import jax.numpy as jnp
import numpy as np
from jax import lax
from jax.experimental import pallas as pl
from jax.experimental.pallas import tpu as pltpu
from jax.sharding import PartitionSpec as P

MAX_DIST = 128
SEG_ROW = 8
TILE = 128
VMEM = 52 * 2**20

epsilon = 1e-06
logit_scale = 50.0
loss_scale = 128.0
masked_value = -1e30
highest = lax.Precision.HIGHEST
f32 = jnp.float32
bf16 = jnp.bfloat16

NN = (((1,), (0,)), ((), ()))
NT = (((1,), (1,)), ((), ()))
TN = (((0,), (0,)), ((), ()))


def dg(a, b, dims):
    return lax.dot_general(a, b, dims, preferred_element_type=f32)


def bucket_of(offsets, bucket_count, distance):
    half_count = bucket_count // 2
    exact_count = half_count // 2
    far_side = np.where(offsets > 0, half_count, 0)
    magnitude = np.abs(offsets)
    logged = (
        np.log(np.maximum(magnitude, exact_count) / exact_count)
        / math.log(distance / exact_count)
        * (half_count - exact_count)
    )
    far_bucket = np.minimum(exact_count + logged.astype(np.int64), half_count - 1)
    return (far_side + np.where(magnitude < exact_count, magnitude, far_bucket)).astype(np.int32)


def cost(flops, moved):
    return pl.CostEstimate(flops=int(flops), bytes_accessed=int(moved), transcendentals=0)


def bias_lanes(bucket_count):
    lanes = np.arange(4 * TILE)
    lanes = np.where(lanes >= 2 * TILE, lanes - 4 * TILE, lanes)
    return np.eye(bucket_count, dtype=np.float32)[bucket_of(-lanes, bucket_count, MAX_DIST)].T


def grad_lanes(bucket_count):
    sub = np.arange(8)[:, None]
    lane = np.arange(4 * TILE)[None, :]
    y = (lane - sub) % (4 * TILE)
    y = np.where(y >= 2 * TILE, y - 4 * TILE, y)
    near = bucket_of(-y, bucket_count, MAX_DIST)
    up = np.full((8, TILE), bucket_of(np.array(MAX_DIST), bucket_count, MAX_DIST))
    down = np.full((8, TILE), bucket_of(np.array(-MAX_DIST), bucket_count, MAX_DIST))
    ids = np.concatenate([near, up, down], 1).reshape(-1)
    return np.eye(bucket_count, dtype=np.float32)[ids]


def bring(place_ref, piece_refs, into, sems):
    slices = piece_refs[0].shape[-2]
    copies = []
    for m, piece in enumerate(piece_refs):
        start = pl.multiple_of(place_ref[m], 16) if slices % 16 == 0 else place_ref[m]
        copy = pltpu.make_async_copy(piece, into.at[:, pl.ds(start, slices), :], sems.at[m])
        copy.start()
        copies.append(copy)
    return copies


def spread_bias(vec_ref, bias_s, heads):
    for h in range(heads):
        wide = jnp.broadcast_to(vec_ref[0, h : h + 1, :], (TILE, 4 * TILE))
        bias_s[h] = pltpu.roll(wide, 0, 1, stride=1, stride_axis=0)


def with_bias(tile, offset, h, bias_s, vec_ref):
    if offset == 0:
        return tile + bias_s[h, :, 0:TILE]
    if offset == 1:
        return tile + bias_s[h, :, 3 * TILE : 4 * TILE]
    if offset == -1:
        return tile + bias_s[h, :, TILE : 2 * TILE]
    lane = 2 * TILE + 1 if offset > 1 else 2 * TILE - 1
    return tile + vec_ref[0, h : h + 1, lane : lane + 1]


def masks(seg):
    hot = lax.broadcasted_iota(jnp.int32, (16, seg.shape[-1]), 0) == seg
    return (
        jnp.where(hot, 0.0, masked_value).astype(bf16),
        jnp.where(hot, 1.0, 0.0).astype(bf16),
    )


def inv_rms(values):
    return lax.rsqrt(jnp.mean(values * values, -1, keepdims=True) + epsilon)


def rounded(value):
    return lax.reduce_precision(value, 8, 7)


def tree(parts):
    while len(parts) > 1:
        parts = [parts[i] + parts[i + 1] for i in range(0, len(parts), 2)]
    return parts[0]


def pack_kernel(q_ref, k_ref, v_ref, o_ref, out_ref):
    cols = q_ref.shape[1]
    for at, ref in enumerate((q_ref, k_ref, v_ref)):
        out_ref[at * cols : (at + 1) * cols] = ref[...].T
    out_ref[3 * cols :] = o_ref[...]


def pack_weights(w_query, w_key, w_value, w_out):
    width = w_query.shape[0]
    return pl.pallas_call(
        pack_kernel,
        out_shape=jax.ShapeDtypeStruct((width, width), bf16),
        compiler_params=pltpu.CompilerParams(vmem_limit_bytes=VMEM),
        cost_estimate=cost(10**9, 2**20),
        name="pack_weights",
    )(w_query, w_key, w_value, w_out)


def stack_kernel(*refs):
    for at, ref in enumerate(refs[:-1]):
        refs[-1][at] = ref[...]


def stack(arrays):
    return pl.pallas_call(
        stack_kernel,
        out_shape=jax.ShapeDtypeStruct((len(arrays),) + arrays[0].shape, arrays[0].dtype),
        cost_estimate=cost(0, 2 * len(arrays) * arrays[0].size * 2),
        name="stack",
    )(*arrays)


def attend_row(heads, hd, weights, a1_ref, vec_ref, seg_ref, qkv_ref, lse_ref, ctx_ref, bias_s):
    length = a1_ref.shape[0]
    blocks = length // TILE

    @pl.when(pl.program_id(1) == 0)
    def _():
        spread_bias(vec_ref, bias_s, heads)

    qkv_ref[0, 0] = dg(weights, a1_ref[...], NT).astype(bf16)
    q_mask, k_mask = masks(seg_ref[0])
    ones = jnp.ones((16, length), bf16)
    for h in range(heads):
        q_t = jnp.concatenate([qkv_ref[0, 0, h * hd : (h + 1) * hd], q_mask], 0)
        k_t = jnp.concatenate([qkv_ref[0, 0, (heads + h) * hd : (heads + h + 1) * hd], k_mask], 0)
        v_t = jnp.concatenate(
            [qkv_ref[0, 0, (2 * heads + h) * hd : (2 * heads + h + 1) * hd], ones], 0
        )
        scores = dg(k_t.T, q_t, NN)
        columns = []
        tops = []
        for i in range(blocks):
            tiles = [
                with_bias(
                    scores[j * TILE : (j + 1) * TILE, i * TILE : (i + 1) * TILE],
                    j - i,
                    h,
                    bias_s,
                    vec_ref,
                )
                for j in range(blocks)
            ]
            top = jnp.max(functools.reduce(jnp.maximum, tiles), 0, keepdims=True)
            tops.append(top)
            columns.append(jnp.concatenate([jnp.exp(t - top).astype(bf16) for t in tiles], 0))
        mixed = dg(v_t, jnp.concatenate(columns, 1), NN)
        total = mixed[hd : hd + 1]
        lse_ref[0, 0, h : h + 1, :] = jnp.concatenate(tops, 1) + jnp.log(total)
        ctx_ref[0, 0, h * hd : (h + 1) * hd, :] = (mixed[:hd] / total).astype(bf16)


def attn_own_kernel(heads, hd, a1_ref, vec_ref, seg_ref, w_ref, *rest):
    attend_row(heads, hd, w_ref[: 3 * heads * hd], a1_ref, vec_ref, seg_ref, *rest)


def attn_far_kernel(heads, hd, count, place_ref, a1_ref, vec_ref, seg_ref, own_ref, *rest):
    pieces = rest[:count]
    qkv_ref, lse_ref, ctx_ref, sorted_ref, bias_s, w_s, sems, out_sems = rest[count + 3 :]
    s, r = pl.program_id(0), pl.program_id(1)
    keep = [
        pltpu.make_async_copy(own_ref, sorted_ref.at[0], out_sems.at[0]),
        pltpu.make_async_copy(w_s, sorted_ref.at[pl.ds(1, w_s.shape[0])], out_sems.at[1]),
    ]

    @pl.when((s == 0) & (r == 0))
    def _():
        for copy in bring(place_ref, pieces, w_s, sems):
            copy.wait()
        for copy in keep:
            copy.start()

    attend_row(
        heads,
        hd,
        w_s[s, : 3 * heads * hd],
        a1_ref,
        vec_ref,
        seg_ref,
        qkv_ref,
        lse_ref,
        ctx_ref,
        bias_s,
    )

    @pl.when((s == pl.num_programs(0) - 1) & (r == pl.num_programs(1) - 1))
    def _():
        for copy in keep:
            copy.wait()


def attention(a1, own_a, vecs, segs, slots, place=None, pieces=None, earlier=None):
    rows, _, length = segs.shape
    width = a1.shape[1]
    heads = vecs.shape[1]
    hd = width // (4 * heads)
    cols = heads * hd
    first = slots - vecs.shape[0] if pieces else 0
    count = slots - 1 if pieces else 1
    anywhere = pl.BlockSpec(memory_space=pl.ANY)
    in_specs = [
        pl.BlockSpec((length, width), lambda s, r, *_: (r, 0)),
        pl.BlockSpec((1, heads, 4 * TILE), lambda s, r, *_: (s + (1 if pieces else 0), 0, 0)),
        pl.BlockSpec((1, 1, length), lambda s, r, *_: (r, 0, 0)),
    ]
    at = 1 if pieces else 0
    out_specs = [
        pl.BlockSpec((1, 1, 3 * cols, length), lambda s, r, *_: (s + at, r, 0, 0)),
        pl.BlockSpec((1, 1, heads, length), lambda s, r, *_: (s + at, r, 0, 0)),
        pl.BlockSpec((1, 1, cols, length), lambda s, r, *_: (s + at, r, 0, 0)),
    ]
    out_shape = [
        jax.ShapeDtypeStruct((slots, rows, 3 * cols, length), bf16),
        jax.ShapeDtypeStruct((slots, rows, heads, length), f32),
        jax.ShapeDtypeStruct((slots, rows, cols, length), bf16),
    ]
    scratch = [pltpu.VMEM((heads, TILE, 4 * TILE), f32)]
    steps = count * rows
    common = dict(
        compiler_params=pltpu.CompilerParams(vmem_limit_bytes=VMEM),
        cost_estimate=cost(steps * 2.5 * 10**9, 2**20),
    )
    if not pieces:
        return pl.pallas_call(
            functools.partial(attn_own_kernel, heads, hd),
            grid=(count, rows),
            in_specs=in_specs + [pl.BlockSpec((width, width), lambda s, r: (0, 0))],
            out_specs=out_specs,
            out_shape=out_shape,
            scratch_shapes=scratch,
            name="attn_own",
            **common,
        )(a1, vecs, segs, own_a)
    n = len(pieces)
    return pl.pallas_call(
        functools.partial(attn_far_kernel, heads, hd, n),
        grid_spec=pltpu.PrefetchScalarGridSpec(
            num_scalar_prefetch=1,
            grid=(count, rows),
            in_specs=in_specs
            + [pl.BlockSpec((width, width), lambda s, r, p: (0, 0))]
            + [anywhere] * (n + 3),
            out_specs=out_specs + [anywhere],
            scratch_shapes=scratch
            + [
                pltpu.VMEM((count, width, width), bf16),
                pltpu.SemaphoreType.DMA((n,)),
                pltpu.SemaphoreType.DMA((2,)),
            ],
        ),
        out_shape=out_shape + [jax.ShapeDtypeStruct((slots, width, width), bf16)],
        input_output_aliases={5 + n: 0, 6 + n: 1, 7 + n: 2},
        name="attn_far",
        **common,
    )(place, a1, vecs, segs, own_a, *pieces, *earlier)


GELU_A = math.sqrt(2.0 / math.pi)
GELU_B = 0.044715


def gelu(v):
    t = jnp.tanh(v * (GELU_A + (GELU_A * GELU_B) * (v * v)))
    half = 0.5 * v
    return half + half * t


def gelu_pair(v):
    square = v * v
    t = jnp.tanh(v * (GELU_A + (GELU_A * GELU_B) * square))
    half = 0.5 * v
    inner = GELU_A + (3.0 * GELU_A * GELU_B) * square
    return half + half * t, 0.5 + 0.5 * t + half * (1.0 - t * t) * inner


def ffn_own_kernel(x_ref, ctx_ref, wo_ref, gain_ref, b_ref, c_ref, mid_ref, a2_ref, part_ref):
    parts = [
        dg(ctx_ref[k, 0], wo_ref[k], TN).astype(bf16).astype(f32) for k in range(ctx_ref.shape[0])
    ]
    mid = (x_ref[...].astype(f32) + tree(parts)).astype(bf16)
    mid_ref[...] = mid
    mid = mid.astype(f32)
    a2 = (mid * inv_rms(mid) * gain_ref[...]).astype(bf16)
    a2_ref[...] = a2
    hidden = gelu(dg(a2, b_ref[...], NN)).astype(bf16)
    part_ref[...] = dg(hidden, c_ref[...], NN).astype(bf16)


def ffn_own(x, ctx, sorted_a, gain, own_b, own_c):
    slots, rows, cols, length = ctx.shape
    tokens, width = x.shape
    units = own_b.shape[1]
    by_row = pl.BlockSpec((length, width), lambda r: (r, 0))
    return pl.pallas_call(
        ffn_own_kernel,
        grid=(rows,),
        in_specs=[
            by_row,
            pl.BlockSpec((slots, 1, cols, length), lambda r: (0, r, 0, 0)),
            pl.BlockSpec((slots, cols, width), lambda r: (0, 3, 0)),
            pl.BlockSpec((1, width), lambda r: (0, 0)),
            pl.BlockSpec((width, units), lambda r: (0, 0)),
            pl.BlockSpec((units, width), lambda r: (0, 0)),
        ],
        out_specs=[by_row] * 3,
        out_shape=[jax.ShapeDtypeStruct((tokens, width), bf16)] * 3,
        compiler_params=pltpu.CompilerParams(vmem_limit_bytes=VMEM),
        cost_estimate=cost(tokens * width * 6 * units, 2**24),
        name="ffn_own",
    )(x, ctx, sorted_a, gain, own_b, own_c)


def ffn_far_kernel(
    count,
    place_ref,
    a2_ref,
    mid_ref,
    part_ref,
    gain_ref,
    seg_ref,
    b_ref,
    c_ref,
    *rest,
):
    pieces = rest[:count]
    out_ref, res_ref, pool_ref, sorted_ref, w_s, sems, out_sems = rest[count:]
    r = pl.program_id(0)
    keep = [
        pltpu.make_async_copy(b_ref, sorted_ref.at[0], out_sems.at[0]),
        pltpu.make_async_copy(c_ref, sorted_ref.at[1], out_sems.at[1]),
        pltpu.make_async_copy(w_s, sorted_ref.at[pl.ds(2, w_s.shape[0])], out_sems.at[2]),
    ]

    @pl.when(r == 0)
    def _():
        for copy in bring(place_ref, pieces, w_s, sems):
            copy.wait()
        for copy in keep:
            copy.start()

    a2 = a2_ref[...]
    parts = [part_ref[...].astype(f32)]
    for k in range(w_s.shape[0] // 2):
        hidden = gelu(dg(a2, w_s[2 * k], NN)).astype(bf16)
        parts.append(dg(hidden, w_s[2 * k + 1], NN).astype(bf16).astype(f32))
    res = mid_ref[...].astype(f32) + tree(parts)
    res_ref[...] = res.astype(bf16)
    final = (res * inv_rms(res) * gain_ref[...]).astype(bf16)
    out_ref[...] = final
    seg = seg_ref[0]
    hot = lax.broadcasted_iota(jnp.int32, (SEG_ROW, seg.shape[-1]), 0) == seg
    member = jnp.where(hot, 1.0, 0.0)
    pool_ref[...] = dg(member.astype(bf16), final, NN) / jnp.sum(member, 1, keepdims=True)

    @pl.when(r == pl.num_programs(0) - 1)
    def _():
        for copy in keep:
            copy.wait()


def ffn_far(place, a2, mid, part, gain, segs, own_b, own_c, pieces):
    rows, _, length = segs.shape
    tokens, width = a2.shape
    units = own_b.shape[1]
    others = pieces[0].shape[0]
    n = len(pieces)
    by_row = pl.BlockSpec((length, width), lambda r, p: (r, 0))
    anywhere = pl.BlockSpec(memory_space=pl.ANY)
    return pl.pallas_call(
        functools.partial(ffn_far_kernel, n),
        grid_spec=pltpu.PrefetchScalarGridSpec(
            num_scalar_prefetch=1,
            grid=(rows,),
            in_specs=[
                by_row,
                by_row,
                by_row,
                pl.BlockSpec((1, width), lambda r, p: (0, 0)),
                pl.BlockSpec((1, 1, length), lambda r, p: (r, 0, 0)),
            ]
            + [pl.BlockSpec((width, units), lambda r, p: (0, 0))]
            + [pl.BlockSpec((units, width), lambda r, p: (0, 0))]
            + [anywhere] * n,
            out_specs=[
                by_row,
                by_row,
                pl.BlockSpec((SEG_ROW, width), lambda r, p: (r, 0)),
                anywhere,
            ],
            scratch_shapes=[
                pltpu.VMEM((others, width, units), bf16),
                pltpu.SemaphoreType.DMA((n,)),
                pltpu.SemaphoreType.DMA((3,)),
            ],
        ),
        out_shape=[
            jax.ShapeDtypeStruct((tokens, width), bf16),
            jax.ShapeDtypeStruct((tokens, width), bf16),
            jax.ShapeDtypeStruct((rows * SEG_ROW, width), f32),
            jax.ShapeDtypeStruct((others + 2, width, units), bf16),
        ],
        compiler_params=pltpu.CompilerParams(vmem_limit_bytes=VMEM),
        cost_estimate=cost(tokens * width * 3 * units * others, 2**24),
        name="ffn_far",
    )(place, a2, mid, part, gain, segs, own_b, own_c, *pieces)


def loss_math(pooled, project, pair_col, pair_row, gain):
    slots = pooled.shape[0]
    projected = dg(pooled, project, NN)
    inv_norm = lax.rsqrt(jnp.sum(projected * projected, -1, keepdims=True) + epsilon)
    unit = projected * inv_norm
    embedded = unit.astype(bf16)
    similar = logit_scale * dg(embedded, embedded, NT)
    rows = lax.broadcasted_iota(jnp.int32, (slots, slots), 0)
    columns = lax.broadcasted_iota(jnp.int32, (slots, slots), 1)
    same = rows == columns
    similar = jnp.where(same, masked_value, similar)
    partner = jnp.where((pair_col == pair_row) & jnp.logical_not(same), 2.0, 0.0)

    def total(axis):
        top = jnp.max(similar, axis, keepdims=True)
        return top + jnp.log(jnp.sum(jnp.exp(similar - top), axis, keepdims=True))

    both = jnp.exp(similar - total(1)) + jnp.exp(similar - total(0)) - partner
    high = both.astype(bf16)
    low = (both - high.astype(f32)).astype(bf16)
    d_unit = (loss_scale * logit_scale) * (dg(high, embedded, NN) + dg(low, embedded, NN))
    d_proj = inv_norm * (d_unit - unit * jnp.sum(d_unit * unit, -1, keepdims=True))
    d_proj = d_proj.astype(bf16)
    d_pooled = dg(d_proj, project, NT)
    d_gain = jnp.sum(d_pooled * pooled.astype(f32), 0, keepdims=True) / gain
    return d_proj, d_pooled, d_gain


def loss_kernel(
    at_ref, pooled_ref, project_ref, pc_ref, pr_ref, gain_ref, dpool_ref, dproj_ref, dgain_ref, a_s, b_s
):
    d_proj, d_pooled, d_gain = loss_math(
        pooled_ref[...], project_ref[...], pc_ref[...], pr_ref[...], gain_ref[...]
    )
    a_s[...] = d_pooled
    b_s[...] = dg(pooled_ref[...], d_proj, TN)
    here = dpool_ref.shape[0]
    block = dproj_ref.shape[0]
    dpool_ref[...] = a_s[pl.ds(pl.multiple_of(at_ref[0] * here, here), here), :]
    dproj_ref[...] = b_s[pl.ds(pl.multiple_of(at_ref[0] * block, block), block), :]
    dgain_ref[...] = d_gain


def loss_head(at, pooled, project, pairs, gain, here, block):
    slots, width = pooled.shape
    pair_col = pairs[:, None]
    pair_row = pairs[None, :]
    if slots > 512:
        d_proj, d_pooled, d_gain = loss_math(pooled, project, pair_col, pair_row, gain)
        own_cols = lax.dynamic_slice_in_dim(pooled, at[0] * block, block, 1)
        d_pooled = lax.dynamic_slice_in_dim(d_pooled, at[0] * here, here, 0)
        return d_pooled, dg(own_cols, d_proj, TN), d_gain
    full = lambda shape: pl.BlockSpec(shape, lambda i, at: (0, 0))
    return pl.pallas_call(
        loss_kernel,
        grid_spec=pltpu.PrefetchScalarGridSpec(
            num_scalar_prefetch=1,
            grid=(1,),
            in_specs=[
                full((slots, width)),
                full(project.shape),
                full((slots, 1)),
                full((1, slots)),
                full((1, width)),
            ],
            out_specs=[full((here, width)), full((block, width)), full((1, width))],
            scratch_shapes=[pltpu.VMEM((slots, width), f32), pltpu.VMEM((width, width), f32)],
        ),
        out_shape=[
            jax.ShapeDtypeStruct((here, width), f32),
            jax.ShapeDtypeStruct((block, width), f32),
            jax.ShapeDtypeStruct((1, width), f32),
        ],
        compiler_params=pltpu.CompilerParams(vmem_limit_bytes=VMEM),
        cost_estimate=cost(3 * 10**9, 2**20),
        name="loss_head",
    )(at, pooled, project, pair_col, pair_row, gain)


def d_result_of(res, seg, d_pool, gain):
    hot = lax.broadcasted_iota(jnp.int32, (SEG_ROW, seg.shape[-1]), 0) == seg
    member = jnp.where(hot, 1.0, 0.0)
    per_token = d_pool / jnp.sum(member, 1, keepdims=True)
    high = per_token.astype(bf16)
    low = (per_token - high.astype(f32)).astype(bf16)
    twice = jnp.concatenate([member, member], 0).astype(bf16)
    d_final = dg(twice, jnp.concatenate([high, low], 0), TN)
    scale = inv_rms(res)
    unit = res * scale
    weighted = d_final * gain
    return scale * (weighted - unit * jnp.mean(weighted * unit, -1, keepdims=True))


def ffn_back_kernel(
    row_ref,
    res_ref,
    mid_ref,
    a2_ref,
    seg_ref,
    dpool_ref,
    gain_end_ref,
    gain_ref,
    bc_ref,
    wo_ref,
    dmid_ref,
    dattn_ref,
    dctx_ref,
    dgain_ref,
    dres_s,
    low_s,
    sum_s,
):
    k = pl.program_id(0)

    @pl.when(k == 0)
    def _():
        d_res = d_result_of(
            res_ref[...].astype(f32), seg_ref[0], dpool_ref[...], gain_end_ref[...]
        )
        dres_s[...] = d_res
        low_s[...] = d_res.astype(bf16)
        sum_s[...] = jnp.zeros_like(sum_s)

    slope = gelu_pair(dg(a2_ref[...], bc_ref[0], NN))[1]
    d_pre = (dg(low_s[...], bc_ref[1], NT) * slope).astype(bf16)
    sum_s[...] += dg(d_pre, bc_ref[0], NT)

    @pl.when(k == pl.num_programs(0) - 1)
    def _():
        mid = mid_ref[...].astype(f32)
        scale = inv_rms(mid)
        unit = mid * scale
        grad = sum_s[...]
        weighted = grad * gain_ref[...]
        d_mid = dres_s[...] + scale * (weighted - unit * jnp.mean(weighted * unit, -1, keepdims=True))
        dgain_ref[...] = jnp.sum(grad * unit, 0, keepdims=True)
        dmid_ref[...] = d_mid
        low = d_mid.astype(bf16)
        dattn_ref[...] = low
        for s in range(wo_ref.shape[0]):
            dctx_ref[s] = dg(wo_ref[s], low, NT).astype(bf16)


def ffn_back(row, res, mid, a2, segs, d_pool, gain_end, gain, sorted_a, sorted_bc):
    rows, _, length = segs.shape
    tokens, width = res.shape
    slots = sorted_a.shape[0]
    units = sorted_bc.shape[-1]
    cols = width // 4
    own = pl.BlockSpec((length, width), lambda k, row: (row[0], 0))
    fixed = lambda k, row: (0, 0)
    return pl.pallas_call(
        ffn_back_kernel,
        grid_spec=pltpu.PrefetchScalarGridSpec(
            num_scalar_prefetch=1,
            grid=(slots,),
            in_specs=[
                own,
                own,
                own,
                pl.BlockSpec((1, 1, length), lambda k, row: (row[0], 0, 0)),
                pl.BlockSpec((SEG_ROW, width), lambda k, row: (row[0], 0)),
                pl.BlockSpec((1, width), fixed),
                pl.BlockSpec((1, width), fixed),
                pl.BlockSpec((2, width, units), lambda k, row: (k, 0, 0)),
                pl.BlockSpec((slots, cols, width), lambda k, row: (0, 3, 0)),
            ],
            out_specs=[
                pl.BlockSpec((length, width), fixed),
                pl.BlockSpec((length, width), fixed),
                pl.BlockSpec((slots, cols, length), lambda k, row: (0, 0, 0)),
                pl.BlockSpec((1, width), fixed),
            ],
            scratch_shapes=[
                pltpu.VMEM((length, width), f32),
                pltpu.VMEM((length, width), bf16),
                pltpu.VMEM((length, width), f32),
            ],
        ),
        out_shape=[
            jax.ShapeDtypeStruct((length, width), f32),
            jax.ShapeDtypeStruct((length, width), bf16),
            jax.ShapeDtypeStruct((slots, cols, length), bf16),
            jax.ShapeDtypeStruct((1, width), f32),
        ],
        compiler_params=pltpu.CompilerParams(vmem_limit_bytes=VMEM),
        cost_estimate=cost(1.2 * 10**10, 2**24),
        name="ffn_back",
    )(row, res, mid, a2, segs, d_pool, gain_end, gain, sorted_bc, sorted_a)


def fold(tile):
    lanes = tile.shape[1]
    total = tile[0:8]
    for b in range(1, TILE // 8):
        total = total + pltpu.roll(tile[8 * b : 8 * b + 8], lanes - 8 * b, 1)
    return total


def attn_back_kernel(
    heads,
    hd,
    row_ref,
    qkv_ref,
    lse_ref,
    ctx_ref,
    dctx_ref,
    vec_ref,
    seg_ref,
    w_ref,
    x_ref,
    dmid_ref,
    gain_ref,
    dqkv_ref,
    fold_ref,
    dtok_ref,
    dgain_ref,
    bias_s,
    sum_s,
):
    slot = pl.program_id(0)
    length = qkv_ref.shape[-1]
    blocks = length // TILE
    spread_bias(vec_ref, bias_s, heads)
    q_mask, k_mask = masks(seg_ref[0])
    for h in range(heads):
        q_low = qkv_ref[0, 0, h * hd : (h + 1) * hd]
        k_low = qkv_ref[0, 0, (heads + h) * hd : (heads + h + 1) * hd]
        v_low = qkv_ref[0, 0, (2 * heads + h) * hd : (2 * heads + h + 1) * hd]
        dc = dctx_ref[0, h * hd : (h + 1) * hd]
        c = ctx_ref[0, 0, h * hd : (h + 1) * hd]
        delta = jnp.sum(dc.astype(f32) * c.astype(f32), 0, keepdims=True)
        lse = lse_ref[0, 0, h : h + 1]
        scores = dg(
            jnp.concatenate([k_low, k_mask], 0).T, jnp.concatenate([q_low, q_mask], 0), NN
        )
        d_probs = dg(v_low.T, dc, NN)
        probs_cols = []
        score_cols = []
        near = [None, None, None]
        far = [None, None]
        for i in range(blocks):
            at = slice(i * TILE, (i + 1) * TILE)
            probs = []
            grads = []
            for j in range(blocks):
                to = slice(j * TILE, (j + 1) * TILE)
                tile = with_bias(scores[to, at], j - i, h, bias_s, vec_ref)
                prob = jnp.exp(tile - lse[:, at])
                grad = prob * (d_probs[to, at] - delta[:, at])
                probs.append(prob.astype(bf16))
                grads.append(grad.astype(bf16))
                if abs(j - i) <= 1:
                    old = near[j - i + 1]
                    near[j - i + 1] = grad if old is None else old + grad
                else:
                    old = far[int(j < i)]
                    far[int(j < i)] = grad if old is None else old + grad
            probs_cols.append(jnp.concatenate(probs, 0))
            score_cols.append(jnp.concatenate(grads, 0))
        probs = jnp.concatenate(probs_cols, 1)
        grads = jnp.concatenate(score_cols, 1)
        dqkv_ref[0, h * hd : (h + 1) * hd] = dg(k_low, grads, NN).astype(bf16)
        dqkv_ref[0, (heads + h) * hd : (heads + h + 1) * hd] = dg(q_low, grads, NT).astype(bf16)
        dqkv_ref[0, (2 * heads + h) * hd : (2 * heads + h + 1) * hd] = dg(dc, probs, NT).astype(
            bf16
        )
        band = jnp.concatenate([near[1], near[0], jnp.zeros_like(near[0]), near[2]], 1)
        fold_ref[0, h, :, : 4 * TILE] = fold(band)
        for side in range(2):
            total = far[side][0:8]
            for b in range(1, TILE // 8):
                total = total + far[side][8 * b : 8 * b + 8]
            fold_ref[0, h, :, (4 + side) * TILE : (5 + side) * TILE] = total
    part = dg(dqkv_ref[0], w_ref[0], TN)

    @pl.when(slot == 0)
    def _():
        sum_s[...] = part

    @pl.when(slot > 0)
    def _():
        sum_s[...] += part

    @pl.when(slot == pl.num_programs(0) - 1)
    def _():
        x = x_ref[...].astype(f32)
        scale = inv_rms(x)
        unit = x * scale
        grad = sum_s[...]
        weighted = grad * gain_ref[...]
        d_tok = dmid_ref[...] + scale * (weighted - unit * jnp.mean(weighted * unit, -1, keepdims=True))
        dtok_ref[...] = d_tok.astype(bf16)
        dgain_ref[...] = jnp.sum(grad * unit, 0, keepdims=True)


def attn_back(row, qkv, lse, ctx, d_ctx, vecs, segs, all_a, x, d_mid, gain):
    slots, rows, cols3, length = qkv.shape
    heads = lse.shape[2]
    cols = cols3 // 3
    width = x.shape[1]
    own4 = lambda k, row: (k, row[0], 0, 0)
    slot = lambda k, row: (k, 0, 0)
    fixed = lambda k, row: (0, 0)
    return pl.pallas_call(
        functools.partial(attn_back_kernel, heads, cols // heads),
        grid_spec=pltpu.PrefetchScalarGridSpec(
            num_scalar_prefetch=1,
            grid=(slots,),
            in_specs=[
                pl.BlockSpec((1, 1, cols3, length), own4),
                pl.BlockSpec((1, 1, heads, length), own4),
                pl.BlockSpec((1, 1, cols, length), own4),
                pl.BlockSpec((1, cols, length), slot),
                pl.BlockSpec((1, heads, 4 * TILE), slot),
                pl.BlockSpec((1, 1, length), lambda k, row: (row[0], 0, 0)),
                pl.BlockSpec((1, cols3, width), slot),
                pl.BlockSpec((length, width), lambda k, row: (row[0], 0)),
                pl.BlockSpec((length, width), fixed),
                pl.BlockSpec((1, width), fixed),
            ],
            out_specs=[
                pl.BlockSpec((1, cols3, length), slot),
                pl.BlockSpec((1, heads, 8, 6 * TILE), lambda k, row: (k, 0, 0, 0)),
                pl.BlockSpec((length, width), fixed),
                pl.BlockSpec((1, width), fixed),
            ],
            scratch_shapes=[
                pltpu.VMEM((heads, TILE, 4 * TILE), f32),
                pltpu.VMEM((length, width), f32),
            ],
        ),
        out_shape=[
            jax.ShapeDtypeStruct((slots, cols3, length), bf16),
            jax.ShapeDtypeStruct((slots, heads, 8, 6 * TILE), f32),
            jax.ShapeDtypeStruct((length, width), bf16),
            jax.ShapeDtypeStruct((1, width), f32),
        ],
        compiler_params=pltpu.CompilerParams(vmem_limit_bytes=VMEM),
        cost_estimate=cost(1.5 * 10**10, 2**24),
        name="attn_back",
    )(row, qkv, lse, ctx, d_ctx, vecs, segs, all_a, x, d_mid, gain)


def split_blocks(core, rel_ref, block, pad, extra, values, keep_ref, give_ref, lead):
    for c in range(2):

        @pl.when(core == c)
        def _():
            for chip in range(4):
                for ref, j in ((keep_ref, 2 * chip + c), (give_ref, 2 * chip + 1 - c)):
                    rows = values(j * block, (j + 1) * block)
                    for at, value in enumerate(rows):
                        ref[rel_ref[chip], lead + at, :block] = value
                    if pad:
                        ref[rel_ref[chip], lead, block:] = extra(j)


def attn_weights_kernel(
    block, place_ref, a1_ref, dattn_ref, dqkv_ref, ctx_ref, extra_ref, *rest
):
    outs, (a1_s, dattn_s, sum_s) = rest[:-3], rest[-3:]

    @pl.when(pl.program_id(0) == 0)
    def _():
        a1_s[...] = a1_ref[...].T
        dattn_s[...] = dattn_ref[...].T

    cols3 = dqkv_ref.shape[1]
    sum_s[:, :cols3] = dg(a1_s[...], dqkv_ref[0], NT).astype(bf16)
    sum_s[:, cols3:] = dg(dattn_s[...], ctx_ref[0, 0], NT).astype(bf16)
    if len(outs) == 1:
        outs[0][0] = sum_s[...]
    else:
        split_blocks(
            place_ref[1],
            place_ref.at[pl.ds(2, 4)],
            block,
            True,
            lambda j: extra_ref[0, j],
            lambda a, b: [sum_s[a:b]],
            outs[0],
            outs[1],
            0,
        )


def attn_weights(place, a1, d_attn, d_qkv, ctx, extra, split):
    slots, cols3, length = d_qkv.shape
    cols = ctx.shape[2]
    width = a1.shape[1]
    _, blocks, pad, _ = extra.shape
    block = width // blocks
    if split:
        shape = (4, slots, block + pad, width)
        out_specs = [pl.BlockSpec((4, 1, block + pad, width), lambda k, p: (0, k, 0, 0))] * 2
        out_shape = [jax.ShapeDtypeStruct(shape, bf16)] * 2
    else:
        out_specs = [pl.BlockSpec((1, width, width), lambda k, p: (k, 0, 0))]
        out_shape = [jax.ShapeDtypeStruct((slots, width, width), bf16)]
    return pl.pallas_call(
        functools.partial(attn_weights_kernel, block),
        grid_spec=pltpu.PrefetchScalarGridSpec(
            num_scalar_prefetch=1,
            grid=(slots,),
            in_specs=[
                pl.BlockSpec((length, width), lambda k, p: (p[0], 0)),
                pl.BlockSpec((length, width), lambda k, p: (0, 0)),
                pl.BlockSpec((1, cols3, length), lambda k, p: (k, 0, 0)),
                pl.BlockSpec((1, 1, cols, length), lambda k, p: (k, p[0], 0, 0)),
                pl.BlockSpec((1, blocks, pad, width), lambda k, p: (k, 0, 0, 0)),
            ],
            out_specs=out_specs,
            scratch_shapes=[
                pltpu.VMEM((width, length), bf16),
                pltpu.VMEM((width, length), bf16),
                pltpu.VMEM((width, width), bf16),
            ],
        ),
        out_shape=out_shape,
        compiler_params=pltpu.CompilerParams(vmem_limit_bytes=VMEM),
        cost_estimate=cost(10**6, 10**6),
        name="attn_weights",
    )(place, a1, d_attn, d_qkv, ctx, extra)


def ffn_weights_kernel(
    block, place_ref, res_ref, seg_ref, dpool_ref, gain_ref, a2_ref, b_ref, c_ref, *rest
):
    outs, (up_s, down_s) = rest[:-2], rest[-2:]
    r = pl.program_id(0)

    @pl.when(r == 0)
    def _():
        up_s[...] = jnp.zeros_like(up_s)
        down_s[...] = jnp.zeros_like(down_s)

    d_res = d_result_of(res_ref[...].astype(f32), seg_ref[0], dpool_ref[...], gain_ref[...])
    low = d_res.astype(bf16)
    a2 = a2_ref[...]
    hidden, slope = gelu_pair(dg(a2, b_ref[...], NN))
    d_pre = (dg(low, c_ref[...], NT) * slope).astype(bf16)
    up_s[...] += dg(a2, d_pre, TN)
    down_s[...] += dg(low, hidden.astype(bf16), TN)

    @pl.when(r == pl.num_programs(0) - 1)
    def _():
        if len(outs) == 1:
            outs[0][0] = up_s[...].astype(bf16)
            outs[0][1] = down_s[...].astype(bf16)
        else:
            split_blocks(
                place_ref[1],
                place_ref.at[pl.ds(2, 4)],
                block,
                False,
                None,
                lambda a, b: [up_s[a:b].astype(bf16), down_s[a:b].astype(bf16)],
                outs[0],
                outs[1],
                0,
            )


def ffn_weights(place, res, segs, d_pool, gain, a2, own_b, own_c, blocks, split):
    rows, _, length = segs.shape
    width = res.shape[1]
    units = own_b.shape[1]
    block = width // blocks
    by_row = pl.BlockSpec((length, width), lambda r, p: (r, 0))
    shape = (4, 2, block, units) if split else (2, width, units)
    zeros = (0,) * len(shape)
    return pl.pallas_call(
        functools.partial(ffn_weights_kernel, block),
        grid_spec=pltpu.PrefetchScalarGridSpec(
            num_scalar_prefetch=1,
            grid=(rows,),
            in_specs=[
                by_row,
                pl.BlockSpec((1, 1, length), lambda r, p: (r, 0, 0)),
                pl.BlockSpec((SEG_ROW, width), lambda r, p: (r, 0)),
                pl.BlockSpec((1, width), lambda r, p: (0, 0)),
                by_row,
                pl.BlockSpec((width, units), lambda r, p: (0, 0)),
                pl.BlockSpec((units, width), lambda r, p: (0, 0)),
            ],
            out_specs=[pl.BlockSpec(shape, lambda r, p: zeros)] * (2 if split else 1),
            scratch_shapes=[pltpu.VMEM((width, units), f32)] * 2,
        ),
        out_shape=[jax.ShapeDtypeStruct(shape, bf16)] * (2 if split else 1),
        compiler_params=pltpu.CompilerParams(vmem_limit_bytes=VMEM),
        cost_estimate=cost(10**6, 10**6),
        name="ffn_weights",
    )(place, res, segs, d_pool, gain, a2, own_b, own_c)


def spread_kernel(order_ref, *refs):
    out_ref = refs[-1]
    for at, ref in enumerate(refs[:-1]):

        @pl.when(pl.program_id(0) == at)
        def _():
            out_ref[...] = ref[...].astype(f32)


def spread_rows(order, parts):
    length, width = parts[0].shape
    n = len(parts)
    return pl.pallas_call(
        spread_kernel,
        grid_spec=pltpu.PrefetchScalarGridSpec(
            num_scalar_prefetch=1,
            grid=(n,),
            in_specs=[pl.BlockSpec((length, width), lambda k, order: (0, 0))] * n,
            out_specs=pl.BlockSpec((length, width), lambda k, order: (order[k], 0)),
        ),
        out_shape=jax.ShapeDtypeStruct((n * length, width), f32),
        compiler_params=pltpu.CompilerParams(vmem_limit_bytes=VMEM),
        cost_estimate=cost(0, 10**7),
        name="spread_rows",
    )(order, *parts)


def shards(
    n_dp,
    n_tp,
    tokens,
    segment_ids,
    pair_order,
    w_query,
    w_key,
    w_value,
    w_out,
    rel_bias,
    gain_attn,
    w_hidden,
    w_down,
    gain_ffn,
    gain_final,
    w_project,
):
    rows, length = segment_ids.shape
    bucket_count, heads = rel_bias.shape
    width = tokens.shape[1]
    units = w_hidden.shape[1]
    dp = lax.axis_index("dp")
    tp = lax.axis_index("tp")
    share = math.gcd(n_dp, 8)
    split = n_dp == 8
    mates = [[(i, i ^ m) for i in range(n_dp)] for m in range(share)]
    levels = [[(i, i ^ k) for i in range(n_tp)] for k in range(n_tp)]

    def over_dp(value, m):
        return lax.ppermute(value, "dp", mates[m])

    def over_tp(value, k):
        return lax.ppermute(value, "tp", levels[k])

    slices = width // share
    low_bits = dp % share
    place = (low_bits ^ jnp.arange(share, dtype=jnp.int32)) * slices

    def from_levels(*packs):
        mine = [lax.dynamic_slice_in_dim(p, low_bits * slices, slices, 0) for p in packs]
        mine = jnp.stack(mine)
        far = stack([over_tp(mine, k) for k in range(1, n_tp)])
        return far.reshape((n_tp - 1) * len(packs), slices, packs[0].shape[1])

    def from_chips(far):
        return [far] + [over_dp(far, m) for m in range(2, share, 2)]

    def from_cores(pieces):
        both = [(piece, over_dp(piece, 1)) for piece in pieces]
        return [piece for pair in both for piece in pair]

    def after(values, others):
        return lax.optimization_barrier((values, others))[0]

    pack_a = pack_weights(w_query, w_key, w_value, w_out)
    far_a = from_levels(pack_a)
    far_bc = from_levels(w_hidden, w_down)
    tables = jnp.stack([rel_bias] + [over_tp(rel_bias, k) for k in range(1, n_tp)])
    vecs = jnp.einsum("kbh,bn->khn", tables, bias_lanes(bucket_count), precision=highest)
    segs = segment_ids[:, None, :]
    row = tp[None].astype(jnp.int32)
    one = gain_attn[None]
    two = gain_ffn[None]
    end = gain_final[None]

    x = tokens.astype(f32)
    a1 = (x * inv_rms(x) * one).astype(bf16)
    state = attention(a1, pack_a, vecs, segs, n_tp)
    far_a = from_cores(after(from_chips(far_a), state))
    far_bc = from_chips(after(far_bc, far_a))
    qkv, lse, ctx, sorted_a = attention(a1, pack_a, vecs, segs, n_tp, place, far_a, state)
    far_bc = from_cores(after(far_bc, lse))
    mid, a2, part = ffn_own(tokens, ctx, sorted_a, two, w_hidden, w_down)
    layer_out, res, pooled, sorted_bc = ffn_far(
        place, a2, mid, part, end, segs, w_hidden, w_down, far_bc
    )
    pooled_all = lax.all_gather(pooled.astype(bf16), "dp", axis=0, tiled=True)
    block = width // n_dp
    d_pool, grad_project, d_gain_end = loss_head(
        dp[None].astype(jnp.int32), pooled_all, w_project, pair_order // 2, end, rows * SEG_ROW, block
    )
    grad_gain_final = lax.dynamic_slice_in_dim(d_gain_end[0], dp * block, block, 0)
    d_mid, d_attn, d_ctx, d_gain_two = ffn_back(
        row, res, mid, a2, segs, d_pool, end, two, sorted_a, sorted_bc
    )
    d_qkv, folded, d_tok, d_gain_one = attn_back(
        row, qkv, lse, ctx, d_ctx, vecs, segs, sorted_a, tokens, d_mid, one
    )
    order = tp ^ jnp.arange(n_tp, dtype=jnp.int32)
    d_tokens = lax.all_gather(d_tok, "tp", axis=0, tiled=True).astype(f32)

    d_rel = jnp.einsum(
        "khn,nb->kbh",
        folded.reshape(n_tp, heads, -1),
        grad_lanes(bucket_count),
        precision=highest,
    )
    gains = jnp.concatenate([d_gain_one, d_gain_two])
    pad = 16
    extra = jnp.zeros((n_tp, n_dp, pad, width), bf16)
    if split:
        small = d_rel.reshape(n_tp, 1, 1, bucket_count * heads).astype(bf16)
        gain_rows = jnp.swapaxes(gains.reshape(2, n_dp, block), 0, 1).astype(bf16)
        extra = jnp.concatenate(
            [
                jnp.broadcast_to(gain_rows[None], (n_tp, n_dp, 2, block)),
                jnp.broadcast_to(small, (n_tp, n_dp, 1, block)),
                jnp.zeros((n_tp, n_dp, pad - 3, block), bf16),
            ],
            2,
        )
        extra = jnp.pad(extra, ((0, 0), (0, 0), (0, 0), (0, width - block)))
    chips = (dp // 2) ^ jnp.arange(4, dtype=jnp.int32)
    spots = jnp.concatenate([row, (dp % 2)[None].astype(jnp.int32), chips])
    parts_a = attn_weights(spots, a1, d_attn, d_qkv, ctx, extra, split)
    parts_f = ffn_weights(
        spots, res, segs, d_pool, end, a2, w_hidden, w_down, n_dp, split
    )

    def reduce_dp(parts):
        if not split:
            wide = parts[0].astype(f32)
            return lax.psum_scatter(wide, "dp", scatter_dimension=1, tiled=True)
        keep, give = parts
        took = over_dp(give, 1)
        pair = [rounded(keep[c].astype(f32) + took[c].astype(f32)) for c in range(4)]
        got = [pair[0]] + [over_dp(pair[c].astype(bf16), 2 * c) for c in range(1, 4)]
        return tree([g.astype(f32) for g in got])

    def reduce_tp(value):
        return tree([value[0]] + [over_tp(value[k], k) for k in range(1, n_tp)])

    own_a = rounded(reduce_dp(parts_a))
    own_f = reduce_dp(parts_f)
    grad_a = tree(
        [own_a[0].astype(f32)] + [over_tp(own_a[k].astype(bf16), k).astype(f32) for k in range(1, n_tp)]
    )
    cols = width // 4
    if split:
        gain_one, gain_two = grad_a[block, :block], grad_a[block + 1, :block]
        d_rel_here = grad_a[block + 2, : bucket_count * heads].reshape(bucket_count, heads)
    else:
        gains = tree([gains] + [over_tp(gains, k) for k in range(1, n_tp)])
        d_rel_here, gains = lax.psum((reduce_tp(d_rel), gains), "dp")
        gain_one, gain_two = lax.dynamic_slice_in_dim(gains, dp * block, block, 1)
    return (
        layer_out,
        d_tokens,
        grad_a[:block, :cols],
        grad_a[:block, cols : 2 * cols],
        grad_a[:block, 2 * cols : 3 * cols],
        grad_a[:block, 3 * cols :].T,
        d_rel_here,
        gain_one,
        own_f[0],
        own_f[1].T,
        gain_two,
        grad_gain_final,
        grad_project,
    )


def solution(mesh):
    placed = (
        P("dp", None),
        P("dp", None),
        P(),
        P(None, "tp"),
        P(None, "tp"),
        P(None, "tp"),
        P("tp", None),
        P(None, "tp"),
        P(),
        P(None, "tp"),
        P("tp", None),
        P(),
        P(),
        P(),
    )
    return jax.shard_map(
        functools.partial(shards, mesh.shape["dp"], mesh.shape["tp"]),
        mesh=mesh,
        in_specs=placed,
        out_specs=(
            P("dp", None),
            P("dp", None),
            P("dp", "tp"),
            P("dp", "tp"),
            P("dp", "tp"),
            P("tp", "dp"),
            P(None, "tp"),
            P("dp"),
            P("dp", "tp"),
            P("tp", "dp"),
            P("dp"),
            P("dp"),
            P("dp", None),
        ),
        check_vma=False,
    )
```

```python
import functools
import math

import jax
import jax.numpy as jnp
import numpy as np
from jax import lax
from jax.experimental import pallas as pl
from jax.experimental.pallas import tpu as pltpu
from jax.sharding import PartitionSpec as P

MAX_DIST = 128
SEG_ROW = 8
TILE = 128
VMEM = 52 * 2**20

epsilon = 1e-06
logit_scale = 50.0
loss_scale = 128.0
masked_value = -1e30
highest = lax.Precision.HIGHEST
f32 = jnp.float32
bf16 = jnp.bfloat16

NN = (((1,), (0,)), ((), ()))
NT = (((1,), (1,)), ((), ()))
TN = (((0,), (0,)), ((), ()))


def dg(a, b, dims):
    return lax.dot_general(a, b, dims, preferred_element_type=f32)


def bucket_of(offsets, bucket_count, distance):
    half_count = bucket_count // 2
    exact_count = half_count // 2
    far_side = np.where(offsets > 0, half_count, 0)
    magnitude = np.abs(offsets)
    logged = (
        np.log(np.maximum(magnitude, exact_count) / exact_count)
        / math.log(distance / exact_count)
        * (half_count - exact_count)
    )
    far_bucket = np.minimum(exact_count + logged.astype(np.int64), half_count - 1)
    return (far_side + np.where(magnitude < exact_count, magnitude, far_bucket)).astype(np.int32)


def cost(flops, moved):
    return pl.CostEstimate(flops=int(flops), bytes_accessed=int(moved), transcendentals=0)


def bias_lanes(bucket_count):
    lanes = np.arange(4 * TILE)
    lanes = np.where(lanes >= 2 * TILE, lanes - 4 * TILE, lanes)
    return np.eye(bucket_count, dtype=np.float32)[bucket_of(-lanes, bucket_count, MAX_DIST)].T


def grad_lanes(bucket_count):
    sub = np.arange(8)[:, None]
    lane = np.arange(4 * TILE)[None, :]
    y = (lane - sub) % (4 * TILE)
    y = np.where(y >= 2 * TILE, y - 4 * TILE, y)
    near = bucket_of(-y, bucket_count, MAX_DIST)
    up = np.full((8, TILE), bucket_of(np.array(MAX_DIST), bucket_count, MAX_DIST))
    down = np.full((8, TILE), bucket_of(np.array(-MAX_DIST), bucket_count, MAX_DIST))
    ids = np.concatenate([near, up, down], 1).reshape(-1)
    return np.eye(bucket_count, dtype=np.float32)[ids]


def bring(place_ref, piece_refs, into, sems):
    slices = piece_refs[0].shape[-2]
    copies = []
    for m, piece in enumerate(piece_refs):
        start = pl.multiple_of(place_ref[m], 16) if slices % 16 == 0 else place_ref[m]
        copy = pltpu.make_async_copy(piece, into.at[:, pl.ds(start, slices), :], sems.at[m])
        copy.start()
        copies.append(copy)
    return copies


def spread_bias(vec_ref, bias_s, heads):
    for h in range(heads):
        wide = jnp.broadcast_to(vec_ref[0, h : h + 1, :], (TILE, 4 * TILE))
        bias_s[h] = pltpu.roll(wide, 0, 1, stride=1, stride_axis=0)


def with_bias(tile, offset, h, bias_s, vec_ref):
    if offset == 0:
        return tile + bias_s[h, :, 0:TILE]
    if offset == 1:
        return tile + bias_s[h, :, 3 * TILE : 4 * TILE]
    if offset == -1:
        return tile + bias_s[h, :, TILE : 2 * TILE]
    lane = 2 * TILE + 1 if offset > 1 else 2 * TILE - 1
    return tile + vec_ref[0, h : h + 1, lane : lane + 1]


def masks(seg):
    hot = lax.broadcasted_iota(jnp.int32, (16, seg.shape[-1]), 0) == seg
    return (
        jnp.where(hot, 0.0, masked_value).astype(bf16),
        jnp.where(hot, 1.0, 0.0).astype(bf16),
    )


def inv_rms(values):
    return lax.rsqrt(jnp.mean(values * values, -1, keepdims=True) + epsilon)


def rounded(value):
    return lax.reduce_precision(value, 8, 7)


def tree(parts):
    while len(parts) > 1:
        parts = [parts[i] + parts[i + 1] for i in range(0, len(parts), 2)]
    return parts[0]


def exact_parts(value):
    parts = []
    for _ in range(3):
        part = value.astype(bf16)
        parts.append(part)
        value = value - part.astype(f32)
    return parts


PAD = 16


def pack_kernel(at_ref, q_ref, k_ref, v_ref, o_ref, rel_ref, out_ref, mine_ref, pack_s):
    cols = q_ref.shape[1]
    for at, ref in enumerate((q_ref, k_ref, v_ref)):
        pack_s[at * cols : (at + 1) * cols] = ref[...].astype(f32).T
    pack_s[3 * cols :] = o_ref[...].astype(f32)
    out_ref[...] = pack_s[...].astype(bf16)
    slices = mine_ref.shape[0] - PAD
    start = at_ref[0] * slices
    if slices % 8 == 0:
        start = pl.multiple_of(start, 8)
    mine_ref[:slices] = pack_s[pl.ds(start, slices), :].astype(bf16)
    mine_ref[slices:] = jnp.zeros_like(mine_ref[slices:])
    buckets, heads = rel_ref.shape
    lane = 0
    for at in range(0, buckets, PAD):
        for part in exact_parts(rel_ref[at : at + PAD]):
            mine_ref[slices:, lane : lane + heads] = part
            lane += TILE


def pack_weights(at, w_query, w_key, w_value, w_out, rel_bias, share):
    width, cols = w_query.shape
    slices = width // share
    full = lambda shape: pl.BlockSpec(shape, lambda i, at: (0, 0))
    return pl.pallas_call(
        pack_kernel,
        grid_spec=pltpu.PrefetchScalarGridSpec(
            num_scalar_prefetch=1,
            grid=(1,),
            in_specs=[full((width, cols))] * 3 + [full((cols, width)), full(rel_bias.shape)],
            out_specs=[full((width, width)), full((slices + PAD, width))],
            scratch_shapes=[pltpu.VMEM((width, width), f32)],
        ),
        out_shape=[
            jax.ShapeDtypeStruct((width, width), bf16),
            jax.ShapeDtypeStruct((slices + PAD, width), bf16),
        ],
        compiler_params=pltpu.CompilerParams(vmem_limit_bytes=VMEM),
        cost_estimate=cost(10**9, 2**20),
        name="pack_weights",
    )(at, w_query, w_key, w_value, w_out, rel_bias)


def unpack_table(pads, buckets, heads):
    rows = []
    lane = 0
    for _ in range(0, buckets, PAD):
        parts = [
            pads[:, :, lane + p * TILE : lane + p * TILE + heads].astype(f32) for p in range(3)
        ]
        rows.append(parts[0] + parts[1] + parts[2])
        lane += 3 * TILE
    return jnp.concatenate(rows, 1)


def stack_kernel(*refs):
    ins, outs = refs[:3], refs[3:]
    slices = outs[0].shape[1]
    for at, ref in enumerate(ins):
        outs[0][at] = ref[:slices]
        if len(outs) == 2:
            outs[1][at] = ref[slices:]


def stack(arrays, slices):
    rows, width = arrays[0].shape
    shapes = [(3, slices, width)] + ([(3, rows - slices, width)] if rows > slices else [])
    return pl.pallas_call(
        stack_kernel,
        out_shape=[jax.ShapeDtypeStruct(shape, bf16) for shape in shapes],
        cost_estimate=cost(0, 12 * arrays[0].size),
        name="stack",
    )(*arrays)


def others_kernel(order_ref, all_ref, *outs):
    slices = outs[0].shape[1]
    for k in range(1, all_ref.shape[0]):
        for at, out in enumerate(outs):
            out[k - 1] = all_ref[order_ref[k], at * slices : (at + 1) * slices]


def others_of(order, everything, count):
    n, total, width = everything.shape
    slices = total // count
    shape = (n - 1, slices, width)
    return pl.pallas_call(
        others_kernel,
        grid_spec=pltpu.PrefetchScalarGridSpec(
            num_scalar_prefetch=1,
            grid=(1,),
            in_specs=[pl.BlockSpec((n, total, width), lambda i, p: (0, 0, 0))],
            out_specs=[pl.BlockSpec(shape, lambda i, p: (0, 0, 0))] * count,
        ),
        out_shape=[jax.ShapeDtypeStruct(shape, bf16)] * count,
        cost_estimate=cost(0, 4 * everything.size),
        name="others_of",
    )(order, everything)


def attend_row(heads, hd, weights, a1_ref, vec_ref, seg_ref, qkv_ref, lse_ref, ctx_ref, bias_s):
    length = a1_ref.shape[0]
    blocks = length // TILE

    @pl.when(pl.program_id(1) == 0)
    def _():
        spread_bias(vec_ref, bias_s, heads)

    qkv_ref[0, 0] = dg(weights, a1_ref[...], NT).astype(bf16)
    q_mask, k_mask = masks(seg_ref[0])
    ones = jnp.ones((16, length), bf16)
    for h in range(heads):
        q_t = jnp.concatenate([qkv_ref[0, 0, h * hd : (h + 1) * hd], q_mask], 0)
        k_t = jnp.concatenate([qkv_ref[0, 0, (heads + h) * hd : (heads + h + 1) * hd], k_mask], 0)
        v_t = jnp.concatenate(
            [qkv_ref[0, 0, (2 * heads + h) * hd : (2 * heads + h + 1) * hd], ones], 0
        )
        scores = dg(k_t.T, q_t, NN)
        columns = []
        tops = []
        for i in range(blocks):
            tiles = [
                with_bias(
                    scores[j * TILE : (j + 1) * TILE, i * TILE : (i + 1) * TILE],
                    j - i,
                    h,
                    bias_s,
                    vec_ref,
                )
                for j in range(blocks)
            ]
            top = jnp.max(functools.reduce(jnp.maximum, tiles), 0, keepdims=True)
            tops.append(top)
            columns.append(jnp.concatenate([jnp.exp(t - top).astype(bf16) for t in tiles], 0))
        mixed = dg(v_t, jnp.concatenate(columns, 1), NN)
        total = mixed[hd : hd + 1]
        lse_ref[0, 0, h : h + 1, :] = jnp.concatenate(tops, 1) + jnp.log(total)
        ctx_ref[0, 0, h * hd : (h + 1) * hd, :] = (mixed[:hd] / total).astype(bf16)


def attn_own_kernel(heads, hd, a1_ref, vec_ref, seg_ref, w_ref, *rest):
    attend_row(heads, hd, w_ref[: 3 * heads * hd], a1_ref, vec_ref, seg_ref, *rest)


def attn_far_kernel(heads, hd, count, place_ref, a1_ref, vec_ref, seg_ref, own_ref, *rest):
    pieces = rest[:count]
    qkv_ref, lse_ref, ctx_ref, sorted_ref, bias_s, w_s, sems, out_sems = rest[count + 3 :]
    s, r = pl.program_id(0), pl.program_id(1)
    keep = [
        pltpu.make_async_copy(own_ref, sorted_ref.at[0], out_sems.at[0]),
        pltpu.make_async_copy(w_s, sorted_ref.at[pl.ds(1, w_s.shape[0])], out_sems.at[1]),
    ]

    @pl.when((s == 0) & (r == 0))
    def _():
        for copy in bring(place_ref, pieces, w_s, sems):
            copy.wait()
        for copy in keep:
            copy.start()

    attend_row(
        heads,
        hd,
        w_s[s, : 3 * heads * hd],
        a1_ref,
        vec_ref,
        seg_ref,
        qkv_ref,
        lse_ref,
        ctx_ref,
        bias_s,
    )

    @pl.when((s == pl.num_programs(0) - 1) & (r == pl.num_programs(1) - 1))
    def _():
        for copy in keep:
            copy.wait()


def attention(a1, own_a, vecs, segs, slots, place=None, pieces=None, earlier=None):
    rows, _, length = segs.shape
    width = a1.shape[1]
    heads = vecs.shape[1]
    hd = width // (4 * heads)
    cols = heads * hd
    first = slots - vecs.shape[0] if pieces else 0
    count = slots - 1 if pieces else 1
    anywhere = pl.BlockSpec(memory_space=pl.ANY)
    in_specs = [
        pl.BlockSpec((length, width), lambda s, r, *_: (r, 0)),
        pl.BlockSpec((1, heads, 4 * TILE), lambda s, r, *_: (s + (1 if pieces else 0), 0, 0)),
        pl.BlockSpec((1, 1, length), lambda s, r, *_: (r, 0, 0)),
    ]
    at = 1 if pieces else 0
    out_specs = [
        pl.BlockSpec((1, 1, 3 * cols, length), lambda s, r, *_: (s + at, r, 0, 0)),
        pl.BlockSpec((1, 1, heads, length), lambda s, r, *_: (s + at, r, 0, 0)),
        pl.BlockSpec((1, 1, cols, length), lambda s, r, *_: (s + at, r, 0, 0)),
    ]
    out_shape = [
        jax.ShapeDtypeStruct((slots, rows, 3 * cols, length), bf16),
        jax.ShapeDtypeStruct((slots, rows, heads, length), f32),
        jax.ShapeDtypeStruct((slots, rows, cols, length), bf16),
    ]
    scratch = [pltpu.VMEM((heads, TILE, 4 * TILE), f32)]
    steps = count * rows
    common = dict(
        compiler_params=pltpu.CompilerParams(vmem_limit_bytes=VMEM),
        cost_estimate=cost(steps * 2.5 * 10**9, 2**20),
    )
    if not pieces:
        return pl.pallas_call(
            functools.partial(attn_own_kernel, heads, hd),
            grid=(count, rows),
            in_specs=in_specs + [pl.BlockSpec((width, width), lambda s, r: (0, 0))],
            out_specs=out_specs,
            out_shape=out_shape,
            scratch_shapes=scratch,
            name="attn_own",
            **common,
        )(a1, vecs, segs, own_a)
    n = len(pieces)
    return pl.pallas_call(
        functools.partial(attn_far_kernel, heads, hd, n),
        grid_spec=pltpu.PrefetchScalarGridSpec(
            num_scalar_prefetch=1,
            grid=(count, rows),
            in_specs=in_specs
            + [pl.BlockSpec((width, width), lambda s, r, p: (0, 0))]
            + [anywhere] * (n + 3),
            out_specs=out_specs + [anywhere],
            scratch_shapes=scratch
            + [
                pltpu.VMEM((count, width, width), bf16),
                pltpu.SemaphoreType.DMA((n,)),
                pltpu.SemaphoreType.DMA((2,)),
            ],
        ),
        out_shape=out_shape + [jax.ShapeDtypeStruct((slots, width, width), bf16)],
        input_output_aliases={5 + n: 0, 6 + n: 1, 7 + n: 2},
        name="attn_far",
        **common,
    )(place, a1, vecs, segs, own_a, *pieces, *earlier)


GELU_A = math.sqrt(2.0 / math.pi)
GELU_B = 0.044715


def gelu(v):
    t = jnp.tanh(v * (GELU_A + (GELU_A * GELU_B) * (v * v)))
    half = 0.5 * v
    return half + half * t


def gelu_pair(v):
    square = v * v
    t = jnp.tanh(v * (GELU_A + (GELU_A * GELU_B) * square))
    half = 0.5 * v
    inner = GELU_A + (3.0 * GELU_A * GELU_B) * square
    return half + half * t, 0.5 + 0.5 * t + half * (1.0 - t * t) * inner


def ffn_own_kernel(x_ref, ctx_ref, wo_ref, gain_ref, b_ref, c_ref, mid_ref, a2_ref, part_ref):
    slots, _, cols, length = ctx_ref.shape
    attn = dg(
        ctx_ref[...].reshape(slots * cols, length),
        wo_ref[...].reshape(slots * cols, wo_ref.shape[-1]),
        TN,
    )
    mid = (x_ref[...].astype(f32) + attn).astype(bf16)
    mid_ref[...] = mid
    mid = mid.astype(f32)
    a2 = (mid * inv_rms(mid) * gain_ref[...]).astype(bf16)
    a2_ref[...] = a2
    hidden = gelu(dg(a2, b_ref[...], NN)).astype(bf16)
    part_ref[...] = dg(hidden, c_ref[...], NN).astype(bf16)


def ffn_own(x, ctx, sorted_a, gain, own_b, own_c):
    slots, rows, cols, length = ctx.shape
    tokens, width = x.shape
    units = own_b.shape[1]
    by_row = pl.BlockSpec((length, width), lambda r: (r, 0))
    return pl.pallas_call(
        ffn_own_kernel,
        grid=(rows,),
        in_specs=[
            by_row,
            pl.BlockSpec((slots, 1, cols, length), lambda r: (0, r, 0, 0)),
            pl.BlockSpec((slots, cols, width), lambda r: (0, 3, 0)),
            pl.BlockSpec((1, width), lambda r: (0, 0)),
            pl.BlockSpec((width, units), lambda r: (0, 0)),
            pl.BlockSpec((units, width), lambda r: (0, 0)),
        ],
        out_specs=[by_row] * 3,
        out_shape=[jax.ShapeDtypeStruct((tokens, width), bf16)] * 3,
        compiler_params=pltpu.CompilerParams(vmem_limit_bytes=VMEM),
        cost_estimate=cost(tokens * width * 6 * units, 2**24),
        name="ffn_own",
    )(x, ctx, sorted_a, gain, own_b, own_c)


def ffn_row(a2, mid, part, up, down, gain_ref, seg_ref, out_ref, res_ref, pool_ref, wait=None):
    res = mid.astype(f32) + part.astype(f32)
    for k in range(len(up)):
        if wait is not None:
            wait(k)
        hidden = gelu(dg(a2, up[k][...], NN)).astype(bf16)
        res = res + dg(hidden, down[k][...], NN)
    res_ref[...] = res.astype(bf16)
    final = (res * inv_rms(res) * gain_ref[...]).astype(bf16)
    out_ref[...] = final
    if pool_ref is not None:
        seg = seg_ref[0]
        hot = lax.broadcasted_iota(jnp.int32, (SEG_ROW, seg.shape[-1]), 0) == seg
        member = jnp.where(hot, 1.0, 0.0)
        pool_ref[...] = dg(member.astype(bf16), final, NN) / jnp.sum(member, 1, keepdims=True)


def ffn_first_kernel(
    count, place_ref, order_ref, a2_ref, mid_ref, part_ref, gain_ref, seg_ref, *rest
):
    pieces, far_c = rest[:count], rest[count]
    out_ref, res_ref, pool_ref, sb_ref, sc_ref, b_s, c_s, sems, out_sems = rest[count + 1 :]
    others = b_s.shape[0]
    slices = far_c.shape[2]
    copies = []
    for k in range(others):
        here = []
        for m in range(count):
            start = pl.multiple_of(place_ref[m], 16) if slices % 16 == 0 else place_ref[m]
            into = b_s.at[k, pl.ds(start, slices), :]
            here.append(pltpu.make_async_copy(pieces[m].at[k], into, sems.at[0, k, m]))
            into = c_s.at[k, pl.ds(m * slices, slices), :]
            here.append(pltpu.make_async_copy(far_c.at[m, k], into, sems.at[1, k, m]))
        copies.append(here)
    keep = []
    for k in range(others):
        keep.append(pltpu.make_async_copy(b_s.at[k], sb_ref.at[k], out_sems.at[0, k]))
        keep.append(pltpu.make_async_copy(c_s.at[k], sc_ref.at[k], out_sems.at[1, k]))
    for here in copies:
        for copy in here:
            copy.start()

    def wait(k):
        for copy in copies[k]:
            copy.wait()
        keep[2 * k].start()
        keep[2 * k + 1].start()

    ffn_row(
        a2_ref[...],
        mid_ref[...],
        part_ref[...],
        [b_s.at[k] for k in range(others)],
        [c_s.at[k] for k in range(others)],
        gain_ref,
        seg_ref,
        out_ref,
        res_ref,
        pool_ref,
        wait,
    )
    for copy in keep:
        copy.wait()


def ffn_first(place, order, a2, mid, part, gain, segs, pieces, far_c):
    rows, _, length = segs.shape
    tokens, width = a2.shape
    units = pieces[0].shape[-1]
    others = pieces[0].shape[0]
    n = len(pieces)
    first = pl.BlockSpec((length, width), lambda r, p, o: (o[0], 0))
    anywhere = pl.BlockSpec(memory_space=pl.ANY)
    return pl.pallas_call(
        functools.partial(ffn_first_kernel, n),
        grid_spec=pltpu.PrefetchScalarGridSpec(
            num_scalar_prefetch=2,
            grid=(1,),
            in_specs=[
                first,
                first,
                first,
                pl.BlockSpec((1, width), lambda r, p, o: (0, 0)),
                pl.BlockSpec((1, 1, length), lambda r, p, o: (o[0], 0, 0)),
            ]
            + [anywhere] * (n + 1),
            out_specs=[
                first,
                first,
                pl.BlockSpec((SEG_ROW, width), lambda r, p, o: (0, 0)),
                anywhere,
                anywhere,
            ],
            scratch_shapes=[
                pltpu.VMEM((others, width, units), bf16),
                pltpu.VMEM((others, units, width), bf16),
                pltpu.SemaphoreType.DMA((2, others, n)),
                pltpu.SemaphoreType.DMA((2, others)),
            ],
        ),
        out_shape=[
            jax.ShapeDtypeStruct((tokens, width), bf16),
            jax.ShapeDtypeStruct((tokens, width), bf16),
            jax.ShapeDtypeStruct((SEG_ROW, width), f32),
            jax.ShapeDtypeStruct((others, width, units), bf16),
            jax.ShapeDtypeStruct((others, units, width), bf16),
        ],
        compiler_params=pltpu.CompilerParams(vmem_limit_bytes=VMEM),
        cost_estimate=cost(length * width * 4 * units * others, 2**24),
        name="ffn_first",
    )(place, order, a2, mid, part, gain, segs, *pieces, far_c)


def ffn_rest_kernel(
    order_ref, a2_ref, mid_ref, part_ref, gain_ref, b_ref, c_ref, _out, _res, out_ref, res_ref
):
    others = b_ref.shape[0]
    ffn_row(
        a2_ref[...],
        mid_ref[...],
        part_ref[...],
        [b_ref.at[k] for k in range(others)],
        [c_ref.at[k] for k in range(others)],
        gain_ref,
        None,
        out_ref,
        res_ref,
        None,
    )


def ffn_rest(order, a2, mid, part, gain, sorted_b, sorted_c, out, res, rows):
    tokens, width = a2.shape
    length = tokens // rows
    slots, _, units = sorted_b.shape
    row = pl.BlockSpec((length, width), lambda r, o: (o[r + 1], 0))
    whole = pl.BlockSpec(sorted_b.shape, lambda r, o: (0, 0, 0))
    anywhere = pl.BlockSpec(memory_space=pl.ANY)
    return pl.pallas_call(
        ffn_rest_kernel,
        grid_spec=pltpu.PrefetchScalarGridSpec(
            num_scalar_prefetch=1,
            grid=(rows - 1,),
            in_specs=[row, row, row, pl.BlockSpec((1, width), lambda r, o: (0, 0)), whole, whole]
            + [anywhere] * 2,
            out_specs=[row, row],
        ),
        out_shape=[jax.ShapeDtypeStruct((tokens, width), bf16)] * 2,
        input_output_aliases={7: 0, 8: 1},
        compiler_params=pltpu.CompilerParams(vmem_limit_bytes=VMEM),
        cost_estimate=cost(tokens * width * 3 * units * slots, 2**24),
        name="ffn_rest",
    )(order, a2, mid, part, gain, sorted_b, sorted_c, out, res)


def loss_math(pooled, project, pair_col, pair_row, gain):
    slots = pooled.shape[0]
    projected = dg(pooled, project, NN)
    inv_norm = lax.rsqrt(jnp.sum(projected * projected, -1, keepdims=True) + epsilon)
    unit = projected * inv_norm
    embedded = unit.astype(bf16)
    similar = logit_scale * dg(embedded, embedded, NT)
    rows = lax.broadcasted_iota(jnp.int32, (slots, slots), 0)
    columns = lax.broadcasted_iota(jnp.int32, (slots, slots), 1)
    same = rows == columns
    similar = jnp.where(same, masked_value, similar)
    partner = jnp.where((pair_col == pair_row) & jnp.logical_not(same), 2.0, 0.0)

    def total(axis):
        top = jnp.max(similar, axis, keepdims=True)
        return top + jnp.log(jnp.sum(jnp.exp(similar - top), axis, keepdims=True))

    both = jnp.exp(similar - total(1)) + jnp.exp(similar - total(0)) - partner
    high = both.astype(bf16)
    low = (both - high.astype(f32)).astype(bf16)
    d_unit = (loss_scale * logit_scale) * (dg(high, embedded, NN) + dg(low, embedded, NN))
    d_proj = inv_norm * (d_unit - unit * jnp.sum(d_unit * unit, -1, keepdims=True))
    d_proj = d_proj.astype(bf16)
    d_pooled = dg(d_proj, project, NT)
    d_gain = jnp.sum(d_pooled * pooled.astype(f32), 0, keepdims=True) / gain
    return d_proj, d_pooled, d_gain


def loss_kernel(count, at_ref, *refs):
    pieces, rest = refs[:count], refs[count:]
    project_ref, pc_ref, pr_ref, gain_ref, dpool_ref, dproj_ref, dgain_ref, a_s, b_s = rest
    each = SEG_ROW
    parts = pieces[0].shape[0] // each
    for m, piece in enumerate(pieces):
        value = piece[...].astype(f32)
        for part in range(parts):
            start = pl.multiple_of(at_ref[1 + m * parts + part] * each, each)
            a_s[pl.ds(start, each), :] = value[part * each : (part + 1) * each]
    pooled = a_s[...].astype(bf16)
    d_proj, d_pooled, d_gain = loss_math(
        pooled, project_ref[...], pc_ref[...], pr_ref[...], gain_ref[...]
    )
    a_s[...] = d_pooled
    b_s[...] = dg(pooled, d_proj, TN)
    here = dpool_ref.shape[0]
    block = dproj_ref.shape[0]
    dpool_ref[...] = a_s[pl.ds(pl.multiple_of(at_ref[0] * here, here), here), :]
    dproj_ref[...] = b_s[pl.ds(pl.multiple_of(at_ref[0] * block, block), block), :]
    dgain_ref[...] = d_gain


def loss_head(at, pieces, project, pairs, gain, here, block):
    slots = sum(piece.shape[0] for piece in pieces)
    width = project.shape[0]
    pair_col = pairs[:, None]
    pair_row = pairs[None, :]
    if len(pieces) == 1:
        pooled = pieces[0]
        d_proj, d_pooled, d_gain = loss_math(pooled, project, pair_col, pair_row, gain)
        own_cols = lax.dynamic_slice_in_dim(pooled, at[0] * block, block, 1)
        d_pooled = lax.dynamic_slice_in_dim(d_pooled, at[0] * here, here, 0)
        return d_pooled, dg(own_cols, d_proj, TN), d_gain
    full = lambda shape: pl.BlockSpec(shape, lambda i, at: (0, 0))
    return pl.pallas_call(
        functools.partial(loss_kernel, len(pieces)),
        grid_spec=pltpu.PrefetchScalarGridSpec(
            num_scalar_prefetch=1,
            grid=(1,),
            in_specs=[full(piece.shape) for piece in pieces]
            + [
                full(project.shape),
                full((slots, 1)),
                full((1, slots)),
                full((1, width)),
            ],
            out_specs=[full((here, width)), full((block, width)), full((1, width))],
            scratch_shapes=[pltpu.VMEM((slots, width), f32), pltpu.VMEM((width, width), f32)],
        ),
        out_shape=[
            jax.ShapeDtypeStruct((here, width), f32),
            jax.ShapeDtypeStruct((block, width), f32),
            jax.ShapeDtypeStruct((1, width), f32),
        ],
        compiler_params=pltpu.CompilerParams(vmem_limit_bytes=VMEM),
        cost_estimate=cost(3 * 10**9, 2**20),
        name="loss_head",
    )(at, *pieces, project, pair_col, pair_row, gain)


def d_result_of(res, seg, d_pool, gain):
    hot = lax.broadcasted_iota(jnp.int32, (SEG_ROW, seg.shape[-1]), 0) == seg
    member = jnp.where(hot, 1.0, 0.0)
    per_token = d_pool / jnp.sum(member, 1, keepdims=True)
    high = per_token.astype(bf16)
    low = (per_token - high.astype(f32)).astype(bf16)
    twice = jnp.concatenate([member, member], 0).astype(bf16)
    d_final = dg(twice, jnp.concatenate([high, low], 0), TN)
    scale = inv_rms(res)
    unit = res * scale
    weighted = d_final * gain
    return scale * (weighted - unit * jnp.mean(weighted * unit, -1, keepdims=True))


def ffn_back_kernel(
    row_ref,
    res_ref,
    mid_ref,
    a2_ref,
    seg_ref,
    dpool_ref,
    gain_end_ref,
    gain_ref,
    own_b_ref,
    own_c_ref,
    b_ref,
    c_ref,
    wo_ref,
    dmid_ref,
    dattn_ref,
    dctx_ref,
    dgain_ref,
    dres_s,
    low_s,
    sum_s,
):
    k = pl.program_id(0)

    @pl.when(k == 0)
    def _():
        d_res = d_result_of(
            res_ref[...].astype(f32), seg_ref[0], dpool_ref[...], gain_end_ref[...]
        )
        dres_s[...] = d_res
        low_s[...] = d_res.astype(bf16)
        sum_s[...] = jnp.zeros_like(sum_s)

    def add(up, down):
        slope = gelu_pair(dg(a2_ref[...], up, NN))[1]
        d_pre = (dg(low_s[...], down, NT) * slope).astype(bf16)
        sum_s[...] += dg(d_pre, up, NT)

    @pl.when(k == 0)
    def _():
        add(own_b_ref[...], own_c_ref[...])

    @pl.when(k > 0)
    def _():
        add(b_ref[0], c_ref[0])

    @pl.when(k == pl.num_programs(0) - 1)
    def _():
        mid = mid_ref[...].astype(f32)
        scale = inv_rms(mid)
        unit = mid * scale
        grad = sum_s[...]
        weighted = grad * gain_ref[...]
        d_mid = dres_s[...] + scale * (weighted - unit * jnp.mean(weighted * unit, -1, keepdims=True))
        dgain_ref[...] = jnp.sum(grad * unit, 0, keepdims=True)
        dmid_ref[...] = d_mid
        low = d_mid.astype(bf16)
        dattn_ref[...] = low
        for s in range(wo_ref.shape[0]):
            dctx_ref[s] = dg(wo_ref[s], low, NT).astype(bf16)


def ffn_back(
    row, res, mid, a2, segs, d_pool, gain_end, gain, sorted_a, own_b, own_c, sorted_b, sorted_c
):
    rows, _, length = segs.shape
    tokens, width = res.shape
    slots = sorted_a.shape[0]
    units = sorted_b.shape[-1]
    cols = width // 4
    own = pl.BlockSpec((length, width), lambda k, row: (row[0], 0))
    fixed = lambda k, row: (0, 0)
    return pl.pallas_call(
        ffn_back_kernel,
        grid_spec=pltpu.PrefetchScalarGridSpec(
            num_scalar_prefetch=1,
            grid=(slots,),
            in_specs=[
                own,
                own,
                own,
                pl.BlockSpec((1, 1, length), lambda k, row: (row[0], 0, 0)),
                pl.BlockSpec((SEG_ROW, width), lambda k, row: (row[0], 0)),
                pl.BlockSpec((1, width), fixed),
                pl.BlockSpec((1, width), fixed),
                pl.BlockSpec((width, units), fixed),
                pl.BlockSpec((units, width), fixed),
                pl.BlockSpec((1, width, units), lambda k, row: (jnp.maximum(k - 1, 0), 0, 0)),
                pl.BlockSpec((1, units, width), lambda k, row: (jnp.maximum(k - 1, 0), 0, 0)),
                pl.BlockSpec((slots, cols, width), lambda k, row: (0, 3, 0)),
            ],
            out_specs=[
                pl.BlockSpec((length, width), fixed),
                pl.BlockSpec((length, width), fixed),
                pl.BlockSpec((slots, cols, length), lambda k, row: (0, 0, 0)),
                pl.BlockSpec((1, width), fixed),
            ],
            scratch_shapes=[
                pltpu.VMEM((length, width), f32),
                pltpu.VMEM((length, width), bf16),
                pltpu.VMEM((length, width), f32),
            ],
        ),
        out_shape=[
            jax.ShapeDtypeStruct((length, width), f32),
            jax.ShapeDtypeStruct((length, width), bf16),
            jax.ShapeDtypeStruct((slots, cols, length), bf16),
            jax.ShapeDtypeStruct((1, width), f32),
        ],
        compiler_params=pltpu.CompilerParams(vmem_limit_bytes=VMEM),
        cost_estimate=cost(1.2 * 10**10, 2**24),
        name="ffn_back",
    )(row, res, mid, a2, segs, d_pool, gain_end, gain, own_b, own_c, sorted_b, sorted_c, sorted_a)


def fold(tile):
    lanes = tile.shape[1]
    total = tile[0:8]
    for b in range(1, TILE // 8):
        total = total + pltpu.roll(tile[8 * b : 8 * b + 8], lanes - 8 * b, 1)
    return total


def attn_back_kernel(
    heads,
    hd,
    row_ref,
    qkv_ref,
    lse_ref,
    ctx_ref,
    dctx_ref,
    vec_ref,
    seg_ref,
    w_ref,
    x_ref,
    dmid_ref,
    gain_ref,
    dqkv_ref,
    fold_ref,
    dtok_ref,
    dgain_ref,
    bias_s,
    sum_s,
):
    slot = pl.program_id(0)
    length = qkv_ref.shape[-1]
    blocks = length // TILE
    spread_bias(vec_ref, bias_s, heads)
    q_mask, k_mask = masks(seg_ref[0])
    for h in range(heads):
        q_low = qkv_ref[0, 0, h * hd : (h + 1) * hd]
        k_low = qkv_ref[0, 0, (heads + h) * hd : (heads + h + 1) * hd]
        v_low = qkv_ref[0, 0, (2 * heads + h) * hd : (2 * heads + h + 1) * hd]
        dc = dctx_ref[0, h * hd : (h + 1) * hd]
        c = ctx_ref[0, 0, h * hd : (h + 1) * hd]
        delta = jnp.sum(dc.astype(f32) * c.astype(f32), 0, keepdims=True)
        lse = lse_ref[0, 0, h : h + 1]
        scores = dg(
            jnp.concatenate([k_low, k_mask], 0).T, jnp.concatenate([q_low, q_mask], 0), NN
        )
        d_probs = dg(v_low.T, dc, NN)
        probs_cols = []
        score_cols = []
        near = [None, None, None]
        far = [None, None]
        for i in range(blocks):
            at = slice(i * TILE, (i + 1) * TILE)
            probs = []
            grads = []
            for j in range(blocks):
                to = slice(j * TILE, (j + 1) * TILE)
                tile = with_bias(scores[to, at], j - i, h, bias_s, vec_ref)
                prob = jnp.exp(tile - lse[:, at])
                grad = prob * (d_probs[to, at] - delta[:, at])
                probs.append(prob.astype(bf16))
                grads.append(grad.astype(bf16))
                if abs(j - i) <= 1:
                    old = near[j - i + 1]
                    near[j - i + 1] = grad if old is None else old + grad
                else:
                    old = far[int(j < i)]
                    far[int(j < i)] = grad if old is None else old + grad
            probs_cols.append(jnp.concatenate(probs, 0))
            score_cols.append(jnp.concatenate(grads, 0))
        probs = jnp.concatenate(probs_cols, 1)
        grads = jnp.concatenate(score_cols, 1)
        dqkv_ref[0, h * hd : (h + 1) * hd] = dg(k_low, grads, NN).astype(bf16)
        dqkv_ref[0, (heads + h) * hd : (heads + h + 1) * hd] = dg(q_low, grads, NT).astype(bf16)
        dqkv_ref[0, (2 * heads + h) * hd : (2 * heads + h + 1) * hd] = dg(dc, probs, NT).astype(
            bf16
        )
        band = jnp.concatenate([near[1], near[0], jnp.zeros_like(near[0]), near[2]], 1)
        fold_ref[0, h, :, : 4 * TILE] = fold(band)
        for side in range(2):
            total = far[side][0:8]
            for b in range(1, TILE // 8):
                total = total + far[side][8 * b : 8 * b + 8]
            fold_ref[0, h, :, (4 + side) * TILE : (5 + side) * TILE] = total
    part = dg(dqkv_ref[0], w_ref[0], TN)

    @pl.when(slot == 0)
    def _():
        sum_s[...] = part

    @pl.when(slot > 0)
    def _():
        sum_s[...] += part

    @pl.when(slot == pl.num_programs(0) - 1)
    def _():
        x = x_ref[...].astype(f32)
        scale = inv_rms(x)
        unit = x * scale
        grad = sum_s[...]
        weighted = grad * gain_ref[...]
        d_tok = dmid_ref[...] + scale * (weighted - unit * jnp.mean(weighted * unit, -1, keepdims=True))
        dtok_ref[...] = d_tok.astype(bf16)
        dgain_ref[...] = jnp.sum(grad * unit, 0, keepdims=True)


def attn_back(row, qkv, lse, ctx, d_ctx, vecs, segs, all_a, x, d_mid, gain):
    slots, rows, cols3, length = qkv.shape
    heads = lse.shape[2]
    cols = cols3 // 3
    width = x.shape[1]
    own4 = lambda k, row: (k, row[0], 0, 0)
    slot = lambda k, row: (k, 0, 0)
    fixed = lambda k, row: (0, 0)
    return pl.pallas_call(
        functools.partial(attn_back_kernel, heads, cols // heads),
        grid_spec=pltpu.PrefetchScalarGridSpec(
            num_scalar_prefetch=1,
            grid=(slots,),
            in_specs=[
                pl.BlockSpec((1, 1, cols3, length), own4),
                pl.BlockSpec((1, 1, heads, length), own4),
                pl.BlockSpec((1, 1, cols, length), own4),
                pl.BlockSpec((1, cols, length), slot),
                pl.BlockSpec((1, heads, 4 * TILE), slot),
                pl.BlockSpec((1, 1, length), lambda k, row: (row[0], 0, 0)),
                pl.BlockSpec((1, cols3, width), slot),
                pl.BlockSpec((length, width), lambda k, row: (row[0], 0)),
                pl.BlockSpec((length, width), fixed),
                pl.BlockSpec((1, width), fixed),
            ],
            out_specs=[
                pl.BlockSpec((1, cols3, length), slot),
                pl.BlockSpec((1, heads, 8, 6 * TILE), lambda k, row: (k, 0, 0, 0)),
                pl.BlockSpec((length, width), fixed),
                pl.BlockSpec((1, width), fixed),
            ],
            scratch_shapes=[
                pltpu.VMEM((heads, TILE, 4 * TILE), f32),
                pltpu.VMEM((length, width), f32),
            ],
        ),
        out_shape=[
            jax.ShapeDtypeStruct((slots, cols3, length), bf16),
            jax.ShapeDtypeStruct((slots, heads, 8, 6 * TILE), f32),
            jax.ShapeDtypeStruct((length, width), bf16),
            jax.ShapeDtypeStruct((1, width), f32),
        ],
        compiler_params=pltpu.CompilerParams(vmem_limit_bytes=VMEM),
        cost_estimate=cost(1.5 * 10**10, 2**24),
        name="attn_back",
    )(row, qkv, lse, ctx, d_ctx, vecs, segs, all_a, x, d_mid, gain)


def split_blocks(core, rel_ref, block, pad, extra, values, keep_ref, give_ref, lead):
    for c in range(2):

        @pl.when(core == c)
        def _():
            for chip in range(4):
                for ref, j in ((keep_ref, 2 * chip + c), (give_ref, 2 * chip + 1 - c)):
                    rows = values(j * block, (j + 1) * block)
                    for at, value in enumerate(rows):
                        ref[rel_ref[chip], lead + at, :block] = value
                    if pad:
                        ref[rel_ref[chip], lead, block:] = extra(j)


def attn_weights_kernel(
    block, place_ref, a1_ref, dattn_ref, dqkv_ref, ctx_ref, extra_ref, *rest
):
    outs, (a1_s, dattn_s, sum_s) = rest[:-3], rest[-3:]

    @pl.when(pl.program_id(0) == 0)
    def _():
        a1_s[...] = a1_ref[...].T
        dattn_s[...] = dattn_ref[...].T

    cols3 = dqkv_ref.shape[1]
    sum_s[:, :cols3] = dg(a1_s[...], dqkv_ref[0], NT).astype(bf16)
    sum_s[:, cols3:] = dg(dattn_s[...], ctx_ref[0, 0], NT).astype(bf16)
    if len(outs) == 1:
        outs[0][0] = sum_s[...]
    else:
        split_blocks(
            place_ref[1],
            place_ref.at[pl.ds(2, 4)],
            block,
            True,
            lambda j: extra_ref[0, j],
            lambda a, b: [sum_s[a:b]],
            outs[0],
            outs[1],
            0,
        )


def attn_weights(place, a1, d_attn, d_qkv, ctx, extra, split):
    slots, cols3, length = d_qkv.shape
    cols = ctx.shape[2]
    width = a1.shape[1]
    _, blocks, pad, _ = extra.shape
    block = width // blocks
    if split:
        shape = (4, slots, block + pad, width)
        out_specs = [pl.BlockSpec((4, 1, block + pad, width), lambda k, p: (0, k, 0, 0))] * 2
        out_shape = [jax.ShapeDtypeStruct(shape, bf16)] * 2
    else:
        out_specs = [pl.BlockSpec((1, width, width), lambda k, p: (k, 0, 0))]
        out_shape = [jax.ShapeDtypeStruct((slots, width, width), bf16)]
    return pl.pallas_call(
        functools.partial(attn_weights_kernel, block),
        grid_spec=pltpu.PrefetchScalarGridSpec(
            num_scalar_prefetch=1,
            grid=(slots,),
            in_specs=[
                pl.BlockSpec((length, width), lambda k, p: (p[0], 0)),
                pl.BlockSpec((length, width), lambda k, p: (0, 0)),
                pl.BlockSpec((1, cols3, length), lambda k, p: (k, 0, 0)),
                pl.BlockSpec((1, 1, cols, length), lambda k, p: (k, p[0], 0, 0)),
                pl.BlockSpec((1, blocks, pad, width), lambda k, p: (k, 0, 0, 0)),
            ],
            out_specs=out_specs,
            scratch_shapes=[
                pltpu.VMEM((width, length), bf16),
                pltpu.VMEM((width, length), bf16),
                pltpu.VMEM((width, width), bf16),
            ],
        ),
        out_shape=out_shape,
        compiler_params=pltpu.CompilerParams(vmem_limit_bytes=VMEM),
        cost_estimate=cost(10**6, 10**6),
        name="attn_weights",
    )(place, a1, d_attn, d_qkv, ctx, extra)


def ffn_grads_kernel(
    res_ref, seg_ref, dpool_ref, gain_ref, a2_ref, b_ref, c_ref, low_ref, hid_ref, dpre_ref
):
    d_res = d_result_of(res_ref[...].astype(f32), seg_ref[0], dpool_ref[...], gain_ref[...])
    low = d_res.astype(bf16)
    low_ref[...] = low
    hidden, slope = gelu_pair(dg(a2_ref[...], b_ref[...], NN))
    hid_ref[...] = hidden.astype(bf16)
    dpre_ref[...] = (dg(low, c_ref[...], NT) * slope).astype(bf16)


def ffn_grads(res, segs, d_pool, gain, a2, own_b, own_c):
    rows, _, length = segs.shape
    tokens, width = res.shape
    units = own_b.shape[1]
    by_row = pl.BlockSpec((length, width), lambda r: (r, 0))
    by_unit = pl.BlockSpec((length, units), lambda r: (r, 0))
    return pl.pallas_call(
        ffn_grads_kernel,
        grid=(rows,),
        in_specs=[
            by_row,
            pl.BlockSpec((1, 1, length), lambda r: (r, 0, 0)),
            pl.BlockSpec((SEG_ROW, width), lambda r: (r, 0)),
            pl.BlockSpec((1, width), lambda r: (0, 0)),
            by_row,
            pl.BlockSpec((width, units), lambda r: (0, 0)),
            pl.BlockSpec((units, width), lambda r: (0, 0)),
        ],
        out_specs=[by_row, by_unit, by_unit],
        out_shape=[
            jax.ShapeDtypeStruct((tokens, width), bf16),
            jax.ShapeDtypeStruct((tokens, units), bf16),
            jax.ShapeDtypeStruct((tokens, units), bf16),
        ],
        compiler_params=pltpu.CompilerParams(vmem_limit_bytes=VMEM),
        cost_estimate=cost(8 * 10**9, 2**24),
        name="ffn_grads",
    )(res, segs, d_pool, gain, a2, own_b, own_c)


def ffn_weights_kernel(block, place_ref, low_ref, hid_ref, a2_ref, dpre_ref, *rest):
    outs, (up_s, down_s) = rest[:-2], rest[-2:]
    r = pl.program_id(0)

    @pl.when(r == 0)
    def _():
        up_s[...] = jnp.zeros_like(up_s)
        down_s[...] = jnp.zeros_like(down_s)

    up_s[...] += dg(a2_ref[...], dpre_ref[...], TN)
    down_s[...] += dg(low_ref[...], hid_ref[...], TN)

    @pl.when(r == pl.num_programs(0) - 1)
    def _():
        if len(outs) == 1:
            outs[0][0] = up_s[...].astype(bf16)
            outs[0][1] = down_s[...].astype(bf16)
        else:
            split_blocks(
                place_ref[1],
                place_ref.at[pl.ds(2, 4)],
                block,
                False,
                None,
                lambda a, b: [up_s[a:b].astype(bf16), down_s[a:b].astype(bf16)],
                outs[0],
                outs[1],
                0,
            )


def ffn_weights(place, low, hidden, a2, d_pre, rows, blocks, split):
    tokens, width = low.shape
    length = tokens // rows
    units = hidden.shape[1]
    block = width // blocks
    by_row = pl.BlockSpec((length, width), lambda r, p: (r, 0))
    by_unit = pl.BlockSpec((length, units), lambda r, p: (r, 0))
    shape = (4, 2, block, units) if split else (2, width, units)
    zeros = (0,) * len(shape)
    return pl.pallas_call(
        functools.partial(ffn_weights_kernel, block),
        grid_spec=pltpu.PrefetchScalarGridSpec(
            num_scalar_prefetch=1,
            grid=(rows,),
            in_specs=[by_row, by_unit, by_row, by_unit],
            out_specs=[pl.BlockSpec(shape, lambda r, p: zeros)] * (2 if split else 1),
            scratch_shapes=[pltpu.VMEM((width, units), f32)] * 2,
        ),
        out_shape=[jax.ShapeDtypeStruct(shape, bf16)] * (2 if split else 1),
        compiler_params=pltpu.CompilerParams(vmem_limit_bytes=VMEM),
        cost_estimate=cost(8 * 10**9, 2**24),
        name="ffn_weights",
    )(place, low, hidden, a2, d_pre)


def shards(
    n_dp,
    n_tp,
    tokens,
    segment_ids,
    pair_order,
    w_query,
    w_key,
    w_value,
    w_out,
    rel_bias,
    gain_attn,
    w_hidden,
    w_down,
    gain_ffn,
    gain_final,
    w_project,
):
    rows, length = segment_ids.shape
    bucket_count, heads = rel_bias.shape
    width = tokens.shape[1]
    units = w_hidden.shape[1]
    dp = lax.axis_index("dp")
    tp = lax.axis_index("tp")
    share = math.gcd(n_dp, 8)
    split = n_dp == 8
    mates = [[(i, i ^ m) for i in range(n_dp)] for m in range(share)]
    levels = [[(i, i ^ k) for i in range(n_tp)] for k in range(n_tp)]

    def over_dp(value, m):
        return lax.ppermute(value, "dp", mates[m])

    def over_tp(value, k):
        return lax.ppermute(value, "tp", levels[k])

    slices = width // share
    low_bits = dp % share
    place = (low_bits ^ jnp.arange(share, dtype=jnp.int32)) * slices

    def from_levels(mine):
        return stack([over_tp(mine, k) for k in range(1, n_tp)], slices)

    def from_chips(far):
        return [far] + [over_dp(far, m) for m in range(2, share, 2)]

    def from_cores(pieces):
        both = [(piece, over_dp(piece, 1)) for piece in pieces]
        return [piece for pair in both for piece in pair]

    def after(values, others):
        return lax.optimization_barrier((values, others))[0]

    order = tp ^ jnp.arange(n_tp, dtype=jnp.int32)
    pack_a, mine_a = pack_weights(
        low_bits[None].astype(jnp.int32), w_query, w_key, w_value, w_out, rel_bias, share
    )
    far_a, pads = from_levels(mine_a)
    mine_bc = jnp.concatenate(
        [
            lax.dynamic_slice_in_dim(w, low_bits * slices, slices, 0)
            for w in (w_hidden, w_down)
        ]
    )
    all_bc = lax.all_gather(mine_bc, "tp", axis=0)
    tables = jnp.concatenate([rel_bias[None], unpack_table(pads, bucket_count, heads)])
    vec_own = jnp.einsum("kbh,bn->khn", tables[:1], bias_lanes(bucket_count), precision=highest)
    vecs = jnp.einsum("kbh,bn->khn", tables, bias_lanes(bucket_count), precision=highest)
    segs = segment_ids[:, None, :]
    row = tp[None].astype(jnp.int32)
    one = gain_attn[None]
    two = gain_ffn[None]
    end = gain_final[None]

    x = tokens.astype(f32)
    a1 = (x * inv_rms(x) * one).astype(bf16)
    state = attention(after(a1, far_a), pack_a, vec_own, segs, n_tp)
    far_a = from_chips(far_a)
    far_b, far_c = others_of(after(order, (state, far_a)), all_bc, 2)
    groups = np.arange(n_dp).reshape(-1, share).tolist()
    far_c = lax.all_gather(far_c, "dp", axis=0, axis_index_groups=groups)
    far_a = from_cores(after(far_a, far_b))
    far_b = from_chips(after(far_b, far_a))
    qkv, lse, ctx, sorted_a = attention(a1, pack_a, vecs, segs, n_tp, place, far_a, state)
    far_b = from_cores(after(far_b, lse))
    mid, a2, part = ffn_own(tokens, ctx, sorted_a, two, w_hidden, w_down)
    layer_out, res, pooled, sorted_b, sorted_c = ffn_first(
        place, order, a2, mid, part, end, segs, far_b, far_c
    )
    block = width // n_dp
    here = rows * SEG_ROW
    pooled = pooled.astype(bf16)
    if split:
        pooled = jnp.concatenate([pooled] + [over_tp(pooled, k) for k in range(1, n_tp)])
        pooled = jnp.concatenate([pooled, over_dp(pooled, 1)])
        pooled_all = from_chips(pooled)
        spots = (dp ^ jnp.arange(n_dp))[:, None] * rows + order[None]
        at = jnp.concatenate([dp[None], spots.reshape(-1)]).astype(jnp.int32)
    else:
        pooled = lax.all_gather(pooled, "tp", axis=0, tiled=True)
        pooled_all = [lax.all_gather(pooled, "dp", axis=0, tiled=True)]
        at = dp[None].astype(jnp.int32)
    d_pool, grad_project, d_gain_end = loss_head(
        at, pooled_all, w_project, pair_order // 2, end, here, block
    )
    grad_gain_final = lax.dynamic_slice_in_dim(d_gain_end[0], dp * block, block, 0)
    d_mid, d_attn, d_ctx, d_gain_two = ffn_back(
        row,
        res,
        mid,
        a2,
        segs,
        d_pool,
        end,
        two,
        sorted_a,
        w_hidden,
        w_down,
        sorted_b,
        sorted_c,
    )
    d_qkv, folded, d_tok, d_gain_one = attn_back(
        row, qkv, lse, ctx, d_ctx, vecs, segs, sorted_a, tokens, d_mid, one
    )
    d_tokens = lax.all_gather(d_tok, "tp", axis=0, tiled=True).astype(f32)

    d_rel = jnp.einsum(
        "khn,nb->kbh",
        folded.reshape(n_tp, heads, -1),
        grad_lanes(bucket_count),
        precision=highest,
    )
    gains = jnp.concatenate([d_gain_one, d_gain_two])
    pad = 16
    extra = jnp.zeros((n_tp, n_dp, pad, width), bf16)
    if split:
        small = d_rel.reshape(n_tp, 1, 1, bucket_count * heads).astype(bf16)
        gain_rows = jnp.swapaxes(gains.reshape(2, n_dp, block), 0, 1).astype(bf16)
        extra = jnp.concatenate(
            [
                jnp.broadcast_to(gain_rows[None], (n_tp, n_dp, 2, block)),
                jnp.broadcast_to(small, (n_tp, n_dp, 1, block)),
                jnp.zeros((n_tp, n_dp, pad - 3, block), bf16),
            ],
            2,
        )
        extra = jnp.pad(extra, ((0, 0), (0, 0), (0, 0), (0, width - block)))
    chips = (dp // 2) ^ jnp.arange(4, dtype=jnp.int32)
    spots = jnp.concatenate([row, (dp % 2)[None].astype(jnp.int32), chips])
    parts_a = attn_weights(spots, a1, d_attn, d_qkv, ctx, extra, split)

    def to_core(parts):
        keep, give = parts
        took = over_dp(give, 1)
        return [rounded(keep[c].astype(f32) + took[c].astype(f32)) for c in range(4)]

    def to_chip(pair):
        return [pair[0]] + [over_dp(pair[c].astype(bf16), 2 * c) for c in range(1, 4)]

    def total(parts):
        return tree([part.astype(f32) for part in parts])

    def scatter(parts):
        return lax.psum_scatter(parts[0].astype(f32), "dp", scatter_dimension=1, tiled=True)

    if split:
        pair_a = to_core(parts_a)
        got_a = to_chip(pair_a)
        first = after(order, pair_a)
    else:
        first = after(order, parts_a)
    layer_out, res = ffn_rest(
        first, a2, mid, part, end, sorted_b, sorted_c, layer_out, res, rows
    )
    low, hidden, d_pre = ffn_grads(res, segs, d_pool, end, a2, w_hidden, w_down)
    parts_f = ffn_weights(spots, low, hidden, a2, d_pre, rows, n_dp, split)
    if split:
        got_f = to_chip(to_core(after(parts_f, got_a)))
        own_a, own_f = rounded(total(after(got_a, got_f))), total(got_f)
    else:
        own_a, own_f = rounded(scatter(parts_a)), scatter(parts_f)

    def reduce_tp(value):
        return tree([value[0]] + [over_tp(value[k], k) for k in range(1, n_tp)])

    grad_a = tree(
        [own_a[0].astype(f32)]
        + [over_tp(own_a[k].astype(bf16), k).astype(f32) for k in range(1, n_tp)]
    )
    cols = width // 4
    if split:
        gain_one, gain_two = grad_a[block, :block], grad_a[block + 1, :block]
        d_rel_here = grad_a[block + 2, : bucket_count * heads].reshape(bucket_count, heads)
    else:
        gains = tree([gains] + [over_tp(gains, k) for k in range(1, n_tp)])
        d_rel_here, gains = lax.psum((reduce_tp(d_rel), gains), "dp")
        gain_one, gain_two = lax.dynamic_slice_in_dim(gains, dp * block, block, 1)
    return (
        layer_out,
        d_tokens,
        grad_a[:block, :cols],
        grad_a[:block, cols : 2 * cols],
        grad_a[:block, 2 * cols : 3 * cols],
        grad_a[:block, 3 * cols :].T,
        d_rel_here,
        gain_one,
        own_f[0],
        own_f[1].T,
        gain_two,
        grad_gain_final,
        grad_project,
    )


def solution(mesh):
    placed = (
        P("dp", None),
        P("dp", None),
        P(),
        P(None, "tp"),
        P(None, "tp"),
        P(None, "tp"),
        P("tp", None),
        P(None, "tp"),
        P(),
        P(None, "tp"),
        P("tp", None),
        P(),
        P(),
        P(),
    )
    return jax.shard_map(
        functools.partial(shards, mesh.shape["dp"], mesh.shape["tp"]),
        mesh=mesh,
        in_specs=placed,
        out_specs=(
            P("dp", None),
            P("dp", None),
            P("dp", "tp"),
            P("dp", "tp"),
            P("dp", "tp"),
            P("tp", "dp"),
            P(None, "tp"),
            P("dp"),
            P("dp", "tp"),
            P("tp", "dp"),
            P("dp"),
            P("dp"),
            P("dp", None),
        ),
        check_vma=False,
    )
```

```python
import functools
import math

import jax
import jax.numpy as jnp
import numpy as np
from jax import lax
from jax.experimental import pallas as pl
from jax.experimental.pallas import tpu as pltpu
from jax.sharding import PartitionSpec as P

MAX_DIST = 128
SEG_ROW = 8
TILE = 128
VMEM = 52 * 2**20

epsilon = 1e-06
logit_scale = 50.0
loss_scale = 128.0
masked_value = -1e30
highest = lax.Precision.HIGHEST
f32 = jnp.float32
bf16 = jnp.bfloat16

NN = (((1,), (0,)), ((), ()))
NT = (((1,), (1,)), ((), ()))
TN = (((0,), (0,)), ((), ()))


def dg(a, b, dims):
    return lax.dot_general(a, b, dims, preferred_element_type=f32)


def bucket_of(offsets, bucket_count, distance):
    half_count = bucket_count // 2
    exact_count = half_count // 2
    far_side = np.where(offsets > 0, half_count, 0)
    magnitude = np.abs(offsets)
    logged = (
        np.log(np.maximum(magnitude, exact_count) / exact_count)
        / math.log(distance / exact_count)
        * (half_count - exact_count)
    )
    far_bucket = np.minimum(exact_count + logged.astype(np.int64), half_count - 1)
    return (far_side + np.where(magnitude < exact_count, magnitude, far_bucket)).astype(np.int32)


def cost(flops, moved):
    return pl.CostEstimate(flops=int(flops), bytes_accessed=int(moved), transcendentals=0)


def bias_lanes(bucket_count):
    lanes = np.arange(4 * TILE)
    lanes = np.where(lanes >= 2 * TILE, lanes - 4 * TILE, lanes)
    return np.eye(bucket_count, dtype=np.float32)[bucket_of(-lanes, bucket_count, MAX_DIST)].T


def grad_lanes(bucket_count):
    sub = np.arange(8)[:, None]
    lane = np.arange(4 * TILE)[None, :]
    y = (lane - sub) % (4 * TILE)
    y = np.where(y >= 2 * TILE, y - 4 * TILE, y)
    near = bucket_of(-y, bucket_count, MAX_DIST)
    up = np.full((8, TILE), bucket_of(np.array(MAX_DIST), bucket_count, MAX_DIST))
    down = np.full((8, TILE), bucket_of(np.array(-MAX_DIST), bucket_count, MAX_DIST))
    ids = np.concatenate([near, up, down], 1).reshape(-1)
    return np.eye(bucket_count, dtype=np.float32)[ids]


def bring(place_ref, piece_refs, into, sems):
    slices = piece_refs[0].shape[-2]
    copies = []
    for m, piece in enumerate(piece_refs):
        start = pl.multiple_of(place_ref[m], 16) if slices % 16 == 0 else place_ref[m]
        copy = pltpu.make_async_copy(piece, into.at[:, pl.ds(start, slices), :], sems.at[m])
        copy.start()
        copies.append(copy)
    return copies


def spread_bias(vec_ref, bias_s, heads):
    for h in range(heads):
        wide = jnp.broadcast_to(vec_ref[0, h : h + 1, :], (TILE, 4 * TILE))
        bias_s[h] = pltpu.roll(wide, 0, 1, stride=1, stride_axis=0)


def with_bias(tile, offset, h, bias_s, vec_ref):
    if offset == 0:
        return tile + bias_s[h, :, 0:TILE]
    if offset == 1:
        return tile + bias_s[h, :, 3 * TILE : 4 * TILE]
    if offset == -1:
        return tile + bias_s[h, :, TILE : 2 * TILE]
    lane = 2 * TILE + 1 if offset > 1 else 2 * TILE - 1
    return tile + vec_ref[0, h : h + 1, lane : lane + 1]


def masks(seg):
    hot = lax.broadcasted_iota(jnp.int32, (16, seg.shape[-1]), 0) == seg
    return (
        jnp.where(hot, 0.0, masked_value).astype(bf16),
        jnp.where(hot, 1.0, 0.0).astype(bf16),
    )


def inv_rms(values):
    return lax.rsqrt(jnp.mean(values * values, -1, keepdims=True) + epsilon)


def rounded(value):
    return lax.reduce_precision(value, 8, 7)


def tree(parts):
    while len(parts) > 1:
        parts = [parts[i] + parts[i + 1] for i in range(0, len(parts), 2)]
    return parts[0]


def exact_parts(value):
    parts = []
    for _ in range(3):
        part = value.astype(bf16)
        parts.append(part)
        value = value - part.astype(f32)
    return parts


PAD = 16


def pack_kernel(at_ref, q_ref, k_ref, v_ref, o_ref, rel_ref, out_ref, mine_ref, pack_s):
    cols = q_ref.shape[1]
    for at, ref in enumerate((q_ref, k_ref, v_ref)):
        pack_s[at * cols : (at + 1) * cols] = ref[...].astype(f32).T
    pack_s[3 * cols :] = o_ref[...].astype(f32)
    out_ref[...] = pack_s[...].astype(bf16)
    slices = mine_ref.shape[0] - PAD
    start = at_ref[0] * slices
    if slices % 8 == 0:
        start = pl.multiple_of(start, 8)
    mine_ref[:slices] = pack_s[pl.ds(start, slices), :].astype(bf16)
    mine_ref[slices:] = jnp.zeros_like(mine_ref[slices:])
    buckets, heads = rel_ref.shape
    lane = 0
    for at in range(0, buckets, PAD):
        for part in exact_parts(rel_ref[at : at + PAD]):
            mine_ref[slices:, lane : lane + heads] = part
            lane += TILE


def pack_weights(at, w_query, w_key, w_value, w_out, rel_bias, share):
    width, cols = w_query.shape
    slices = width // share
    full = lambda shape: pl.BlockSpec(shape, lambda i, at: (0, 0))
    return pl.pallas_call(
        pack_kernel,
        grid_spec=pltpu.PrefetchScalarGridSpec(
            num_scalar_prefetch=1,
            grid=(1,),
            in_specs=[full((width, cols))] * 3 + [full((cols, width)), full(rel_bias.shape)],
            out_specs=[full((width, width)), full((slices + PAD, width))],
            scratch_shapes=[pltpu.VMEM((width, width), f32)],
        ),
        out_shape=[
            jax.ShapeDtypeStruct((width, width), bf16),
            jax.ShapeDtypeStruct((slices + PAD, width), bf16),
        ],
        compiler_params=pltpu.CompilerParams(vmem_limit_bytes=VMEM),
        cost_estimate=cost(10**9, 2**20),
        name="pack_weights",
    )(at, w_query, w_key, w_value, w_out, rel_bias)


def unpack_table(pads, buckets, heads):
    rows = []
    lane = 0
    for _ in range(0, buckets, PAD):
        parts = [
            pads[:, :, lane + p * TILE : lane + p * TILE + heads].astype(f32) for p in range(3)
        ]
        rows.append(parts[0] + parts[1] + parts[2])
        lane += 3 * TILE
    return jnp.concatenate(rows, 1)


def stack_kernel(*refs):
    ins, outs = refs[:3], refs[3:]
    slices = outs[0].shape[1]
    for at, ref in enumerate(ins):
        outs[0][at] = ref[:slices]
        if len(outs) == 2:
            outs[1][at] = ref[slices:]


def stack(arrays, slices):
    rows, width = arrays[0].shape
    shapes = [(3, slices, width)] + ([(3, rows - slices, width)] if rows > slices else [])
    return pl.pallas_call(
        stack_kernel,
        out_shape=[jax.ShapeDtypeStruct(shape, bf16) for shape in shapes],
        cost_estimate=cost(0, 12 * arrays[0].size),
        name="stack",
    )(*arrays)


def others_kernel(order_ref, all_ref, *outs):
    slices = outs[0].shape[1]
    for k in range(1, all_ref.shape[0]):
        for at, out in enumerate(outs):
            out[k - 1] = all_ref[order_ref[k], at * slices : (at + 1) * slices]


def others_of(order, everything, count):
    n, total, width = everything.shape
    slices = total // count
    shape = (n - 1, slices, width)
    return pl.pallas_call(
        others_kernel,
        grid_spec=pltpu.PrefetchScalarGridSpec(
            num_scalar_prefetch=1,
            grid=(1,),
            in_specs=[pl.BlockSpec((n, total, width), lambda i, p: (0, 0, 0))],
            out_specs=[pl.BlockSpec(shape, lambda i, p: (0, 0, 0))] * count,
        ),
        out_shape=[jax.ShapeDtypeStruct(shape, bf16)] * count,
        cost_estimate=cost(0, 4 * everything.size),
        name="others_of",
    )(order, everything)


def attend_row(heads, hd, weights, a1_ref, vec_ref, seg_ref, qkv_ref, lse_ref, ctx_ref, bias_s):
    length = a1_ref.shape[0]
    blocks = length // TILE

    @pl.when(pl.program_id(1) == 0)
    def _():
        spread_bias(vec_ref, bias_s, heads)

    qkv_ref[0, 0] = dg(weights, a1_ref[...], NT).astype(bf16)
    q_mask, k_mask = masks(seg_ref[0])
    ones = jnp.ones((16, length), bf16)
    for h in range(heads):
        q_t = jnp.concatenate([qkv_ref[0, 0, h * hd : (h + 1) * hd], q_mask], 0)
        k_t = jnp.concatenate([qkv_ref[0, 0, (heads + h) * hd : (heads + h + 1) * hd], k_mask], 0)
        v_t = jnp.concatenate(
            [qkv_ref[0, 0, (2 * heads + h) * hd : (2 * heads + h + 1) * hd], ones], 0
        )
        scores = dg(k_t.T, q_t, NN)
        columns = []
        tops = []
        for i in range(blocks):
            tiles = [
                with_bias(
                    scores[j * TILE : (j + 1) * TILE, i * TILE : (i + 1) * TILE],
                    j - i,
                    h,
                    bias_s,
                    vec_ref,
                )
                for j in range(blocks)
            ]
            top = jnp.max(functools.reduce(jnp.maximum, tiles), 0, keepdims=True)
            tops.append(top)
            columns.append(jnp.concatenate([jnp.exp(t - top).astype(bf16) for t in tiles], 0))
        mixed = dg(v_t, jnp.concatenate(columns, 1), NN)
        total = mixed[hd : hd + 1]
        lse_ref[0, 0, h : h + 1, :] = jnp.concatenate(tops, 1) + jnp.log(total)
        ctx_ref[0, 0, h * hd : (h + 1) * hd, :] = (mixed[:hd] / total).astype(bf16)


def attn_own_kernel(heads, hd, a1_ref, vec_ref, seg_ref, w_ref, *rest):
    attend_row(heads, hd, w_ref[: 3 * heads * hd], a1_ref, vec_ref, seg_ref, *rest)


def attn_far_kernel(heads, hd, count, place_ref, a1_ref, vec_ref, seg_ref, own_ref, *rest):
    pieces = rest[:count]
    qkv_ref, lse_ref, ctx_ref, sorted_ref, bias_s, w_s, sems, out_sems = rest[count + 3 :]
    s, r = pl.program_id(0), pl.program_id(1)
    keep = [
        pltpu.make_async_copy(own_ref, sorted_ref.at[0], out_sems.at[0]),
        pltpu.make_async_copy(w_s, sorted_ref.at[pl.ds(1, w_s.shape[0])], out_sems.at[1]),
    ]

    @pl.when((s == 0) & (r == 0))
    def _():
        for copy in bring(place_ref, pieces, w_s, sems):
            copy.wait()
        for copy in keep:
            copy.start()

    attend_row(
        heads,
        hd,
        w_s[s, : 3 * heads * hd],
        a1_ref,
        vec_ref,
        seg_ref,
        qkv_ref,
        lse_ref,
        ctx_ref,
        bias_s,
    )

    @pl.when((s == pl.num_programs(0) - 1) & (r == pl.num_programs(1) - 1))
    def _():
        for copy in keep:
            copy.wait()


def attention(a1, own_a, vecs, segs, slots, place=None, pieces=None, earlier=None):
    rows, _, length = segs.shape
    width = a1.shape[1]
    heads = vecs.shape[1]
    hd = width // (4 * heads)
    cols = heads * hd
    first = slots - vecs.shape[0] if pieces else 0
    count = slots - 1 if pieces else 1
    anywhere = pl.BlockSpec(memory_space=pl.ANY)
    in_specs = [
        pl.BlockSpec((length, width), lambda s, r, *_: (r, 0)),
        pl.BlockSpec((1, heads, 4 * TILE), lambda s, r, *_: (s + (1 if pieces else 0), 0, 0)),
        pl.BlockSpec((1, 1, length), lambda s, r, *_: (r, 0, 0)),
    ]
    at = 1 if pieces else 0
    out_specs = [
        pl.BlockSpec((1, 1, 3 * cols, length), lambda s, r, *_: (s + at, r, 0, 0)),
        pl.BlockSpec((1, 1, heads, length), lambda s, r, *_: (s + at, r, 0, 0)),
        pl.BlockSpec((1, 1, cols, length), lambda s, r, *_: (s + at, r, 0, 0)),
    ]
    out_shape = [
        jax.ShapeDtypeStruct((slots, rows, 3 * cols, length), bf16),
        jax.ShapeDtypeStruct((slots, rows, heads, length), f32),
        jax.ShapeDtypeStruct((slots, rows, cols, length), bf16),
    ]
    scratch = [pltpu.VMEM((heads, TILE, 4 * TILE), f32)]
    steps = count * rows
    common = dict(
        compiler_params=pltpu.CompilerParams(vmem_limit_bytes=VMEM),
        cost_estimate=cost(steps * 2.5 * 10**9, 2**20),
    )
    if not pieces:
        return pl.pallas_call(
            functools.partial(attn_own_kernel, heads, hd),
            grid=(count, rows),
            in_specs=in_specs + [pl.BlockSpec((width, width), lambda s, r: (0, 0))],
            out_specs=out_specs,
            out_shape=out_shape,
            scratch_shapes=scratch,
            name="attn_own",
            **common,
        )(a1, vecs, segs, own_a)
    n = len(pieces)
    return pl.pallas_call(
        functools.partial(attn_far_kernel, heads, hd, n),
        grid_spec=pltpu.PrefetchScalarGridSpec(
            num_scalar_prefetch=1,
            grid=(count, rows),
            in_specs=in_specs
            + [pl.BlockSpec((width, width), lambda s, r, p: (0, 0))]
            + [anywhere] * (n + 3),
            out_specs=out_specs + [anywhere],
            scratch_shapes=scratch
            + [
                pltpu.VMEM((count, width, width), bf16),
                pltpu.SemaphoreType.DMA((n,)),
                pltpu.SemaphoreType.DMA((2,)),
            ],
        ),
        out_shape=out_shape + [jax.ShapeDtypeStruct((slots, width, width), bf16)],
        input_output_aliases={5 + n: 0, 6 + n: 1, 7 + n: 2},
        name="attn_far",
        **common,
    )(place, a1, vecs, segs, own_a, *pieces, *earlier)


GELU_A = math.sqrt(2.0 / math.pi)
GELU_B = 0.044715


def gelu(v):
    t = jnp.tanh(v * (GELU_A + (GELU_A * GELU_B) * (v * v)))
    half = 0.5 * v
    return half + half * t


def gelu_pair(v):
    square = v * v
    t = jnp.tanh(v * (GELU_A + (GELU_A * GELU_B) * square))
    half = 0.5 * v
    inner = GELU_A + (3.0 * GELU_A * GELU_B) * square
    return half + half * t, 0.5 + 0.5 * t + half * (1.0 - t * t) * inner


def ffn_own_kernel(x_ref, ctx_ref, wo_ref, gain_ref, b_ref, c_ref, mid_ref, a2_ref, part_ref):
    slots, _, cols, length = ctx_ref.shape
    attn = dg(
        ctx_ref[...].reshape(slots * cols, length),
        wo_ref[...].reshape(slots * cols, wo_ref.shape[-1]),
        TN,
    )
    mid = (x_ref[...].astype(f32) + attn).astype(bf16)
    mid_ref[...] = mid
    mid = mid.astype(f32)
    a2 = (mid * inv_rms(mid) * gain_ref[...]).astype(bf16)
    a2_ref[...] = a2
    hidden = gelu(dg(a2, b_ref[...], NN)).astype(bf16)
    part_ref[...] = dg(hidden, c_ref[...], NN).astype(bf16)


def ffn_own(x, ctx, sorted_a, gain, own_b, own_c):
    slots, rows, cols, length = ctx.shape
    tokens, width = x.shape
    units = own_b.shape[1]
    by_row = pl.BlockSpec((length, width), lambda r: (r, 0))
    return pl.pallas_call(
        ffn_own_kernel,
        grid=(rows,),
        in_specs=[
            by_row,
            pl.BlockSpec((slots, 1, cols, length), lambda r: (0, r, 0, 0)),
            pl.BlockSpec((slots, cols, width), lambda r: (0, 3, 0)),
            pl.BlockSpec((1, width), lambda r: (0, 0)),
            pl.BlockSpec((width, units), lambda r: (0, 0)),
            pl.BlockSpec((units, width), lambda r: (0, 0)),
        ],
        out_specs=[by_row] * 3,
        out_shape=[jax.ShapeDtypeStruct((tokens, width), bf16)] * 3,
        compiler_params=pltpu.CompilerParams(vmem_limit_bytes=VMEM),
        cost_estimate=cost(tokens * width * 6 * units, 2**24),
        name="ffn_own",
    )(x, ctx, sorted_a, gain, own_b, own_c)


def ffn_row(a2, mid, part, up, down, gain_ref, seg_ref, out_ref, res_ref, pool_ref, wait=None):
    res = mid.astype(f32) + part.astype(f32)
    for k in range(len(up)):
        if wait is not None:
            wait(k)
        hidden = gelu(dg(a2, up[k][...], NN)).astype(bf16)
        res = res + dg(hidden, down[k][...], NN)
    res_ref[...] = res.astype(bf16)
    final = (res * inv_rms(res) * gain_ref[...]).astype(bf16)
    out_ref[...] = final
    if pool_ref is not None:
        seg = seg_ref[0]
        hot = lax.broadcasted_iota(jnp.int32, (SEG_ROW, seg.shape[-1]), 0) == seg
        member = jnp.where(hot, 1.0, 0.0)
        pool_ref[...] = dg(member.astype(bf16), final, NN) / jnp.sum(member, 1, keepdims=True)


def ffn_first_kernel(
    count, place_ref, order_ref, a2_ref, mid_ref, part_ref, gain_ref, seg_ref, *rest
):
    pieces, far_c = rest[:count], rest[count]
    out_ref, res_ref, pool_ref, sb_ref, sc_ref, b_s, c_s, sems, out_sems = rest[count + 1 :]
    others = b_s.shape[0]
    slices = far_c.shape[2]
    copies = []
    for k in range(others):
        here = []
        for m in range(count):
            start = pl.multiple_of(place_ref[m], 16) if slices % 16 == 0 else place_ref[m]
            into = b_s.at[k, pl.ds(start, slices), :]
            here.append(pltpu.make_async_copy(pieces[m].at[k], into, sems.at[0, k, m]))
            into = c_s.at[k, pl.ds(m * slices, slices), :]
            here.append(pltpu.make_async_copy(far_c.at[m, k], into, sems.at[1, k, m]))
        copies.append(here)
    keep = []
    for k in range(others):
        keep.append(pltpu.make_async_copy(b_s.at[k], sb_ref.at[k], out_sems.at[0, k]))
        keep.append(pltpu.make_async_copy(c_s.at[k], sc_ref.at[k], out_sems.at[1, k]))
    for here in copies:
        for copy in here:
            copy.start()

    def wait(k):
        for copy in copies[k]:
            copy.wait()
        keep[2 * k].start()
        keep[2 * k + 1].start()

    ffn_row(
        a2_ref[...],
        mid_ref[...],
        part_ref[...],
        [b_s.at[k] for k in range(others)],
        [c_s.at[k] for k in range(others)],
        gain_ref,
        seg_ref,
        out_ref,
        res_ref,
        pool_ref,
        wait,
    )
    for copy in keep:
        copy.wait()


def ffn_first(place, order, a2, mid, part, gain, segs, pieces, far_c):
    rows, _, length = segs.shape
    tokens, width = a2.shape
    units = pieces[0].shape[-1]
    others = pieces[0].shape[0]
    n = len(pieces)
    first = pl.BlockSpec((length, width), lambda r, p, o: (o[0], 0))
    anywhere = pl.BlockSpec(memory_space=pl.ANY)
    return pl.pallas_call(
        functools.partial(ffn_first_kernel, n),
        grid_spec=pltpu.PrefetchScalarGridSpec(
            num_scalar_prefetch=2,
            grid=(1,),
            in_specs=[
                first,
                first,
                first,
                pl.BlockSpec((1, width), lambda r, p, o: (0, 0)),
                pl.BlockSpec((1, 1, length), lambda r, p, o: (o[0], 0, 0)),
            ]
            + [anywhere] * (n + 1),
            out_specs=[
                first,
                pl.BlockSpec((length, width), lambda r, p, o: (0, 0)),
                pl.BlockSpec((SEG_ROW, width), lambda r, p, o: (0, 0)),
                anywhere,
                anywhere,
            ],
            scratch_shapes=[
                pltpu.VMEM((others, width, units), bf16),
                pltpu.VMEM((others, units, width), bf16),
                pltpu.SemaphoreType.DMA((2, others, n)),
                pltpu.SemaphoreType.DMA((2, others)),
            ],
        ),
        out_shape=[
            jax.ShapeDtypeStruct((tokens, width), bf16),
            jax.ShapeDtypeStruct((length, width), bf16),
            jax.ShapeDtypeStruct((SEG_ROW, width), f32),
            jax.ShapeDtypeStruct((others, width, units), bf16),
            jax.ShapeDtypeStruct((others, units, width), bf16),
        ],
        compiler_params=pltpu.CompilerParams(vmem_limit_bytes=VMEM),
        cost_estimate=cost(length * width * 4 * units * others, 2**24),
        name="ffn_first",
    )(place, order, a2, mid, part, gain, segs, *pieces, far_c)


def loss_math(pooled, project, pair_col, pair_row, gain):
    slots = pooled.shape[0]
    projected = dg(pooled, project, NN)
    inv_norm = lax.rsqrt(jnp.sum(projected * projected, -1, keepdims=True) + epsilon)
    unit = projected * inv_norm
    embedded = unit.astype(bf16)
    similar = logit_scale * dg(embedded, embedded, NT)
    rows = lax.broadcasted_iota(jnp.int32, (slots, slots), 0)
    columns = lax.broadcasted_iota(jnp.int32, (slots, slots), 1)
    same = rows == columns
    similar = jnp.where(same, masked_value, similar)
    partner = jnp.where((pair_col == pair_row) & jnp.logical_not(same), 2.0, 0.0)

    def total(axis):
        top = jnp.max(similar, axis, keepdims=True)
        return top + jnp.log(jnp.sum(jnp.exp(similar - top), axis, keepdims=True))

    both = jnp.exp(similar - total(1)) + jnp.exp(similar - total(0)) - partner
    high = both.astype(bf16)
    low = (both - high.astype(f32)).astype(bf16)
    d_unit = (loss_scale * logit_scale) * (dg(high, embedded, NN) + dg(low, embedded, NN))
    d_proj = inv_norm * (d_unit - unit * jnp.sum(d_unit * unit, -1, keepdims=True))
    d_proj = d_proj.astype(bf16)
    d_pooled = dg(d_proj, project, NT)
    d_gain = jnp.sum(d_pooled * pooled.astype(f32), 0, keepdims=True) / gain
    return d_proj, d_pooled, d_gain


def loss_kernel(count, at_ref, *refs):
    pieces, rest = refs[:count], refs[count:]
    project_ref, pc_ref, pr_ref, gain_ref, dpool_ref, dproj_ref, dgain_ref, a_s, b_s = rest
    each = SEG_ROW
    parts = pieces[0].shape[0] // each
    for m, piece in enumerate(pieces):
        value = piece[...].astype(f32)
        for part in range(parts):
            start = pl.multiple_of(at_ref[1 + m * parts + part] * each, each)
            a_s[pl.ds(start, each), :] = value[part * each : (part + 1) * each]
    pooled = a_s[...].astype(bf16)
    d_proj, d_pooled, d_gain = loss_math(
        pooled, project_ref[...], pc_ref[...], pr_ref[...], gain_ref[...]
    )
    a_s[...] = d_pooled
    b_s[...] = dg(pooled, d_proj, TN)
    here = dpool_ref.shape[0]
    block = dproj_ref.shape[0]
    dpool_ref[...] = a_s[pl.ds(pl.multiple_of(at_ref[0] * here, here), here), :]
    dproj_ref[...] = b_s[pl.ds(pl.multiple_of(at_ref[0] * block, block), block), :]
    dgain_ref[...] = d_gain


def loss_head(at, pieces, project, pairs, gain, here, block):
    slots = sum(piece.shape[0] for piece in pieces)
    width = project.shape[0]
    pair_col = pairs[:, None]
    pair_row = pairs[None, :]
    if len(pieces) == 1:
        pooled = pieces[0]
        d_proj, d_pooled, d_gain = loss_math(pooled, project, pair_col, pair_row, gain)
        own_cols = lax.dynamic_slice_in_dim(pooled, at[0] * block, block, 1)
        d_pooled = lax.dynamic_slice_in_dim(d_pooled, at[0] * here, here, 0)
        return d_pooled, dg(own_cols, d_proj, TN), d_gain
    full = lambda shape: pl.BlockSpec(shape, lambda i, at: (0, 0))
    return pl.pallas_call(
        functools.partial(loss_kernel, len(pieces)),
        grid_spec=pltpu.PrefetchScalarGridSpec(
            num_scalar_prefetch=1,
            grid=(1,),
            in_specs=[full(piece.shape) for piece in pieces]
            + [
                full(project.shape),
                full((slots, 1)),
                full((1, slots)),
                full((1, width)),
            ],
            out_specs=[full((here, width)), full((block, width)), full((1, width))],
            scratch_shapes=[pltpu.VMEM((slots, width), f32), pltpu.VMEM((width, width), f32)],
        ),
        out_shape=[
            jax.ShapeDtypeStruct((here, width), f32),
            jax.ShapeDtypeStruct((block, width), f32),
            jax.ShapeDtypeStruct((1, width), f32),
        ],
        compiler_params=pltpu.CompilerParams(vmem_limit_bytes=VMEM),
        cost_estimate=cost(3 * 10**9, 2**20),
        name="loss_head",
    )(at, *pieces, project, pair_col, pair_row, gain)


def d_result_of(res, seg, d_pool, gain):
    hot = lax.broadcasted_iota(jnp.int32, (SEG_ROW, seg.shape[-1]), 0) == seg
    member = jnp.where(hot, 1.0, 0.0)
    per_token = d_pool / jnp.sum(member, 1, keepdims=True)
    high = per_token.astype(bf16)
    low = (per_token - high.astype(f32)).astype(bf16)
    twice = jnp.concatenate([member, member], 0).astype(bf16)
    d_final = dg(twice, jnp.concatenate([high, low], 0), TN)
    scale = inv_rms(res)
    unit = res * scale
    weighted = d_final * gain
    return scale * (weighted - unit * jnp.mean(weighted * unit, -1, keepdims=True))


def ffn_back_kernel(
    row_ref,
    res_ref,
    mid_ref,
    a2_ref,
    seg_ref,
    dpool_ref,
    gain_end_ref,
    gain_ref,
    own_b_ref,
    own_c_ref,
    b_ref,
    c_ref,
    wo_ref,
    dmid_ref,
    dattn_ref,
    dctx_ref,
    dgain_ref,
    dres_s,
    low_s,
    sum_s,
):
    k = pl.program_id(0)

    @pl.when(k == 0)
    def _():
        d_res = d_result_of(
            res_ref[...].astype(f32), seg_ref[0], dpool_ref[...], gain_end_ref[...]
        )
        dres_s[...] = d_res
        low_s[...] = d_res.astype(bf16)
        sum_s[...] = jnp.zeros_like(sum_s)

    def add(up, down):
        slope = gelu_pair(dg(a2_ref[...], up, NN))[1]
        d_pre = (dg(low_s[...], down, NT) * slope).astype(bf16)
        sum_s[...] += dg(d_pre, up, NT)

    @pl.when(k == 0)
    def _():
        add(own_b_ref[...], own_c_ref[...])

    @pl.when(k > 0)
    def _():
        add(b_ref[0], c_ref[0])

    @pl.when(k == pl.num_programs(0) - 1)
    def _():
        mid = mid_ref[...].astype(f32)
        scale = inv_rms(mid)
        unit = mid * scale
        grad = sum_s[...]
        weighted = grad * gain_ref[...]
        d_mid = dres_s[...] + scale * (weighted - unit * jnp.mean(weighted * unit, -1, keepdims=True))
        dgain_ref[...] = jnp.sum(grad * unit, 0, keepdims=True)
        dmid_ref[...] = d_mid
        low = d_mid.astype(bf16)
        dattn_ref[...] = low
        for s in range(wo_ref.shape[0]):
            dctx_ref[s] = dg(wo_ref[s], low, NT).astype(bf16)


def ffn_back(
    row, res, mid, a2, segs, d_pool, gain_end, gain, sorted_a, own_b, own_c, sorted_b, sorted_c
):
    rows, _, length = segs.shape
    tokens, width = mid.shape
    slots = sorted_a.shape[0]
    units = sorted_b.shape[-1]
    cols = width // 4
    own = pl.BlockSpec((length, width), lambda k, row: (row[0], 0))
    fixed = lambda k, row: (0, 0)
    return pl.pallas_call(
        ffn_back_kernel,
        grid_spec=pltpu.PrefetchScalarGridSpec(
            num_scalar_prefetch=1,
            grid=(slots,),
            in_specs=[
                pl.BlockSpec((length, width), fixed),
                own,
                own,
                pl.BlockSpec((1, 1, length), lambda k, row: (row[0], 0, 0)),
                pl.BlockSpec((SEG_ROW, width), lambda k, row: (row[0], 0)),
                pl.BlockSpec((1, width), fixed),
                pl.BlockSpec((1, width), fixed),
                pl.BlockSpec((width, units), fixed),
                pl.BlockSpec((units, width), fixed),
                pl.BlockSpec((1, width, units), lambda k, row: (jnp.maximum(k - 1, 0), 0, 0)),
                pl.BlockSpec((1, units, width), lambda k, row: (jnp.maximum(k - 1, 0), 0, 0)),
                pl.BlockSpec((slots, cols, width), lambda k, row: (0, 3, 0)),
            ],
            out_specs=[
                pl.BlockSpec((length, width), fixed),
                pl.BlockSpec((length, width), fixed),
                pl.BlockSpec((slots, cols, length), lambda k, row: (0, 0, 0)),
                pl.BlockSpec((1, width), fixed),
            ],
            scratch_shapes=[
                pltpu.VMEM((length, width), f32),
                pltpu.VMEM((length, width), bf16),
                pltpu.VMEM((length, width), f32),
            ],
        ),
        out_shape=[
            jax.ShapeDtypeStruct((length, width), f32),
            jax.ShapeDtypeStruct((length, width), bf16),
            jax.ShapeDtypeStruct((slots, cols, length), bf16),
            jax.ShapeDtypeStruct((1, width), f32),
        ],
        compiler_params=pltpu.CompilerParams(vmem_limit_bytes=VMEM),
        cost_estimate=cost(1.2 * 10**10, 2**24),
        name="ffn_back",
    )(row, res, mid, a2, segs, d_pool, gain_end, gain, own_b, own_c, sorted_b, sorted_c, sorted_a)


def fold(tile):
    lanes = tile.shape[1]
    total = tile[0:8]
    for b in range(1, TILE // 8):
        total = total + pltpu.roll(tile[8 * b : 8 * b + 8], lanes - 8 * b, 1)
    return total


def attn_back_kernel(
    heads,
    hd,
    row_ref,
    qkv_ref,
    lse_ref,
    ctx_ref,
    dctx_ref,
    vec_ref,
    seg_ref,
    w_ref,
    x_ref,
    dmid_ref,
    gain_ref,
    dqkv_ref,
    fold_ref,
    dtok_ref,
    dgain_ref,
    bias_s,
    sum_s,
):
    slot = pl.program_id(0)
    length = qkv_ref.shape[-1]
    blocks = length // TILE
    spread_bias(vec_ref, bias_s, heads)
    q_mask, k_mask = masks(seg_ref[0])
    for h in range(heads):
        q_low = qkv_ref[0, 0, h * hd : (h + 1) * hd]
        k_low = qkv_ref[0, 0, (heads + h) * hd : (heads + h + 1) * hd]
        v_low = qkv_ref[0, 0, (2 * heads + h) * hd : (2 * heads + h + 1) * hd]
        dc = dctx_ref[0, h * hd : (h + 1) * hd]
        c = ctx_ref[0, 0, h * hd : (h + 1) * hd]
        delta = jnp.sum(dc.astype(f32) * c.astype(f32), 0, keepdims=True)
        lse = lse_ref[0, 0, h : h + 1]
        scores = dg(
            jnp.concatenate([k_low, k_mask], 0).T, jnp.concatenate([q_low, q_mask], 0), NN
        )
        d_probs = dg(v_low.T, dc, NN)
        probs_cols = []
        score_cols = []
        near = [None, None, None]
        far = [None, None]
        for i in range(blocks):
            at = slice(i * TILE, (i + 1) * TILE)
            probs = []
            grads = []
            for j in range(blocks):
                to = slice(j * TILE, (j + 1) * TILE)
                tile = with_bias(scores[to, at], j - i, h, bias_s, vec_ref)
                prob = jnp.exp(tile - lse[:, at])
                grad = prob * (d_probs[to, at] - delta[:, at])
                probs.append(prob.astype(bf16))
                grads.append(grad.astype(bf16))
                if abs(j - i) <= 1:
                    old = near[j - i + 1]
                    near[j - i + 1] = grad if old is None else old + grad
                else:
                    old = far[int(j < i)]
                    far[int(j < i)] = grad if old is None else old + grad
            probs_cols.append(jnp.concatenate(probs, 0))
            score_cols.append(jnp.concatenate(grads, 0))
        probs = jnp.concatenate(probs_cols, 1)
        grads = jnp.concatenate(score_cols, 1)
        dqkv_ref[0, h * hd : (h + 1) * hd] = dg(k_low, grads, NN).astype(bf16)
        dqkv_ref[0, (heads + h) * hd : (heads + h + 1) * hd] = dg(q_low, grads, NT).astype(bf16)
        dqkv_ref[0, (2 * heads + h) * hd : (2 * heads + h + 1) * hd] = dg(dc, probs, NT).astype(
            bf16
        )
        band = jnp.concatenate([near[1], near[0], jnp.zeros_like(near[0]), near[2]], 1)
        fold_ref[0, h, :, : 4 * TILE] = fold(band)
        for side in range(2):
            total = far[side][0:8]
            for b in range(1, TILE // 8):
                total = total + far[side][8 * b : 8 * b + 8]
            fold_ref[0, h, :, (4 + side) * TILE : (5 + side) * TILE] = total
    part = dg(dqkv_ref[0], w_ref[0], TN)

    @pl.when(slot == 0)
    def _():
        sum_s[...] = part

    @pl.when(slot > 0)
    def _():
        sum_s[...] += part

    @pl.when(slot == pl.num_programs(0) - 1)
    def _():
        x = x_ref[...].astype(f32)
        scale = inv_rms(x)
        unit = x * scale
        grad = sum_s[...]
        weighted = grad * gain_ref[...]
        d_tok = dmid_ref[...] + scale * (weighted - unit * jnp.mean(weighted * unit, -1, keepdims=True))
        dtok_ref[...] = d_tok.astype(bf16)
        dgain_ref[...] = jnp.sum(grad * unit, 0, keepdims=True)


def attn_back(row, qkv, lse, ctx, d_ctx, vecs, segs, all_a, x, d_mid, gain):
    slots, rows, cols3, length = qkv.shape
    heads = lse.shape[2]
    cols = cols3 // 3
    width = x.shape[1]
    own4 = lambda k, row: (k, row[0], 0, 0)
    slot = lambda k, row: (k, 0, 0)
    fixed = lambda k, row: (0, 0)
    return pl.pallas_call(
        functools.partial(attn_back_kernel, heads, cols // heads),
        grid_spec=pltpu.PrefetchScalarGridSpec(
            num_scalar_prefetch=1,
            grid=(slots,),
            in_specs=[
                pl.BlockSpec((1, 1, cols3, length), own4),
                pl.BlockSpec((1, 1, heads, length), own4),
                pl.BlockSpec((1, 1, cols, length), own4),
                pl.BlockSpec((1, cols, length), slot),
                pl.BlockSpec((1, heads, 4 * TILE), slot),
                pl.BlockSpec((1, 1, length), lambda k, row: (row[0], 0, 0)),
                pl.BlockSpec((1, cols3, width), slot),
                pl.BlockSpec((length, width), lambda k, row: (row[0], 0)),
                pl.BlockSpec((length, width), fixed),
                pl.BlockSpec((1, width), fixed),
            ],
            out_specs=[
                pl.BlockSpec((1, cols3, length), slot),
                pl.BlockSpec((1, heads, 8, 6 * TILE), lambda k, row: (k, 0, 0, 0)),
                pl.BlockSpec((length, width), fixed),
                pl.BlockSpec((1, width), fixed),
            ],
            scratch_shapes=[
                pltpu.VMEM((heads, TILE, 4 * TILE), f32),
                pltpu.VMEM((length, width), f32),
            ],
        ),
        out_shape=[
            jax.ShapeDtypeStruct((slots, cols3, length), bf16),
            jax.ShapeDtypeStruct((slots, heads, 8, 6 * TILE), f32),
            jax.ShapeDtypeStruct((length, width), bf16),
            jax.ShapeDtypeStruct((1, width), f32),
        ],
        compiler_params=pltpu.CompilerParams(vmem_limit_bytes=VMEM),
        cost_estimate=cost(1.5 * 10**10, 2**24),
        name="attn_back",
    )(row, qkv, lse, ctx, d_ctx, vecs, segs, all_a, x, d_mid, gain)


def split_blocks(core, rel_ref, block, pad, extra, values, keep_ref, give_ref, lead):
    for c in range(2):

        @pl.when(core == c)
        def _():
            for chip in range(4):
                for ref, j in ((keep_ref, 2 * chip + c), (give_ref, 2 * chip + 1 - c)):
                    rows = values(j * block, (j + 1) * block)
                    to = chip if rel_ref is None else rel_ref[chip]
                    for at, value in enumerate(rows):
                        ref[to, lead + at, :block] = value
                    if pad:
                        ref[to, lead, block:] = extra(j)


def attn_weights_kernel(
    block, place_ref, a1_ref, dattn_ref, dqkv_ref, ctx_ref, extra_ref, *rest
):
    outs, (a1_s, dattn_s, sum_s) = rest[:-3], rest[-3:]

    @pl.when(pl.program_id(0) == 0)
    def _():
        a1_s[...] = a1_ref[...].T
        dattn_s[...] = dattn_ref[...].T

    cols3 = dqkv_ref.shape[1]
    sum_s[:, :cols3] = dg(a1_s[...], dqkv_ref[0], NT).astype(bf16)
    sum_s[:, cols3:] = dg(dattn_s[...], ctx_ref[0, 0], NT).astype(bf16)
    if len(outs) == 1:
        outs[0][0] = sum_s[...]
    else:
        split_blocks(
            place_ref[1],
            place_ref.at[pl.ds(2, 4)],
            block,
            True,
            lambda j: extra_ref[0, j],
            lambda a, b: [sum_s[a:b]],
            outs[0],
            outs[1],
            0,
        )


def attn_weights(place, a1, d_attn, d_qkv, ctx, extra, split):
    slots, cols3, length = d_qkv.shape
    cols = ctx.shape[2]
    width = a1.shape[1]
    _, blocks, pad, _ = extra.shape
    block = width // blocks
    if split:
        shape = (4, slots, block + pad, width)
        out_specs = [pl.BlockSpec((4, 1, block + pad, width), lambda k, p: (0, k, 0, 0))] * 2
        out_shape = [jax.ShapeDtypeStruct(shape, bf16)] * 2
    else:
        out_specs = [pl.BlockSpec((1, width, width), lambda k, p: (k, 0, 0))]
        out_shape = [jax.ShapeDtypeStruct((slots, width, width), bf16)]
    return pl.pallas_call(
        functools.partial(attn_weights_kernel, block),
        grid_spec=pltpu.PrefetchScalarGridSpec(
            num_scalar_prefetch=1,
            grid=(slots,),
            in_specs=[
                pl.BlockSpec((length, width), lambda k, p: (p[0], 0)),
                pl.BlockSpec((length, width), lambda k, p: (0, 0)),
                pl.BlockSpec((1, cols3, length), lambda k, p: (k, 0, 0)),
                pl.BlockSpec((1, 1, cols, length), lambda k, p: (k, p[0], 0, 0)),
                pl.BlockSpec((1, blocks, pad, width), lambda k, p: (k, 0, 0, 0)),
            ],
            out_specs=out_specs,
            scratch_shapes=[
                pltpu.VMEM((width, length), bf16),
                pltpu.VMEM((width, length), bf16),
                pltpu.VMEM((width, width), bf16),
            ],
        ),
        out_shape=out_shape,
        compiler_params=pltpu.CompilerParams(vmem_limit_bytes=VMEM),
        cost_estimate=cost(10**6, 10**6),
        name="attn_weights",
    )(place, a1, d_attn, d_qkv, ctx, extra)


def ffn_tail_kernel(
    block,
    place_ref,
    order_ref,
    a2_ref,
    mid_ref,
    part_ref,
    own_ref,
    seg_ref,
    dpool_ref,
    gain_ref,
    own_b_ref,
    own_c_ref,
    b_ref,
    c_ref,
    _out,
    out_ref,
    *rest,
):
    outs, (res_s, up_s, down_s) = rest[:-3], rest[-3:]
    r = pl.program_id(0)
    others = b_ref.shape[0]

    @pl.when(r == 0)
    def _():
        res_s[...] = own_ref[...]
        up_s[...] = jnp.zeros_like(up_s)
        down_s[...] = jnp.zeros_like(down_s)

    @pl.when(r > 0)
    def _():
        ffn_row(
            a2_ref[...],
            mid_ref[...],
            part_ref[...],
            [b_ref.at[k] for k in range(others)],
            [c_ref.at[k] for k in range(others)],
            gain_ref,
            None,
            out_ref,
            res_s,
            None,
        )

    d_res = d_result_of(res_s[...].astype(f32), seg_ref[0], dpool_ref[...], gain_ref[...])
    low = d_res.astype(bf16)
    a2 = a2_ref[...]
    hidden, slope = gelu_pair(dg(a2, own_b_ref[...], NN))
    down_s[...] += dg(low, hidden.astype(bf16), TN)
    d_pre = (dg(low, own_c_ref[...], NT) * slope).astype(bf16)
    up_s[...] += dg(a2, d_pre, TN)

    @pl.when(r == pl.num_programs(0) - 1)
    def _():
        if len(outs) == 1:
            outs[0][0] = up_s[...].astype(bf16)
            outs[0][1] = down_s[...].astype(bf16)
        else:
            split_blocks(
                place_ref[1],
                None,
                block,
                False,
                None,
                lambda a, b: [up_s[a:b].astype(bf16), down_s[a:b].astype(bf16)],
                outs[0],
                outs[1],
                0,
            )


def ffn_tail(
    place, order, a2, mid, part, res, segs, d_pool, gain, own_b, own_c, far_b, far_c, out, blocks, split
):
    rows, _, length = segs.shape
    tokens, width = a2.shape
    units = own_b.shape[1]
    others = far_b.shape[0]
    block = width // blocks
    row = pl.BlockSpec((length, width), lambda r, p, o: (o[r], 0))
    later = pl.BlockSpec((length, width), lambda r, p, o: (o[jnp.maximum(r, 1)], 0))

    def fixed(shape):
        zeros = (0,) * len(shape)
        return pl.BlockSpec(shape, lambda r, p, o: zeros, pipeline_mode=pl.Buffered(1))

    shape = (4, 2, block, units) if split else (2, width, units)
    zeros = (0,) * len(shape)
    n = 2 if split else 1
    return pl.pallas_call(
        functools.partial(ffn_tail_kernel, block),
        grid_spec=pltpu.PrefetchScalarGridSpec(
            num_scalar_prefetch=2,
            grid=(rows,),
            in_specs=[
                row,
                later,
                later,
                fixed((length, width)),
                pl.BlockSpec((1, 1, length), lambda r, p, o: (o[r], 0, 0)),
                pl.BlockSpec((SEG_ROW, width), lambda r, p, o: (o[r], 0)),
                fixed((1, width)),
                fixed((width, units)),
                fixed((units, width)),
                fixed((others, width, units)),
                fixed((others, units, width)),
                pl.BlockSpec(memory_space=pl.ANY),
            ],
            out_specs=[later] + [pl.BlockSpec(shape, lambda r, p, o: zeros)] * n,
            scratch_shapes=[
                pltpu.VMEM((length, width), bf16),
                pltpu.VMEM((width, units), f32),
                pltpu.VMEM((width, units), f32),
            ],
        ),
        out_shape=[jax.ShapeDtypeStruct((tokens, width), bf16)]
        + [jax.ShapeDtypeStruct(shape, bf16)] * n,
        input_output_aliases={13: 0},
        compiler_params=pltpu.CompilerParams(vmem_limit_bytes=VMEM),
        cost_estimate=cost(2 * 10**10, 2**24),
        name="ffn_tail",
    )(place, order, a2, mid, part, res, segs, d_pool, gain, own_b, own_c, far_b, far_c, out)


def shards(
    n_dp,
    n_tp,
    tokens,
    segment_ids,
    pair_order,
    w_query,
    w_key,
    w_value,
    w_out,
    rel_bias,
    gain_attn,
    w_hidden,
    w_down,
    gain_ffn,
    gain_final,
    w_project,
):
    rows, length = segment_ids.shape
    bucket_count, heads = rel_bias.shape
    width = tokens.shape[1]
    units = w_hidden.shape[1]
    dp = lax.axis_index("dp")
    tp = lax.axis_index("tp")
    share = math.gcd(n_dp, 8)
    split = n_dp == 8
    mates = [[(i, i ^ m) for i in range(n_dp)] for m in range(share)]
    levels = [[(i, i ^ k) for i in range(n_tp)] for k in range(n_tp)]

    def over_dp(value, m):
        return lax.ppermute(value, "dp", mates[m])

    def over_tp(value, k):
        return lax.ppermute(value, "tp", levels[k])

    slices = width // share
    low_bits = dp % share
    place = (low_bits ^ jnp.arange(share, dtype=jnp.int32)) * slices

    def from_levels(mine):
        return stack([over_tp(mine, k) for k in range(1, n_tp)], slices)

    def from_chips(far):
        return [far] + [over_dp(far, m) for m in range(2, share, 2)]

    def from_cores(pieces):
        both = [(piece, over_dp(piece, 1)) for piece in pieces]
        return [piece for pair in both for piece in pair]

    def after(values, others):
        return lax.optimization_barrier((values, others))[0]

    order = tp ^ jnp.arange(n_tp, dtype=jnp.int32)
    pack_a, mine_a = pack_weights(
        low_bits[None].astype(jnp.int32), w_query, w_key, w_value, w_out, rel_bias, share
    )
    far_a, pads = from_levels(mine_a)
    mine_bc = jnp.concatenate(
        [
            lax.dynamic_slice_in_dim(w, low_bits * slices, slices, 0)
            for w in (w_hidden, w_down)
        ]
    )
    all_bc = lax.all_gather(mine_bc, "tp", axis=0)
    tables = jnp.concatenate([rel_bias[None], unpack_table(pads, bucket_count, heads)])
    vec_own = jnp.einsum("kbh,bn->khn", tables[:1], bias_lanes(bucket_count), precision=highest)
    vecs = jnp.einsum("kbh,bn->khn", tables, bias_lanes(bucket_count), precision=highest)
    segs = segment_ids[:, None, :]
    row = tp[None].astype(jnp.int32)
    one = gain_attn[None]
    two = gain_ffn[None]
    end = gain_final[None]

    x = tokens.astype(f32)
    a1 = (x * inv_rms(x) * one).astype(bf16)
    state = attention(after(a1, far_a), pack_a, vec_own, segs, n_tp)
    far_a = from_chips(far_a)
    far_b, far_c = others_of(after(order, (state, far_a)), all_bc, 2)
    groups = np.arange(n_dp).reshape(-1, share).tolist()
    far_c = lax.all_gather(far_c, "dp", axis=0, axis_index_groups=groups)
    far_a = from_cores(after(far_a, far_b))
    far_b = from_chips(after(far_b, far_a))
    qkv, lse, ctx, sorted_a = attention(a1, pack_a, vecs, segs, n_tp, place, far_a, state)
    far_b = from_cores(after(far_b, lse))
    mid, a2, part = ffn_own(tokens, ctx, sorted_a, two, w_hidden, w_down)
    layer_out, res, pooled, sorted_b, sorted_c = ffn_first(
        place, order, a2, mid, part, end, segs, far_b, far_c
    )
    block = width // n_dp
    here = rows * SEG_ROW
    pooled = pooled.astype(bf16)
    if split:
        pooled = jnp.concatenate([pooled] + [over_tp(pooled, k) for k in range(1, n_tp)])
        pooled = jnp.concatenate([pooled, over_dp(pooled, 1)])
        pooled_all = from_chips(pooled)
        spots = (dp ^ jnp.arange(n_dp))[:, None] * rows + order[None]
        at = jnp.concatenate([dp[None], spots.reshape(-1)]).astype(jnp.int32)
    else:
        pooled = lax.all_gather(pooled, "tp", axis=0, tiled=True)
        pooled_all = [lax.all_gather(pooled, "dp", axis=0, tiled=True)]
        at = dp[None].astype(jnp.int32)
    d_pool, grad_project, d_gain_end = loss_head(
        at, pooled_all, w_project, pair_order // 2, end, here, block
    )
    grad_gain_final = lax.dynamic_slice_in_dim(d_gain_end[0], dp * block, block, 0)
    d_mid, d_attn, d_ctx, d_gain_two = ffn_back(
        row,
        res,
        mid,
        a2,
        segs,
        d_pool,
        end,
        two,
        sorted_a,
        w_hidden,
        w_down,
        sorted_b,
        sorted_c,
    )
    d_qkv, folded, d_tok, d_gain_one = attn_back(
        row, qkv, lse, ctx, d_ctx, vecs, segs, sorted_a, tokens, d_mid, one
    )
    d_tokens = lax.all_gather(d_tok, "tp", axis=0, tiled=True).astype(f32)

    d_rel = jnp.einsum(
        "khn,nb->kbh",
        folded.reshape(n_tp, heads, -1),
        grad_lanes(bucket_count),
        precision=highest,
    )
    gains = jnp.concatenate([d_gain_one, d_gain_two])
    pad = 16
    extra = jnp.zeros((n_tp, n_dp, pad, width), bf16)
    if split:
        small = d_rel.reshape(n_tp, 1, 1, bucket_count * heads).astype(bf16)
        gain_rows = jnp.swapaxes(gains.reshape(2, n_dp, block), 0, 1).astype(bf16)
        extra = jnp.concatenate(
            [
                jnp.broadcast_to(gain_rows[None], (n_tp, n_dp, 2, block)),
                jnp.broadcast_to(small, (n_tp, n_dp, 1, block)),
                jnp.zeros((n_tp, n_dp, pad - 3, block), bf16),
            ],
            2,
        )
        extra = jnp.pad(extra, ((0, 0), (0, 0), (0, 0), (0, width - block)))
    chips = (dp // 2) ^ jnp.arange(4, dtype=jnp.int32)
    spots = jnp.concatenate([row, (dp % 2)[None].astype(jnp.int32), chips])
    parts_a = attn_weights(spots, a1, d_attn, d_qkv, ctx, extra, split)

    def to_core(parts):
        keep, give = parts
        took = over_dp(give, 1)
        return [rounded(keep[c].astype(f32) + took[c].astype(f32)) for c in range(4)]

    def to_chip(pair):
        return [pair[0]] + [over_dp(pair[c].astype(bf16), 2 * c) for c in range(1, 4)]

    def total(parts):
        return tree([part.astype(f32) for part in parts])

    def scatter(parts):
        return lax.psum_scatter(parts[0].astype(f32), "dp", scatter_dimension=1, tiled=True)

    if split:
        pair_a = to_core(parts_a)
        got_a = to_chip(pair_a)
        first = after(order, pair_a)
    else:
        first = after(order, parts_a)
    layer_out, *parts_f = ffn_tail(
        spots, first, a2, mid, part, res, segs, d_pool, end,
        w_hidden, w_down, sorted_b, sorted_c, layer_out, n_dp, split,
    )
    if split:
        chips = [[c + core for c in range(0, n_dp, 2)] for core in range(2)]
        give_f = over_dp(after(parts_f[1], got_a), 1)
        pair_f = parts_f[0].astype(f32) + give_f.astype(f32)
        own_a = rounded(total(got_a))
        swapped = lax.all_to_all(
            pair_f.astype(bf16), "dp", 0, 0, axis_index_groups=chips, tiled=True
        )
        own_f = jnp.sum(swapped.astype(f32), 0)
    else:
        own_a, own_f = rounded(scatter(parts_a)), scatter(parts_f)

    def reduce_tp(value):
        return tree([value[0]] + [over_tp(value[k], k) for k in range(1, n_tp)])

    grad_a = tree(
        [own_a[0].astype(f32)]
        + [over_tp(own_a[k].astype(bf16), k).astype(f32) for k in range(1, n_tp)]
    )
    cols = width // 4
    if split:
        gain_one, gain_two = grad_a[block, :block], grad_a[block + 1, :block]
        d_rel_here = grad_a[block + 2, : bucket_count * heads].reshape(bucket_count, heads)
    else:
        gains = tree([gains] + [over_tp(gains, k) for k in range(1, n_tp)])
        d_rel_here, gains = lax.psum((reduce_tp(d_rel), gains), "dp")
        gain_one, gain_two = lax.dynamic_slice_in_dim(gains, dp * block, block, 1)
    return (
        layer_out,
        d_tokens,
        grad_a[:block, :cols],
        grad_a[:block, cols : 2 * cols],
        grad_a[:block, 2 * cols : 3 * cols],
        grad_a[:block, 3 * cols :].T,
        d_rel_here,
        gain_one,
        own_f[0],
        own_f[1].T,
        gain_two,
        grad_gain_final,
        grad_project,
    )


def solution(mesh):
    placed = (
        P("dp", None),
        P("dp", None),
        P(),
        P(None, "tp"),
        P(None, "tp"),
        P(None, "tp"),
        P("tp", None),
        P(None, "tp"),
        P(),
        P(None, "tp"),
        P("tp", None),
        P(),
        P(),
        P(),
    )
    return jax.shard_map(
        functools.partial(shards, mesh.shape["dp"], mesh.shape["tp"]),
        mesh=mesh,
        in_specs=placed,
        out_specs=(
            P("dp", None),
            P("dp", None),
            P("dp", "tp"),
            P("dp", "tp"),
            P("dp", "tp"),
            P("tp", "dp"),
            P(None, "tp"),
            P("dp"),
            P("dp", "tp"),
            P("tp", "dp"),
            P("dp"),
            P("dp"),
            P("dp", None),
        ),
        check_vma=False,
    )
```

```python
import functools
import math

import jax
import jax.numpy as jnp
import numpy as np
from jax import lax
from jax.experimental import pallas as pl
from jax.experimental.pallas import tpu as pltpu
from jax.sharding import PartitionSpec as P

MAX_DIST = 128
SEG_ROW = 8
TILE = 128
VMEM = 52 * 2**20

epsilon = 1e-06
logit_scale = 50.0
loss_scale = 128.0
masked_value = -1e30
highest = lax.Precision.HIGHEST
f32 = jnp.float32
bf16 = jnp.bfloat16

NN = (((1,), (0,)), ((), ()))
NT = (((1,), (1,)), ((), ()))
TN = (((0,), (0,)), ((), ()))


def dg(a, b, dims):
    return lax.dot_general(a, b, dims, preferred_element_type=f32)


def bucket_of(offsets, bucket_count, distance):
    half_count = bucket_count // 2
    exact_count = half_count // 2
    far_side = np.where(offsets > 0, half_count, 0)
    magnitude = np.abs(offsets)
    logged = (
        np.log(np.maximum(magnitude, exact_count) / exact_count)
        / math.log(distance / exact_count)
        * (half_count - exact_count)
    )
    far_bucket = np.minimum(exact_count + logged.astype(np.int64), half_count - 1)
    return (far_side + np.where(magnitude < exact_count, magnitude, far_bucket)).astype(np.int32)


def cost(flops, moved):
    return pl.CostEstimate(flops=int(flops), bytes_accessed=int(moved), transcendentals=0)


def bias_lanes(bucket_count):
    lanes = np.arange(4 * TILE)
    lanes = np.where(lanes >= 2 * TILE, lanes - 4 * TILE, lanes)
    return np.eye(bucket_count, dtype=np.float32)[bucket_of(-lanes, bucket_count, MAX_DIST)].T


def grad_lanes(bucket_count):
    sub = np.arange(8)[:, None]
    lane = np.arange(4 * TILE)[None, :]
    y = (lane - sub) % (4 * TILE)
    y = np.where(y >= 2 * TILE, y - 4 * TILE, y)
    near = bucket_of(-y, bucket_count, MAX_DIST)
    up = np.full((8, TILE), bucket_of(np.array(MAX_DIST), bucket_count, MAX_DIST))
    down = np.full((8, TILE), bucket_of(np.array(-MAX_DIST), bucket_count, MAX_DIST))
    ids = np.concatenate([near, up, down], 1).reshape(-1)
    return np.eye(bucket_count, dtype=np.float32)[ids]


def bring(place_ref, piece_refs, into, sems):
    width = into.shape[1]
    slices = width // len(piece_refs)
    copies = []
    for m, piece in enumerate(piece_refs):
        start = pl.multiple_of(place_ref[m], 16) if slices % 16 == 0 else place_ref[m]
        if len(piece.shape) == 2:
            piece, to = piece.at[pl.ds(0, slices)], into.at[0, pl.ds(start, slices)]
        else:
            to = into.at[:, pl.ds(start, slices), :]
        copy = pltpu.make_async_copy(piece, to, sems.at[m])
        copy.start()
        copies.append(copy)
    return copies


def spread_bias(vec_ref, bias_s, heads, at=0):
    for h in range(heads):
        wide = jnp.broadcast_to(vec_ref[0, h : h + 1, :], (TILE, 4 * TILE))
        bias_s[at + h] = pltpu.roll(wide, 0, 1, stride=1, stride_axis=0)


def with_bias(tile, offset, h, bias_s, vec_ref, first=0):
    if offset == 0:
        return tile + bias_s[first + h, :, 0:TILE]
    if offset == 1:
        return tile + bias_s[first + h, :, 3 * TILE : 4 * TILE]
    if offset == -1:
        return tile + bias_s[first + h, :, TILE : 2 * TILE]
    lane = 2 * TILE + 1 if offset > 1 else 2 * TILE - 1
    return tile + vec_ref[0, h : h + 1, lane : lane + 1]


def masks(seg):
    hot = lax.broadcasted_iota(jnp.int32, (16, seg.shape[-1]), 0) == seg
    return (
        jnp.where(hot, 0.0, masked_value).astype(bf16),
        jnp.where(hot, 1.0, 0.0).astype(bf16),
    )


def inv_rms(values):
    return lax.rsqrt(jnp.mean(values * values, -1, keepdims=True) + epsilon)


def rounded(value):
    return lax.reduce_precision(value, 8, 7)


def tree(parts):
    while len(parts) > 1:
        parts = [parts[i] + parts[i + 1] for i in range(0, len(parts), 2)]
    return parts[0]


def exact_parts(value):
    parts = []
    for _ in range(3):
        part = value.astype(bf16)
        parts.append(part)
        value = value - part.astype(f32)
    return parts


PAD = 16


def pack_kernel(at_ref, q_ref, k_ref, v_ref, o_ref, rel_ref, out_ref, mine_ref, pack_s):
    cols = q_ref.shape[1]
    for at, ref in enumerate((q_ref, k_ref, v_ref)):
        pack_s[at * cols : (at + 1) * cols] = ref[...].astype(f32).T
    pack_s[3 * cols :] = o_ref[...].astype(f32)
    out_ref[...] = pack_s[...].astype(bf16)
    slices = mine_ref.shape[0] - PAD
    start = at_ref[0] * slices
    if slices % 8 == 0:
        start = pl.multiple_of(start, 8)
    mine_ref[:slices] = pack_s[pl.ds(start, slices), :].astype(bf16)
    mine_ref[slices:] = jnp.zeros_like(mine_ref[slices:])
    buckets, heads = rel_ref.shape
    lane = 0
    for at in range(0, buckets, PAD):
        for part in exact_parts(rel_ref[at : at + PAD]):
            mine_ref[slices:, lane : lane + heads] = part
            lane += TILE


def pack_weights(at, w_query, w_key, w_value, w_out, rel_bias, share):
    width, cols = w_query.shape
    slices = width // share
    full = lambda shape: pl.BlockSpec(shape, lambda i, at: (0, 0))
    return pl.pallas_call(
        pack_kernel,
        grid_spec=pltpu.PrefetchScalarGridSpec(
            num_scalar_prefetch=1,
            grid=(1,),
            in_specs=[full((width, cols))] * 3 + [full((cols, width)), full(rel_bias.shape)],
            out_specs=[full((width, width)), full((slices + PAD, width))],
            scratch_shapes=[pltpu.VMEM((width, width), f32)],
        ),
        out_shape=[
            jax.ShapeDtypeStruct((width, width), bf16),
            jax.ShapeDtypeStruct((slices + PAD, width), bf16),
        ],
        compiler_params=pltpu.CompilerParams(vmem_limit_bytes=VMEM),
        cost_estimate=cost(10**9, 2**20),
        name="pack_weights",
    )(at, w_query, w_key, w_value, w_out, rel_bias)


def unpack_table(pads, buckets, heads):
    rows = []
    lane = 0
    for _ in range(0, buckets, PAD):
        parts = [
            pads[:, :, lane + p * TILE : lane + p * TILE + heads].astype(f32) for p in range(3)
        ]
        rows.append(parts[0] + parts[1] + parts[2])
        lane += 3 * TILE
    return jnp.concatenate(rows, 1)


def stack_kernel(*refs):
    ins, outs = refs[:3], refs[3:]
    slices = outs[0].shape[1]
    for at, ref in enumerate(ins):
        outs[0][at] = ref[:slices]
        if len(outs) == 2:
            outs[1][at] = ref[slices:]


def stack(arrays, slices):
    rows, width = arrays[0].shape
    shapes = [(3, slices, width)] + ([(3, rows - slices, width)] if rows > slices else [])
    return pl.pallas_call(
        stack_kernel,
        out_shape=[jax.ShapeDtypeStruct(shape, bf16) for shape in shapes],
        cost_estimate=cost(0, 12 * arrays[0].size),
        name="stack",
    )(*arrays)


def others_kernel(order_ref, all_ref, *outs):
    slices = outs[0].shape[1]
    for k in range(1, all_ref.shape[0]):
        for at, out in enumerate(outs):
            out[k - 1] = all_ref[order_ref[k], at * slices : (at + 1) * slices]


def others_of(order, everything, count):
    n, total, width = everything.shape
    slices = total // count
    shape = (n - 1, slices, width)
    return pl.pallas_call(
        others_kernel,
        grid_spec=pltpu.PrefetchScalarGridSpec(
            num_scalar_prefetch=1,
            grid=(1,),
            in_specs=[pl.BlockSpec((n, total, width), lambda i, p: (0, 0, 0))],
            out_specs=[pl.BlockSpec(shape, lambda i, p: (0, 0, 0))] * count,
        ),
        out_shape=[jax.ShapeDtypeStruct(shape, bf16)] * count,
        cost_estimate=cost(0, 4 * everything.size),
        name="others_of",
    )(order, everything)


def attend_row(heads, hd, weights, a1_ref, vec_ref, seg_ref, qkv_s, lse_s, ctx_ref, bias_s, first):
    length = a1_ref.shape[0]
    blocks = length // TILE
    qkv_s[...] = dg(weights, a1_ref[...], NT).astype(bf16)
    q_mask, k_mask = masks(seg_ref[0])
    ones = jnp.ones((16, length), bf16)
    for h in range(heads):
        q_t = jnp.concatenate([qkv_s[h * hd : (h + 1) * hd], q_mask], 0)
        k_t = jnp.concatenate([qkv_s[(heads + h) * hd : (heads + h + 1) * hd], k_mask], 0)
        v_t = jnp.concatenate([qkv_s[(2 * heads + h) * hd : (2 * heads + h + 1) * hd], ones], 0)
        scores = dg(k_t.T, q_t, NN)
        columns = []
        tops = []
        for i in range(blocks):
            tiles = [
                with_bias(
                    scores[j * TILE : (j + 1) * TILE, i * TILE : (i + 1) * TILE],
                    j - i,
                    h,
                    bias_s,
                    vec_ref,
                    first,
                )
                for j in range(blocks)
            ]
            top = jnp.max(functools.reduce(jnp.maximum, tiles), 0, keepdims=True)
            tops.append(top)
            columns.append(jnp.concatenate([jnp.exp(t - top).astype(bf16) for t in tiles], 0))
        mixed = dg(v_t, jnp.concatenate(columns, 1), NN)
        total = mixed[hd : hd + 1]
        lse_s[h : h + 1, :] = jnp.concatenate(tops, 1) + jnp.log(total)
        ctx_ref[0, 0, h * hd : (h + 1) * hd, :] = (mixed[:hd] / total).astype(bf16)


def attn_kernel(heads, hd, n, low, keeps, place_ref, order_ref, a1_ref, vec_ref, seg_ref, *rest):
    sources = rest[: max(n, 1)]
    rest = rest[max(n, 1) + (0 if low == 0 else 4 if keeps else 1) :]
    if keeps:
        qkv_ref, lse_ref, ctx_ref, sorted_ref, bias_s, qkv_s, lse_s, w_s, sems, out_sem = rest
    else:
        ctx_ref, bias_s, qkv_s, lse_s = rest
    r, s = pl.program_id(0), pl.program_id(1)
    first = s * heads

    @pl.when(r == 0)
    def _():
        spread_bias(vec_ref, bias_s, heads, first)

    if keeps:
        count = w_s.shape[0]
        source = w_s if n else sources[0]
        into = sorted_ref.at[pl.ds(low, count)] if n else sorted_ref.at[low]
        keep = pltpu.make_async_copy(source, into, out_sem)

        @pl.when((s == 0) & (r == 0))
        def _():
            if n:
                for copy in bring(place_ref, sources, w_s, sems):
                    copy.wait()
            keep.start()

        weights = w_s[s, : 3 * heads * hd] if n else sources[0][: 3 * heads * hd]
    else:
        weights = sources[0][s, : 3 * heads * hd]
    attend_row(
        heads, hd, weights, a1_ref, vec_ref, seg_ref, qkv_s, lse_s, ctx_ref, bias_s, first
    )
    if keeps:

        @pl.when(r == 0)
        def _():
            qkv_ref[0] = qkv_s[...]
            lse_ref[0] = lse_s[...]

        @pl.when((s == pl.num_programs(1) - 1) & (r == pl.num_programs(0) - 1))
        def _():
            keep.wait()


def attention(name, a1, vecs, segs, place, order, low, first_row, n_rows, weights, chain):
    rows, _, length = segs.shape
    width = a1.shape[1]
    count, heads, _ = vecs.shape
    slots = order.shape[0]
    hd = width // (4 * heads)
    cols = heads * hd
    n = len(weights) if weights[0].shape[0] != slots and len(weights) > 1 else 0
    keeps = first_row == 0
    anywhere = pl.BlockSpec(memory_space=pl.ANY)
    at = lambda r, o: o[r + first_row]
    slot = lambda r, s: low + jnp.where(r == 0, s, count - 1)
    if n:
        w_specs = [anywhere] * n
    elif keeps:
        w_specs = [pl.BlockSpec((width, width), lambda r, s, p, o: (0, 0))]
    else:
        w_specs = [pl.BlockSpec((count, width, width), lambda r, s, p, o: (low // count, 0, 0))]
    out_specs = [
        pl.BlockSpec((1, 3 * cols, length), lambda r, s, p, o: (slot(r, s), 0, 0)),
        pl.BlockSpec((1, heads, length), lambda r, s, p, o: (slot(r, s), 0, 0)),
        pl.BlockSpec((1, 1, cols, length), lambda r, s, p, o: (s + low, at(r, o), 0, 0)),
        anywhere,
    ]
    out_shape = [
        jax.ShapeDtypeStruct((slots, 3 * cols, length), bf16),
        jax.ShapeDtypeStruct((slots, heads, length), f32),
        jax.ShapeDtypeStruct((slots, rows, cols, length), bf16),
        jax.ShapeDtypeStruct((slots, width, width), bf16),
    ]
    scratch = [
        pltpu.VMEM((count * heads, TILE, 4 * TILE), f32),
        pltpu.VMEM((3 * cols, length), bf16),
        pltpu.VMEM((heads, length), f32),
    ]
    if keeps:
        scratch += [
            pltpu.VMEM((count, width, width) if n else (1, 16, TILE), bf16),
            pltpu.SemaphoreType.DMA((max(n, 1),)),
            pltpu.SemaphoreType.DMA(()),
        ]
        linked = [] if chain is None else list(chain)
    else:
        out_specs, out_shape, linked = out_specs[2:3], out_shape[2:3], [chain[2]]
    base = 5 + len(w_specs)
    return pl.pallas_call(
        functools.partial(attn_kernel, heads, hd, n, low, keeps),
        grid_spec=pltpu.PrefetchScalarGridSpec(
            num_scalar_prefetch=2,
            grid=(n_rows, count),
            in_specs=[
                pl.BlockSpec((length, width), lambda r, s, p, o: (at(r, o), 0)),
                pl.BlockSpec((1, heads, 4 * TILE), lambda r, s, p, o: (s, 0, 0)),
                pl.BlockSpec((1, 1, length), lambda r, s, p, o: (at(r, o), 0, 0)),
            ]
            + w_specs
            + [anywhere] * len(linked),
            out_specs=out_specs,
            scratch_shapes=scratch,
        ),
        out_shape=out_shape,
        input_output_aliases={base + i: i for i in range(len(linked))},
        compiler_params=pltpu.CompilerParams(vmem_limit_bytes=VMEM),
        cost_estimate=cost(n_rows * count * 2.5 * 10**9, 2**20),
        name=name,
    )(place, order, a1, vecs, segs, *weights, *linked)


GELU_A = math.sqrt(2.0 / math.pi)
GELU_B = 0.044715


def gelu(v):
    t = jnp.tanh(v * (GELU_A + (GELU_A * GELU_B) * (v * v)))
    half = 0.5 * v
    return half + half * t


def gelu_pair(v):
    square = v * v
    t = jnp.tanh(v * (GELU_A + (GELU_A * GELU_B) * square))
    half = 0.5 * v
    inner = GELU_A + (3.0 * GELU_A * GELU_B) * square
    return half + half * t, 0.5 + 0.5 * t + half * (1.0 - t * t) * inner


def ffn_own_kernel(x_ref, ctx_ref, wo_ref, gain_ref, b_ref, c_ref, mid_ref, a2_ref, part_ref):
    slots, _, cols, length = ctx_ref.shape
    attn = dg(
        ctx_ref[...].reshape(slots * cols, length),
        wo_ref[...].reshape(slots * cols, wo_ref.shape[-1]),
        TN,
    )
    mid = (x_ref[...].astype(f32) + attn).astype(bf16)
    mid_ref[...] = mid
    mid = mid.astype(f32)
    a2 = (mid * inv_rms(mid) * gain_ref[...]).astype(bf16)
    a2_ref[...] = a2
    hidden = gelu(dg(a2, b_ref[...], NN)).astype(bf16)
    part_ref[...] = dg(hidden, c_ref[...], NN).astype(bf16)


def ffn_own(x, ctx, sorted_a, gain, own_b, own_c):
    slots, rows, cols, length = ctx.shape
    tokens, width = x.shape
    units = own_b.shape[1]
    by_row = pl.BlockSpec((length, width), lambda r: (r, 0))
    return pl.pallas_call(
        ffn_own_kernel,
        grid=(rows,),
        in_specs=[
            by_row,
            pl.BlockSpec((slots, 1, cols, length), lambda r: (0, r, 0, 0)),
            pl.BlockSpec((slots, cols, width), lambda r: (0, 3, 0)),
            pl.BlockSpec((1, width), lambda r: (0, 0)),
            pl.BlockSpec((width, units), lambda r: (0, 0)),
            pl.BlockSpec((units, width), lambda r: (0, 0)),
        ],
        out_specs=[by_row] * 3,
        out_shape=[jax.ShapeDtypeStruct((tokens, width), bf16)] * 3,
        compiler_params=pltpu.CompilerParams(vmem_limit_bytes=VMEM),
        cost_estimate=cost(tokens * width * 6 * units, 2**24),
        name="ffn_own",
    )(x, ctx, sorted_a, gain, own_b, own_c)


def ffn_row(a2, mid, part, up, down, gain_ref, seg_ref, out_ref, res_ref, pool_ref, wait=None):
    res = mid.astype(f32) + part.astype(f32)
    for k in range(len(up)):
        if wait is not None:
            wait(k)
        hidden = gelu(dg(a2, up[k][...], NN)).astype(bf16)
        res = res + dg(hidden, down[k][...], NN)
    res_ref[...] = res.astype(bf16)
    final = (res * inv_rms(res) * gain_ref[...]).astype(bf16)
    out_ref[...] = final
    if pool_ref is not None:
        seg = seg_ref[0]
        hot = lax.broadcasted_iota(jnp.int32, (SEG_ROW, seg.shape[-1]), 0) == seg
        member = jnp.where(hot, 1.0, 0.0)
        pool_ref[...] = dg(member.astype(bf16), final, NN) / jnp.sum(member, 1, keepdims=True)


def ffn_first_kernel(
    count, place_ref, order_ref, a2_ref, mid_ref, part_ref, gain_ref, seg_ref, *rest
):
    pieces, far_c = rest[:count], rest[count]
    out_ref, res_ref, pool_ref, sb_ref, sc_ref, b_s, c_s, sems, out_sems = rest[count + 1 :]
    others = b_s.shape[0]
    slices = far_c.shape[2]
    copies = []
    for k in range(others):
        here = []
        for m in range(count):
            start = pl.multiple_of(place_ref[m], 16) if slices % 16 == 0 else place_ref[m]
            into = b_s.at[k, pl.ds(start, slices), :]
            here.append(pltpu.make_async_copy(pieces[m].at[k], into, sems.at[0, k, m]))
            into = c_s.at[k, pl.ds(m * slices, slices), :]
            here.append(pltpu.make_async_copy(far_c.at[m, k], into, sems.at[1, k, m]))
        copies.append(here)
    keep = []
    for k in range(others):
        keep.append(pltpu.make_async_copy(b_s.at[k], sb_ref.at[k], out_sems.at[0, k]))
        keep.append(pltpu.make_async_copy(c_s.at[k], sc_ref.at[k], out_sems.at[1, k]))
    for here in copies:
        for copy in here:
            copy.start()

    def wait(k):
        for copy in copies[k]:
            copy.wait()
        keep[2 * k].start()
        keep[2 * k + 1].start()

    ffn_row(
        a2_ref[...],
        mid_ref[...],
        part_ref[...],
        [b_s.at[k] for k in range(others)],
        [c_s.at[k] for k in range(others)],
        gain_ref,
        seg_ref,
        out_ref,
        res_ref,
        pool_ref,
        wait,
    )
    for copy in keep:
        copy.wait()


def ffn_first(place, order, a2, mid, part, gain, segs, pieces, far_c):
    rows, _, length = segs.shape
    tokens, width = a2.shape
    units = pieces[0].shape[-1]
    others = pieces[0].shape[0]
    n = len(pieces)
    first = pl.BlockSpec((length, width), lambda r, p, o: (o[0], 0))
    anywhere = pl.BlockSpec(memory_space=pl.ANY)
    return pl.pallas_call(
        functools.partial(ffn_first_kernel, n),
        grid_spec=pltpu.PrefetchScalarGridSpec(
            num_scalar_prefetch=2,
            grid=(1,),
            in_specs=[
                first,
                first,
                first,
                pl.BlockSpec((1, width), lambda r, p, o: (0, 0)),
                pl.BlockSpec((1, 1, length), lambda r, p, o: (o[0], 0, 0)),
            ]
            + [anywhere] * (n + 1),
            out_specs=[
                first,
                pl.BlockSpec((length, width), lambda r, p, o: (0, 0)),
                pl.BlockSpec((SEG_ROW, width), lambda r, p, o: (0, 0)),
                anywhere,
                anywhere,
            ],
            scratch_shapes=[
                pltpu.VMEM((others, width, units), bf16),
                pltpu.VMEM((others, units, width), bf16),
                pltpu.SemaphoreType.DMA((2, others, n)),
                pltpu.SemaphoreType.DMA((2, others)),
            ],
        ),
        out_shape=[
            jax.ShapeDtypeStruct((tokens, width), bf16),
            jax.ShapeDtypeStruct((length, width), bf16),
            jax.ShapeDtypeStruct((SEG_ROW, width), f32),
            jax.ShapeDtypeStruct((others, width, units), bf16),
            jax.ShapeDtypeStruct((others, units, width), bf16),
        ],
        compiler_params=pltpu.CompilerParams(vmem_limit_bytes=VMEM),
        cost_estimate=cost(length * width * 4 * units * others, 2**24),
        name="ffn_first",
    )(place, order, a2, mid, part, gain, segs, *pieces, far_c)


def loss_math(pooled, project, pair_col, pair_row, gain):
    slots = pooled.shape[0]
    projected = dg(pooled, project, NN)
    inv_norm = lax.rsqrt(jnp.sum(projected * projected, -1, keepdims=True) + epsilon)
    unit = projected * inv_norm
    embedded = unit.astype(bf16)
    similar = logit_scale * dg(embedded, embedded, NT)
    rows = lax.broadcasted_iota(jnp.int32, (slots, slots), 0)
    columns = lax.broadcasted_iota(jnp.int32, (slots, slots), 1)
    same = rows == columns
    similar = jnp.where(same, masked_value, similar)
    partner = jnp.where((pair_col == pair_row) & jnp.logical_not(same), 2.0, 0.0)

    def total(axis):
        top = jnp.max(similar, axis, keepdims=True)
        return top + jnp.log(jnp.sum(jnp.exp(similar - top), axis, keepdims=True))

    both = jnp.exp(similar - total(1)) + jnp.exp(similar - total(0)) - partner
    high = both.astype(bf16)
    low = (both - high.astype(f32)).astype(bf16)
    d_unit = (loss_scale * logit_scale) * (dg(high, embedded, NN) + dg(low, embedded, NN))
    d_proj = inv_norm * (d_unit - unit * jnp.sum(d_unit * unit, -1, keepdims=True))
    d_proj = d_proj.astype(bf16)
    d_pooled = dg(d_proj, project, NT)
    d_gain = jnp.sum(d_pooled * pooled.astype(f32), 0, keepdims=True) / gain
    return d_proj, d_pooled, d_gain


def d_result_of(res, seg, d_pool, gain):
    hot = lax.broadcasted_iota(jnp.int32, (SEG_ROW, seg.shape[-1]), 0) == seg
    member = jnp.where(hot, 1.0, 0.0)
    per_token = d_pool / jnp.sum(member, 1, keepdims=True)
    high = per_token.astype(bf16)
    low = (per_token - high.astype(f32)).astype(bf16)
    twice = jnp.concatenate([member, member], 0).astype(bf16)
    d_final = dg(twice, jnp.concatenate([high, low], 0), TN)
    scale = inv_rms(res)
    unit = res * scale
    weighted = d_final * gain
    return scale * (weighted - unit * jnp.mean(weighted * unit, -1, keepdims=True))


def fold(tile):
    lanes = tile.shape[1]
    total = tile[0:8]
    for b in range(1, TILE // 8):
        total = total + pltpu.roll(tile[8 * b : 8 * b + 8], lanes - 8 * b, 1)
    return total


def loss_step(pieces, at_ref, project_ref, pc_ref, pr_ref, gain_ref, dpool_ref, dproj_ref, dgain_ref, a_s, b_s):
    each = SEG_ROW
    parts = pieces[0].shape[0] // each
    for m, piece in enumerate(pieces):
        value = piece[...].astype(f32)
        for part in range(parts):
            start = pl.multiple_of(at_ref[1 + m * parts + part] * each, each)
            a_s[pl.ds(start, each), :] = value[part * each : (part + 1) * each]
    pooled = a_s[...].astype(bf16)
    d_proj, d_pooled, d_gain = loss_math(
        pooled, project_ref[...], pc_ref[...], pr_ref[...], gain_ref[...]
    )
    a_s[...] = d_pooled
    b_s[...] = dg(pooled, d_proj, TN)
    here = dpool_ref.shape[0]
    block = dproj_ref.shape[0]
    dpool_ref[...] = a_s[pl.ds(pl.multiple_of(at_ref[0] * here, here), here), :]
    dproj_ref[...] = b_s[pl.ds(pl.multiple_of(at_ref[0] * block, block), block), :]
    dgain_ref[...] = d_gain


def norm_back(grad, values, gain):
    scale = inv_rms(values)
    unit = values * scale
    weighted = grad * gain
    d_values = scale * (weighted - unit * jnp.mean(weighted * unit, -1, keepdims=True))
    return d_values, jnp.sum(grad * unit, 0, keepdims=True)


def row_back_kernel(count, with_loss, heads, hd, at_ref, row_ref, *refs):
    pieces, refs = refs[:count], refs[count:]
    project_ref, pc_ref, pr_ref, gain_end_ref, gain_two_ref, gain_one_ref, seg_ref = refs[:7]
    lse_ref, vec_ref, res_any, mid_any, a2_any, x_any, own_b, own_c, far_b, far_c = refs[7:17]
    far_a, qkv_any, ctx_any = refs[17:20]
    dpool_ref, dproj_ref, dend_ref, dtwo_ref, dattn_ref = refs[20:25]
    dqkv_ref, fold_ref, dtok_ref, done_ref = refs[25:29]
    a_s, p_s, b_s, c_s, wo_s, wa_s, res_s, mid_s, a2_s, x_s, qkv_s, ctx_s = refs[29:41]
    dres_s, low_s, sum_s, dctx_s, bias_s, b_sems, c_sems, sems = refs[41:]
    step = pl.program_id(0)
    slots = b_s.shape[0]
    length = res_s.shape[0]
    cols = heads * hd
    row = row_ref[0]
    mine = pl.ds(pl.multiple_of(row * length, length), length)
    res_copy = pltpu.make_async_copy(res_any, res_s, sems.at[0])
    a2_copy = pltpu.make_async_copy(a2_any.at[mine], a2_s, sems.at[1])
    mid_copy = pltpu.make_async_copy(mid_any.at[mine], mid_s, sems.at[2])
    wo_copy = pltpu.make_async_copy(far_a.at[:, pl.ds(3 * cols, cols)], wo_s, sems.at[3])
    qkv_copy = pltpu.make_async_copy(qkv_any, qkv_s, sems.at[4])
    ctx_copy = pltpu.make_async_copy(ctx_any.at[:, row], ctx_s, sems.at[5])
    wa_copy = pltpu.make_async_copy(far_a.at[:, pl.ds(0, 3 * cols)], wa_s, sems.at[6])
    x_copy = pltpu.make_async_copy(x_any.at[mine], x_s, sems.at[7])

    def weight_copies(k):
        b_from, c_from = (own_b, own_c) if k == 0 else (far_b.at[k - 1], far_c.at[k - 1])
        return [
            pltpu.make_async_copy(b_from, b_s.at[k], b_sems.at[k]),
            pltpu.make_async_copy(c_from, c_s.at[k], c_sems.at[k]),
        ]

    @pl.when(step == 0)
    def _():
        res_copy.start()
        a2_copy.start()
        for k in range(slots):
            for copy in weight_copies(k):
                copy.start()
        for copy in (mid_copy, wo_copy, qkv_copy, ctx_copy, wa_copy, x_copy):
            copy.start()
        if with_loss:
            loss_step(
                pieces,
                at_ref,
                project_ref,
                pc_ref,
                pr_ref,
                gain_end_ref,
                dpool_ref,
                dproj_ref,
                dend_ref,
                a_s,
                p_s,
            )
        else:
            dpool_ref[...] = pieces[0][...]
            dproj_ref[...] = jnp.zeros_like(dproj_ref)
            dend_ref[...] = jnp.zeros_like(dend_ref)
        res_copy.wait()
        a2_copy.wait()
        d_pool = dpool_ref[pl.ds(pl.multiple_of(row * SEG_ROW, SEG_ROW), SEG_ROW), :]
        d_res = d_result_of(res_s[...].astype(f32), seg_ref[0], d_pool, gain_end_ref[...])
        dres_s[...] = d_res
        low_s[...] = d_res.astype(bf16)
        sum_s[...] = jnp.zeros_like(sum_s)

    for k in range(slots):

        @pl.when(step == k + 1)
        def _():
            for copy in weight_copies(k):
                copy.wait()

    @pl.when((step >= 1) & (step <= slots))
    def _():
        up, down = b_s.at[step - 1], c_s.at[step - 1]
        slope = gelu_pair(dg(a2_s[...], up[...], NN))[1]
        d_pre = (dg(low_s[...], down[...], NT) * slope).astype(bf16)
        sum_s[...] += dg(d_pre, up[...], NT)

    @pl.when(step == slots)
    def _():
        mid_copy.wait()
        wo_copy.wait()
        d_mid, dtwo_ref[...] = norm_back(
            sum_s[...], mid_s[...].astype(f32), gain_two_ref[...]
        )
        d_mid = dres_s[...] + d_mid
        dres_s[...] = d_mid
        low = d_mid.astype(bf16)
        dattn_ref[...] = low
        sum_s[...] = jnp.zeros_like(sum_s)
        for k in range(slots):
            dctx_s[k] = dg(wo_s[k], low, NT).astype(bf16)
        qkv_copy.wait()
        ctx_copy.wait()
        wa_copy.wait()
        x_copy.wait()

    @pl.when(step > slots)
    def _():
        slot = step - slots - 1
        blocks = length // TILE
        spread_bias(vec_ref.at[pl.ds(slot, 1)], bias_s, heads)
        q_mask, k_mask = masks(seg_ref[0])
        for h in range(heads):
            q_low = qkv_s[slot, h * hd : (h + 1) * hd]
            k_low = qkv_s[slot, (heads + h) * hd : (heads + h + 1) * hd]
            v_low = qkv_s[slot, (2 * heads + h) * hd : (2 * heads + h + 1) * hd]
            dc = dctx_s[slot, h * hd : (h + 1) * hd]
            c = ctx_s[slot, h * hd : (h + 1) * hd]
            delta = jnp.sum(dc.astype(f32) * c.astype(f32), 0, keepdims=True)
            lse = lse_ref[slot, h : h + 1]
            scores = dg(
                jnp.concatenate([k_low, k_mask], 0).T, jnp.concatenate([q_low, q_mask], 0), NN
            )
            d_probs = dg(v_low.T, dc, NN)
            probs_cols = []
            score_cols = []
            near = [None, None, None]
            far = [None, None]
            for i in range(blocks):
                at = slice(i * TILE, (i + 1) * TILE)
                probs = []
                grads = []
                for j in range(blocks):
                    to = slice(j * TILE, (j + 1) * TILE)
                    tile = with_bias(scores[to, at], j - i, h, bias_s, vec_ref.at[pl.ds(slot, 1)])
                    prob = jnp.exp(tile - lse[:, at])
                    grad = prob * (d_probs[to, at] - delta[:, at])
                    probs.append(prob.astype(bf16))
                    grads.append(grad.astype(bf16))
                    if abs(j - i) <= 1:
                        old = near[j - i + 1]
                        near[j - i + 1] = grad if old is None else old + grad
                    else:
                        old = far[int(j < i)]
                        far[int(j < i)] = grad if old is None else old + grad
                probs_cols.append(jnp.concatenate(probs, 0))
                score_cols.append(jnp.concatenate(grads, 0))
            probs = jnp.concatenate(probs_cols, 1)
            grads = jnp.concatenate(score_cols, 1)
            dqkv_ref[0, h * hd : (h + 1) * hd] = dg(k_low, grads, NN).astype(bf16)
            dqkv_ref[0, (heads + h) * hd : (heads + h + 1) * hd] = dg(q_low, grads, NT).astype(bf16)
            dqkv_ref[0, (2 * heads + h) * hd : (2 * heads + h + 1) * hd] = dg(dc, probs, NT).astype(
                bf16
            )
            band = jnp.concatenate([near[1], near[0], jnp.zeros_like(near[0]), near[2]], 1)
            fold_ref[0, h, :, : 4 * TILE] = fold(band)
            for side in range(2):
                total = far[side][0:8]
                for b in range(1, TILE // 8):
                    total = total + far[side][8 * b : 8 * b + 8]
                fold_ref[0, h, :, (4 + side) * TILE : (5 + side) * TILE] = total
        sum_s[...] += dg(dqkv_ref[0], wa_s[slot], TN)

    @pl.when(step == 2 * slots)
    def _():
        d_x, done_ref[...] = norm_back(sum_s[...], x_s[...].astype(f32), gain_one_ref[...])
        dtok_ref[...] = (dres_s[...] + d_x).astype(bf16)


def row_back(
    at,
    row,
    pieces,
    with_loss,
    project,
    pairs,
    gains,
    segs,
    lse,
    vecs,
    res,
    mid,
    a2,
    x,
    own_b,
    own_c,
    far_b,
    far_c,
    sorted_a,
    qkv,
    ctx,
    here,
    block,
):
    slots, heads, _ = vecs.shape
    length, width = res.shape
    units = own_b.shape[1]
    cols = width // 4
    n_all = pairs.shape[0]
    anywhere = pl.BlockSpec(memory_space=pl.ANY)

    def full(shape):
        zeros = (0,) * len(shape)
        return pl.BlockSpec(shape, lambda i, at, row: zeros)

    def slot(i):
        return jnp.maximum(i - slots - 1, 0)

    row_shape = (length, width)
    return pl.pallas_call(
        functools.partial(row_back_kernel, len(pieces), with_loss, heads, cols // heads),
        grid_spec=pltpu.PrefetchScalarGridSpec(
            num_scalar_prefetch=2,
            grid=(2 * slots + 1,),
            in_specs=[full(piece.shape) for piece in pieces]
            + [full(project.shape), full((n_all, 1)), full((1, n_all))]
            + [full((1, width))] * 3
            + [
                pl.BlockSpec((1, 1, length), lambda i, at, row: (row[0], 0, 0)),
                full(lse.shape),
                full(vecs.shape),
            ]
            + [anywhere] * 11,
            out_specs=[
                full((here, width)),
                full((block, width)),
                full((1, width)),
                full((1, width)),
                full(row_shape),
                pl.BlockSpec((1, 3 * cols, length), lambda i, at, row: (slot(i), 0, 0)),
                pl.BlockSpec((1, heads, 8, 6 * TILE), lambda i, at, row: (slot(i), 0, 0, 0)),
                full(row_shape),
                full((1, width)),
            ],
            scratch_shapes=[
                pltpu.VMEM((n_all if with_loss else 8, width), f32),
                pltpu.VMEM((width, width), f32),
                pltpu.VMEM((slots, width, units), bf16),
                pltpu.VMEM((slots, units, width), bf16),
                pltpu.VMEM((slots, cols, width), bf16),
                pltpu.VMEM((slots, 3 * cols, width), bf16),
                pltpu.VMEM(row_shape, bf16),
                pltpu.VMEM(row_shape, bf16),
                pltpu.VMEM(row_shape, bf16),
                pltpu.VMEM(row_shape, bf16),
                pltpu.VMEM((slots, 3 * cols, length), bf16),
                pltpu.VMEM((slots, cols, length), bf16),
                pltpu.VMEM(row_shape, f32),
                pltpu.VMEM(row_shape, bf16),
                pltpu.VMEM(row_shape, f32),
                pltpu.VMEM((slots, cols, length), bf16),
                pltpu.VMEM((heads, TILE, 4 * TILE), f32),
                pltpu.SemaphoreType.DMA((slots,)),
                pltpu.SemaphoreType.DMA((slots,)),
                pltpu.SemaphoreType.DMA((8,)),
            ],
        ),
        out_shape=[
            jax.ShapeDtypeStruct((here, width), f32),
            jax.ShapeDtypeStruct((block, width), f32),
            jax.ShapeDtypeStruct((1, width), f32),
            jax.ShapeDtypeStruct((1, width), f32),
            jax.ShapeDtypeStruct(row_shape, bf16),
            jax.ShapeDtypeStruct((slots, 3 * cols, length), bf16),
            jax.ShapeDtypeStruct((slots, heads, 8, 6 * TILE), f32),
            jax.ShapeDtypeStruct(row_shape, bf16),
            jax.ShapeDtypeStruct((1, width), f32),
        ],
        compiler_params=pltpu.CompilerParams(vmem_limit_bytes=VMEM),
        cost_estimate=cost(3 * 10**10, 2**24),
        name="row_back",
    )(
        at,
        row,
        *pieces,
        project,
        pairs[:, None],
        pairs[None, :],
        *gains,
        segs,
        lse,
        vecs,
        res,
        mid,
        a2,
        x,
        own_b,
        own_c,
        far_b,
        far_c,
        sorted_a,
        qkv,
        ctx,
    )


def split_blocks(core, rel_ref, block, pad, extra, values, keep_ref, give_ref, lead):
    for c in range(2):

        @pl.when(core == c)
        def _():
            for chip in range(4):
                for ref, j in ((keep_ref, 2 * chip + c), (give_ref, 2 * chip + 1 - c)):
                    rows = values(j * block, (j + 1) * block)
                    to = chip if rel_ref is None else rel_ref[chip]
                    for at, value in enumerate(rows):
                        ref[to, lead + at, :block] = value
                    if pad:
                        ref[to, lead, block:] = extra(j)


def attn_weights_kernel(
    block, place_ref, a1_ref, dattn_ref, dqkv_ref, ctx_ref, extra_ref, *rest
):
    outs, (a1_s, dattn_s, sum_s) = rest[:-3], rest[-3:]

    @pl.when(pl.program_id(0) == 0)
    def _():
        a1_s[...] = a1_ref[...].T
        dattn_s[...] = dattn_ref[...].T

    cols3 = dqkv_ref.shape[1]
    sum_s[:, :cols3] = dg(a1_s[...], dqkv_ref[0], NT).astype(bf16)
    sum_s[:, cols3:] = dg(dattn_s[...], ctx_ref[0, 0], NT).astype(bf16)
    if len(outs) == 1:
        outs[0][0] = sum_s[...]
    else:
        split_blocks(
            place_ref[1],
            place_ref.at[pl.ds(2, 4)],
            block,
            True,
            lambda j: extra_ref[0, j],
            lambda a, b: [sum_s[a:b]],
            outs[0],
            outs[1],
            0,
        )


def attn_weights(place, a1, d_attn, d_qkv, ctx, extra, split):
    slots, cols3, length = d_qkv.shape
    cols = ctx.shape[2]
    width = a1.shape[1]
    _, blocks, pad, _ = extra.shape
    block = width // blocks
    if split:
        shape = (4, slots, block + pad, width)
        out_specs = [pl.BlockSpec((4, 1, block + pad, width), lambda k, p: (0, k, 0, 0))] * 2
        out_shape = [jax.ShapeDtypeStruct(shape, bf16)] * 2
    else:
        out_specs = [pl.BlockSpec((1, width, width), lambda k, p: (k, 0, 0))]
        out_shape = [jax.ShapeDtypeStruct((slots, width, width), bf16)]
    return pl.pallas_call(
        functools.partial(attn_weights_kernel, block),
        grid_spec=pltpu.PrefetchScalarGridSpec(
            num_scalar_prefetch=1,
            grid=(slots,),
            in_specs=[
                pl.BlockSpec((length, width), lambda k, p: (p[0], 0)),
                pl.BlockSpec((length, width), lambda k, p: (0, 0)),
                pl.BlockSpec((1, cols3, length), lambda k, p: (k, 0, 0)),
                pl.BlockSpec((1, 1, cols, length), lambda k, p: (k, p[0], 0, 0)),
                pl.BlockSpec((1, blocks, pad, width), lambda k, p: (k, 0, 0, 0)),
            ],
            out_specs=out_specs,
            scratch_shapes=[
                pltpu.VMEM((width, length), bf16),
                pltpu.VMEM((width, length), bf16),
                pltpu.VMEM((width, width), bf16),
            ],
        ),
        out_shape=out_shape,
        compiler_params=pltpu.CompilerParams(vmem_limit_bytes=VMEM),
        cost_estimate=cost(10**6, 10**6),
        name="attn_weights",
    )(place, a1, d_attn, d_qkv, ctx, extra)


def ffn_tail_kernel(
    block,
    place_ref,
    order_ref,
    a2_ref,
    mid_ref,
    part_ref,
    own_ref,
    seg_ref,
    dpool_ref,
    gain_ref,
    own_b_ref,
    own_c_ref,
    b_ref,
    c_ref,
    _out,
    out_ref,
    *rest,
):
    outs, (res_s, up_s, down_s) = rest[:-3], rest[-3:]
    r = pl.program_id(0)
    others = b_ref.shape[0]

    @pl.when(r == 0)
    def _():
        res_s[...] = own_ref[...]
        up_s[...] = jnp.zeros_like(up_s)
        down_s[...] = jnp.zeros_like(down_s)

    @pl.when(r > 0)
    def _():
        ffn_row(
            a2_ref[...],
            mid_ref[...],
            part_ref[...],
            [b_ref.at[k] for k in range(others)],
            [c_ref.at[k] for k in range(others)],
            gain_ref,
            None,
            out_ref,
            res_s,
            None,
        )

    d_res = d_result_of(res_s[...].astype(f32), seg_ref[0], dpool_ref[...], gain_ref[...])
    low = d_res.astype(bf16)
    a2 = a2_ref[...]
    hidden, slope = gelu_pair(dg(a2, own_b_ref[...], NN))
    down_s[...] += dg(low, hidden.astype(bf16), TN)
    d_pre = (dg(low, own_c_ref[...], NT) * slope).astype(bf16)
    up_s[...] += dg(a2, d_pre, TN)

    @pl.when(r == pl.num_programs(0) - 1)
    def _():
        if len(outs) == 1:
            outs[0][0] = up_s[...].astype(bf16)
            outs[0][1] = down_s[...].astype(bf16)
        else:
            split_blocks(
                place_ref[1],
                None,
                block,
                False,
                None,
                lambda a, b: [up_s[a:b].astype(bf16), down_s[a:b].astype(bf16)],
                outs[0],
                outs[1],
                0,
            )


def ffn_tail(
    place, order, a2, mid, part, res, segs, d_pool, gain, own_b, own_c, far_b, far_c, out, blocks, split
):
    rows, _, length = segs.shape
    tokens, width = a2.shape
    units = own_b.shape[1]
    others = far_b.shape[0]
    block = width // blocks
    row = pl.BlockSpec((length, width), lambda r, p, o: (o[r], 0))
    later = pl.BlockSpec((length, width), lambda r, p, o: (o[jnp.maximum(r, 1)], 0))

    def fixed(shape):
        zeros = (0,) * len(shape)
        return pl.BlockSpec(shape, lambda r, p, o: zeros, pipeline_mode=pl.Buffered(1))

    shape = (4, 2, block, units) if split else (2, width, units)
    zeros = (0,) * len(shape)
    n = 2 if split else 1
    return pl.pallas_call(
        functools.partial(ffn_tail_kernel, block),
        grid_spec=pltpu.PrefetchScalarGridSpec(
            num_scalar_prefetch=2,
            grid=(rows,),
            in_specs=[
                row,
                later,
                later,
                fixed((length, width)),
                pl.BlockSpec((1, 1, length), lambda r, p, o: (o[r], 0, 0)),
                pl.BlockSpec((SEG_ROW, width), lambda r, p, o: (o[r], 0)),
                fixed((1, width)),
                fixed((width, units)),
                fixed((units, width)),
                fixed((others, width, units)),
                fixed((others, units, width)),
                pl.BlockSpec(memory_space=pl.ANY),
            ],
            out_specs=[later] + [pl.BlockSpec(shape, lambda r, p, o: zeros)] * n,
            scratch_shapes=[
                pltpu.VMEM((length, width), bf16),
                pltpu.VMEM((width, units), f32),
                pltpu.VMEM((width, units), f32),
            ],
        ),
        out_shape=[jax.ShapeDtypeStruct((tokens, width), bf16)]
        + [jax.ShapeDtypeStruct(shape, bf16)] * n,
        input_output_aliases={13: 0},
        compiler_params=pltpu.CompilerParams(vmem_limit_bytes=VMEM),
        cost_estimate=cost(2 * 10**10, 2**24),
        name="ffn_tail",
    )(place, order, a2, mid, part, res, segs, d_pool, gain, own_b, own_c, far_b, far_c, out)


def shards(
    n_dp,
    n_tp,
    tokens,
    segment_ids,
    pair_order,
    w_query,
    w_key,
    w_value,
    w_out,
    rel_bias,
    gain_attn,
    w_hidden,
    w_down,
    gain_ffn,
    gain_final,
    w_project,
):
    rows, length = segment_ids.shape
    bucket_count, heads = rel_bias.shape
    width = tokens.shape[1]
    units = w_hidden.shape[1]
    dp = lax.axis_index("dp")
    tp = lax.axis_index("tp")
    share = math.gcd(n_dp, 8)
    split = n_dp == 8
    mates = [[(i, i ^ m) for i in range(n_dp)] for m in range(share)]
    levels = [[(i, i ^ k) for i in range(n_tp)] for k in range(n_tp)]

    def over_dp(value, m):
        return lax.ppermute(value, "dp", mates[m])

    def over_tp(value, k):
        return lax.ppermute(value, "tp", levels[k])

    slices = width // share
    low_bits = dp % share
    place = (low_bits ^ jnp.arange(share, dtype=jnp.int32)) * slices

    def from_levels(mine):
        return stack([over_tp(mine, k) for k in range(1, n_tp)], slices)

    def from_chips(far):
        return [far] + [over_dp(far, m) for m in range(2, share, 2)]

    def from_cores(pieces):
        both = [(piece, over_dp(piece, 1)) for piece in pieces]
        return [piece for pair in both for piece in pair]

    def after(values, others):
        return lax.optimization_barrier((values, others))[0]

    order = tp ^ jnp.arange(n_tp, dtype=jnp.int32)
    pack_a, mine_a = pack_weights(
        low_bits[None].astype(jnp.int32), w_query, w_key, w_value, w_out, rel_bias, share
    )
    far_a, pads = from_levels(mine_a)
    mine_bc = jnp.concatenate(
        [
            lax.dynamic_slice_in_dim(w, low_bits * slices, slices, 0)
            for w in (w_hidden, w_down)
        ]
    )
    all_bc = lax.all_gather(mine_bc, "tp", axis=0)
    tables = jnp.concatenate([rel_bias[None], unpack_table(pads, bucket_count, heads)])
    vec_own = jnp.einsum("kbh,bn->khn", tables[:1], bias_lanes(bucket_count), precision=highest)
    vecs = jnp.einsum("kbh,bn->khn", tables, bias_lanes(bucket_count), precision=highest)
    segs = segment_ids[:, None, :]
    row = tp[None].astype(jnp.int32)
    one = gain_attn[None]
    two = gain_ffn[None]
    end = gain_final[None]

    x = tokens.astype(f32)
    a1 = (x * inv_rms(x) * one).astype(bf16)
    state = attention(
        "attn_own", after(a1, far_a), vec_own, segs, place, order, 0, 0, rows, [pack_a], None
    )
    far_a = from_chips(far_a)
    far_b, far_c = others_of(after(order, (state, far_a)), all_bc, 2)
    groups = np.arange(n_dp).reshape(-1, share).tolist()
    far_c = lax.all_gather(far_c, "dp", axis=0, axis_index_groups=groups)
    far_a = from_cores(after(far_a, far_b))
    far_b = from_chips(after(far_b, far_a))
    qkv, lse, ctx, sorted_a = attention(
        "attn_far", a1, vecs[1:], segs, place, order, 1, 0, rows, far_a, state
    )
    far_b = from_cores(after(far_b, lse))
    mid, a2, part = ffn_own(tokens, ctx, sorted_a, two, w_hidden, w_down)
    layer_out, res, pooled, sorted_b, sorted_c = ffn_first(
        place, order, a2, mid, part, end, segs, far_b, far_c
    )
    block = width // n_dp
    here = rows * SEG_ROW
    pooled = pooled.astype(bf16)
    if split:
        pooled = jnp.concatenate([pooled] + [over_tp(pooled, k) for k in range(1, n_tp)])
        pooled = jnp.concatenate([pooled, over_dp(pooled, 1)])
        pooled_all = from_chips(pooled)
        spots = (dp ^ jnp.arange(n_dp))[:, None] * rows + order[None]
        at = jnp.concatenate([dp[None], spots.reshape(-1)]).astype(jnp.int32)
    else:
        pooled = lax.all_gather(pooled, "tp", axis=0, tiled=True)
        pooled_all = [lax.all_gather(pooled, "dp", axis=0, tiled=True)]
        at = dp[None].astype(jnp.int32)
    pairs = pair_order // 2
    if not split:
        everything = pooled_all[0]
        d_proj, d_pool, d_gain_end = loss_math(
            everything, w_project, pairs[:, None], pairs[None, :], end
        )
        own_cols = lax.dynamic_slice_in_dim(everything, dp * block, block, 1)
        grad_project = dg(own_cols, d_proj, TN)
        pooled_all = [lax.dynamic_slice_in_dim(d_pool, dp * here, here, 0)]
    made = row_back(
        at,
        row,
        pooled_all,
        split,
        w_project,
        pairs,
        (end, two, one),
        segs,
        lse,
        vecs,
        res,
        mid,
        a2,
        tokens,
        w_hidden,
        w_down,
        sorted_b,
        sorted_c,
        sorted_a,
        qkv,
        ctx,
        here,
        block,
    )
    d_pool, d_gain_two, d_attn, d_qkv, folded, d_tok, d_gain_one = made[0], *made[3:]
    if split:
        grad_project, d_gain_end = made[1], made[2]
    grad_gain_final = lax.dynamic_slice_in_dim(d_gain_end[0], dp * block, block, 0)
    d_tokens = lax.all_gather(d_tok, "tp", axis=0, tiled=True).astype(f32)

    d_rel = jnp.einsum(
        "khn,nb->kbh",
        folded.reshape(n_tp, heads, -1),
        grad_lanes(bucket_count),
        precision=highest,
    )
    gains = jnp.concatenate([d_gain_one, d_gain_two])
    pad = 16
    extra = jnp.zeros((n_tp, n_dp, pad, width), bf16)
    if split:
        small = d_rel.reshape(n_tp, 1, 1, bucket_count * heads).astype(bf16)
        gain_rows = jnp.swapaxes(gains.reshape(2, n_dp, block), 0, 1).astype(bf16)
        extra = jnp.concatenate(
            [
                jnp.broadcast_to(gain_rows[None], (n_tp, n_dp, 2, block)),
                jnp.broadcast_to(small, (n_tp, n_dp, 1, block)),
                jnp.zeros((n_tp, n_dp, pad - 3, block), bf16),
            ],
            2,
        )
        extra = jnp.pad(extra, ((0, 0), (0, 0), (0, 0), (0, width - block)))
    chips = (dp // 2) ^ jnp.arange(4, dtype=jnp.int32)
    spots = jnp.concatenate([row, (dp % 2)[None].astype(jnp.int32), chips])
    parts_a = attn_weights(spots, a1, d_attn, d_qkv, ctx, extra, split)

    def to_core(parts):
        keep, give = parts
        took = over_dp(give, 1)
        return [rounded(keep[c].astype(f32) + took[c].astype(f32)) for c in range(4)]

    def to_chip(pair):
        return [pair[0]] + [over_dp(pair[c].astype(bf16), 2 * c) for c in range(1, 4)]

    def total(parts):
        return tree([part.astype(f32) for part in parts])

    def scatter(parts):
        return lax.psum_scatter(parts[0].astype(f32), "dp", scatter_dimension=1, tiled=True)

    if split:
        pair_a = to_core(parts_a)
        got_a = to_chip(pair_a)
        first = after(order, pair_a)
    else:
        first = after(order, parts_a)
    layer_out, *parts_f = ffn_tail(
        spots, first, a2, mid, part, res, segs, d_pool, end,
        w_hidden, w_down, sorted_b, sorted_c, layer_out, n_dp, split,
    )
    if split:
        chips = [[c + core for c in range(0, n_dp, 2)] for core in range(2)]
        give_f = over_dp(after(parts_f[1], got_a), 1)
        pair_f = parts_f[0].astype(f32) + give_f.astype(f32)
        own_a = rounded(total(got_a))
        swapped = lax.all_to_all(
            pair_f.astype(bf16), "dp", 0, 0, axis_index_groups=chips, tiled=True
        )
        own_f = jnp.sum(swapped.astype(f32), 0)
    else:
        own_a, own_f = rounded(scatter(parts_a)), scatter(parts_f)

    def reduce_tp(value):
        return tree([value[0]] + [over_tp(value[k], k) for k in range(1, n_tp)])

    grad_a = tree(
        [own_a[0].astype(f32)]
        + [over_tp(own_a[k].astype(bf16), k).astype(f32) for k in range(1, n_tp)]
    )
    cols = width // 4
    if split:
        gain_one, gain_two = grad_a[block, :block], grad_a[block + 1, :block]
        d_rel_here = grad_a[block + 2, : bucket_count * heads].reshape(bucket_count, heads)
    else:
        gains = tree([gains] + [over_tp(gains, k) for k in range(1, n_tp)])
        d_rel_here, gains = lax.psum((reduce_tp(d_rel), gains), "dp")
        gain_one, gain_two = lax.dynamic_slice_in_dim(gains, dp * block, block, 1)
    return (
        layer_out,
        d_tokens,
        grad_a[:block, :cols],
        grad_a[:block, cols : 2 * cols],
        grad_a[:block, 2 * cols : 3 * cols],
        grad_a[:block, 3 * cols :].T,
        d_rel_here,
        gain_one,
        own_f[0],
        own_f[1].T,
        gain_two,
        grad_gain_final,
        grad_project,
    )


def solution(mesh):
    placed = (
        P("dp", None),
        P("dp", None),
        P(),
        P(None, "tp"),
        P(None, "tp"),
        P(None, "tp"),
        P("tp", None),
        P(None, "tp"),
        P(),
        P(None, "tp"),
        P("tp", None),
        P(),
        P(),
        P(),
    )
    return jax.shard_map(
        functools.partial(shards, mesh.shape["dp"], mesh.shape["tp"]),
        mesh=mesh,
        in_specs=placed,
        out_specs=(
            P("dp", None),
            P("dp", None),
            P("dp", "tp"),
            P("dp", "tp"),
            P("dp", "tp"),
            P("tp", "dp"),
            P(None, "tp"),
            P("dp"),
            P("dp", "tp"),
            P("tp", "dp"),
            P("dp"),
            P("dp"),
            P("dp", None),
        ),
        check_vma=False,
    )
```

```python
import functools
import math

import jax
import jax.numpy as jnp
import numpy as np
from jax import lax
from jax.experimental import pallas as pl
from jax.experimental.pallas import tpu as pltpu
from jax.sharding import PartitionSpec as P

MAX_DIST = 128
SEG_ROW = 8
TILE = 128
VMEM = 52 * 2**20

epsilon = 1e-06
logit_scale = 50.0
loss_scale = 128.0
masked_value = -1e30
highest = lax.Precision.HIGHEST
f32 = jnp.float32
bf16 = jnp.bfloat16

NN = (((1,), (0,)), ((), ()))
NT = (((1,), (1,)), ((), ()))
TN = (((0,), (0,)), ((), ()))


def dg(a, b, dims):
    return lax.dot_general(a, b, dims, preferred_element_type=f32)


def bucket_of(offsets, bucket_count, distance):
    half_count = bucket_count // 2
    exact_count = half_count // 2
    far_side = np.where(offsets > 0, half_count, 0)
    magnitude = np.abs(offsets)
    logged = (
        np.log(np.maximum(magnitude, exact_count) / exact_count)
        / math.log(distance / exact_count)
        * (half_count - exact_count)
    )
    far_bucket = np.minimum(exact_count + logged.astype(np.int64), half_count - 1)
    return (far_side + np.where(magnitude < exact_count, magnitude, far_bucket)).astype(np.int32)


def cost(flops, moved):
    return pl.CostEstimate(flops=int(flops), bytes_accessed=int(moved), transcendentals=0)


def bias_lanes(bucket_count):
    lanes = np.arange(4 * TILE)
    lanes = np.where(lanes >= 2 * TILE, lanes - 4 * TILE, lanes)
    return np.eye(bucket_count, dtype=np.float32)[bucket_of(-lanes, bucket_count, MAX_DIST)].T


def grad_lanes(bucket_count):
    sub = np.arange(8)[:, None]
    lane = np.arange(4 * TILE)[None, :]
    y = (lane - sub) % (4 * TILE)
    y = np.where(y >= 2 * TILE, y - 4 * TILE, y)
    near = bucket_of(-y, bucket_count, MAX_DIST)
    up = np.full((8, TILE), bucket_of(np.array(MAX_DIST), bucket_count, MAX_DIST))
    down = np.full((8, TILE), bucket_of(np.array(-MAX_DIST), bucket_count, MAX_DIST))
    ids = np.concatenate([near, up, down], 1).reshape(-1)
    return np.eye(bucket_count, dtype=np.float32)[ids]


def bring(place_ref, piece_refs, into, sems):
    width = into.shape[1]
    slices = width // len(piece_refs)
    copies = []
    for m, piece in enumerate(piece_refs):
        start = pl.multiple_of(place_ref[m], 16) if slices % 16 == 0 else place_ref[m]
        if len(piece.shape) == 2:
            piece, to = piece.at[pl.ds(0, slices)], into.at[0, pl.ds(start, slices)]
        else:
            to = into.at[:, pl.ds(start, slices), :]
        copy = pltpu.make_async_copy(piece, to, sems.at[m])
        copy.start()
        copies.append(copy)
    return copies


def spread_bias(vec_ref, bias_s, heads, at=0):
    for h in range(heads):
        wide = jnp.broadcast_to(vec_ref[0, h : h + 1, :], (TILE, 4 * TILE))
        bias_s[at + h] = pltpu.roll(wide, 0, 1, stride=1, stride_axis=0)


def with_bias(tile, offset, h, bias_s, vec_ref, first=0):
    if offset == 0:
        return tile + bias_s[first + h, :, 0:TILE]
    if offset == 1:
        return tile + bias_s[first + h, :, 3 * TILE : 4 * TILE]
    if offset == -1:
        return tile + bias_s[first + h, :, TILE : 2 * TILE]
    lane = 2 * TILE + 1 if offset > 1 else 2 * TILE - 1
    return tile + vec_ref[0, h : h + 1, lane : lane + 1]


def masks(seg):
    hot = lax.broadcasted_iota(jnp.int32, (16, seg.shape[-1]), 0) == seg
    return (
        jnp.where(hot, 0.0, masked_value).astype(bf16),
        jnp.where(hot, 1.0, 0.0).astype(bf16),
    )


def inv_rms(values):
    return lax.rsqrt(jnp.mean(values * values, -1, keepdims=True) + epsilon)


def rounded(value):
    return lax.reduce_precision(value, 8, 7)


def tree(parts):
    while len(parts) > 1:
        parts = [parts[i] + parts[i + 1] for i in range(0, len(parts), 2)]
    return parts[0]


def exact_parts(value):
    parts = []
    for _ in range(3):
        part = value.astype(bf16)
        parts.append(part)
        value = value - part.astype(f32)
    return parts


PAD = 16


def pack_kernel(at_ref, q_ref, k_ref, v_ref, o_ref, rel_ref, out_ref, mine_ref, pack_s):
    cols = q_ref.shape[1]
    for at, ref in enumerate((q_ref, k_ref, v_ref)):
        pack_s[at * cols : (at + 1) * cols] = ref[...].astype(f32).T
    pack_s[3 * cols :] = o_ref[...].astype(f32)
    out_ref[...] = pack_s[...].astype(bf16)
    slices = mine_ref.shape[0] - PAD
    start = at_ref[0] * slices
    if slices % 8 == 0:
        start = pl.multiple_of(start, 8)
    mine_ref[:slices] = pack_s[pl.ds(start, slices), :].astype(bf16)
    mine_ref[slices:] = jnp.zeros_like(mine_ref[slices:])
    buckets, heads = rel_ref.shape
    lane = 0
    for at in range(0, buckets, PAD):
        for part in exact_parts(rel_ref[at : at + PAD]):
            mine_ref[slices:, lane : lane + heads] = part
            lane += TILE


def pack_weights(at, w_query, w_key, w_value, w_out, rel_bias, share):
    width, cols = w_query.shape
    slices = width // share
    full = lambda shape: pl.BlockSpec(shape, lambda i, at: (0, 0))
    return pl.pallas_call(
        pack_kernel,
        grid_spec=pltpu.PrefetchScalarGridSpec(
            num_scalar_prefetch=1,
            grid=(1,),
            in_specs=[full((width, cols))] * 3 + [full((cols, width)), full(rel_bias.shape)],
            out_specs=[full((width, width)), full((slices + PAD, width))],
            scratch_shapes=[pltpu.VMEM((width, width), f32)],
        ),
        out_shape=[
            jax.ShapeDtypeStruct((width, width), bf16),
            jax.ShapeDtypeStruct((slices + PAD, width), bf16),
        ],
        compiler_params=pltpu.CompilerParams(vmem_limit_bytes=VMEM),
        cost_estimate=cost(10**9, 2**20),
        name="pack_weights",
    )(at, w_query, w_key, w_value, w_out, rel_bias)


def unpack_table(pads, buckets, heads):
    rows = []
    lane = 0
    for _ in range(0, buckets, PAD):
        parts = [
            pads[:, :, lane + p * TILE : lane + p * TILE + heads].astype(f32) for p in range(3)
        ]
        rows.append(parts[0] + parts[1] + parts[2])
        lane += 3 * TILE
    return jnp.concatenate(rows, 1)


def stack_kernel(*refs):
    ins, outs = refs[:3], refs[3:]
    slices = outs[0].shape[1]
    for at, ref in enumerate(ins):
        outs[0][at] = ref[:slices]
        if len(outs) == 2:
            outs[1][at] = ref[slices:]


def stack(arrays, slices):
    rows, width = arrays[0].shape
    shapes = [(3, slices, width)] + ([(3, rows - slices, width)] if rows > slices else [])
    return pl.pallas_call(
        stack_kernel,
        out_shape=[jax.ShapeDtypeStruct(shape, bf16) for shape in shapes],
        cost_estimate=cost(0, 12 * arrays[0].size),
        name="stack",
    )(*arrays)


def others_kernel(order_ref, all_ref, *outs):
    slices = outs[0].shape[1]
    for k in range(1, all_ref.shape[0]):
        for at, out in enumerate(outs):
            out[k - 1] = all_ref[order_ref[k], at * slices : (at + 1) * slices]


def others_of(order, everything, count):
    n, total, width = everything.shape
    slices = total // count
    shape = (n - 1, slices, width)
    return pl.pallas_call(
        others_kernel,
        grid_spec=pltpu.PrefetchScalarGridSpec(
            num_scalar_prefetch=1,
            grid=(1,),
            in_specs=[pl.BlockSpec((n, total, width), lambda i, p: (0, 0, 0))],
            out_specs=[pl.BlockSpec(shape, lambda i, p: (0, 0, 0))] * count,
        ),
        out_shape=[jax.ShapeDtypeStruct(shape, bf16)] * count,
        cost_estimate=cost(0, 4 * everything.size),
        name="others_of",
    )(order, everything)


def attend_row(heads, hd, weights, a1_ref, vec_ref, seg_ref, qkv_s, lse_s, ctx_ref, bias_s, first):
    length = a1_ref.shape[0]
    blocks = length // TILE
    qkv_s[...] = dg(weights, a1_ref[...], NT).astype(bf16)
    q_mask, k_mask = masks(seg_ref[0])
    ones = jnp.ones((16, length), bf16)
    for h in range(heads):
        q_t = jnp.concatenate([qkv_s[h * hd : (h + 1) * hd], q_mask], 0)
        k_t = jnp.concatenate([qkv_s[(heads + h) * hd : (heads + h + 1) * hd], k_mask], 0)
        v_t = jnp.concatenate([qkv_s[(2 * heads + h) * hd : (2 * heads + h + 1) * hd], ones], 0)
        scores = dg(k_t.T, q_t, NN)
        columns = []
        tops = []
        for i in range(blocks):
            tiles = [
                with_bias(
                    scores[j * TILE : (j + 1) * TILE, i * TILE : (i + 1) * TILE],
                    j - i,
                    h,
                    bias_s,
                    vec_ref,
                    first,
                )
                for j in range(blocks)
            ]
            top = jnp.max(functools.reduce(jnp.maximum, tiles), 0, keepdims=True)
            tops.append(top)
            columns.append(jnp.concatenate([jnp.exp(t - top).astype(bf16) for t in tiles], 0))
        mixed = dg(v_t, jnp.concatenate(columns, 1), NN)
        total = mixed[hd : hd + 1]
        lse_s[h : h + 1, :] = jnp.concatenate(tops, 1) + jnp.log(total)
        ctx_ref[0, 0, h * hd : (h + 1) * hd, :] = (mixed[:hd] / total).astype(bf16)


def attn_kernel(heads, hd, n, low, keeps, place_ref, order_ref, a1_ref, vec_ref, seg_ref, *rest):
    sources = rest[: max(n, 1)]
    rest = rest[max(n, 1) + (0 if low == 0 else 4 if keeps else 1) :]
    if keeps:
        qkv_ref, lse_ref, ctx_ref, sorted_ref, bias_s, qkv_s, lse_s, w_s, sems, out_sem = rest
    else:
        ctx_ref, bias_s, qkv_s, lse_s = rest
    r, s = pl.program_id(0), pl.program_id(1)
    first = s * heads

    @pl.when(r == 0)
    def _():
        spread_bias(vec_ref, bias_s, heads, first)

    if keeps:
        count = w_s.shape[0]
        source = w_s if n else sources[0]
        into = sorted_ref.at[pl.ds(low, count)] if n else sorted_ref.at[low]
        keep = pltpu.make_async_copy(source, into, out_sem)

        @pl.when((s == 0) & (r == 0))
        def _():
            if n:
                for copy in bring(place_ref, sources, w_s, sems):
                    copy.wait()
            keep.start()

        weights = w_s[s, : 3 * heads * hd] if n else sources[0][: 3 * heads * hd]
    else:
        weights = sources[0][s, : 3 * heads * hd]
    attend_row(
        heads, hd, weights, a1_ref, vec_ref, seg_ref, qkv_s, lse_s, ctx_ref, bias_s, first
    )
    if keeps:

        @pl.when(r == 0)
        def _():
            qkv_ref[0] = qkv_s[...]
            lse_ref[0] = lse_s[...]

        @pl.when((s == pl.num_programs(1) - 1) & (r == pl.num_programs(0) - 1))
        def _():
            keep.wait()


def attention(name, a1, vecs, segs, place, order, low, first_row, n_rows, weights, chain):
    rows, _, length = segs.shape
    width = a1.shape[1]
    count, heads, _ = vecs.shape
    slots = order.shape[0]
    hd = width // (4 * heads)
    cols = heads * hd
    n = len(weights) if weights[0].shape[0] != slots and len(weights) > 1 else 0
    keeps = first_row == 0
    anywhere = pl.BlockSpec(memory_space=pl.ANY)
    at = lambda r, o: o[r + first_row]
    slot = lambda r, s: low + jnp.where(r == 0, s, count - 1)
    if n:
        w_specs = [anywhere] * n
    elif keeps:
        w_specs = [pl.BlockSpec((width, width), lambda r, s, p, o: (0, 0))]
    else:
        w_specs = [pl.BlockSpec((count, width, width), lambda r, s, p, o: (low // count, 0, 0))]
    out_specs = [
        pl.BlockSpec((1, 3 * cols, length), lambda r, s, p, o: (slot(r, s), 0, 0)),
        pl.BlockSpec((1, heads, length), lambda r, s, p, o: (slot(r, s), 0, 0)),
        pl.BlockSpec((1, 1, cols, length), lambda r, s, p, o: (s + low, at(r, o), 0, 0)),
        anywhere,
    ]
    out_shape = [
        jax.ShapeDtypeStruct((slots, 3 * cols, length), bf16),
        jax.ShapeDtypeStruct((slots, heads, length), f32),
        jax.ShapeDtypeStruct((slots, rows, cols, length), bf16),
        jax.ShapeDtypeStruct((slots, width, width), bf16),
    ]
    scratch = [
        pltpu.VMEM((count * heads, TILE, 4 * TILE), f32),
        pltpu.VMEM((3 * cols, length), bf16),
        pltpu.VMEM((heads, length), f32),
    ]
    if keeps:
        scratch += [
            pltpu.VMEM((count, width, width) if n else (1, 16, TILE), bf16),
            pltpu.SemaphoreType.DMA((max(n, 1),)),
            pltpu.SemaphoreType.DMA(()),
        ]
        linked = [] if chain is None else list(chain)
    else:
        out_specs, out_shape, linked = out_specs[2:3], out_shape[2:3], [chain[2]]
    base = 5 + len(w_specs)
    return pl.pallas_call(
        functools.partial(attn_kernel, heads, hd, n, low, keeps),
        grid_spec=pltpu.PrefetchScalarGridSpec(
            num_scalar_prefetch=2,
            grid=(n_rows, count),
            in_specs=[
                pl.BlockSpec((length, width), lambda r, s, p, o: (at(r, o), 0)),
                pl.BlockSpec((1, heads, 4 * TILE), lambda r, s, p, o: (s, 0, 0)),
                pl.BlockSpec((1, 1, length), lambda r, s, p, o: (at(r, o), 0, 0)),
            ]
            + w_specs
            + [anywhere] * len(linked),
            out_specs=out_specs,
            scratch_shapes=scratch,
        ),
        out_shape=out_shape,
        input_output_aliases={base + i: i for i in range(len(linked))},
        compiler_params=pltpu.CompilerParams(vmem_limit_bytes=VMEM),
        cost_estimate=cost(n_rows * count * 2.5 * 10**9, 2**20),
        name=name,
    )(place, order, a1, vecs, segs, *weights, *linked)


GELU_A = math.sqrt(2.0 / math.pi)
GELU_B = 0.044715


def gelu(v):
    t = jnp.tanh(v * (GELU_A + (GELU_A * GELU_B) * (v * v)))
    half = 0.5 * v
    return half + half * t


def gelu_pair(v):
    square = v * v
    t = jnp.tanh(v * (GELU_A + (GELU_A * GELU_B) * square))
    half = 0.5 * v
    inner = GELU_A + (3.0 * GELU_A * GELU_B) * square
    return half + half * t, 0.5 + 0.5 * t + half * (1.0 - t * t) * inner


def ffn_own_kernel(x_ref, ctx_ref, wo_ref, gain_ref, b_ref, c_ref, mid_ref, a2_ref, part_ref):
    slots, _, cols, length = ctx_ref.shape
    attn = dg(
        ctx_ref[...].reshape(slots * cols, length),
        wo_ref[...].reshape(slots * cols, wo_ref.shape[-1]),
        TN,
    )
    mid = (x_ref[...].astype(f32) + attn).astype(bf16)
    mid_ref[...] = mid
    mid = mid.astype(f32)
    a2 = (mid * inv_rms(mid) * gain_ref[...]).astype(bf16)
    a2_ref[...] = a2
    hidden = gelu(dg(a2, b_ref[...], NN)).astype(bf16)
    part_ref[...] = dg(hidden, c_ref[...], NN).astype(bf16)


def ffn_own(x, ctx, sorted_a, gain, own_b, own_c):
    slots, rows, cols, length = ctx.shape
    tokens, width = x.shape
    units = own_b.shape[1]
    by_row = pl.BlockSpec((length, width), lambda r: (r, 0))
    return pl.pallas_call(
        ffn_own_kernel,
        grid=(rows,),
        in_specs=[
            by_row,
            pl.BlockSpec((slots, 1, cols, length), lambda r: (0, r, 0, 0)),
            pl.BlockSpec((slots, cols, width), lambda r: (0, 3, 0)),
            pl.BlockSpec((1, width), lambda r: (0, 0)),
            pl.BlockSpec((width, units), lambda r: (0, 0)),
            pl.BlockSpec((units, width), lambda r: (0, 0)),
        ],
        out_specs=[by_row] * 3,
        out_shape=[jax.ShapeDtypeStruct((tokens, width), bf16)] * 3,
        compiler_params=pltpu.CompilerParams(vmem_limit_bytes=VMEM),
        cost_estimate=cost(tokens * width * 6 * units, 2**24),
        name="ffn_own",
    )(x, ctx, sorted_a, gain, own_b, own_c)


def ffn_row(a2, mid, part, up, down, gain_ref, seg_ref, out_ref, res_ref, pool_ref, wait=None):
    res = mid.astype(f32) + part.astype(f32)
    for k in range(len(up)):
        if wait is not None:
            wait(k)
        hidden = gelu(dg(a2, up[k][...], NN)).astype(bf16)
        res = res + dg(hidden, down[k][...], NN)
    res_ref[...] = res.astype(bf16)
    final = (res * inv_rms(res) * gain_ref[...]).astype(bf16)
    out_ref[...] = final
    if pool_ref is not None:
        seg = seg_ref[0]
        hot = lax.broadcasted_iota(jnp.int32, (SEG_ROW, seg.shape[-1]), 0) == seg
        member = jnp.where(hot, 1.0, 0.0)
        pool_ref[...] = dg(member.astype(bf16), final, NN) / jnp.sum(member, 1, keepdims=True)


def ffn_first_kernel(
    count, place_ref, order_ref, a2_ref, mid_ref, part_ref, gain_ref, seg_ref, *rest
):
    pieces, far_c = rest[:count], rest[count]
    out_ref, res_ref, pool_ref, sb_ref, sc_ref, b_s, c_s, sems, out_sems = rest[count + 1 :]
    others = b_s.shape[0]
    slices = far_c.shape[2]
    copies = []
    for k in range(others):
        here = []
        for m in range(count):
            start = pl.multiple_of(place_ref[m], 16) if slices % 16 == 0 else place_ref[m]
            into = b_s.at[k, pl.ds(start, slices), :]
            here.append(pltpu.make_async_copy(pieces[m].at[k], into, sems.at[0, k, m]))
            into = c_s.at[k, pl.ds(m * slices, slices), :]
            here.append(pltpu.make_async_copy(far_c.at[m, k], into, sems.at[1, k, m]))
        copies.append(here)
    keep = []
    for k in range(others):
        keep.append(pltpu.make_async_copy(b_s.at[k], sb_ref.at[k], out_sems.at[0, k]))
        keep.append(pltpu.make_async_copy(c_s.at[k], sc_ref.at[k], out_sems.at[1, k]))
    for here in copies:
        for copy in here:
            copy.start()

    def wait(k):
        for copy in copies[k]:
            copy.wait()
        keep[2 * k].start()
        keep[2 * k + 1].start()

    ffn_row(
        a2_ref[...],
        mid_ref[...],
        part_ref[...],
        [b_s.at[k] for k in range(others)],
        [c_s.at[k] for k in range(others)],
        gain_ref,
        seg_ref,
        out_ref,
        res_ref,
        pool_ref,
        wait,
    )
    for copy in keep:
        copy.wait()


def ffn_first(place, order, a2, mid, part, gain, segs, pieces, far_c):
    rows, _, length = segs.shape
    tokens, width = a2.shape
    units = pieces[0].shape[-1]
    others = pieces[0].shape[0]
    n = len(pieces)
    first = pl.BlockSpec((length, width), lambda r, p, o: (o[0], 0))
    anywhere = pl.BlockSpec(memory_space=pl.ANY)
    return pl.pallas_call(
        functools.partial(ffn_first_kernel, n),
        grid_spec=pltpu.PrefetchScalarGridSpec(
            num_scalar_prefetch=2,
            grid=(1,),
            in_specs=[
                first,
                first,
                first,
                pl.BlockSpec((1, width), lambda r, p, o: (0, 0)),
                pl.BlockSpec((1, 1, length), lambda r, p, o: (o[0], 0, 0)),
            ]
            + [anywhere] * (n + 1),
            out_specs=[
                first,
                pl.BlockSpec((length, width), lambda r, p, o: (0, 0)),
                pl.BlockSpec((SEG_ROW, width), lambda r, p, o: (0, 0)),
                anywhere,
                anywhere,
            ],
            scratch_shapes=[
                pltpu.VMEM((others, width, units), bf16),
                pltpu.VMEM((others, units, width), bf16),
                pltpu.SemaphoreType.DMA((2, others, n)),
                pltpu.SemaphoreType.DMA((2, others)),
            ],
        ),
        out_shape=[
            jax.ShapeDtypeStruct((tokens, width), bf16),
            jax.ShapeDtypeStruct((length, width), bf16),
            jax.ShapeDtypeStruct((SEG_ROW, width), f32),
            jax.ShapeDtypeStruct((others, width, units), bf16),
            jax.ShapeDtypeStruct((others, units, width), bf16),
        ],
        compiler_params=pltpu.CompilerParams(vmem_limit_bytes=VMEM),
        cost_estimate=cost(length * width * 4 * units * others, 2**24),
        name="ffn_first",
    )(place, order, a2, mid, part, gain, segs, *pieces, far_c)


def loss_math(pooled, project, pair_col, pair_row, gain):
    slots = pooled.shape[0]
    projected = dg(pooled, project, NN)
    inv_norm = lax.rsqrt(jnp.sum(projected * projected, -1, keepdims=True) + epsilon)
    unit = projected * inv_norm
    embedded = unit.astype(bf16)
    similar = logit_scale * dg(embedded, embedded, NT)
    rows = lax.broadcasted_iota(jnp.int32, (slots, slots), 0)
    columns = lax.broadcasted_iota(jnp.int32, (slots, slots), 1)
    same = rows == columns
    similar = jnp.where(same, masked_value, similar)
    partner = jnp.where((pair_col == pair_row) & jnp.logical_not(same), 2.0, 0.0)

    def total(axis):
        top = jnp.max(similar, axis, keepdims=True)
        return top + jnp.log(jnp.sum(jnp.exp(similar - top), axis, keepdims=True))

    both = jnp.exp(similar - total(1)) + jnp.exp(similar - total(0)) - partner
    high = both.astype(bf16)
    low = (both - high.astype(f32)).astype(bf16)
    d_unit = (loss_scale * logit_scale) * (dg(high, embedded, NN) + dg(low, embedded, NN))
    d_proj = inv_norm * (d_unit - unit * jnp.sum(d_unit * unit, -1, keepdims=True))
    d_proj = d_proj.astype(bf16)
    d_pooled = dg(d_proj, project, NT)
    d_gain = jnp.sum(d_pooled * pooled.astype(f32), 0, keepdims=True) / gain
    return d_proj, d_pooled, d_gain


def d_result_of(res, seg, d_pool, gain):
    hot = lax.broadcasted_iota(jnp.int32, (SEG_ROW, seg.shape[-1]), 0) == seg
    member = jnp.where(hot, 1.0, 0.0)
    per_token = d_pool / jnp.sum(member, 1, keepdims=True)
    high = per_token.astype(bf16)
    low = (per_token - high.astype(f32)).astype(bf16)
    twice = jnp.concatenate([member, member], 0).astype(bf16)
    d_final = dg(twice, jnp.concatenate([high, low], 0), TN)
    scale = inv_rms(res)
    unit = res * scale
    weighted = d_final * gain
    return scale * (weighted - unit * jnp.mean(weighted * unit, -1, keepdims=True))


def fold(tile):
    lanes = tile.shape[1]
    total = tile[0:8]
    for b in range(1, TILE // 8):
        total = total + pltpu.roll(tile[8 * b : 8 * b + 8], lanes - 8 * b, 1)
    return total


def loss_step(pieces, at_ref, project_ref, pc_ref, pr_ref, gain_ref, dpool_ref, dproj_ref, dgain_ref, a_s, b_s):
    each = SEG_ROW
    parts = pieces[0].shape[0] // each
    for m, piece in enumerate(pieces):
        value = piece[...].astype(f32)
        for part in range(parts):
            start = pl.multiple_of(at_ref[1 + m * parts + part] * each, each)
            a_s[pl.ds(start, each), :] = value[part * each : (part + 1) * each]
    pooled = a_s[...].astype(bf16)
    d_proj, d_pooled, d_gain = loss_math(
        pooled, project_ref[...], pc_ref[...], pr_ref[...], gain_ref[...]
    )
    a_s[...] = d_pooled
    b_s[...] = dg(pooled, d_proj, TN)
    here = dpool_ref.shape[0]
    block = dproj_ref.shape[0]
    dpool_ref[...] = a_s[pl.ds(pl.multiple_of(at_ref[0] * here, here), here), :]
    dproj_ref[...] = b_s[pl.ds(pl.multiple_of(at_ref[0] * block, block), block), :]
    dgain_ref[...] = d_gain


def norm_back(grad, values, gain):
    scale = inv_rms(values)
    unit = values * scale
    weighted = grad * gain
    d_values = scale * (weighted - unit * jnp.mean(weighted * unit, -1, keepdims=True))
    return d_values, jnp.sum(grad * unit, 0, keepdims=True)


def row_back_kernel(count, with_loss, heads, hd, at_ref, row_ref, *refs):
    pieces, refs = refs[:count], refs[count:]
    project_ref, pc_ref, pr_ref, gain_end_ref, gain_two_ref, gain_one_ref, seg_ref = refs[:7]
    lse_ref, vec_ref, res_any, mid_any, a2_any, x_any, own_b, own_c, far_b, far_c = refs[7:17]
    far_a, qkv_any, ctx_any = refs[17:20]
    dpool_ref, dproj_ref, dend_ref, dtwo_ref, dattn_ref = refs[20:25]
    dqkv_ref, fold_ref, dtok_ref, done_ref = refs[25:29]
    a_s, p_s, b_s, c_s, wo_s, wa_s, res_s, mid_s, a2_s, x_s, qkv_s, ctx_s = refs[29:41]
    dres_s, low_s, sum_s, dctx_s, bias_s, b_sems, c_sems, sems = refs[41:]
    step = pl.program_id(0)
    slots = b_s.shape[0]
    length = res_s.shape[0]
    cols = heads * hd
    row = row_ref[0]
    mine = pl.ds(pl.multiple_of(row * length, length), length)
    res_copy = pltpu.make_async_copy(res_any, res_s, sems.at[0])
    a2_copy = pltpu.make_async_copy(a2_any.at[mine], a2_s, sems.at[1])
    mid_copy = pltpu.make_async_copy(mid_any.at[mine], mid_s, sems.at[2])
    wo_copy = pltpu.make_async_copy(far_a.at[:, pl.ds(3 * cols, cols)], wo_s, sems.at[3])
    qkv_copy = pltpu.make_async_copy(qkv_any, qkv_s, sems.at[4])
    ctx_copy = pltpu.make_async_copy(ctx_any.at[:, row], ctx_s, sems.at[5])
    wa_copy = pltpu.make_async_copy(far_a.at[:, pl.ds(0, 3 * cols)], wa_s, sems.at[6])
    x_copy = pltpu.make_async_copy(x_any.at[mine], x_s, sems.at[7])

    def weight_copies(k):
        b_from, c_from = (own_b, own_c) if k == 0 else (far_b.at[k - 1], far_c.at[k - 1])
        return [
            pltpu.make_async_copy(b_from, b_s.at[k], b_sems.at[k]),
            pltpu.make_async_copy(c_from, c_s.at[k], c_sems.at[k]),
        ]

    @pl.when(step == 0)
    def _():
        res_copy.start()
        a2_copy.start()
        for k in range(slots):
            for copy in weight_copies(k):
                copy.start()
        for copy in (mid_copy, wo_copy, qkv_copy, ctx_copy, wa_copy, x_copy):
            copy.start()
        if with_loss:
            loss_step(
                pieces,
                at_ref,
                project_ref,
                pc_ref,
                pr_ref,
                gain_end_ref,
                dpool_ref,
                dproj_ref,
                dend_ref,
                a_s,
                p_s,
            )
        else:
            dpool_ref[...] = pieces[0][...]
            dproj_ref[...] = jnp.zeros_like(dproj_ref)
            dend_ref[...] = jnp.zeros_like(dend_ref)
        res_copy.wait()
        a2_copy.wait()
        d_pool = dpool_ref[pl.ds(pl.multiple_of(row * SEG_ROW, SEG_ROW), SEG_ROW), :]
        d_res = d_result_of(res_s[...].astype(f32), seg_ref[0], d_pool, gain_end_ref[...])
        dres_s[...] = d_res
        low_s[...] = d_res.astype(bf16)
        sum_s[...] = jnp.zeros_like(sum_s)

    for k in range(slots):

        @pl.when(step == k + 1)
        def _():
            for copy in weight_copies(k):
                copy.wait()

    @pl.when((step >= 1) & (step <= slots))
    def _():
        up, down = b_s.at[step - 1], c_s.at[step - 1]
        slope = gelu_pair(dg(a2_s[...], up[...], NN))[1]
        d_pre = (dg(low_s[...], down[...], NT) * slope).astype(bf16)
        sum_s[...] += dg(d_pre, up[...], NT)

    @pl.when(step == slots)
    def _():
        mid_copy.wait()
        wo_copy.wait()
        d_mid, dtwo_ref[...] = norm_back(
            sum_s[...], mid_s[...].astype(f32), gain_two_ref[...]
        )
        d_mid = dres_s[...] + d_mid
        dres_s[...] = d_mid
        low = d_mid.astype(bf16)
        dattn_ref[...] = low
        sum_s[...] = jnp.zeros_like(sum_s)
        for k in range(slots):
            dctx_s[k] = dg(wo_s[k], low, NT).astype(bf16)
        qkv_copy.wait()
        ctx_copy.wait()
        wa_copy.wait()
        x_copy.wait()

    @pl.when(step > slots)
    def _():
        slot = step - slots - 1
        blocks = length // TILE
        spread_bias(vec_ref.at[pl.ds(slot, 1)], bias_s, heads)
        q_mask, k_mask = masks(seg_ref[0])
        for h in range(heads):
            q_low = qkv_s[slot, h * hd : (h + 1) * hd]
            k_low = qkv_s[slot, (heads + h) * hd : (heads + h + 1) * hd]
            v_low = qkv_s[slot, (2 * heads + h) * hd : (2 * heads + h + 1) * hd]
            dc = dctx_s[slot, h * hd : (h + 1) * hd]
            c = ctx_s[slot, h * hd : (h + 1) * hd]
            delta = jnp.sum(dc.astype(f32) * c.astype(f32), 0, keepdims=True)
            lse = lse_ref[slot, h : h + 1]
            scores = dg(
                jnp.concatenate([k_low, k_mask], 0).T, jnp.concatenate([q_low, q_mask], 0), NN
            )
            d_probs = dg(v_low.T, dc, NN)
            probs_cols = []
            score_cols = []
            near = [None, None, None]
            far = [None, None]
            for i in range(blocks):
                at = slice(i * TILE, (i + 1) * TILE)
                probs = []
                grads = []
                for j in range(blocks):
                    to = slice(j * TILE, (j + 1) * TILE)
                    tile = with_bias(scores[to, at], j - i, h, bias_s, vec_ref.at[pl.ds(slot, 1)])
                    prob = jnp.exp(tile - lse[:, at])
                    grad = prob * (d_probs[to, at] - delta[:, at])
                    probs.append(prob.astype(bf16))
                    grads.append(grad.astype(bf16))
                    if abs(j - i) <= 1:
                        old = near[j - i + 1]
                        near[j - i + 1] = grad if old is None else old + grad
                    else:
                        old = far[int(j < i)]
                        far[int(j < i)] = grad if old is None else old + grad
                probs_cols.append(jnp.concatenate(probs, 0))
                score_cols.append(jnp.concatenate(grads, 0))
            probs = jnp.concatenate(probs_cols, 1)
            grads = jnp.concatenate(score_cols, 1)
            dqkv_ref[0, h * hd : (h + 1) * hd] = dg(k_low, grads, NN).astype(bf16)
            dqkv_ref[0, (heads + h) * hd : (heads + h + 1) * hd] = dg(q_low, grads, NT).astype(bf16)
            dqkv_ref[0, (2 * heads + h) * hd : (2 * heads + h + 1) * hd] = dg(dc, probs, NT).astype(
                bf16
            )
            band = jnp.concatenate([near[1], near[0], jnp.zeros_like(near[0]), near[2]], 1)
            fold_ref[0, h, :, : 4 * TILE] = fold(band)
            for side in range(2):
                total = far[side][0:8]
                for b in range(1, TILE // 8):
                    total = total + far[side][8 * b : 8 * b + 8]
                fold_ref[0, h, :, (4 + side) * TILE : (5 + side) * TILE] = total
        sum_s[...] += dg(dqkv_ref[0], wa_s[slot], TN)

    @pl.when(step == 2 * slots)
    def _():
        d_x, done_ref[...] = norm_back(sum_s[...], x_s[...].astype(f32), gain_one_ref[...])
        dtok_ref[...] = (dres_s[...] + d_x).astype(bf16)


def row_back(
    at,
    row,
    pieces,
    with_loss,
    project,
    pairs,
    gains,
    segs,
    lse,
    vecs,
    res,
    mid,
    a2,
    x,
    own_b,
    own_c,
    far_b,
    far_c,
    sorted_a,
    qkv,
    ctx,
    here,
    block,
):
    slots, heads, _ = vecs.shape
    length, width = res.shape
    units = own_b.shape[1]
    cols = width // 4
    n_all = pairs.shape[0]
    anywhere = pl.BlockSpec(memory_space=pl.ANY)

    def full(shape):
        zeros = (0,) * len(shape)
        return pl.BlockSpec(shape, lambda i, at, row: zeros)

    def slot(i):
        return jnp.maximum(i - slots - 1, 0)

    row_shape = (length, width)
    return pl.pallas_call(
        functools.partial(row_back_kernel, len(pieces), with_loss, heads, cols // heads),
        grid_spec=pltpu.PrefetchScalarGridSpec(
            num_scalar_prefetch=2,
            grid=(2 * slots + 1,),
            in_specs=[full(piece.shape) for piece in pieces]
            + [full(project.shape), full((n_all, 1)), full((1, n_all))]
            + [full((1, width))] * 3
            + [
                pl.BlockSpec((1, 1, length), lambda i, at, row: (row[0], 0, 0)),
                full(lse.shape),
                full(vecs.shape),
            ]
            + [anywhere] * 11,
            out_specs=[
                full((here, width)),
                full((block, width)),
                full((1, width)),
                full((1, width)),
                full(row_shape),
                pl.BlockSpec((1, 3 * cols, length), lambda i, at, row: (slot(i), 0, 0)),
                pl.BlockSpec((1, heads, 8, 6 * TILE), lambda i, at, row: (slot(i), 0, 0, 0)),
                full(row_shape),
                full((1, width)),
            ],
            scratch_shapes=[
                pltpu.VMEM((n_all if with_loss else 8, width), f32),
                pltpu.VMEM((width, width), f32),
                pltpu.VMEM((slots, width, units), bf16),
                pltpu.VMEM((slots, units, width), bf16),
                pltpu.VMEM((slots, cols, width), bf16),
                pltpu.VMEM((slots, 3 * cols, width), bf16),
                pltpu.VMEM(row_shape, bf16),
                pltpu.VMEM(row_shape, bf16),
                pltpu.VMEM(row_shape, bf16),
                pltpu.VMEM(row_shape, bf16),
                pltpu.VMEM((slots, 3 * cols, length), bf16),
                pltpu.VMEM((slots, cols, length), bf16),
                pltpu.VMEM(row_shape, f32),
                pltpu.VMEM(row_shape, bf16),
                pltpu.VMEM(row_shape, f32),
                pltpu.VMEM((slots, cols, length), bf16),
                pltpu.VMEM((heads, TILE, 4 * TILE), f32),
                pltpu.SemaphoreType.DMA((slots,)),
                pltpu.SemaphoreType.DMA((slots,)),
                pltpu.SemaphoreType.DMA((8,)),
            ],
        ),
        out_shape=[
            jax.ShapeDtypeStruct((here, width), f32),
            jax.ShapeDtypeStruct((block, width), f32),
            jax.ShapeDtypeStruct((1, width), f32),
            jax.ShapeDtypeStruct((1, width), f32),
            jax.ShapeDtypeStruct(row_shape, bf16),
            jax.ShapeDtypeStruct((slots, 3 * cols, length), bf16),
            jax.ShapeDtypeStruct((slots, heads, 8, 6 * TILE), f32),
            jax.ShapeDtypeStruct(row_shape, bf16),
            jax.ShapeDtypeStruct((1, width), f32),
        ],
        compiler_params=pltpu.CompilerParams(vmem_limit_bytes=VMEM),
        cost_estimate=cost(3 * 10**10, 2**24),
        name="row_back",
    )(
        at,
        row,
        *pieces,
        project,
        pairs[:, None],
        pairs[None, :],
        *gains,
        segs,
        lse,
        vecs,
        res,
        mid,
        a2,
        x,
        own_b,
        own_c,
        far_b,
        far_c,
        sorted_a,
        qkv,
        ctx,
    )


def split_blocks(core, rel_ref, block, pad, extra, values, keep_ref, give_ref, lead):
    for c in range(2):

        @pl.when(core == c)
        def _():
            for chip in range(4):
                for ref, j in ((keep_ref, 2 * chip + c), (give_ref, 2 * chip + 1 - c)):
                    rows = values(j * block, (j + 1) * block)
                    to = chip if rel_ref is None else rel_ref[chip]
                    for at, value in enumerate(rows):
                        ref[to, lead + at, :block] = value
                    if pad:
                        ref[to, lead, block:] = extra(j)


def attn_weights_kernel(
    block, place_ref, a1_ref, dattn_ref, dqkv_ref, ctx_ref, extra_ref, *rest
):
    outs, (a1_s, dattn_s, sum_s) = rest[:-3], rest[-3:]

    @pl.when(pl.program_id(0) == 0)
    def _():
        a1_s[...] = a1_ref[...].T
        dattn_s[...] = dattn_ref[...].T

    cols3 = dqkv_ref.shape[1]
    sum_s[:, :cols3] = dg(a1_s[...], dqkv_ref[0], NT).astype(bf16)
    sum_s[:, cols3:] = dg(dattn_s[...], ctx_ref[0, 0], NT).astype(bf16)
    if len(outs) == 1:
        outs[0][0] = sum_s[...]
    else:
        split_blocks(
            place_ref[1],
            place_ref.at[pl.ds(2, 4)],
            block,
            True,
            lambda j: extra_ref[0, j],
            lambda a, b: [sum_s[a:b]],
            outs[0],
            outs[1],
            0,
        )


def attn_weights(place, a1, d_attn, d_qkv, ctx, extra, split):
    slots, cols3, length = d_qkv.shape
    cols = ctx.shape[2]
    width = a1.shape[1]
    _, blocks, pad, _ = extra.shape
    block = width // blocks
    if split:
        shape = (4, slots, block + pad, width)
        out_specs = [pl.BlockSpec((4, 1, block + pad, width), lambda k, p: (0, k, 0, 0))] * 2
        out_shape = [jax.ShapeDtypeStruct(shape, bf16)] * 2
    else:
        out_specs = [pl.BlockSpec((1, width, width), lambda k, p: (k, 0, 0))]
        out_shape = [jax.ShapeDtypeStruct((slots, width, width), bf16)]
    return pl.pallas_call(
        functools.partial(attn_weights_kernel, block),
        grid_spec=pltpu.PrefetchScalarGridSpec(
            num_scalar_prefetch=1,
            grid=(slots,),
            in_specs=[
                pl.BlockSpec((length, width), lambda k, p: (p[0], 0)),
                pl.BlockSpec((length, width), lambda k, p: (0, 0)),
                pl.BlockSpec((1, cols3, length), lambda k, p: (k, 0, 0)),
                pl.BlockSpec((1, 1, cols, length), lambda k, p: (k, p[0], 0, 0)),
                pl.BlockSpec((1, blocks, pad, width), lambda k, p: (k, 0, 0, 0)),
            ],
            out_specs=out_specs,
            scratch_shapes=[
                pltpu.VMEM((width, length), bf16),
                pltpu.VMEM((width, length), bf16),
                pltpu.VMEM((width, width), bf16),
            ],
        ),
        out_shape=out_shape,
        compiler_params=pltpu.CompilerParams(vmem_limit_bytes=VMEM),
        cost_estimate=cost(10**6, 10**6),
        name="attn_weights",
    )(place, a1, d_attn, d_qkv, ctx, extra)


def ffn_tail_kernel(
    block,
    place_ref,
    order_ref,
    a2_ref,
    mid_ref,
    part_ref,
    own_ref,
    seg_ref,
    dpool_ref,
    gain_ref,
    own_b_ref,
    own_c_ref,
    b_ref,
    c_ref,
    _out,
    out_ref,
    *rest,
):
    outs, (res_s, up_s, down_s) = rest[:-3], rest[-3:]
    r = pl.program_id(0)
    others = b_ref.shape[0]

    @pl.when(r == 0)
    def _():
        res_s[...] = own_ref[...]
        up_s[...] = jnp.zeros_like(up_s)
        down_s[...] = jnp.zeros_like(down_s)

    @pl.when(r > 0)
    def _():
        ffn_row(
            a2_ref[...],
            mid_ref[...],
            part_ref[...],
            [b_ref.at[k] for k in range(others)],
            [c_ref.at[k] for k in range(others)],
            gain_ref,
            None,
            out_ref,
            res_s,
            None,
        )

    d_res = d_result_of(res_s[...].astype(f32), seg_ref[0], dpool_ref[...], gain_ref[...])
    low = d_res.astype(bf16)
    a2 = a2_ref[...]
    hidden, slope = gelu_pair(dg(a2, own_b_ref[...], NN))
    down_s[...] += dg(low, hidden.astype(bf16), TN)
    d_pre = (dg(low, own_c_ref[...], NT) * slope).astype(bf16)
    up_s[...] += dg(a2, d_pre, TN)

    @pl.when(r == pl.num_programs(0) - 1)
    def _():
        if len(outs) == 1:
            outs[0][0] = up_s[...].astype(bf16)
            outs[0][1] = down_s[...].astype(bf16)
        else:
            split_blocks(
                place_ref[1],
                None,
                block,
                False,
                None,
                lambda a, b: [up_s[a:b].astype(bf16), down_s[a:b].astype(bf16)],
                outs[0],
                outs[1],
                0,
            )


def ffn_tail(
    place, order, a2, mid, part, res, segs, d_pool, gain, own_b, own_c, far_b, far_c, out, blocks, split
):
    rows, _, length = segs.shape
    tokens, width = a2.shape
    units = own_b.shape[1]
    others = far_b.shape[0]
    block = width // blocks
    row = pl.BlockSpec((length, width), lambda r, p, o: (o[r], 0))
    later = pl.BlockSpec((length, width), lambda r, p, o: (o[jnp.maximum(r, 1)], 0))

    def fixed(shape):
        zeros = (0,) * len(shape)
        return pl.BlockSpec(shape, lambda r, p, o: zeros, pipeline_mode=pl.Buffered(1))

    shape = (4, 2, block, units) if split else (2, width, units)
    zeros = (0,) * len(shape)
    n = 2 if split else 1
    return pl.pallas_call(
        functools.partial(ffn_tail_kernel, block),
        grid_spec=pltpu.PrefetchScalarGridSpec(
            num_scalar_prefetch=2,
            grid=(rows,),
            in_specs=[
                row,
                later,
                later,
                fixed((length, width)),
                pl.BlockSpec((1, 1, length), lambda r, p, o: (o[r], 0, 0)),
                pl.BlockSpec((SEG_ROW, width), lambda r, p, o: (o[r], 0)),
                fixed((1, width)),
                fixed((width, units)),
                fixed((units, width)),
                fixed((others, width, units)),
                fixed((others, units, width)),
                pl.BlockSpec(memory_space=pl.ANY),
            ],
            out_specs=[later] + [pl.BlockSpec(shape, lambda r, p, o: zeros)] * n,
            scratch_shapes=[
                pltpu.VMEM((length, width), bf16),
                pltpu.VMEM((width, units), f32),
                pltpu.VMEM((width, units), f32),
            ],
        ),
        out_shape=[jax.ShapeDtypeStruct((tokens, width), bf16)]
        + [jax.ShapeDtypeStruct(shape, bf16)] * n,
        input_output_aliases={13: 0},
        compiler_params=pltpu.CompilerParams(vmem_limit_bytes=VMEM),
        cost_estimate=cost(10**6, 10**6),
        name="ffn_tail",
    )(place, order, a2, mid, part, res, segs, d_pool, gain, own_b, own_c, far_b, far_c, out)


def shards(
    n_dp,
    n_tp,
    tokens,
    segment_ids,
    pair_order,
    w_query,
    w_key,
    w_value,
    w_out,
    rel_bias,
    gain_attn,
    w_hidden,
    w_down,
    gain_ffn,
    gain_final,
    w_project,
):
    rows, length = segment_ids.shape
    bucket_count, heads = rel_bias.shape
    width = tokens.shape[1]
    units = w_hidden.shape[1]
    dp = lax.axis_index("dp")
    tp = lax.axis_index("tp")
    share = math.gcd(n_dp, 8)
    split = n_dp == 8
    mates = [[(i, i ^ m) for i in range(n_dp)] for m in range(share)]
    levels = [[(i, i ^ k) for i in range(n_tp)] for k in range(n_tp)]

    def over_dp(value, m):
        return lax.ppermute(value, "dp", mates[m])

    def over_tp(value, k):
        return lax.ppermute(value, "tp", levels[k])

    slices = width // share
    low_bits = dp % share
    place = (low_bits ^ jnp.arange(share, dtype=jnp.int32)) * slices

    def from_levels(mine):
        return stack([over_tp(mine, k) for k in range(1, n_tp)], slices)

    def from_chips(far):
        return [far] + [over_dp(far, m) for m in range(2, share, 2)]

    def from_cores(pieces):
        both = [(piece, over_dp(piece, 1)) for piece in pieces]
        return [piece for pair in both for piece in pair]

    def after(values, others):
        return lax.optimization_barrier((values, others))[0]

    order = tp ^ jnp.arange(n_tp, dtype=jnp.int32)
    pack_a, mine_a = pack_weights(
        low_bits[None].astype(jnp.int32), w_query, w_key, w_value, w_out, rel_bias, share
    )
    far_a, pads = from_levels(mine_a)
    mine_bc = jnp.concatenate(
        [
            lax.dynamic_slice_in_dim(w, low_bits * slices, slices, 0)
            for w in (w_hidden, w_down)
        ]
    )
    all_bc = lax.all_gather(mine_bc, "tp", axis=0)
    tables = jnp.concatenate([rel_bias[None], unpack_table(pads, bucket_count, heads)])
    vec_own = jnp.einsum("kbh,bn->khn", tables[:1], bias_lanes(bucket_count), precision=highest)
    vecs = jnp.einsum("kbh,bn->khn", tables, bias_lanes(bucket_count), precision=highest)
    segs = segment_ids[:, None, :]
    row = tp[None].astype(jnp.int32)
    one = gain_attn[None]
    two = gain_ffn[None]
    end = gain_final[None]

    x = tokens.astype(f32)
    a1 = (x * inv_rms(x) * one).astype(bf16)
    state = attention(
        "attn_own", after(a1, far_a), vec_own, segs, place, order, 0, 0, rows, [pack_a], None
    )
    far_a = from_chips(far_a)
    far_b, far_c = others_of(after(order, (state, far_a)), all_bc, 2)
    groups = np.arange(n_dp).reshape(-1, share).tolist()
    far_c = lax.all_gather(far_c, "dp", axis=0, axis_index_groups=groups)
    far_a = from_cores(after(far_a, far_b))
    far_b = from_chips(after(far_b, far_a))
    qkv, lse, ctx, sorted_a = attention(
        "attn_far", a1, vecs[1:], segs, place, order, 1, 0, rows, far_a, state
    )
    far_b = from_cores(after(far_b, lse))
    mid, a2, part = ffn_own(tokens, ctx, sorted_a, two, w_hidden, w_down)
    layer_out, res, pooled, sorted_b, sorted_c = ffn_first(
        place, order, a2, mid, part, end, segs, far_b, far_c
    )
    block = width // n_dp
    here = rows * SEG_ROW
    pooled = pooled.astype(bf16)
    if split:
        pooled = jnp.concatenate([pooled] + [over_tp(pooled, k) for k in range(1, n_tp)])
        pooled = jnp.concatenate([pooled, over_dp(pooled, 1)])
        pooled_all = from_chips(pooled)
        spots = (dp ^ jnp.arange(n_dp))[:, None] * rows + order[None]
        at = jnp.concatenate([dp[None], spots.reshape(-1)]).astype(jnp.int32)
    else:
        pooled = lax.all_gather(pooled, "tp", axis=0, tiled=True)
        pooled_all = [lax.all_gather(pooled, "dp", axis=0, tiled=True)]
        at = dp[None].astype(jnp.int32)
    pairs = pair_order // 2
    if not split:
        everything = pooled_all[0]
        d_proj, d_pool, d_gain_end = loss_math(
            everything, w_project, pairs[:, None], pairs[None, :], end
        )
        own_cols = lax.dynamic_slice_in_dim(everything, dp * block, block, 1)
        grad_project = dg(own_cols, d_proj, TN)
        pooled_all = [lax.dynamic_slice_in_dim(d_pool, dp * here, here, 0)]
    made = row_back(
        at,
        row,
        pooled_all,
        split,
        w_project,
        pairs,
        (end, two, one),
        segs,
        lse,
        vecs,
        res,
        mid,
        a2,
        tokens,
        w_hidden,
        w_down,
        sorted_b,
        sorted_c,
        sorted_a,
        qkv,
        ctx,
        here,
        block,
    )
    d_pool, d_gain_two, d_attn, d_qkv, folded, d_tok, d_gain_one = made[0], *made[3:]
    if split:
        grad_project, d_gain_end = made[1], made[2]
    grad_gain_final = lax.dynamic_slice_in_dim(d_gain_end[0], dp * block, block, 0)
    d_tokens = lax.all_gather(d_tok, "tp", axis=0, tiled=True)

    d_rel = jnp.einsum(
        "khn,nb->kbh",
        folded.reshape(n_tp, heads, -1),
        grad_lanes(bucket_count),
        precision=highest,
    )
    gains = jnp.concatenate([d_gain_one, d_gain_two])
    pad = 16
    extra = jnp.zeros((n_tp, n_dp, pad, width), bf16)
    if split:
        small = d_rel.reshape(n_tp, 1, 1, bucket_count * heads).astype(bf16)
        gain_rows = jnp.swapaxes(gains.reshape(2, n_dp, block), 0, 1).astype(bf16)
        extra = jnp.concatenate(
            [
                jnp.broadcast_to(gain_rows[None], (n_tp, n_dp, 2, block)),
                jnp.broadcast_to(small, (n_tp, n_dp, 1, block)),
                jnp.zeros((n_tp, n_dp, pad - 3, block), bf16),
            ],
            2,
        )
        extra = jnp.pad(extra, ((0, 0), (0, 0), (0, 0), (0, width - block)))
    chips = (dp // 2) ^ jnp.arange(4, dtype=jnp.int32)
    spots = jnp.concatenate([row, (dp % 2)[None].astype(jnp.int32), chips])
    parts_a = attn_weights(spots, a1, d_attn, d_qkv, ctx, extra, split)

    def to_core(parts):
        keep, give = parts
        took = over_dp(give, 1)
        return [rounded(keep[c].astype(f32) + took[c].astype(f32)) for c in range(4)]

    def to_chip(pair):
        return [pair[0]] + [over_dp(pair[c].astype(bf16), 2 * c) for c in range(1, 4)]

    def total(parts):
        return tree([part.astype(f32) for part in parts])

    def scatter(parts):
        return lax.psum_scatter(parts[0].astype(f32), "dp", scatter_dimension=1, tiled=True)

    if split:
        pair_a = to_core(parts_a)
        got_a = to_chip(pair_a)
        first = after(order, pair_a)
    else:
        first = after(order, parts_a)
    layer_out, *parts_f = ffn_tail(
        spots, first, a2, mid, part, res, segs, d_pool, end,
        w_hidden, w_down, sorted_b, sorted_c, layer_out, n_dp, split,
    )
    if split:
        chips = [[c + core for c in range(0, n_dp, 2)] for core in range(2)]
        give_f = over_dp(after(parts_f[1], got_a), 1)
        pair_f = parts_f[0].astype(f32) + give_f.astype(f32)
        own_a = rounded(total(after(got_a, (d_tokens, pair_f))))
        swapped = lax.all_to_all(
            pair_f.astype(bf16), "dp", 0, 0, axis_index_groups=chips, tiled=True
        )
        own_f = jnp.sum(swapped.astype(f32), 0)
    else:
        own_a, own_f = rounded(scatter(parts_a)), scatter(parts_f)

    def reduce_tp(value):
        return tree([value[0]] + [over_tp(value[k], k) for k in range(1, n_tp)])

    grad_a = tree(
        [own_a[0].astype(f32)]
        + [over_tp(own_a[k].astype(bf16), k).astype(f32) for k in range(1, n_tp)]
    )
    cols = width // 4
    if split:
        gain_one, gain_two = grad_a[block, :block], grad_a[block + 1, :block]
        d_rel_here = grad_a[block + 2, : bucket_count * heads].reshape(bucket_count, heads)
    else:
        gains = tree([gains] + [over_tp(gains, k) for k in range(1, n_tp)])
        d_rel_here, gains = lax.psum((reduce_tp(d_rel), gains), "dp")
        gain_one, gain_two = lax.dynamic_slice_in_dim(gains, dp * block, block, 1)
    return (
        layer_out,
        d_tokens.astype(f32),
        grad_a[:block, :cols],
        grad_a[:block, cols : 2 * cols],
        grad_a[:block, 2 * cols : 3 * cols],
        grad_a[:block, 3 * cols :].T,
        d_rel_here,
        gain_one,
        own_f[0],
        own_f[1].T,
        gain_two,
        grad_gain_final,
        grad_project,
    )


def solution(mesh):
    placed = (
        P("dp", None),
        P("dp", None),
        P(),
        P(None, "tp"),
        P(None, "tp"),
        P(None, "tp"),
        P("tp", None),
        P(None, "tp"),
        P(),
        P(None, "tp"),
        P("tp", None),
        P(),
        P(),
        P(),
    )
    return jax.shard_map(
        functools.partial(shards, mesh.shape["dp"], mesh.shape["tp"]),
        mesh=mesh,
        in_specs=placed,
        out_specs=(
            P("dp", None),
            P("dp", None),
            P("dp", "tp"),
            P("dp", "tp"),
            P("dp", "tp"),
            P("tp", "dp"),
            P(None, "tp"),
            P("dp"),
            P("dp", "tp"),
            P("tp", "dp"),
            P("dp"),
            P("dp"),
            P("dp", None),
        ),
        check_vma=False,
    )
```

```python
import functools
import math

import jax
import jax.numpy as jnp
import numpy as np
from jax import lax
from jax.experimental import pallas as pl
from jax.experimental.pallas import tpu as pltpu
from jax.sharding import PartitionSpec as P

MAX_DIST = 128
SEG_ROW = 8
TILE = 128
LONGEST = 256
VMEM = 52 * 2**20

epsilon = 1e-06
logit_scale = 50.0
loss_scale = 128.0
masked_value = -1e30
highest = lax.Precision.HIGHEST
f32 = jnp.float32
bf16 = jnp.bfloat16

NN = (((1,), (0,)), ((), ()))
NT = (((1,), (1,)), ((), ()))
TN = (((0,), (0,)), ((), ()))


def dg(a, b, dims):
    return lax.dot_general(a, b, dims, preferred_element_type=f32)


def bucket_of(offsets, bucket_count, distance):
    half_count = bucket_count // 2
    exact_count = half_count // 2
    far_side = np.where(offsets > 0, half_count, 0)
    magnitude = np.abs(offsets)
    logged = (
        np.log(np.maximum(magnitude, exact_count) / exact_count)
        / math.log(distance / exact_count)
        * (half_count - exact_count)
    )
    far_bucket = np.minimum(exact_count + logged.astype(np.int64), half_count - 1)
    return (far_side + np.where(magnitude < exact_count, magnitude, far_bucket)).astype(np.int32)


def cost(flops, moved):
    return pl.CostEstimate(flops=int(flops), bytes_accessed=int(moved), transcendentals=0)


def bias_lanes(bucket_count):
    lanes = np.arange(4 * TILE)
    lanes = np.where(lanes >= 2 * TILE, lanes - 4 * TILE, lanes)
    return np.eye(bucket_count, dtype=np.float32)[bucket_of(-lanes, bucket_count, MAX_DIST)].T


def grad_lanes(bucket_count):
    sub = np.arange(8)[:, None]
    lane = np.arange(4 * TILE)[None, :]
    y = (lane - sub) % (4 * TILE)
    y = np.where(y >= 2 * TILE, y - 4 * TILE, y)
    near = bucket_of(-y, bucket_count, MAX_DIST)
    up = np.full((8, TILE), bucket_of(np.array(MAX_DIST), bucket_count, MAX_DIST))
    down = np.full((8, TILE), bucket_of(np.array(-MAX_DIST), bucket_count, MAX_DIST))
    ids = np.concatenate([near, up, down], 1).reshape(-1)
    return np.eye(bucket_count, dtype=np.float32)[ids]


def bring(place_ref, piece_refs, into, sems):
    slices = into.shape[1] // len(piece_refs)
    copies = []
    for k in range(into.shape[0]):
        here = []
        for m, piece in enumerate(piece_refs):
            start = pl.multiple_of(place_ref[m], 16) if slices % 16 == 0 else place_ref[m]
            to = into.at[k, pl.ds(start, slices), :]
            here.append(pltpu.make_async_copy(piece.at[k], to, sems.at[k, m]))
        copies.append(here)
    return copies


def spread_bias(vec_ref, bias_s, heads, at=0):
    for h in range(heads):
        wide = jnp.broadcast_to(vec_ref[0, h : h + 1, :], (TILE, 4 * TILE))
        bias_s[at + h] = pltpu.roll(wide, 0, 1, stride=1, stride_axis=0)


def with_bias(tile, offset, h, bias_s, vec_ref, first=0):
    if offset == 0:
        return tile + bias_s[first + h, :, 0:TILE]
    if offset == 1:
        return tile + bias_s[first + h, :, 3 * TILE : 4 * TILE]
    if offset == -1:
        return tile + bias_s[first + h, :, TILE : 2 * TILE]
    lane = 2 * TILE + 1 if offset > 1 else 2 * TILE - 1
    return tile + vec_ref[0, h : h + 1, lane : lane + 1]


def apart(i, j):
    return (abs(i - j) - 1) * TILE + 1 >= LONGEST


def masks(seg):
    hot = lax.broadcasted_iota(jnp.int32, (16, seg.shape[-1]), 0) == seg
    return (
        jnp.where(hot, 0.0, masked_value).astype(bf16),
        jnp.where(hot, 1.0, 0.0).astype(bf16),
    )


def inv_rms(values):
    return lax.rsqrt(jnp.mean(values * values, -1, keepdims=True) + epsilon)


def rounded(value):
    return lax.reduce_precision(value, 8, 7)


def tree(parts):
    while len(parts) > 1:
        parts = [parts[i] + parts[i + 1] for i in range(0, len(parts), 2)]
    return parts[0]


def exact_parts(value):
    parts = []
    for _ in range(3):
        part = value.astype(bf16)
        parts.append(part)
        value = value - part.astype(f32)
    return parts


PAD = 16


def pack_kernel(at_ref, q_ref, k_ref, v_ref, o_ref, rel_ref, out_ref, mine_ref, pack_s):
    cols = q_ref.shape[1]
    for at, ref in enumerate((q_ref, k_ref, v_ref)):
        pack_s[at * cols : (at + 1) * cols] = ref[...].astype(f32).T
    pack_s[3 * cols :] = o_ref[...].astype(f32)
    out_ref[...] = pack_s[...].astype(bf16)
    slices = mine_ref.shape[0] - PAD
    start = at_ref[0] * slices
    if slices % 8 == 0:
        start = pl.multiple_of(start, 8)
    mine_ref[:slices] = pack_s[pl.ds(start, slices), :].astype(bf16)
    mine_ref[slices:] = jnp.zeros_like(mine_ref[slices:])
    buckets, heads = rel_ref.shape
    lane = 0
    for at in range(0, buckets, PAD):
        for part in exact_parts(rel_ref[at : at + PAD]):
            mine_ref[slices:, lane : lane + heads] = part
            lane += TILE


def pack_weights(at, w_query, w_key, w_value, w_out, rel_bias, share):
    width, cols = w_query.shape
    slices = width // share
    full = lambda shape: pl.BlockSpec(shape, lambda i, at: (0, 0))
    return pl.pallas_call(
        pack_kernel,
        grid_spec=pltpu.PrefetchScalarGridSpec(
            num_scalar_prefetch=1,
            grid=(1,),
            in_specs=[full((width, cols))] * 3 + [full((cols, width)), full(rel_bias.shape)],
            out_specs=[full((width, width)), full((slices + PAD, width))],
            scratch_shapes=[pltpu.VMEM((width, width), f32)],
        ),
        out_shape=[
            jax.ShapeDtypeStruct((width, width), bf16),
            jax.ShapeDtypeStruct((slices + PAD, width), bf16),
        ],
        compiler_params=pltpu.CompilerParams(vmem_limit_bytes=VMEM),
        cost_estimate=cost(10**9, 2**20),
        name="pack_weights",
    )(at, w_query, w_key, w_value, w_out, rel_bias)


def unpack_table(pads, buckets, heads):
    rows = []
    lane = 0
    for _ in range(0, buckets, PAD):
        parts = [
            pads[:, :, lane + p * TILE : lane + p * TILE + heads].astype(f32) for p in range(3)
        ]
        rows.append(parts[0] + parts[1] + parts[2])
        lane += 3 * TILE
    return jnp.concatenate(rows, 1)


def stack_kernel(*refs):
    ins, outs = refs[:3], refs[3:]
    slices = outs[0].shape[1]
    for at, ref in enumerate(ins):
        outs[0][at] = ref[:slices]
        if len(outs) == 2:
            outs[1][at] = ref[slices:]


def stack(arrays, slices):
    rows, width = arrays[0].shape
    shapes = [(3, slices, width)] + ([(3, rows - slices, width)] if rows > slices else [])
    return pl.pallas_call(
        stack_kernel,
        out_shape=[jax.ShapeDtypeStruct(shape, bf16) for shape in shapes],
        cost_estimate=cost(0, 12 * arrays[0].size),
        name="stack",
    )(*arrays)


def others_kernel(order_ref, all_ref, *outs):
    slices = outs[0].shape[1]
    for k in range(1, all_ref.shape[0]):
        for at, out in enumerate(outs):
            out[k - 1] = all_ref[order_ref[k], at * slices : (at + 1) * slices]


def others_of(order, everything, count):
    n, total, width = everything.shape
    slices = total // count
    shape = (n - 1, slices, width)
    return pl.pallas_call(
        others_kernel,
        grid_spec=pltpu.PrefetchScalarGridSpec(
            num_scalar_prefetch=1,
            grid=(1,),
            in_specs=[pl.BlockSpec((n, total, width), lambda i, p: (0, 0, 0))],
            out_specs=[pl.BlockSpec(shape, lambda i, p: (0, 0, 0))] * count,
        ),
        out_shape=[jax.ShapeDtypeStruct(shape, bf16)] * count,
        cost_estimate=cost(0, 4 * everything.size),
        name="others_of",
    )(order, everything)


def attend_row(heads, hd, weights, a1_ref, vec_ref, seg_ref, qkv_s, lse_s, ctx_ref, bias_s, first):
    length = a1_ref.shape[0]
    blocks = length // TILE
    qkv_s[...] = dg(weights, a1_ref[...], NT).astype(bf16)
    q_mask, k_mask = masks(seg_ref[0])
    ones = jnp.ones((16, length), bf16)
    for h in range(heads):
        q_t = jnp.concatenate([qkv_s[h * hd : (h + 1) * hd], q_mask], 0)
        k_t = jnp.concatenate([qkv_s[(heads + h) * hd : (heads + h + 1) * hd], k_mask], 0)
        v_t = jnp.concatenate([qkv_s[(2 * heads + h) * hd : (2 * heads + h + 1) * hd], ones], 0)
        scores = dg(k_t.T, q_t, NN)
        columns = []
        tops = []
        for i in range(blocks):
            at = slice(i * TILE, (i + 1) * TILE)
            tiles = [
                None
                if apart(i, j)
                else with_bias(
                    scores[j * TILE : (j + 1) * TILE, at], j - i, h, bias_s, vec_ref, first
                )
                for j in range(blocks)
            ]
            live = [tile for tile in tiles if tile is not None]
            top = jnp.max(functools.reduce(jnp.maximum, live), 0, keepdims=True)
            tops.append(top)
            none = jnp.zeros((TILE, TILE), bf16)
            exps = [none if t is None else jnp.exp(t - top).astype(bf16) for t in tiles]
            columns.append(jnp.concatenate(exps, 0))
        mixed = dg(v_t, jnp.concatenate(columns, 1), NN)
        total = mixed[hd : hd + 1]
        lse_s[h : h + 1, :] = jnp.concatenate(tops, 1) + jnp.log(total)
        ctx_ref[0, 0, h * hd : (h + 1) * hd, :] = (mixed[:hd] / total).astype(bf16)


def attn_kernel(heads, hd, n, low, keeps, place_ref, order_ref, a1_ref, vec_ref, seg_ref, *rest):
    sources = rest[: max(n, 1)]
    rest = rest[max(n, 1) + (0 if low == 0 else 4 if keeps else 1) :]
    if keeps:
        qkv_ref, lse_ref, ctx_ref, sorted_ref, bias_s, qkv_s, lse_s, w_s, sems, out_sem = rest
    else:
        ctx_ref, bias_s, qkv_s, lse_s = rest
    r, s = pl.program_id(0), pl.program_id(1)
    first = s * heads

    @pl.when(r == 0)
    def _():
        spread_bias(vec_ref, bias_s, heads, first)

    if keeps:
        count = w_s.shape[0] if n else 1
        copies = bring(place_ref, sources, w_s, sems) if n else [[]]
        keep = [
            pltpu.make_async_copy(
                w_s.at[k] if n else sources[0], sorted_ref.at[low + k], out_sem.at[k]
            )
            for k in range(count)
        ]

        @pl.when((s == 0) & (r == 0))
        def _():
            for here in copies:
                for copy in here:
                    copy.start()

        for k in range(count):

            @pl.when((s == k) & (r == 0))
            def _():
                for copy in copies[k]:
                    copy.wait()
                keep[k].start()

        weights = w_s[s, : 3 * heads * hd] if n else sources[0][: 3 * heads * hd]
    else:
        weights = sources[0][s, : 3 * heads * hd]
    attend_row(
        heads, hd, weights, a1_ref, vec_ref, seg_ref, qkv_s, lse_s, ctx_ref, bias_s, first
    )
    if keeps:

        @pl.when(r == 0)
        def _():
            qkv_ref[0] = qkv_s[...]
            lse_ref[0] = lse_s[...]

        @pl.when((s == pl.num_programs(1) - 1) & (r == pl.num_programs(0) - 1))
        def _():
            for copy in keep:
                copy.wait()


def attention(name, a1, vecs, segs, place, order, low, first_row, n_rows, weights, chain):
    rows, _, length = segs.shape
    width = a1.shape[1]
    count, heads, _ = vecs.shape
    slots = order.shape[0]
    hd = width // (4 * heads)
    cols = heads * hd
    n = len(weights) if weights[0].shape[0] != slots and len(weights) > 1 else 0
    keeps = first_row == 0
    anywhere = pl.BlockSpec(memory_space=pl.ANY)
    at = lambda r, o: o[r + first_row]
    slot = lambda r, s: low + jnp.where(r == 0, s, count - 1)
    if n:
        w_specs = [anywhere] * n
    elif keeps:
        w_specs = [pl.BlockSpec((width, width), lambda r, s, p, o: (0, 0))]
    else:
        w_specs = [pl.BlockSpec((count, width, width), lambda r, s, p, o: (low // count, 0, 0))]
    out_specs = [
        pl.BlockSpec((1, 3 * cols, length), lambda r, s, p, o: (slot(r, s), 0, 0)),
        pl.BlockSpec((1, heads, length), lambda r, s, p, o: (slot(r, s), 0, 0)),
        pl.BlockSpec((1, 1, cols, length), lambda r, s, p, o: (s + low, at(r, o), 0, 0)),
        anywhere,
    ]
    out_shape = [
        jax.ShapeDtypeStruct((slots, 3 * cols, length), bf16),
        jax.ShapeDtypeStruct((slots, heads, length), f32),
        jax.ShapeDtypeStruct((slots, rows, cols, length), bf16),
        jax.ShapeDtypeStruct((slots, width, width), bf16),
    ]
    scratch = [
        pltpu.VMEM((count * heads, TILE, 4 * TILE), f32),
        pltpu.VMEM((3 * cols, length), bf16),
        pltpu.VMEM((heads, length), f32),
    ]
    if keeps:
        scratch += [
            pltpu.VMEM((count, width, width) if n else (1, 16, TILE), bf16),
            pltpu.SemaphoreType.DMA((count, max(n, 1))),
            pltpu.SemaphoreType.DMA((count,)),
        ]
        linked = [] if chain is None else list(chain)
    else:
        out_specs, out_shape, linked = out_specs[2:3], out_shape[2:3], [chain[2]]
    base = 5 + len(w_specs)
    return pl.pallas_call(
        functools.partial(attn_kernel, heads, hd, n, low, keeps),
        grid_spec=pltpu.PrefetchScalarGridSpec(
            num_scalar_prefetch=2,
            grid=(n_rows, count),
            in_specs=[
                pl.BlockSpec((length, width), lambda r, s, p, o: (at(r, o), 0)),
                pl.BlockSpec((1, heads, 4 * TILE), lambda r, s, p, o: (s, 0, 0)),
                pl.BlockSpec((1, 1, length), lambda r, s, p, o: (at(r, o), 0, 0)),
            ]
            + w_specs
            + [anywhere] * len(linked),
            out_specs=out_specs,
            scratch_shapes=scratch,
        ),
        out_shape=out_shape,
        input_output_aliases={base + i: i for i in range(len(linked))},
        compiler_params=pltpu.CompilerParams(vmem_limit_bytes=VMEM),
        cost_estimate=cost(n_rows * count * 2.5 * 10**9, 2**20),
        name=name,
    )(place, order, a1, vecs, segs, *weights, *linked)


GELU_A = math.sqrt(2.0 / math.pi)
GELU_B = 0.044715


def gelu(v):
    t = jnp.tanh(v * (GELU_A + (GELU_A * GELU_B) * (v * v)))
    half = 0.5 * v
    return half + half * t


def gelu_pair(v):
    square = v * v
    t = jnp.tanh(v * (GELU_A + (GELU_A * GELU_B) * square))
    half = 0.5 * v
    inner = GELU_A + (3.0 * GELU_A * GELU_B) * square
    return half + half * t, 0.5 + 0.5 * t + half * (1.0 - t * t) * inner


def ffn_own_kernel(x_ref, ctx_ref, wo_ref, gain_ref, b_ref, c_ref, mid_ref, a2_ref, part_ref):
    slots, _, cols, length = ctx_ref.shape
    attn = dg(
        ctx_ref[...].reshape(slots * cols, length),
        wo_ref[...].reshape(slots * cols, wo_ref.shape[-1]),
        TN,
    )
    mid = (x_ref[...].astype(f32) + attn).astype(bf16)
    mid_ref[...] = mid
    mid = mid.astype(f32)
    a2 = (mid * inv_rms(mid) * gain_ref[...]).astype(bf16)
    a2_ref[...] = a2
    hidden = gelu(dg(a2, b_ref[...], NN)).astype(bf16)
    part_ref[...] = dg(hidden, c_ref[...], NN).astype(bf16)


def ffn_own(x, ctx, sorted_a, gain, own_b, own_c):
    slots, rows, cols, length = ctx.shape
    tokens, width = x.shape
    units = own_b.shape[1]
    by_row = pl.BlockSpec((length, width), lambda r: (r, 0))
    return pl.pallas_call(
        ffn_own_kernel,
        grid=(rows,),
        in_specs=[
            by_row,
            pl.BlockSpec((slots, 1, cols, length), lambda r: (0, r, 0, 0)),
            pl.BlockSpec((slots, cols, width), lambda r: (0, 3, 0)),
            pl.BlockSpec((1, width), lambda r: (0, 0)),
            pl.BlockSpec((width, units), lambda r: (0, 0)),
            pl.BlockSpec((units, width), lambda r: (0, 0)),
        ],
        out_specs=[by_row] * 3,
        out_shape=[jax.ShapeDtypeStruct((tokens, width), bf16)] * 3,
        compiler_params=pltpu.CompilerParams(vmem_limit_bytes=VMEM),
        cost_estimate=cost(tokens * width * 6 * units, 2**24),
        name="ffn_own",
    )(x, ctx, sorted_a, gain, own_b, own_c)


def ffn_row(a2, mid, part, up, down, gain_ref, seg_ref, out_ref, res_ref, pool_ref, wait=None):
    res = mid.astype(f32) + part.astype(f32)
    for k in range(len(up)):
        if wait is not None:
            wait(k)
        hidden = gelu(dg(a2, up[k][...], NN)).astype(bf16)
        res = res + dg(hidden, down[k][...], NN)
    res_ref[...] = res.astype(bf16)
    final = (res * inv_rms(res) * gain_ref[...]).astype(bf16)
    out_ref[...] = final
    if pool_ref is not None:
        seg = seg_ref[0]
        hot = lax.broadcasted_iota(jnp.int32, (SEG_ROW, seg.shape[-1]), 0) == seg
        member = jnp.where(hot, 1.0, 0.0)
        pool_ref[...] = dg(member.astype(bf16), final, NN) / jnp.sum(member, 1, keepdims=True)


def ffn_first_kernel(
    count, place_ref, order_ref, a2_ref, mid_ref, part_ref, gain_ref, seg_ref, *rest
):
    pieces, far_c = rest[:count], rest[count]
    out_ref, res_ref, pool_ref, sb_ref, sc_ref, b_s, c_s, sems, out_sems = rest[count + 1 :]
    others = b_s.shape[0]
    slices = far_c.shape[2]
    copies = []
    for k in range(others):
        here = []
        for m in range(count):
            start = pl.multiple_of(place_ref[m], 16) if slices % 16 == 0 else place_ref[m]
            into = b_s.at[k, pl.ds(start, slices), :]
            here.append(pltpu.make_async_copy(pieces[m].at[k], into, sems.at[0, k, m]))
            into = c_s.at[k, pl.ds(m * slices, slices), :]
            here.append(pltpu.make_async_copy(far_c.at[m, k], into, sems.at[1, k, m]))
        copies.append(here)
    keep = []
    for k in range(others):
        keep.append(pltpu.make_async_copy(b_s.at[k], sb_ref.at[k], out_sems.at[0, k]))
        keep.append(pltpu.make_async_copy(c_s.at[k], sc_ref.at[k], out_sems.at[1, k]))
    for here in copies:
        for copy in here:
            copy.start()

    def wait(k):
        for copy in copies[k]:
            copy.wait()
        keep[2 * k].start()
        keep[2 * k + 1].start()

    ffn_row(
        a2_ref[...],
        mid_ref[...],
        part_ref[...],
        [b_s.at[k] for k in range(others)],
        [c_s.at[k] for k in range(others)],
        gain_ref,
        seg_ref,
        out_ref,
        res_ref,
        pool_ref,
        wait,
    )
    for copy in keep:
        copy.wait()


def ffn_first(place, order, a2, mid, part, gain, segs, pieces, far_c):
    rows, _, length = segs.shape
    tokens, width = a2.shape
    units = pieces[0].shape[-1]
    others = pieces[0].shape[0]
    n = len(pieces)
    first = pl.BlockSpec((length, width), lambda r, p, o: (o[0], 0))
    anywhere = pl.BlockSpec(memory_space=pl.ANY)
    return pl.pallas_call(
        functools.partial(ffn_first_kernel, n),
        grid_spec=pltpu.PrefetchScalarGridSpec(
            num_scalar_prefetch=2,
            grid=(1,),
            in_specs=[
                first,
                first,
                first,
                pl.BlockSpec((1, width), lambda r, p, o: (0, 0)),
                pl.BlockSpec((1, 1, length), lambda r, p, o: (o[0], 0, 0)),
            ]
            + [anywhere] * (n + 1),
            out_specs=[
                first,
                pl.BlockSpec((length, width), lambda r, p, o: (0, 0)),
                pl.BlockSpec((SEG_ROW, width), lambda r, p, o: (0, 0)),
                anywhere,
                anywhere,
            ],
            scratch_shapes=[
                pltpu.VMEM((others, width, units), bf16),
                pltpu.VMEM((others, units, width), bf16),
                pltpu.SemaphoreType.DMA((2, others, n)),
                pltpu.SemaphoreType.DMA((2, others)),
            ],
        ),
        out_shape=[
            jax.ShapeDtypeStruct((tokens, width), bf16),
            jax.ShapeDtypeStruct((length, width), bf16),
            jax.ShapeDtypeStruct((SEG_ROW, width), f32),
            jax.ShapeDtypeStruct((others, width, units), bf16),
            jax.ShapeDtypeStruct((others, units, width), bf16),
        ],
        compiler_params=pltpu.CompilerParams(vmem_limit_bytes=VMEM),
        cost_estimate=cost(length * width * 4 * units * others, 2**24),
        name="ffn_first",
    )(place, order, a2, mid, part, gain, segs, *pieces, far_c)


def loss_math(pooled, project, pair_col, pair_row, gain):
    slots = pooled.shape[0]
    projected = dg(pooled, project, NN)
    inv_norm = lax.rsqrt(jnp.sum(projected * projected, -1, keepdims=True) + epsilon)
    unit = projected * inv_norm
    embedded = unit.astype(bf16)
    similar = logit_scale * dg(embedded, embedded, NT)
    rows = lax.broadcasted_iota(jnp.int32, (slots, slots), 0)
    columns = lax.broadcasted_iota(jnp.int32, (slots, slots), 1)
    same = rows == columns
    similar = jnp.where(same, masked_value, similar)
    partner = jnp.where((pair_col == pair_row) & jnp.logical_not(same), 2.0, 0.0)

    def total(axis):
        top = jnp.max(similar, axis, keepdims=True)
        return top + jnp.log(jnp.sum(jnp.exp(similar - top), axis, keepdims=True))

    both = jnp.exp(similar - total(1)) + jnp.exp(similar - total(0)) - partner
    high = both.astype(bf16)
    low = (both - high.astype(f32)).astype(bf16)
    d_unit = (loss_scale * logit_scale) * (dg(high, embedded, NN) + dg(low, embedded, NN))
    d_proj = inv_norm * (d_unit - unit * jnp.sum(d_unit * unit, -1, keepdims=True))
    d_proj = d_proj.astype(bf16)
    d_pooled = dg(d_proj, project, NT)
    d_gain = jnp.sum(d_pooled * pooled.astype(f32), 0, keepdims=True) / gain
    return d_proj, d_pooled, d_gain


def d_result_of(res, seg, d_pool, gain):
    hot = lax.broadcasted_iota(jnp.int32, (SEG_ROW, seg.shape[-1]), 0) == seg
    member = jnp.where(hot, 1.0, 0.0)
    per_token = d_pool / jnp.sum(member, 1, keepdims=True)
    high = per_token.astype(bf16)
    low = (per_token - high.astype(f32)).astype(bf16)
    twice = jnp.concatenate([member, member], 0).astype(bf16)
    d_final = dg(twice, jnp.concatenate([high, low], 0), TN)
    scale = inv_rms(res)
    unit = res * scale
    weighted = d_final * gain
    return scale * (weighted - unit * jnp.mean(weighted * unit, -1, keepdims=True))


def fold(tile):
    lanes = tile.shape[1]
    total = tile[0:8]
    for b in range(1, TILE // 8):
        total = total + pltpu.roll(tile[8 * b : 8 * b + 8], lanes - 8 * b, 1)
    return total


def loss_step(pieces, at_ref, project_ref, pc_ref, pr_ref, gain_ref, dpool_ref, dproj_ref, dgain_ref, a_s, b_s):
    each = SEG_ROW
    parts = pieces[0].shape[0] // each
    for m, piece in enumerate(pieces):
        value = piece[...].astype(f32)
        for part in range(parts):
            start = pl.multiple_of(at_ref[1 + m * parts + part] * each, each)
            a_s[pl.ds(start, each), :] = value[part * each : (part + 1) * each]
    pooled = a_s[...].astype(bf16)
    d_proj, d_pooled, d_gain = loss_math(
        pooled, project_ref[...], pc_ref[...], pr_ref[...], gain_ref[...]
    )
    a_s[...] = d_pooled
    b_s[...] = dg(pooled, d_proj, TN)
    here = dpool_ref.shape[0]
    block = dproj_ref.shape[0]
    dpool_ref[...] = a_s[pl.ds(pl.multiple_of(at_ref[0] * here, here), here), :]
    dproj_ref[...] = b_s[pl.ds(pl.multiple_of(at_ref[0] * block, block), block), :]
    dgain_ref[...] = d_gain


def norm_back(grad, values, gain):
    scale = inv_rms(values)
    unit = values * scale
    weighted = grad * gain
    d_values = scale * (weighted - unit * jnp.mean(weighted * unit, -1, keepdims=True))
    return d_values, jnp.sum(grad * unit, 0, keepdims=True)


def row_back_kernel(count, with_loss, heads, hd, at_ref, row_ref, *refs):
    pieces, refs = refs[:count], refs[count:]
    project_ref, pc_ref, pr_ref, gain_end_ref, gain_two_ref, gain_one_ref, seg_ref = refs[:7]
    lse_ref, vec_ref, res_any, mid_any, a2_any, x_any, own_b, own_c, far_b, far_c = refs[7:17]
    far_a, qkv_any, ctx_any = refs[17:20]
    dpool_ref, dproj_ref, dend_ref, dtwo_ref, dattn_ref = refs[20:25]
    dqkv_ref, fold_ref, dtok_ref, done_ref = refs[25:29]
    a_s, p_s, b_s, c_s, wo_s, wa_s, res_s, mid_s, a2_s, x_s, qkv_s, ctx_s = refs[29:41]
    dres_s, low_s, sum_s, dctx_s, bias_s, b_sems, c_sems, sems = refs[41:]
    step = pl.program_id(0)
    slots = b_s.shape[0]
    length = res_s.shape[0]
    cols = heads * hd
    row = row_ref[0]
    mine = pl.ds(pl.multiple_of(row * length, length), length)
    res_copy = pltpu.make_async_copy(res_any, res_s, sems.at[0])
    a2_copy = pltpu.make_async_copy(a2_any.at[mine], a2_s, sems.at[1])
    mid_copy = pltpu.make_async_copy(mid_any.at[mine], mid_s, sems.at[2])
    wo_copy = pltpu.make_async_copy(far_a.at[:, pl.ds(3 * cols, cols)], wo_s, sems.at[3])
    qkv_copy = pltpu.make_async_copy(qkv_any, qkv_s, sems.at[4])
    ctx_copy = pltpu.make_async_copy(ctx_any.at[:, row], ctx_s, sems.at[5])
    wa_copy = pltpu.make_async_copy(far_a.at[:, pl.ds(0, 3 * cols)], wa_s, sems.at[6])
    x_copy = pltpu.make_async_copy(x_any.at[mine], x_s, sems.at[7])

    def weight_copies(k):
        b_from, c_from = (own_b, own_c) if k == 0 else (far_b.at[k - 1], far_c.at[k - 1])
        return [
            pltpu.make_async_copy(b_from, b_s.at[k], b_sems.at[k]),
            pltpu.make_async_copy(c_from, c_s.at[k], c_sems.at[k]),
        ]

    @pl.when(step == 0)
    def _():
        res_copy.start()
        a2_copy.start()
        for k in range(slots):
            for copy in weight_copies(k):
                copy.start()
        for copy in (mid_copy, wo_copy, qkv_copy, ctx_copy, wa_copy, x_copy):
            copy.start()
        if with_loss:
            loss_step(
                pieces,
                at_ref,
                project_ref,
                pc_ref,
                pr_ref,
                gain_end_ref,
                dpool_ref,
                dproj_ref,
                dend_ref,
                a_s,
                p_s,
            )
        else:
            dpool_ref[...] = pieces[0][...]
            dproj_ref[...] = jnp.zeros_like(dproj_ref)
            dend_ref[...] = jnp.zeros_like(dend_ref)
        res_copy.wait()
        a2_copy.wait()
        d_pool = dpool_ref[pl.ds(pl.multiple_of(row * SEG_ROW, SEG_ROW), SEG_ROW), :]
        d_res = d_result_of(res_s[...].astype(f32), seg_ref[0], d_pool, gain_end_ref[...])
        dres_s[...] = d_res
        low_s[...] = d_res.astype(bf16)
        sum_s[...] = jnp.zeros_like(sum_s)

    for k in range(slots):

        @pl.when(step == k + 1)
        def _():
            for copy in weight_copies(k):
                copy.wait()

    @pl.when((step >= 1) & (step <= slots))
    def _():
        up, down = b_s.at[step - 1], c_s.at[step - 1]
        slope = gelu_pair(dg(a2_s[...], up[...], NN))[1]
        d_pre = (dg(low_s[...], down[...], NT) * slope).astype(bf16)
        sum_s[...] += dg(d_pre, up[...], NT)

    @pl.when(step == slots)
    def _():
        mid_copy.wait()
        wo_copy.wait()
        d_mid, dtwo_ref[...] = norm_back(
            sum_s[...], mid_s[...].astype(f32), gain_two_ref[...]
        )
        d_mid = dres_s[...] + d_mid
        dres_s[...] = d_mid
        low = d_mid.astype(bf16)
        dattn_ref[...] = low
        sum_s[...] = jnp.zeros_like(sum_s)
        for k in range(slots):
            dctx_s[k] = dg(wo_s[k], low, NT).astype(bf16)
        qkv_copy.wait()
        ctx_copy.wait()
        wa_copy.wait()
        x_copy.wait()

    @pl.when(step > slots)
    def _():
        slot = step - slots - 1
        blocks = length // TILE
        spread_bias(vec_ref.at[pl.ds(slot, 1)], bias_s, heads)
        q_mask, k_mask = masks(seg_ref[0])
        for h in range(heads):
            q_low = qkv_s[slot, h * hd : (h + 1) * hd]
            k_low = qkv_s[slot, (heads + h) * hd : (heads + h + 1) * hd]
            v_low = qkv_s[slot, (2 * heads + h) * hd : (2 * heads + h + 1) * hd]
            dc = dctx_s[slot, h * hd : (h + 1) * hd]
            c = ctx_s[slot, h * hd : (h + 1) * hd]
            delta = jnp.sum(dc.astype(f32) * c.astype(f32), 0, keepdims=True)
            lse = lse_ref[slot, h : h + 1]
            scores = dg(
                jnp.concatenate([k_low, k_mask], 0).T, jnp.concatenate([q_low, q_mask], 0), NN
            )
            d_probs = dg(v_low.T, dc, NN)
            probs_cols = []
            score_cols = []
            near = [None, None, None]
            far = [None, None]
            for i in range(blocks):
                at = slice(i * TILE, (i + 1) * TILE)
                probs = []
                grads = []
                for j in range(blocks):
                    if apart(i, j):
                        probs.append(jnp.zeros((TILE, TILE), bf16))
                        grads.append(jnp.zeros((TILE, TILE), bf16))
                        continue
                    to = slice(j * TILE, (j + 1) * TILE)
                    tile = with_bias(scores[to, at], j - i, h, bias_s, vec_ref.at[pl.ds(slot, 1)])
                    prob = jnp.exp(tile - lse[:, at])
                    grad = prob * (d_probs[to, at] - delta[:, at])
                    probs.append(prob.astype(bf16))
                    grads.append(grad.astype(bf16))
                    if abs(j - i) <= 1:
                        old = near[j - i + 1]
                        near[j - i + 1] = grad if old is None else old + grad
                    else:
                        old = far[int(j < i)]
                        far[int(j < i)] = grad if old is None else old + grad
                probs_cols.append(jnp.concatenate(probs, 0))
                score_cols.append(jnp.concatenate(grads, 0))
            probs = jnp.concatenate(probs_cols, 1)
            grads = jnp.concatenate(score_cols, 1)
            dqkv_ref[0, h * hd : (h + 1) * hd] = dg(k_low, grads, NN).astype(bf16)
            dqkv_ref[0, (heads + h) * hd : (heads + h + 1) * hd] = dg(q_low, grads, NT).astype(bf16)
            dqkv_ref[0, (2 * heads + h) * hd : (2 * heads + h + 1) * hd] = dg(dc, probs, NT).astype(
                bf16
            )
            band = jnp.concatenate([near[1], near[0], jnp.zeros_like(near[0]), near[2]], 1)
            fold_ref[0, h, :, : 4 * TILE] = fold(band)
            for side in range(2):
                total = far[side][0:8]
                for b in range(1, TILE // 8):
                    total = total + far[side][8 * b : 8 * b + 8]
                fold_ref[0, h, :, (4 + side) * TILE : (5 + side) * TILE] = total
        sum_s[...] += dg(dqkv_ref[0], wa_s[slot], TN)

    @pl.when(step == 2 * slots)
    def _():
        d_x, done_ref[...] = norm_back(sum_s[...], x_s[...].astype(f32), gain_one_ref[...])
        dtok_ref[...] = (dres_s[...] + d_x).astype(bf16)


def row_back(
    at,
    row,
    pieces,
    with_loss,
    project,
    pairs,
    gains,
    segs,
    lse,
    vecs,
    res,
    mid,
    a2,
    x,
    own_b,
    own_c,
    far_b,
    far_c,
    sorted_a,
    qkv,
    ctx,
    here,
    block,
):
    slots, heads, _ = vecs.shape
    length, width = res.shape
    units = own_b.shape[1]
    cols = width // 4
    n_all = pairs.shape[0]
    anywhere = pl.BlockSpec(memory_space=pl.ANY)

    def full(shape):
        zeros = (0,) * len(shape)
        return pl.BlockSpec(shape, lambda i, at, row: zeros)

    def slot(i):
        return jnp.maximum(i - slots - 1, 0)

    row_shape = (length, width)
    return pl.pallas_call(
        functools.partial(row_back_kernel, len(pieces), with_loss, heads, cols // heads),
        grid_spec=pltpu.PrefetchScalarGridSpec(
            num_scalar_prefetch=2,
            grid=(2 * slots + 1,),
            in_specs=[full(piece.shape) for piece in pieces]
            + [full(project.shape), full((n_all, 1)), full((1, n_all))]
            + [full((1, width))] * 3
            + [
                pl.BlockSpec((1, 1, length), lambda i, at, row: (row[0], 0, 0)),
                full(lse.shape),
                full(vecs.shape),
            ]
            + [anywhere] * 11,
            out_specs=[
                full((here, width)),
                full((block, width)),
                full((1, width)),
                full((1, width)),
                full(row_shape),
                pl.BlockSpec((1, 3 * cols, length), lambda i, at, row: (slot(i), 0, 0)),
                pl.BlockSpec((1, heads, 8, 6 * TILE), lambda i, at, row: (slot(i), 0, 0, 0)),
                full(row_shape),
                full((1, width)),
            ],
            scratch_shapes=[
                pltpu.VMEM((n_all if with_loss else 8, width), f32),
                pltpu.VMEM((width, width), f32),
                pltpu.VMEM((slots, width, units), bf16),
                pltpu.VMEM((slots, units, width), bf16),
                pltpu.VMEM((slots, cols, width), bf16),
                pltpu.VMEM((slots, 3 * cols, width), bf16),
                pltpu.VMEM(row_shape, bf16),
                pltpu.VMEM(row_shape, bf16),
                pltpu.VMEM(row_shape, bf16),
                pltpu.VMEM(row_shape, bf16),
                pltpu.VMEM((slots, 3 * cols, length), bf16),
                pltpu.VMEM((slots, cols, length), bf16),
                pltpu.VMEM(row_shape, f32),
                pltpu.VMEM(row_shape, bf16),
                pltpu.VMEM(row_shape, f32),
                pltpu.VMEM((slots, cols, length), bf16),
                pltpu.VMEM((heads, TILE, 4 * TILE), f32),
                pltpu.SemaphoreType.DMA((slots,)),
                pltpu.SemaphoreType.DMA((slots,)),
                pltpu.SemaphoreType.DMA((8,)),
            ],
        ),
        out_shape=[
            jax.ShapeDtypeStruct((here, width), f32),
            jax.ShapeDtypeStruct((block, width), f32),
            jax.ShapeDtypeStruct((1, width), f32),
            jax.ShapeDtypeStruct((1, width), f32),
            jax.ShapeDtypeStruct(row_shape, bf16),
            jax.ShapeDtypeStruct((slots, 3 * cols, length), bf16),
            jax.ShapeDtypeStruct((slots, heads, 8, 6 * TILE), f32),
            jax.ShapeDtypeStruct(row_shape, bf16),
            jax.ShapeDtypeStruct((1, width), f32),
        ],
        compiler_params=pltpu.CompilerParams(vmem_limit_bytes=VMEM),
        cost_estimate=cost(3 * 10**10, 2**24),
        name="row_back",
    )(
        at,
        row,
        *pieces,
        project,
        pairs[:, None],
        pairs[None, :],
        *gains,
        segs,
        lse,
        vecs,
        res,
        mid,
        a2,
        x,
        own_b,
        own_c,
        far_b,
        far_c,
        sorted_a,
        qkv,
        ctx,
    )


def split_blocks(core, rel_ref, block, pad, extra, values, keep_ref, give_ref, lead):
    for c in range(2):

        @pl.when(core == c)
        def _():
            for chip in range(4):
                for ref, j in ((keep_ref, 2 * chip + c), (give_ref, 2 * chip + 1 - c)):
                    rows = values(j * block, (j + 1) * block)
                    to = chip if rel_ref is None else rel_ref[chip]
                    for at, value in enumerate(rows):
                        ref[to, lead + at, :block] = value
                    if pad:
                        ref[to, lead, block:] = extra(j)


def attn_weights_kernel(
    block, place_ref, a1_ref, dattn_ref, dqkv_ref, ctx_ref, extra_ref, *rest
):
    outs, (a1_s, dattn_s, sum_s) = rest[:-3], rest[-3:]

    @pl.when(pl.program_id(0) == 0)
    def _():
        a1_s[...] = a1_ref[...].T
        dattn_s[...] = dattn_ref[...].T

    cols3 = dqkv_ref.shape[1]
    sum_s[:, :cols3] = dg(a1_s[...], dqkv_ref[0], NT).astype(bf16)
    sum_s[:, cols3:] = dg(dattn_s[...], ctx_ref[0, 0], NT).astype(bf16)
    if len(outs) == 1:
        outs[0][0] = sum_s[...]
    else:
        split_blocks(
            place_ref[1],
            place_ref.at[pl.ds(2, 4)],
            block,
            True,
            lambda j: extra_ref[0, j],
            lambda a, b: [sum_s[a:b]],
            outs[0],
            outs[1],
            0,
        )


def attn_weights(place, a1, d_attn, d_qkv, ctx, extra, split):
    slots, cols3, length = d_qkv.shape
    cols = ctx.shape[2]
    width = a1.shape[1]
    _, blocks, pad, _ = extra.shape
    block = width // blocks
    if split:
        shape = (4, slots, block + pad, width)
        out_specs = [pl.BlockSpec((4, 1, block + pad, width), lambda k, p: (0, k, 0, 0))] * 2
        out_shape = [jax.ShapeDtypeStruct(shape, bf16)] * 2
    else:
        out_specs = [pl.BlockSpec((1, width, width), lambda k, p: (k, 0, 0))]
        out_shape = [jax.ShapeDtypeStruct((slots, width, width), bf16)]
    return pl.pallas_call(
        functools.partial(attn_weights_kernel, block),
        grid_spec=pltpu.PrefetchScalarGridSpec(
            num_scalar_prefetch=1,
            grid=(slots,),
            in_specs=[
                pl.BlockSpec((length, width), lambda k, p: (p[0], 0)),
                pl.BlockSpec((length, width), lambda k, p: (0, 0)),
                pl.BlockSpec((1, cols3, length), lambda k, p: (k, 0, 0)),
                pl.BlockSpec((1, 1, cols, length), lambda k, p: (k, p[0], 0, 0)),
                pl.BlockSpec((1, blocks, pad, width), lambda k, p: (k, 0, 0, 0)),
            ],
            out_specs=out_specs,
            scratch_shapes=[
                pltpu.VMEM((width, length), bf16),
                pltpu.VMEM((width, length), bf16),
                pltpu.VMEM((width, width), bf16),
            ],
        ),
        out_shape=out_shape,
        compiler_params=pltpu.CompilerParams(vmem_limit_bytes=VMEM),
        cost_estimate=cost(10**6, 10**6),
        name="attn_weights",
    )(place, a1, d_attn, d_qkv, ctx, extra)


def ffn_tail_kernel(
    block,
    place_ref,
    order_ref,
    a2_ref,
    mid_ref,
    part_ref,
    own_ref,
    seg_ref,
    dpool_ref,
    gain_ref,
    own_b_ref,
    own_c_ref,
    b_any,
    c_any,
    _out,
    out_ref,
    *rest,
):
    outs, (b_ref, c_ref, sems, res_s, up_s, down_s) = rest[:-6], rest[-6:]
    r = pl.program_id(0)
    others = b_ref.shape[0]
    copies = [
        pltpu.make_async_copy(b_any, b_ref, sems.at[0]),
        pltpu.make_async_copy(c_any, c_ref, sems.at[1]),
    ]

    @pl.when(r == 1)
    def _():
        for copy in copies:
            copy.wait()

    @pl.when(r == 0)
    def _():
        for copy in copies:
            copy.start()
        res_s[...] = own_ref[...]
        up_s[...] = jnp.zeros_like(up_s)
        down_s[...] = jnp.zeros_like(down_s)

    @pl.when(r > 0)
    def _():
        ffn_row(
            a2_ref[...],
            mid_ref[...],
            part_ref[...],
            [b_ref.at[k] for k in range(others)],
            [c_ref.at[k] for k in range(others)],
            gain_ref,
            None,
            out_ref,
            res_s,
            None,
        )

    d_res = d_result_of(res_s[...].astype(f32), seg_ref[0], dpool_ref[...], gain_ref[...])
    low = d_res.astype(bf16)
    a2 = a2_ref[...]
    hidden, slope = gelu_pair(dg(a2, own_b_ref[...], NN))
    down_s[...] += dg(low, hidden.astype(bf16), TN)
    d_pre = (dg(low, own_c_ref[...], NT) * slope).astype(bf16)
    up_s[...] += dg(a2, d_pre, TN)

    @pl.when(r == pl.num_programs(0) - 1)
    def _():
        if len(outs) == 1:
            outs[0][0] = up_s[...].astype(bf16)
            outs[0][1] = down_s[...].astype(bf16)
        else:
            split_blocks(
                place_ref[1],
                None,
                block,
                False,
                None,
                lambda a, b: [up_s[a:b].astype(bf16), down_s[a:b].astype(bf16)],
                outs[0],
                outs[1],
                0,
            )


def ffn_tail(
    place, order, a2, mid, part, res, segs, d_pool, gain, own_b, own_c, far_b, far_c, out, blocks, split
):
    rows, _, length = segs.shape
    tokens, width = a2.shape
    units = own_b.shape[1]
    others = far_b.shape[0]
    block = width // blocks
    row = pl.BlockSpec((length, width), lambda r, p, o: (o[r], 0))
    later = pl.BlockSpec((length, width), lambda r, p, o: (o[jnp.maximum(r, 1)], 0))

    def fixed(shape):
        zeros = (0,) * len(shape)
        return pl.BlockSpec(shape, lambda r, p, o: zeros, pipeline_mode=pl.Buffered(1))

    shape = (4, 2, block, units) if split else (2, width, units)
    zeros = (0,) * len(shape)
    n = 2 if split else 1
    return pl.pallas_call(
        functools.partial(ffn_tail_kernel, block),
        grid_spec=pltpu.PrefetchScalarGridSpec(
            num_scalar_prefetch=2,
            grid=(rows,),
            in_specs=[
                row,
                later,
                later,
                fixed((length, width)),
                pl.BlockSpec((1, 1, length), lambda r, p, o: (o[r], 0, 0)),
                pl.BlockSpec((SEG_ROW, width), lambda r, p, o: (o[r], 0)),
                fixed((1, width)),
                fixed((width, units)),
                fixed((units, width)),
            ]
            + [pl.BlockSpec(memory_space=pl.ANY)] * 3,
            out_specs=[later] + [pl.BlockSpec(shape, lambda r, p, o: zeros)] * n,
            scratch_shapes=[
                pltpu.VMEM((others, width, units), bf16),
                pltpu.VMEM((others, units, width), bf16),
                pltpu.SemaphoreType.DMA((2,)),
                pltpu.VMEM((length, width), bf16),
                pltpu.VMEM((width, units), f32),
                pltpu.VMEM((width, units), f32),
            ],
        ),
        out_shape=[jax.ShapeDtypeStruct((tokens, width), bf16)]
        + [jax.ShapeDtypeStruct(shape, bf16)] * n,
        input_output_aliases={13: 0},
        compiler_params=pltpu.CompilerParams(vmem_limit_bytes=VMEM),
        cost_estimate=cost(10**6, 10**6),
        name="ffn_tail",
    )(place, order, a2, mid, part, res, segs, d_pool, gain, own_b, own_c, far_b, far_c, out)


def shards(
    n_dp,
    n_tp,
    tokens,
    segment_ids,
    pair_order,
    w_query,
    w_key,
    w_value,
    w_out,
    rel_bias,
    gain_attn,
    w_hidden,
    w_down,
    gain_ffn,
    gain_final,
    w_project,
):
    rows, length = segment_ids.shape
    bucket_count, heads = rel_bias.shape
    width = tokens.shape[1]
    units = w_hidden.shape[1]
    dp = lax.axis_index("dp")
    tp = lax.axis_index("tp")
    share = math.gcd(n_dp, 8)
    split = n_dp == 8
    mates = [[(i, i ^ m) for i in range(n_dp)] for m in range(share)]
    levels = [[(i, i ^ k) for i in range(n_tp)] for k in range(n_tp)]

    def over_dp(value, m):
        return lax.ppermute(value, "dp", mates[m])

    def over_tp(value, k):
        return lax.ppermute(value, "tp", levels[k])

    slices = width // share
    low_bits = dp % share
    place = (low_bits ^ jnp.arange(share, dtype=jnp.int32)) * slices

    def from_levels(mine):
        return stack([over_tp(mine, k) for k in range(1, n_tp)], slices)

    def from_chips(far):
        return [far] + [over_dp(far, m) for m in range(2, share, 2)]

    def from_cores(pieces):
        both = [(piece, over_dp(piece, 1)) for piece in pieces]
        return [piece for pair in both for piece in pair]

    def after(values, others):
        return lax.optimization_barrier((values, others))[0]

    order = tp ^ jnp.arange(n_tp, dtype=jnp.int32)
    pack_a, mine_a = pack_weights(
        low_bits[None].astype(jnp.int32), w_query, w_key, w_value, w_out, rel_bias, share
    )
    far_a, pads = from_levels(mine_a)
    mine_bc = jnp.concatenate(
        [
            lax.dynamic_slice_in_dim(w, low_bits * slices, slices, 0)
            for w in (w_hidden, w_down)
        ]
    )
    all_bc = lax.all_gather(mine_bc, "tp", axis=0)
    tables = jnp.concatenate([rel_bias[None], unpack_table(pads, bucket_count, heads)])
    vec_own = jnp.einsum("kbh,bn->khn", tables[:1], bias_lanes(bucket_count), precision=highest)
    vecs = jnp.einsum("kbh,bn->khn", tables, bias_lanes(bucket_count), precision=highest)
    segs = segment_ids[:, None, :]
    row = tp[None].astype(jnp.int32)
    one = gain_attn[None]
    two = gain_ffn[None]
    end = gain_final[None]

    x = tokens.astype(f32)
    a1 = (x * inv_rms(x) * one).astype(bf16)
    state = attention(
        "attn_own", after(a1, far_a), vec_own, segs, place, order, 0, 0, rows, [pack_a], None
    )
    far_a = from_chips(far_a)
    far_b, far_c = others_of(after(order, (state, far_a)), all_bc, 2)
    groups = np.arange(n_dp).reshape(-1, share).tolist()
    far_c = lax.all_gather(far_c, "dp", axis=0, axis_index_groups=groups)
    far_a = from_cores(after(far_a, far_b))
    far_b = from_chips(after(far_b, far_a))
    qkv, lse, ctx, sorted_a = attention(
        "attn_far", a1, vecs[1:], segs, place, order, 1, 0, rows, far_a, state
    )
    far_b = from_cores(after(far_b, lse))
    mid, a2, part = ffn_own(tokens, ctx, sorted_a, two, w_hidden, w_down)
    layer_out, res, pooled, sorted_b, sorted_c = ffn_first(
        place, order, a2, mid, part, end, segs, far_b, far_c
    )
    block = width // n_dp
    here = rows * SEG_ROW
    pooled = pooled.astype(bf16)
    if split:
        pooled = jnp.concatenate([pooled] + [over_tp(pooled, k) for k in range(1, n_tp)])
        pooled = jnp.concatenate([pooled, over_dp(pooled, 1)])
        pooled_all = from_chips(pooled)
        spots = (dp ^ jnp.arange(n_dp))[:, None] * rows + order[None]
        at = jnp.concatenate([dp[None], spots.reshape(-1)]).astype(jnp.int32)
    else:
        pooled = lax.all_gather(pooled, "tp", axis=0, tiled=True)
        pooled_all = [lax.all_gather(pooled, "dp", axis=0, tiled=True)]
        at = dp[None].astype(jnp.int32)
    pairs = pair_order // 2
    if not split:
        everything = pooled_all[0]
        d_proj, d_pool, d_gain_end = loss_math(
            everything, w_project, pairs[:, None], pairs[None, :], end
        )
        own_cols = lax.dynamic_slice_in_dim(everything, dp * block, block, 1)
        grad_project = dg(own_cols, d_proj, TN)
        pooled_all = [lax.dynamic_slice_in_dim(d_pool, dp * here, here, 0)]
    made = row_back(
        at,
        row,
        pooled_all,
        split,
        w_project,
        pairs,
        (end, two, one),
        segs,
        lse,
        vecs,
        res,
        mid,
        a2,
        tokens,
        w_hidden,
        w_down,
        sorted_b,
        sorted_c,
        sorted_a,
        qkv,
        ctx,
        here,
        block,
    )
    d_pool, d_gain_two, d_attn, d_qkv, folded, d_tok, d_gain_one = made[0], *made[3:]
    if split:
        grad_project, d_gain_end = made[1], made[2]
    grad_gain_final = lax.dynamic_slice_in_dim(d_gain_end[0], dp * block, block, 0)
    d_tokens = lax.all_gather(d_tok, "tp", axis=0, tiled=True)

    d_rel = jnp.einsum(
        "khn,nb->kbh",
        folded.reshape(n_tp, heads, -1),
        grad_lanes(bucket_count),
        precision=highest,
    )
    gains = jnp.concatenate([d_gain_one, d_gain_two])
    pad = 16
    extra = jnp.zeros((n_tp, n_dp, pad, width), bf16)
    if split:
        small = d_rel.reshape(n_tp, 1, 1, bucket_count * heads).astype(bf16)
        gain_rows = jnp.swapaxes(gains.reshape(2, n_dp, block), 0, 1).astype(bf16)
        extra = jnp.concatenate(
            [
                jnp.broadcast_to(gain_rows[None], (n_tp, n_dp, 2, block)),
                jnp.broadcast_to(small, (n_tp, n_dp, 1, block)),
                jnp.zeros((n_tp, n_dp, pad - 3, block), bf16),
            ],
            2,
        )
        extra = jnp.pad(extra, ((0, 0), (0, 0), (0, 0), (0, width - block)))
    chips = (dp // 2) ^ jnp.arange(4, dtype=jnp.int32)
    spots = jnp.concatenate([row, (dp % 2)[None].astype(jnp.int32), chips])
    parts_a = attn_weights(spots, a1, d_attn, d_qkv, ctx, extra, split)

    def to_core(parts):
        keep, give = parts
        took = over_dp(give, 1)
        return [rounded(keep[c].astype(f32) + took[c].astype(f32)) for c in range(4)]

    def to_chip(pair):
        return [pair[0]] + [over_dp(pair[c].astype(bf16), 2 * c) for c in range(1, 4)]

    def total(parts):
        return tree([part.astype(f32) for part in parts])

    def scatter(parts):
        return lax.psum_scatter(parts[0].astype(f32), "dp", scatter_dimension=1, tiled=True)

    if split:
        pair_a = to_core(parts_a)
        got_a = to_chip(pair_a)
        first = after(order, pair_a)
    else:
        first = after(order, parts_a)
    layer_out, *parts_f = ffn_tail(
        spots, first, a2, mid, part, res, segs, d_pool, end,
        w_hidden, w_down, sorted_b, sorted_c, layer_out, n_dp, split,
    )
    if split:
        chips = [[c + core for c in range(0, n_dp, 2)] for core in range(2)]
        give_f = over_dp(after(parts_f[1], got_a), 1)
        pair_f = parts_f[0].astype(f32) + give_f.astype(f32)
        own_a = rounded(total(after(got_a, (d_tokens, pair_f))))
        swapped = lax.all_to_all(
            pair_f.astype(bf16), "dp", 0, 0, axis_index_groups=chips, tiled=True
        )
        own_f = jnp.sum(swapped.astype(f32), 0)
    else:
        own_a, own_f = rounded(scatter(parts_a)), scatter(parts_f)

    def reduce_tp(value):
        return tree([value[0]] + [over_tp(value[k], k) for k in range(1, n_tp)])

    grad_a = tree(
        [own_a[0].astype(f32)]
        + [over_tp(own_a[k].astype(bf16), k).astype(f32) for k in range(1, n_tp)]
    )
    cols = width // 4
    if split:
        gain_one, gain_two = grad_a[block, :block], grad_a[block + 1, :block]
        d_rel_here = grad_a[block + 2, : bucket_count * heads].reshape(bucket_count, heads)
    else:
        gains = tree([gains] + [over_tp(gains, k) for k in range(1, n_tp)])
        d_rel_here, gains = lax.psum((reduce_tp(d_rel), gains), "dp")
        gain_one, gain_two = lax.dynamic_slice_in_dim(gains, dp * block, block, 1)
    return (
        layer_out,
        d_tokens.astype(f32),
        grad_a[:block, :cols],
        grad_a[:block, cols : 2 * cols],
        grad_a[:block, 2 * cols : 3 * cols],
        grad_a[:block, 3 * cols :].T,
        d_rel_here,
        gain_one,
        own_f[0],
        own_f[1].T,
        gain_two,
        grad_gain_final,
        grad_project,
    )


def solution(mesh):
    placed = (
        P("dp", None),
        P("dp", None),
        P(),
        P(None, "tp"),
        P(None, "tp"),
        P(None, "tp"),
        P("tp", None),
        P(None, "tp"),
        P(),
        P(None, "tp"),
        P("tp", None),
        P(),
        P(),
        P(),
    )
    return jax.shard_map(
        functools.partial(shards, mesh.shape["dp"], mesh.shape["tp"]),
        mesh=mesh,
        in_specs=placed,
        out_specs=(
            P("dp", None),
            P("dp", None),
            P("dp", "tp"),
            P("dp", "tp"),
            P("dp", "tp"),
            P("tp", "dp"),
            P(None, "tp"),
            P("dp"),
            P("dp", "tp"),
            P("tp", "dp"),
            P("dp"),
            P("dp"),
            P("dp", None),
        ),
        check_vma=False,
    )
```

```python
import functools
import math

import jax
import jax.numpy as jnp
import numpy as np
from jax import lax
from jax.experimental import pallas as pl
from jax.experimental.pallas import tpu as pltpu
from jax.sharding import PartitionSpec as P

MAX_DIST = 128
SEG_ROW = 8
TILE = 128
LONGEST = 256
VMEM = 52 * 2**20

epsilon = 1e-06
logit_scale = 50.0
loss_scale = 128.0
masked_value = -1e30
highest = lax.Precision.HIGHEST
f32 = jnp.float32
bf16 = jnp.bfloat16

NN = (((1,), (0,)), ((), ()))
NT = (((1,), (1,)), ((), ()))
TN = (((0,), (0,)), ((), ()))


def dg(a, b, dims):
    return lax.dot_general(a, b, dims, preferred_element_type=f32)


def bucket_of(offsets, bucket_count, distance):
    half_count = bucket_count // 2
    exact_count = half_count // 2
    far_side = np.where(offsets > 0, half_count, 0)
    magnitude = np.abs(offsets)
    logged = (
        np.log(np.maximum(magnitude, exact_count) / exact_count)
        / math.log(distance / exact_count)
        * (half_count - exact_count)
    )
    far_bucket = np.minimum(exact_count + logged.astype(np.int64), half_count - 1)
    return (far_side + np.where(magnitude < exact_count, magnitude, far_bucket)).astype(np.int32)


def cost(flops, moved):
    return pl.CostEstimate(flops=int(flops), bytes_accessed=int(moved), transcendentals=0)


def bias_lanes(bucket_count):
    lanes = np.arange(4 * TILE)
    lanes = np.where(lanes >= 2 * TILE, lanes - 4 * TILE, lanes)
    return np.eye(bucket_count, dtype=np.float32)[bucket_of(-lanes, bucket_count, MAX_DIST)].T


def grad_lanes(bucket_count):
    sub = np.arange(8)[:, None]
    lane = np.arange(4 * TILE)[None, :]
    y = (lane - sub) % (4 * TILE)
    y = np.where(y >= 2 * TILE, y - 4 * TILE, y)
    near = bucket_of(-y, bucket_count, MAX_DIST)
    up = np.full((8, TILE), bucket_of(np.array(MAX_DIST), bucket_count, MAX_DIST))
    down = np.full((8, TILE), bucket_of(np.array(-MAX_DIST), bucket_count, MAX_DIST))
    ids = np.concatenate([near, up, down], 1).reshape(-1)
    return np.eye(bucket_count, dtype=np.float32)[ids]


def bring(place_ref, piece_refs, into, sems):
    slices = into.shape[1] // len(piece_refs)
    copies = []
    for k in range(into.shape[0]):
        here = []
        for m, piece in enumerate(piece_refs):
            start = pl.multiple_of(place_ref[m], 16) if slices % 16 == 0 else place_ref[m]
            to = into.at[k, pl.ds(start, slices), :]
            here.append(pltpu.make_async_copy(piece.at[k], to, sems.at[k, m]))
        copies.append(here)
    return copies


def spread_bias(vec_ref, bias_s, heads, at=0):
    for h in range(heads):
        wide = jnp.broadcast_to(vec_ref[0, h : h + 1, :], (TILE, 4 * TILE))
        bias_s[at + h] = pltpu.roll(wide, 0, 1, stride=1, stride_axis=0)


def with_bias(tile, offset, h, bias_s, vec_ref, first=0):
    if offset == 0:
        return tile + bias_s[first + h, :, 0:TILE]
    if offset == 1:
        return tile + bias_s[first + h, :, 3 * TILE : 4 * TILE]
    if offset == -1:
        return tile + bias_s[first + h, :, TILE : 2 * TILE]
    lane = 2 * TILE + 1 if offset > 1 else 2 * TILE - 1
    return tile + vec_ref[0, h : h + 1, lane : lane + 1]


def apart(i, j):
    return (abs(i - j) - 1) * TILE + 1 >= LONGEST


def masks(seg):
    hot = lax.broadcasted_iota(jnp.int32, (16, seg.shape[-1]), 0) == seg
    return (
        jnp.where(hot, 0.0, masked_value).astype(bf16),
        jnp.where(hot, 1.0, 0.0).astype(bf16),
    )


def inv_rms(values):
    return lax.rsqrt(jnp.mean(values * values, -1, keepdims=True) + epsilon)


def rounded(value):
    return lax.reduce_precision(value, 8, 7)


def tree(parts):
    while len(parts) > 1:
        parts = [parts[i] + parts[i + 1] for i in range(0, len(parts), 2)]
    return parts[0]


def exact_parts(value):
    parts = []
    for _ in range(3):
        part = value.astype(bf16)
        parts.append(part)
        value = value - part.astype(f32)
    return parts


PAD = 16


def pack_kernel(at_ref, q_ref, k_ref, v_ref, o_ref, rel_ref, out_ref, mine_ref, pack_s):
    cols = q_ref.shape[1]
    for at, ref in enumerate((q_ref, k_ref, v_ref)):
        pack_s[at * cols : (at + 1) * cols] = ref[...].astype(f32).T
    pack_s[3 * cols :] = o_ref[...].astype(f32)
    out_ref[...] = pack_s[...].astype(bf16)
    slices = mine_ref.shape[0] - PAD
    start = at_ref[0] * slices
    if slices % 8 == 0:
        start = pl.multiple_of(start, 8)
    mine_ref[:slices] = pack_s[pl.ds(start, slices), :].astype(bf16)
    mine_ref[slices:] = jnp.zeros_like(mine_ref[slices:])
    buckets, heads = rel_ref.shape
    lane = 0
    for at in range(0, buckets, PAD):
        for part in exact_parts(rel_ref[at : at + PAD]):
            mine_ref[slices:, lane : lane + heads] = part
            lane += TILE


def pack_weights(at, w_query, w_key, w_value, w_out, rel_bias, share):
    width, cols = w_query.shape
    slices = width // share
    full = lambda shape: pl.BlockSpec(shape, lambda i, at: (0, 0))
    return pl.pallas_call(
        pack_kernel,
        grid_spec=pltpu.PrefetchScalarGridSpec(
            num_scalar_prefetch=1,
            grid=(1,),
            in_specs=[full((width, cols))] * 3 + [full((cols, width)), full(rel_bias.shape)],
            out_specs=[full((width, width)), full((slices + PAD, width))],
            scratch_shapes=[pltpu.VMEM((width, width), f32)],
        ),
        out_shape=[
            jax.ShapeDtypeStruct((width, width), bf16),
            jax.ShapeDtypeStruct((slices + PAD, width), bf16),
        ],
        compiler_params=pltpu.CompilerParams(vmem_limit_bytes=VMEM),
        cost_estimate=cost(10**9, 2**20),
        name="pack_weights",
    )(at, w_query, w_key, w_value, w_out, rel_bias)


def unpack_table(pads, buckets, heads):
    rows = []
    lane = 0
    for _ in range(0, buckets, PAD):
        parts = [
            pads[:, :, lane + p * TILE : lane + p * TILE + heads].astype(f32) for p in range(3)
        ]
        rows.append(parts[0] + parts[1] + parts[2])
        lane += 3 * TILE
    return jnp.concatenate(rows, 1)


def stack_kernel(*refs):
    ins, outs = refs[:3], refs[3:]
    slices = outs[0].shape[1]
    for at, ref in enumerate(ins):
        outs[0][at] = ref[:slices]
        if len(outs) == 2:
            outs[1][at] = ref[slices:]


def stack(arrays, slices):
    rows, width = arrays[0].shape
    shapes = [(3, slices, width)] + ([(3, rows - slices, width)] if rows > slices else [])
    return pl.pallas_call(
        stack_kernel,
        out_shape=[jax.ShapeDtypeStruct(shape, bf16) for shape in shapes],
        compiler_params=pltpu.CompilerParams(vmem_limit_bytes=VMEM),
        cost_estimate=cost(0, 12 * arrays[0].size),
        name="stack",
    )(*arrays)


def others_kernel(order_ref, all_ref, *outs):
    slices = outs[0].shape[1]
    for k in range(1, all_ref.shape[0]):
        for at, out in enumerate(outs):
            out[k - 1] = all_ref[order_ref[k], at * slices : (at + 1) * slices]


def others_of(order, everything, count):
    n, total, width = everything.shape
    slices = total // count
    shape = (n - 1, slices, width)
    return pl.pallas_call(
        others_kernel,
        grid_spec=pltpu.PrefetchScalarGridSpec(
            num_scalar_prefetch=1,
            grid=(1,),
            in_specs=[pl.BlockSpec((n, total, width), lambda i, p: (0, 0, 0))],
            out_specs=[pl.BlockSpec(shape, lambda i, p: (0, 0, 0))] * count,
        ),
        out_shape=[jax.ShapeDtypeStruct(shape, bf16)] * count,
        compiler_params=pltpu.CompilerParams(vmem_limit_bytes=VMEM),
        cost_estimate=cost(0, 4 * everything.size),
        name="others_of",
    )(order, everything)


def attend_row(heads, hd, weights, a1_ref, vec_ref, seg_ref, qkv_s, lse_s, ctx_ref, bias_s, first):
    length = a1_ref.shape[0]
    blocks = length // TILE
    qkv_s[...] = dg(weights, a1_ref[...], NT).astype(bf16)
    q_mask, k_mask = masks(seg_ref[0])
    ones = jnp.ones((16, length), bf16)
    for h in range(heads):
        q_t = jnp.concatenate([qkv_s[h * hd : (h + 1) * hd], q_mask], 0)
        k_t = jnp.concatenate([qkv_s[(heads + h) * hd : (heads + h + 1) * hd], k_mask], 0)
        v_t = jnp.concatenate([qkv_s[(2 * heads + h) * hd : (2 * heads + h + 1) * hd], ones], 0)
        scores = dg(k_t.T, q_t, NN)
        columns = []
        tops = []
        for i in range(blocks):
            at = slice(i * TILE, (i + 1) * TILE)
            tiles = [
                None
                if apart(i, j)
                else with_bias(
                    scores[j * TILE : (j + 1) * TILE, at], j - i, h, bias_s, vec_ref, first
                )
                for j in range(blocks)
            ]
            live = [tile for tile in tiles if tile is not None]
            top = jnp.max(functools.reduce(jnp.maximum, live), 0, keepdims=True)
            tops.append(top)
            none = jnp.zeros((TILE, TILE), bf16)
            exps = [none if t is None else jnp.exp(t - top).astype(bf16) for t in tiles]
            columns.append(jnp.concatenate(exps, 0))
        mixed = dg(v_t, jnp.concatenate(columns, 1), NN)
        total = mixed[hd : hd + 1]
        lse_s[h : h + 1, :] = jnp.concatenate(tops, 1) + jnp.log(total)
        ctx_ref[0, 0, h * hd : (h + 1) * hd, :] = (mixed[:hd] / total).astype(bf16)


def attn_kernel(heads, hd, n, low, keeps, place_ref, order_ref, a1_ref, vec_ref, seg_ref, *rest):
    sources = rest[: max(n, 1)]
    rest = rest[max(n, 1) + (0 if low == 0 else 4 if keeps else 1) :]
    if keeps:
        qkv_ref, lse_ref, ctx_ref, sorted_ref, bias_s, qkv_s, lse_s, w_s, sems, out_sem = rest
    else:
        ctx_ref, bias_s, qkv_s, lse_s = rest
    r, s = pl.program_id(0), pl.program_id(1)
    first = s * heads

    @pl.when(r == 0)
    def _():
        spread_bias(vec_ref, bias_s, heads, first)

    if keeps:
        count = w_s.shape[0] if n else 1
        copies = bring(place_ref, sources, w_s, sems) if n else [[]]
        keep = [
            pltpu.make_async_copy(
                w_s.at[k] if n else sources[0], sorted_ref.at[low + k], out_sem.at[k]
            )
            for k in range(count)
        ]

        @pl.when((s == 0) & (r == 0))
        def _():
            for here in copies:
                for copy in here:
                    copy.start()

        for k in range(count):

            @pl.when((s == k) & (r == 0))
            def _():
                for copy in copies[k]:
                    copy.wait()
                keep[k].start()

        weights = w_s[s, : 3 * heads * hd] if n else sources[0][: 3 * heads * hd]
    else:
        weights = sources[0][s, : 3 * heads * hd]
    attend_row(
        heads, hd, weights, a1_ref, vec_ref, seg_ref, qkv_s, lse_s, ctx_ref, bias_s, first
    )
    if keeps:

        @pl.when(r == 0)
        def _():
            qkv_ref[0] = qkv_s[...]
            lse_ref[0] = lse_s[...]

        @pl.when((s == pl.num_programs(1) - 1) & (r == pl.num_programs(0) - 1))
        def _():
            for copy in keep:
                copy.wait()


def attention(name, a1, vecs, segs, place, order, low, first_row, n_rows, weights, chain):
    rows, _, length = segs.shape
    width = a1.shape[1]
    count, heads, _ = vecs.shape
    slots = order.shape[0]
    hd = width // (4 * heads)
    cols = heads * hd
    n = len(weights) if weights[0].shape[0] != slots and len(weights) > 1 else 0
    keeps = first_row == 0
    anywhere = pl.BlockSpec(memory_space=pl.ANY)
    at = lambda r, o: o[r + first_row]
    slot = lambda r, s: low + jnp.where(r == 0, s, count - 1)
    if n:
        w_specs = [anywhere] * n
    elif keeps:
        w_specs = [pl.BlockSpec((width, width), lambda r, s, p, o: (0, 0))]
    else:
        w_specs = [pl.BlockSpec((count, width, width), lambda r, s, p, o: (low // count, 0, 0))]
    out_specs = [
        pl.BlockSpec((1, 3 * cols, length), lambda r, s, p, o: (slot(r, s), 0, 0)),
        pl.BlockSpec((1, heads, length), lambda r, s, p, o: (slot(r, s), 0, 0)),
        pl.BlockSpec((1, 1, cols, length), lambda r, s, p, o: (s + low, at(r, o), 0, 0)),
        anywhere,
    ]
    out_shape = [
        jax.ShapeDtypeStruct((slots, 3 * cols, length), bf16),
        jax.ShapeDtypeStruct((slots, heads, length), f32),
        jax.ShapeDtypeStruct((slots, rows, cols, length), bf16),
        jax.ShapeDtypeStruct((slots, width, width), bf16),
    ]
    scratch = [
        pltpu.VMEM((count * heads, TILE, 4 * TILE), f32),
        pltpu.VMEM((3 * cols, length), bf16),
        pltpu.VMEM((heads, length), f32),
    ]
    if keeps:
        scratch += [
            pltpu.VMEM((count, width, width) if n else (1, 16, TILE), bf16),
            pltpu.SemaphoreType.DMA((count, max(n, 1))),
            pltpu.SemaphoreType.DMA((count,)),
        ]
        linked = [] if chain is None else list(chain)
    else:
        out_specs, out_shape, linked = out_specs[2:3], out_shape[2:3], [chain[2]]
    base = 5 + len(w_specs)
    return pl.pallas_call(
        functools.partial(attn_kernel, heads, hd, n, low, keeps),
        grid_spec=pltpu.PrefetchScalarGridSpec(
            num_scalar_prefetch=2,
            grid=(n_rows, count),
            in_specs=[
                pl.BlockSpec((length, width), lambda r, s, p, o: (at(r, o), 0)),
                pl.BlockSpec((1, heads, 4 * TILE), lambda r, s, p, o: (s, 0, 0)),
                pl.BlockSpec((1, 1, length), lambda r, s, p, o: (at(r, o), 0, 0)),
            ]
            + w_specs
            + [anywhere] * len(linked),
            out_specs=out_specs,
            scratch_shapes=scratch,
        ),
        out_shape=out_shape,
        input_output_aliases={base + i: i for i in range(len(linked))},
        compiler_params=pltpu.CompilerParams(vmem_limit_bytes=VMEM),
        cost_estimate=cost(n_rows * count * 2.5 * 10**9, 2**20),
        name=name,
    )(place, order, a1, vecs, segs, *weights, *linked)


GELU_A = math.sqrt(2.0 / math.pi)
GELU_B = 0.044715


def gelu(v):
    t = jnp.tanh(v * (GELU_A + (GELU_A * GELU_B) * (v * v)))
    half = 0.5 * v
    return half + half * t


def gelu_pair(v):
    square = v * v
    t = jnp.tanh(v * (GELU_A + (GELU_A * GELU_B) * square))
    half = 0.5 * v
    inner = GELU_A + (3.0 * GELU_A * GELU_B) * square
    return half + half * t, 0.5 + 0.5 * t + half * (1.0 - t * t) * inner


def ffn_own_kernel(x_ref, ctx_ref, wo_ref, gain_ref, b_ref, c_ref, mid_ref, a2_ref, part_ref):
    slots, _, cols, length = ctx_ref.shape
    attn = dg(
        ctx_ref[...].reshape(slots * cols, length),
        wo_ref[...].reshape(slots * cols, wo_ref.shape[-1]),
        TN,
    )
    mid = (x_ref[...].astype(f32) + attn).astype(bf16)
    mid_ref[...] = mid
    mid = mid.astype(f32)
    a2 = (mid * inv_rms(mid) * gain_ref[...]).astype(bf16)
    a2_ref[...] = a2
    hidden = gelu(dg(a2, b_ref[...], NN)).astype(bf16)
    part_ref[...] = dg(hidden, c_ref[...], NN).astype(bf16)


def ffn_own(x, ctx, sorted_a, gain, own_b, own_c):
    slots, rows, cols, length = ctx.shape
    tokens, width = x.shape
    units = own_b.shape[1]
    by_row = pl.BlockSpec((length, width), lambda r: (r, 0))
    return pl.pallas_call(
        ffn_own_kernel,
        grid=(rows,),
        in_specs=[
            by_row,
            pl.BlockSpec((slots, 1, cols, length), lambda r: (0, r, 0, 0)),
            pl.BlockSpec((slots, cols, width), lambda r: (0, 3, 0)),
            pl.BlockSpec((1, width), lambda r: (0, 0)),
            pl.BlockSpec((width, units), lambda r: (0, 0)),
            pl.BlockSpec((units, width), lambda r: (0, 0)),
        ],
        out_specs=[by_row] * 3,
        out_shape=[jax.ShapeDtypeStruct((tokens, width), bf16)] * 3,
        compiler_params=pltpu.CompilerParams(vmem_limit_bytes=VMEM),
        cost_estimate=cost(tokens * width * 6 * units, 2**24),
        name="ffn_own",
    )(x, ctx, sorted_a, gain, own_b, own_c)


def ffn_row(a2, mid, part, up, down, gain_ref, seg_ref, out_ref, res_ref, pool_ref, wait=None):
    res = mid.astype(f32) + part.astype(f32)
    for k in range(len(up)):
        if wait is not None:
            wait(k)
        hidden = gelu(dg(a2, up[k][...], NN)).astype(bf16)
        res = res + dg(hidden, down[k][...], NN)
    res_ref[...] = res.astype(bf16)
    final = (res * inv_rms(res) * gain_ref[...]).astype(bf16)
    out_ref[...] = final
    if pool_ref is not None:
        seg = seg_ref[0]
        hot = lax.broadcasted_iota(jnp.int32, (SEG_ROW, seg.shape[-1]), 0) == seg
        member = jnp.where(hot, 1.0, 0.0)
        pool_ref[...] = dg(member.astype(bf16), final, NN) / jnp.sum(member, 1, keepdims=True)


def ffn_first_kernel(
    count, place_ref, order_ref, a2_ref, mid_ref, part_ref, gain_ref, seg_ref, *rest
):
    pieces, far_c = rest[:count], rest[count]
    out_ref, res_ref, pool_ref, sb_ref, sc_ref, b_s, c_s, sems, out_sems = rest[count + 1 :]
    others = b_s.shape[0]
    slices = far_c.shape[2]
    copies = []
    for k in range(others):
        here = []
        for m in range(count):
            start = pl.multiple_of(place_ref[m], 16) if slices % 16 == 0 else place_ref[m]
            into = b_s.at[k, pl.ds(start, slices), :]
            here.append(pltpu.make_async_copy(pieces[m].at[k], into, sems.at[0, k, m]))
            into = c_s.at[k, pl.ds(m * slices, slices), :]
            here.append(pltpu.make_async_copy(far_c.at[m, k], into, sems.at[1, k, m]))
        copies.append(here)
    keep = []
    for k in range(others):
        keep.append(pltpu.make_async_copy(b_s.at[k], sb_ref.at[k], out_sems.at[0, k]))
        keep.append(pltpu.make_async_copy(c_s.at[k], sc_ref.at[k], out_sems.at[1, k]))
    for here in copies:
        for copy in here:
            copy.start()

    def wait(k):
        for copy in copies[k]:
            copy.wait()
        keep[2 * k].start()
        keep[2 * k + 1].start()

    ffn_row(
        a2_ref[...],
        mid_ref[...],
        part_ref[...],
        [b_s.at[k] for k in range(others)],
        [c_s.at[k] for k in range(others)],
        gain_ref,
        seg_ref,
        out_ref,
        res_ref,
        pool_ref,
        wait,
    )
    for copy in keep:
        copy.wait()


def ffn_first(place, order, a2, mid, part, gain, segs, pieces, far_c):
    rows, _, length = segs.shape
    tokens, width = a2.shape
    units = pieces[0].shape[-1]
    others = pieces[0].shape[0]
    n = len(pieces)
    first = pl.BlockSpec((length, width), lambda r, p, o: (o[0], 0))
    anywhere = pl.BlockSpec(memory_space=pl.ANY)
    return pl.pallas_call(
        functools.partial(ffn_first_kernel, n),
        grid_spec=pltpu.PrefetchScalarGridSpec(
            num_scalar_prefetch=2,
            grid=(1,),
            in_specs=[
                first,
                first,
                first,
                pl.BlockSpec((1, width), lambda r, p, o: (0, 0)),
                pl.BlockSpec((1, 1, length), lambda r, p, o: (o[0], 0, 0)),
            ]
            + [anywhere] * (n + 1),
            out_specs=[
                first,
                pl.BlockSpec((length, width), lambda r, p, o: (0, 0)),
                pl.BlockSpec((SEG_ROW, width), lambda r, p, o: (0, 0)),
                anywhere,
                anywhere,
            ],
            scratch_shapes=[
                pltpu.VMEM((others, width, units), bf16),
                pltpu.VMEM((others, units, width), bf16),
                pltpu.SemaphoreType.DMA((2, others, n)),
                pltpu.SemaphoreType.DMA((2, others)),
            ],
        ),
        out_shape=[
            jax.ShapeDtypeStruct((tokens, width), bf16),
            jax.ShapeDtypeStruct((length, width), bf16),
            jax.ShapeDtypeStruct((SEG_ROW, width), f32),
            jax.ShapeDtypeStruct((others, width, units), bf16),
            jax.ShapeDtypeStruct((others, units, width), bf16),
        ],
        compiler_params=pltpu.CompilerParams(vmem_limit_bytes=VMEM),
        cost_estimate=cost(length * width * 4 * units * others, 2**24),
        name="ffn_first",
    )(place, order, a2, mid, part, gain, segs, *pieces, far_c)


def loss_math(pooled, project, pair_col, pair_row, gain):
    slots = pooled.shape[0]
    projected = dg(pooled, project, NN)
    inv_norm = lax.rsqrt(jnp.sum(projected * projected, -1, keepdims=True) + epsilon)
    unit = projected * inv_norm
    embedded = unit.astype(bf16)
    similar = logit_scale * dg(embedded, embedded, NT)
    rows = lax.broadcasted_iota(jnp.int32, (slots, slots), 0)
    columns = lax.broadcasted_iota(jnp.int32, (slots, slots), 1)
    same = rows == columns
    similar = jnp.where(same, masked_value, similar)
    partner = jnp.where((pair_col == pair_row) & jnp.logical_not(same), 2.0, 0.0)

    def total(axis):
        top = jnp.max(similar, axis, keepdims=True)
        return top + jnp.log(jnp.sum(jnp.exp(similar - top), axis, keepdims=True))

    both = jnp.exp(similar - total(1)) + jnp.exp(similar - total(0)) - partner
    high = both.astype(bf16)
    low = (both - high.astype(f32)).astype(bf16)
    d_unit = (loss_scale * logit_scale) * (dg(high, embedded, NN) + dg(low, embedded, NN))
    d_proj = inv_norm * (d_unit - unit * jnp.sum(d_unit * unit, -1, keepdims=True))
    d_proj = d_proj.astype(bf16)
    d_pooled = dg(d_proj, project, NT)
    d_gain = jnp.sum(d_pooled * pooled.astype(f32), 0, keepdims=True) / gain
    return d_proj, d_pooled, d_gain


def d_result_of(res, seg, d_pool, gain):
    hot = lax.broadcasted_iota(jnp.int32, (SEG_ROW, seg.shape[-1]), 0) == seg
    member = jnp.where(hot, 1.0, 0.0)
    per_token = d_pool / jnp.sum(member, 1, keepdims=True)
    high = per_token.astype(bf16)
    low = (per_token - high.astype(f32)).astype(bf16)
    twice = jnp.concatenate([member, member], 0).astype(bf16)
    d_final = dg(twice, jnp.concatenate([high, low], 0), TN)
    scale = inv_rms(res)
    unit = res * scale
    weighted = d_final * gain
    return scale * (weighted - unit * jnp.mean(weighted * unit, -1, keepdims=True))


def fold(tile):
    lanes = tile.shape[1]
    total = tile[0:8]
    for b in range(1, TILE // 8):
        total = total + pltpu.roll(tile[8 * b : 8 * b + 8], lanes - 8 * b, 1)
    return total


def loss_step(pieces, at_ref, project_ref, pc_ref, pr_ref, gain_ref, dpool_ref, dproj_ref, dgain_ref, a_s, b_s):
    each = SEG_ROW
    parts = pieces[0].shape[0] // each
    for m, piece in enumerate(pieces):
        value = piece[...].astype(f32)
        for part in range(parts):
            start = pl.multiple_of(at_ref[1 + m * parts + part] * each, each)
            a_s[pl.ds(start, each), :] = value[part * each : (part + 1) * each]
    pooled = a_s[...].astype(bf16)
    d_proj, d_pooled, d_gain = loss_math(
        pooled, project_ref[...], pc_ref[...], pr_ref[...], gain_ref[...]
    )
    a_s[...] = d_pooled
    b_s[...] = dg(pooled, d_proj, TN)
    here = dpool_ref.shape[0]
    block = dproj_ref.shape[0]
    dpool_ref[...] = a_s[pl.ds(pl.multiple_of(at_ref[0] * here, here), here), :]
    dproj_ref[...] = b_s[pl.ds(pl.multiple_of(at_ref[0] * block, block), block), :]
    dgain_ref[...] = d_gain


def norm_back(grad, values, gain):
    scale = inv_rms(values)
    unit = values * scale
    weighted = grad * gain
    d_values = scale * (weighted - unit * jnp.mean(weighted * unit, -1, keepdims=True))
    return d_values, jnp.sum(grad * unit, 0, keepdims=True)


def row_back_kernel(count, with_loss, heads, hd, at_ref, row_ref, *refs):
    pieces, refs = refs[:count], refs[count:]
    project_ref, pc_ref, pr_ref, gain_end_ref, gain_two_ref, gain_one_ref, seg_ref = refs[:7]
    lse_ref, vec_ref, res_any, mid_any, a2_any, x_any, own_b, own_c, far_b, far_c = refs[7:17]
    far_a, qkv_any, ctx_any = refs[17:20]
    dpool_ref, dproj_ref, dend_ref, dtwo_ref, dattn_ref = refs[20:25]
    dqkv_ref, fold_ref, dtok_ref, done_ref = refs[25:29]
    a_s, p_s, b_s, c_s, wo_s, wa_s, res_s, mid_s, a2_s, x_s, qkv_s, ctx_s = refs[29:41]
    dres_s, low_s, sum_s, dctx_s, bias_s, b_sems, c_sems, sems = refs[41:]
    step = pl.program_id(0)
    slots = b_s.shape[0]
    length = res_s.shape[0]
    cols = heads * hd
    row = row_ref[0]
    mine = pl.ds(pl.multiple_of(row * length, length), length)
    res_copy = pltpu.make_async_copy(res_any, res_s, sems.at[0])
    a2_copy = pltpu.make_async_copy(a2_any.at[mine], a2_s, sems.at[1])
    mid_copy = pltpu.make_async_copy(mid_any.at[mine], mid_s, sems.at[2])
    wo_copy = pltpu.make_async_copy(far_a.at[:, pl.ds(3 * cols, cols)], wo_s, sems.at[3])
    qkv_copy = pltpu.make_async_copy(qkv_any, qkv_s, sems.at[4])
    ctx_copy = pltpu.make_async_copy(ctx_any.at[:, row], ctx_s, sems.at[5])
    wa_copy = pltpu.make_async_copy(far_a.at[:, pl.ds(0, 3 * cols)], wa_s, sems.at[6])
    x_copy = pltpu.make_async_copy(x_any.at[mine], x_s, sems.at[7])

    def weight_copies(k):
        b_from, c_from = (own_b, own_c) if k == 0 else (far_b.at[k - 1], far_c.at[k - 1])
        return [
            pltpu.make_async_copy(b_from, b_s.at[k], b_sems.at[k]),
            pltpu.make_async_copy(c_from, c_s.at[k], c_sems.at[k]),
        ]

    @pl.when(step == 0)
    def _():
        res_copy.start()
        a2_copy.start()
        for k in range(slots):
            for copy in weight_copies(k):
                copy.start()
        for copy in (mid_copy, wo_copy, qkv_copy, ctx_copy, wa_copy, x_copy):
            copy.start()
        if with_loss:
            loss_step(
                pieces,
                at_ref,
                project_ref,
                pc_ref,
                pr_ref,
                gain_end_ref,
                dpool_ref,
                dproj_ref,
                dend_ref,
                a_s,
                p_s,
            )
        else:
            dpool_ref[...] = pieces[0][...]
            dproj_ref[...] = jnp.zeros_like(dproj_ref)
            dend_ref[...] = jnp.zeros_like(dend_ref)
        res_copy.wait()
        a2_copy.wait()
        d_pool = dpool_ref[pl.ds(pl.multiple_of(row * SEG_ROW, SEG_ROW), SEG_ROW), :]
        d_res = d_result_of(res_s[...].astype(f32), seg_ref[0], d_pool, gain_end_ref[...])
        dres_s[...] = d_res
        low_s[...] = d_res.astype(bf16)
        sum_s[...] = jnp.zeros_like(sum_s)

    for k in range(slots):

        @pl.when(step == k + 1)
        def _():
            for copy in weight_copies(k):
                copy.wait()

    @pl.when((step >= 1) & (step <= slots))
    def _():
        up, down = b_s.at[step - 1], c_s.at[step - 1]
        slope = gelu_pair(dg(a2_s[...], up[...], NN))[1]
        d_pre = (dg(low_s[...], down[...], NT) * slope).astype(bf16)
        sum_s[...] += dg(d_pre, up[...], NT)

    @pl.when(step == slots)
    def _():
        mid_copy.wait()
        wo_copy.wait()
        d_mid, dtwo_ref[...] = norm_back(
            sum_s[...], mid_s[...].astype(f32), gain_two_ref[...]
        )
        d_mid = dres_s[...] + d_mid
        dres_s[...] = d_mid
        low = d_mid.astype(bf16)
        dattn_ref[...] = low
        sum_s[...] = jnp.zeros_like(sum_s)
        for k in range(slots):
            dctx_s[k] = dg(wo_s[k], low, NT).astype(bf16)
        qkv_copy.wait()
        ctx_copy.wait()
        wa_copy.wait()
        x_copy.wait()

    @pl.when(step > slots)
    def _():
        slot = step - slots - 1
        blocks = length // TILE
        spread_bias(vec_ref.at[pl.ds(slot, 1)], bias_s, heads)
        q_mask, k_mask = masks(seg_ref[0])
        for h in range(heads):
            q_low = qkv_s[slot, h * hd : (h + 1) * hd]
            k_low = qkv_s[slot, (heads + h) * hd : (heads + h + 1) * hd]
            v_low = qkv_s[slot, (2 * heads + h) * hd : (2 * heads + h + 1) * hd]
            dc = dctx_s[slot, h * hd : (h + 1) * hd]
            c = ctx_s[slot, h * hd : (h + 1) * hd]
            delta = jnp.sum(dc.astype(f32) * c.astype(f32), 0, keepdims=True)
            lse = lse_ref[slot, h : h + 1]
            scores = dg(
                jnp.concatenate([k_low, k_mask], 0).T, jnp.concatenate([q_low, q_mask], 0), NN
            )
            d_probs = dg(v_low.T, dc, NN)
            probs_cols = []
            score_cols = []
            near = [None, None, None]
            far = [None, None]
            for i in range(blocks):
                at = slice(i * TILE, (i + 1) * TILE)
                probs = []
                grads = []
                for j in range(blocks):
                    if apart(i, j):
                        probs.append(jnp.zeros((TILE, TILE), bf16))
                        grads.append(jnp.zeros((TILE, TILE), bf16))
                        continue
                    to = slice(j * TILE, (j + 1) * TILE)
                    tile = with_bias(scores[to, at], j - i, h, bias_s, vec_ref.at[pl.ds(slot, 1)])
                    prob = jnp.exp(tile - lse[:, at])
                    grad = prob * (d_probs[to, at] - delta[:, at])
                    probs.append(prob.astype(bf16))
                    grads.append(grad.astype(bf16))
                    if abs(j - i) <= 1:
                        old = near[j - i + 1]
                        near[j - i + 1] = grad if old is None else old + grad
                    else:
                        old = far[int(j < i)]
                        far[int(j < i)] = grad if old is None else old + grad
                probs_cols.append(jnp.concatenate(probs, 0))
                score_cols.append(jnp.concatenate(grads, 0))
            probs = jnp.concatenate(probs_cols, 1)
            grads = jnp.concatenate(score_cols, 1)
            dqkv_ref[0, h * hd : (h + 1) * hd] = dg(k_low, grads, NN).astype(bf16)
            dqkv_ref[0, (heads + h) * hd : (heads + h + 1) * hd] = dg(q_low, grads, NT).astype(bf16)
            dqkv_ref[0, (2 * heads + h) * hd : (2 * heads + h + 1) * hd] = dg(dc, probs, NT).astype(
                bf16
            )
            band = jnp.concatenate([near[1], near[0], jnp.zeros_like(near[0]), near[2]], 1)
            fold_ref[0, h, :, : 4 * TILE] = fold(band)
            for side in range(2):
                total = far[side][0:8]
                for b in range(1, TILE // 8):
                    total = total + far[side][8 * b : 8 * b + 8]
                fold_ref[0, h, :, (4 + side) * TILE : (5 + side) * TILE] = total
        sum_s[...] += dg(dqkv_ref[0], wa_s[slot], TN)

    @pl.when(step == 2 * slots)
    def _():
        d_x, done_ref[...] = norm_back(sum_s[...], x_s[...].astype(f32), gain_one_ref[...])
        dtok_ref[...] = (dres_s[...] + d_x).astype(bf16)


def row_back(
    at,
    row,
    pieces,
    with_loss,
    project,
    pairs,
    gains,
    segs,
    lse,
    vecs,
    res,
    mid,
    a2,
    x,
    own_b,
    own_c,
    far_b,
    far_c,
    sorted_a,
    qkv,
    ctx,
    here,
    block,
):
    slots, heads, _ = vecs.shape
    length, width = res.shape
    units = own_b.shape[1]
    cols = width // 4
    n_all = pairs.shape[0]
    anywhere = pl.BlockSpec(memory_space=pl.ANY)

    def full(shape):
        zeros = (0,) * len(shape)
        return pl.BlockSpec(shape, lambda i, at, row: zeros)

    def slot(i):
        return jnp.maximum(i - slots - 1, 0)

    row_shape = (length, width)
    return pl.pallas_call(
        functools.partial(row_back_kernel, len(pieces), with_loss, heads, cols // heads),
        grid_spec=pltpu.PrefetchScalarGridSpec(
            num_scalar_prefetch=2,
            grid=(2 * slots + 1,),
            in_specs=[full(piece.shape) for piece in pieces]
            + [full(project.shape), full((n_all, 1)), full((1, n_all))]
            + [full((1, width))] * 3
            + [
                pl.BlockSpec((1, 1, length), lambda i, at, row: (row[0], 0, 0)),
                full(lse.shape),
                full(vecs.shape),
            ]
            + [anywhere] * 11,
            out_specs=[
                full((here, width)),
                full((block, width)),
                full((1, width)),
                full((1, width)),
                full(row_shape),
                pl.BlockSpec((1, 3 * cols, length), lambda i, at, row: (slot(i), 0, 0)),
                pl.BlockSpec((1, heads, 8, 6 * TILE), lambda i, at, row: (slot(i), 0, 0, 0)),
                full(row_shape),
                full((1, width)),
            ],
            scratch_shapes=[
                pltpu.VMEM((n_all if with_loss else 8, width), f32),
                pltpu.VMEM((width, width), f32),
                pltpu.VMEM((slots, width, units), bf16),
                pltpu.VMEM((slots, units, width), bf16),
                pltpu.VMEM((slots, cols, width), bf16),
                pltpu.VMEM((slots, 3 * cols, width), bf16),
                pltpu.VMEM(row_shape, bf16),
                pltpu.VMEM(row_shape, bf16),
                pltpu.VMEM(row_shape, bf16),
                pltpu.VMEM(row_shape, bf16),
                pltpu.VMEM((slots, 3 * cols, length), bf16),
                pltpu.VMEM((slots, cols, length), bf16),
                pltpu.VMEM(row_shape, f32),
                pltpu.VMEM(row_shape, bf16),
                pltpu.VMEM(row_shape, f32),
                pltpu.VMEM((slots, cols, length), bf16),
                pltpu.VMEM((heads, TILE, 4 * TILE), f32),
                pltpu.SemaphoreType.DMA((slots,)),
                pltpu.SemaphoreType.DMA((slots,)),
                pltpu.SemaphoreType.DMA((8,)),
            ],
        ),
        out_shape=[
            jax.ShapeDtypeStruct((here, width), f32),
            jax.ShapeDtypeStruct((block, width), f32),
            jax.ShapeDtypeStruct((1, width), f32),
            jax.ShapeDtypeStruct((1, width), f32),
            jax.ShapeDtypeStruct(row_shape, bf16),
            jax.ShapeDtypeStruct((slots, 3 * cols, length), bf16),
            jax.ShapeDtypeStruct((slots, heads, 8, 6 * TILE), f32),
            jax.ShapeDtypeStruct(row_shape, bf16),
            jax.ShapeDtypeStruct((1, width), f32),
        ],
        compiler_params=pltpu.CompilerParams(vmem_limit_bytes=VMEM),
        cost_estimate=cost(3 * 10**10, 2**24),
        name="row_back",
    )(
        at,
        row,
        *pieces,
        project,
        pairs[:, None],
        pairs[None, :],
        *gains,
        segs,
        lse,
        vecs,
        res,
        mid,
        a2,
        x,
        own_b,
        own_c,
        far_b,
        far_c,
        sorted_a,
        qkv,
        ctx,
    )


def split_blocks(core, rel_ref, block, pad, extra, values, keep_ref, give_ref, lead):
    for c in range(2):

        @pl.when(core == c)
        def _():
            for chip in range(4):
                for ref, j in ((keep_ref, 2 * chip + c), (give_ref, 2 * chip + 1 - c)):
                    rows = values(j * block, (j + 1) * block)
                    to = chip if rel_ref is None else rel_ref[chip]
                    for at, value in enumerate(rows):
                        ref[to, lead + at, :block] = value
                    if pad:
                        ref[to, lead, block:] = extra(j)


def attn_weights_kernel(
    block, place_ref, a1_ref, dattn_ref, dqkv_ref, ctx_ref, extra_ref, *rest
):
    outs, (a1_s, dattn_s, sum_s) = rest[:-3], rest[-3:]

    @pl.when(pl.program_id(0) == 0)
    def _():
        a1_s[...] = a1_ref[...].T
        dattn_s[...] = dattn_ref[...].T

    cols3 = dqkv_ref.shape[1]
    sum_s[:, :cols3] = dg(a1_s[...], dqkv_ref[0], NT).astype(bf16)
    sum_s[:, cols3:] = dg(dattn_s[...], ctx_ref[0, 0], NT).astype(bf16)
    if len(outs) == 1:
        outs[0][0] = sum_s[...]
    else:
        split_blocks(
            place_ref[1],
            place_ref.at[pl.ds(2, 4)],
            block,
            True,
            lambda j: extra_ref[0, j],
            lambda a, b: [sum_s[a:b]],
            outs[0],
            outs[1],
            0,
        )


def attn_weights(place, a1, d_attn, d_qkv, ctx, extra, split):
    slots, cols3, length = d_qkv.shape
    cols = ctx.shape[2]
    width = a1.shape[1]
    _, blocks, pad, _ = extra.shape
    block = width // blocks
    if split:
        shape = (4, slots, block + pad, width)
        out_specs = [pl.BlockSpec((4, 1, block + pad, width), lambda k, p: (0, k, 0, 0))] * 2
        out_shape = [jax.ShapeDtypeStruct(shape, bf16)] * 2
    else:
        out_specs = [pl.BlockSpec((1, width, width), lambda k, p: (k, 0, 0))]
        out_shape = [jax.ShapeDtypeStruct((slots, width, width), bf16)]
    return pl.pallas_call(
        functools.partial(attn_weights_kernel, block),
        grid_spec=pltpu.PrefetchScalarGridSpec(
            num_scalar_prefetch=1,
            grid=(slots,),
            in_specs=[
                pl.BlockSpec((length, width), lambda k, p: (p[0], 0)),
                pl.BlockSpec((length, width), lambda k, p: (0, 0)),
                pl.BlockSpec((1, cols3, length), lambda k, p: (k, 0, 0)),
                pl.BlockSpec((1, 1, cols, length), lambda k, p: (k, p[0], 0, 0)),
                pl.BlockSpec((1, blocks, pad, width), lambda k, p: (k, 0, 0, 0)),
            ],
            out_specs=out_specs,
            scratch_shapes=[
                pltpu.VMEM((width, length), bf16),
                pltpu.VMEM((width, length), bf16),
                pltpu.VMEM((width, width), bf16),
            ],
        ),
        out_shape=out_shape,
        compiler_params=pltpu.CompilerParams(vmem_limit_bytes=VMEM),
        cost_estimate=cost(10**6, 10**6),
        name="attn_weights",
    )(place, a1, d_attn, d_qkv, ctx, extra)


def ffn_tail_kernel(
    block,
    place_ref,
    order_ref,
    a2_ref,
    mid_ref,
    part_ref,
    own_ref,
    seg_ref,
    dpool_ref,
    gain_ref,
    own_b_ref,
    own_c_ref,
    b_any,
    c_any,
    _out,
    out_ref,
    *rest,
):
    outs, (b_ref, c_ref, sems, res_s, up_s, down_s) = rest[:-6], rest[-6:]
    r = pl.program_id(0)
    others = b_ref.shape[0]
    copies = [
        pltpu.make_async_copy(b_any, b_ref, sems.at[0]),
        pltpu.make_async_copy(c_any, c_ref, sems.at[1]),
    ]

    @pl.when(r == 1)
    def _():
        for copy in copies:
            copy.wait()

    @pl.when(r == 0)
    def _():
        for copy in copies:
            copy.start()
        res_s[...] = own_ref[...]
        up_s[...] = jnp.zeros_like(up_s)
        down_s[...] = jnp.zeros_like(down_s)

    @pl.when(r > 0)
    def _():
        ffn_row(
            a2_ref[...],
            mid_ref[...],
            part_ref[...],
            [b_ref.at[k] for k in range(others)],
            [c_ref.at[k] for k in range(others)],
            gain_ref,
            None,
            out_ref,
            res_s,
            None,
        )

    d_res = d_result_of(res_s[...].astype(f32), seg_ref[0], dpool_ref[...], gain_ref[...])
    low = d_res.astype(bf16)
    a2 = a2_ref[...]
    hidden, slope = gelu_pair(dg(a2, own_b_ref[...], NN))
    down_s[...] += dg(low, hidden.astype(bf16), TN)
    d_pre = (dg(low, own_c_ref[...], NT) * slope).astype(bf16)
    up_s[...] += dg(a2, d_pre, TN)

    @pl.when(r == pl.num_programs(0) - 1)
    def _():
        if len(outs) == 1:
            outs[0][0] = up_s[...].astype(bf16)
            outs[0][1] = down_s[...].astype(bf16)
        else:
            split_blocks(
                place_ref[1],
                None,
                block,
                False,
                None,
                lambda a, b: [up_s[a:b].astype(bf16), down_s[a:b].astype(bf16)],
                outs[0],
                outs[1],
                0,
            )


def ffn_tail(
    place, order, a2, mid, part, res, segs, d_pool, gain, own_b, own_c, far_b, far_c, out, blocks, split
):
    rows, _, length = segs.shape
    tokens, width = a2.shape
    units = own_b.shape[1]
    others = far_b.shape[0]
    block = width // blocks
    row = pl.BlockSpec((length, width), lambda r, p, o: (o[r], 0))
    later = pl.BlockSpec((length, width), lambda r, p, o: (o[jnp.maximum(r, 1)], 0))

    def fixed(shape):
        zeros = (0,) * len(shape)
        return pl.BlockSpec(shape, lambda r, p, o: zeros, pipeline_mode=pl.Buffered(1))

    shape = (4, 2, block, units) if split else (2, width, units)
    zeros = (0,) * len(shape)
    n = 2 if split else 1
    return pl.pallas_call(
        functools.partial(ffn_tail_kernel, block),
        grid_spec=pltpu.PrefetchScalarGridSpec(
            num_scalar_prefetch=2,
            grid=(rows,),
            in_specs=[
                row,
                later,
                later,
                fixed((length, width)),
                pl.BlockSpec((1, 1, length), lambda r, p, o: (o[r], 0, 0)),
                pl.BlockSpec((SEG_ROW, width), lambda r, p, o: (o[r], 0)),
                fixed((1, width)),
                fixed((width, units)),
                fixed((units, width)),
            ]
            + [pl.BlockSpec(memory_space=pl.ANY)] * 3,
            out_specs=[later] + [pl.BlockSpec(shape, lambda r, p, o: zeros)] * n,
            scratch_shapes=[
                pltpu.VMEM((others, width, units), bf16),
                pltpu.VMEM((others, units, width), bf16),
                pltpu.SemaphoreType.DMA((2,)),
                pltpu.VMEM((length, width), bf16),
                pltpu.VMEM((width, units), f32),
                pltpu.VMEM((width, units), f32),
            ],
        ),
        out_shape=[jax.ShapeDtypeStruct((tokens, width), bf16)]
        + [jax.ShapeDtypeStruct(shape, bf16)] * n,
        input_output_aliases={13: 0},
        compiler_params=pltpu.CompilerParams(vmem_limit_bytes=VMEM),
        cost_estimate=cost(10**6, 10**6),
        name="ffn_tail",
    )(place, order, a2, mid, part, res, segs, d_pool, gain, own_b, own_c, far_b, far_c, out)


def shards(
    n_dp,
    n_tp,
    tokens,
    segment_ids,
    pair_order,
    w_query,
    w_key,
    w_value,
    w_out,
    rel_bias,
    gain_attn,
    w_hidden,
    w_down,
    gain_ffn,
    gain_final,
    w_project,
):
    rows, length = segment_ids.shape
    bucket_count, heads = rel_bias.shape
    width = tokens.shape[1]
    units = w_hidden.shape[1]
    dp = lax.axis_index("dp")
    tp = lax.axis_index("tp")
    share = math.gcd(n_dp, 8)
    split = n_dp == 8
    mates = [[(i, i ^ m) for i in range(n_dp)] for m in range(share)]
    levels = [[(i, i ^ k) for i in range(n_tp)] for k in range(n_tp)]

    def over_dp(value, m):
        return lax.ppermute(value, "dp", mates[m])

    def over_tp(value, k):
        return lax.ppermute(value, "tp", levels[k])

    slices = width // share
    low_bits = dp % share
    place = (low_bits ^ jnp.arange(share, dtype=jnp.int32)) * slices

    def from_levels(mine):
        return stack([over_tp(mine, k) for k in range(1, n_tp)], slices)

    def from_chips(far):
        return [far] + [over_dp(far, m) for m in range(2, share, 2)]

    def from_cores(pieces):
        both = [(piece, over_dp(piece, 1)) for piece in pieces]
        return [piece for pair in both for piece in pair]

    def after(values, others):
        return lax.optimization_barrier((values, others))[0]

    order = tp ^ jnp.arange(n_tp, dtype=jnp.int32)
    pack_a, mine_a = pack_weights(
        low_bits[None].astype(jnp.int32), w_query, w_key, w_value, w_out, rel_bias, share
    )
    far_a, pads = from_levels(mine_a)
    mine_bc = jnp.concatenate(
        [
            lax.dynamic_slice_in_dim(w, low_bits * slices, slices, 0)
            for w in (w_hidden, w_down)
        ]
    )
    all_bc = lax.all_gather(mine_bc, "tp", axis=0)
    tables = jnp.concatenate([rel_bias[None], unpack_table(pads, bucket_count, heads)])
    vec_own = jnp.einsum("kbh,bn->khn", tables[:1], bias_lanes(bucket_count), precision=highest)
    vecs = jnp.einsum("kbh,bn->khn", tables, bias_lanes(bucket_count), precision=highest)
    segs = segment_ids[:, None, :]
    row = tp[None].astype(jnp.int32)
    one = gain_attn[None]
    two = gain_ffn[None]
    end = gain_final[None]

    x = tokens.astype(f32)
    a1 = (x * inv_rms(x) * one).astype(bf16)
    state = attention(
        "attn_own", after(a1, far_a), vec_own, segs, place, order, 0, 0, rows, [pack_a], None
    )
    far_a = from_chips(far_a)
    far_b, far_c = others_of(after(order, (state, far_a)), all_bc, 2)
    groups = np.arange(n_dp).reshape(-1, share).tolist()
    far_c = lax.all_gather(far_c, "dp", axis=0, axis_index_groups=groups)
    far_a = from_cores(after(far_a, far_b))
    far_b = from_chips(after(far_b, far_a))
    qkv, lse, ctx, sorted_a = attention(
        "attn_far", a1, vecs[1:], segs, place, order, 1, 0, rows, far_a, state
    )
    far_b = from_cores(after(far_b, lse))
    mid, a2, part = ffn_own(tokens, ctx, sorted_a, two, w_hidden, w_down)
    layer_out, res, pooled, sorted_b, sorted_c = ffn_first(
        place, order, a2, mid, part, end, segs, far_b, far_c
    )
    block = width // n_dp
    here = rows * SEG_ROW
    pooled = pooled.astype(bf16)
    if split:
        pooled = jnp.concatenate([pooled] + [over_tp(pooled, k) for k in range(1, n_tp)])
        pooled = jnp.concatenate([pooled, over_dp(pooled, 1)])
        pooled_all = from_chips(pooled)
        spots = (dp ^ jnp.arange(n_dp))[:, None] * rows + order[None]
        at = jnp.concatenate([dp[None], spots.reshape(-1)]).astype(jnp.int32)
    else:
        pooled = lax.all_gather(pooled, "tp", axis=0, tiled=True)
        pooled_all = [lax.all_gather(pooled, "dp", axis=0, tiled=True)]
        at = dp[None].astype(jnp.int32)
    pairs = pair_order // 2
    if not split:
        everything = pooled_all[0]
        d_proj, d_pool, d_gain_end = loss_math(
            everything, w_project, pairs[:, None], pairs[None, :], end
        )
        own_cols = lax.dynamic_slice_in_dim(everything, dp * block, block, 1)
        grad_project = dg(own_cols, d_proj, TN)
        pooled_all = [lax.dynamic_slice_in_dim(d_pool, dp * here, here, 0)]
    made = row_back(
        at,
        row,
        pooled_all,
        split,
        w_project,
        pairs,
        (end, two, one),
        segs,
        lse,
        vecs,
        res,
        mid,
        a2,
        tokens,
        w_hidden,
        w_down,
        sorted_b,
        sorted_c,
        sorted_a,
        qkv,
        ctx,
        here,
        block,
    )
    d_pool, d_gain_two, d_attn, d_qkv, folded, d_tok, d_gain_one = made[0], *made[3:]
    if split:
        grad_project, d_gain_end = made[1], made[2]
    grad_gain_final = lax.dynamic_slice_in_dim(d_gain_end[0], dp * block, block, 0)
    d_tokens = lax.all_gather(d_tok, "tp", axis=0, tiled=True)

    d_rel = jnp.einsum(
        "khn,nb->kbh",
        folded.reshape(n_tp, heads, -1),
        grad_lanes(bucket_count),
        precision=highest,
    )
    gains = jnp.concatenate([d_gain_one, d_gain_two])
    pad = 16
    extra = jnp.zeros((n_tp, n_dp, pad, width), bf16)
    if split:
        small = d_rel.reshape(n_tp, 1, 1, bucket_count * heads).astype(bf16)
        gain_rows = jnp.swapaxes(gains.reshape(2, n_dp, block), 0, 1).astype(bf16)
        extra = jnp.concatenate(
            [
                jnp.broadcast_to(gain_rows[None], (n_tp, n_dp, 2, block)),
                jnp.broadcast_to(small, (n_tp, n_dp, 1, block)),
                jnp.zeros((n_tp, n_dp, pad - 3, block), bf16),
            ],
            2,
        )
        extra = jnp.pad(extra, ((0, 0), (0, 0), (0, 0), (0, width - block)))
    chips = (dp // 2) ^ jnp.arange(4, dtype=jnp.int32)
    spots = jnp.concatenate([row, (dp % 2)[None].astype(jnp.int32), chips])
    parts_a = attn_weights(spots, a1, d_attn, d_qkv, ctx, extra, split)

    def to_core(parts):
        keep, give = parts
        took = over_dp(give, 1)
        return [rounded(keep[c].astype(f32) + took[c].astype(f32)) for c in range(4)]

    def to_chip(pair):
        return [pair[0]] + [over_dp(pair[c].astype(bf16), 2 * c) for c in range(1, 4)]

    def total(parts):
        return tree([part.astype(f32) for part in parts])

    def scatter(parts):
        return lax.psum_scatter(parts[0].astype(f32), "dp", scatter_dimension=1, tiled=True)

    if split:
        pair_a = to_core(parts_a)
        got_a = to_chip(pair_a)
        first = after(order, pair_a)
    else:
        first = after(order, parts_a)
    layer_out, *parts_f = ffn_tail(
        spots, first, a2, mid, part, res, segs, d_pool, end,
        w_hidden, w_down, sorted_b, sorted_c, layer_out, n_dp, split,
    )
    if split:
        chips = [[c + core for c in range(0, n_dp, 2)] for core in range(2)]
        give_f = over_dp(after(parts_f[1], got_a), 1)
        pair_f = parts_f[0].astype(f32) + give_f.astype(f32)
        own_a = rounded(total(after(got_a, (d_tokens, pair_f))))
        swapped = lax.all_to_all(
            pair_f.astype(bf16), "dp", 0, 0, axis_index_groups=chips, tiled=True
        )
        own_f = jnp.sum(swapped.astype(f32), 0)
    else:
        own_a, own_f = rounded(scatter(parts_a)), scatter(parts_f)

    def reduce_tp(value):
        return tree([value[0]] + [over_tp(value[k], k) for k in range(1, n_tp)])

    grad_a = tree(
        [own_a[0].astype(f32)]
        + [over_tp(own_a[k].astype(bf16), k).astype(f32) for k in range(1, n_tp)]
    )
    cols = width // 4
    if split:
        gain_one, gain_two = grad_a[block, :block], grad_a[block + 1, :block]
        d_rel_here = grad_a[block + 2, : bucket_count * heads].reshape(bucket_count, heads)
    else:
        gains = tree([gains] + [over_tp(gains, k) for k in range(1, n_tp)])
        d_rel_here, gains = lax.psum((reduce_tp(d_rel), gains), "dp")
        gain_one, gain_two = lax.dynamic_slice_in_dim(gains, dp * block, block, 1)
    return (
        layer_out,
        d_tokens.astype(f32),
        grad_a[:block, :cols],
        grad_a[:block, cols : 2 * cols],
        grad_a[:block, 2 * cols : 3 * cols],
        grad_a[:block, 3 * cols :].T,
        d_rel_here,
        gain_one,
        own_f[0],
        own_f[1].T,
        gain_two,
        grad_gain_final,
        grad_project,
    )


def solution(mesh):
    placed = (
        P("dp", None),
        P("dp", None),
        P(),
        P(None, "tp"),
        P(None, "tp"),
        P(None, "tp"),
        P("tp", None),
        P(None, "tp"),
        P(),
        P(None, "tp"),
        P("tp", None),
        P(),
        P(),
        P(),
    )
    return jax.shard_map(
        functools.partial(shards, mesh.shape["dp"], mesh.shape["tp"]),
        mesh=mesh,
        in_specs=placed,
        out_specs=(
            P("dp", None),
            P("dp", None),
            P("dp", "tp"),
            P("dp", "tp"),
            P("dp", "tp"),
            P("tp", "dp"),
            P(None, "tp"),
            P("dp"),
            P("dp", "tp"),
            P("tp", "dp"),
            P("dp"),
            P("dp"),
            P("dp", None),
        ),
        check_vma=False,
    )
```
